32 devices in a mesh: wide: 8 (over z, x), narrow: 4 (over y, core).
Axes of the slice: x: 2, y: 2, z: 4, core: 2. Of those that a mesh axis runs over, the one named last changes fastest.
Arguments:
- image_feats: bfloat16 [1536, 1152], P(('wide', 'narrow')), may hold values from -400 to 400
- proj_weight: bfloat16 [1152, 1152], replicated, may hold values from -0.1875 to 0.1875
- text_embed: bfloat16 [1536, 1152], P(('wide', 'narrow')), may hold values from -400 to 400
- log_scale: float32 [1], replicated, may hold values from 1.6 to 2.4
- logit_bias: float32 [1], replicated, may hold values from -7 to -4
Outputs:
- image_loss: float32 [1536], P(('wide', 'narrow'))
- d_text_unit: float32 [1536, 1152], P(('wide', 'narrow'))
- d_proj: float32 [1152, 1152], P('wide', 'narrow')
The draws below stay inside these ranges and needn't reach their ends.
All inputs are finite; a program needn't handle non-finite values.
Results may differ from the reference program's by a relative error of at most 0.0037.
Values may be sent and summed in bfloat16 or wider, within the bound.
No kernel may reach another device: no remote copies, remote signals or barrier semaphores. Data moves between devices by JAX's collectives and lax.ppermute only.
A program may use at most 64 MiB of HBM per device.

```python
import math
import jax
import jax.numpy as jnp
from jax import lax

D = 1152
BATCH = 1536


def scale_factors(key):
    row_key, col_key = jax.random.split(key, 2)
    row_scale = jnp.exp(jax.random.uniform(row_key, (BATCH, 1), jnp.float32) * math.log(10.0))
    col_scale = jnp.exp(jax.random.uniform(col_key, (1, D), jnp.float32) * math.log(10.0))
    return row_scale * col_scale


def draw_image_feats(key, part):
    inner = jax.random.fold_in(key, 11)
    scale_key, noise_key = jax.random.split(inner, 2)
    factors = scale_factors(scale_key)
    noise = jax.random.truncated_normal(noise_key, -4.0, 4.0, (BATCH, D), jnp.float32)
    return (factors * noise).astype(jnp.bfloat16)


def draw_text_embed(key, part):
    inner = jax.random.fold_in(key, 23)
    scale_key, noise_key = jax.random.split(inner, 2)
    factors = scale_factors(scale_key)
    noise = jax.random.truncated_normal(noise_key, -4.0, 4.0, (BATCH, D), jnp.float32)
    return (factors * noise).astype(jnp.bfloat16)


def gaussian(stream_key, dims, spread, most, kind=jnp.bfloat16):
    return jnp.clip(spread * jax.random.normal(stream_key, dims, jnp.float32), -most, most).astype(kind)


def setup_inputs(seed: int = 0) -> dict:
    seeds = jax.random.split(jax.random.key(seed), 6)
    image_feats = draw_image_feats(jax.random.fold_in(seeds[5], 71), 0)
    proj_weight = gaussian(seeds[1], (D, D), D ** -0.5, 0.1875)
    text_embed = draw_text_embed(jax.random.fold_in(seeds[5], 71), 0)
    log_scale = jnp.clip(jax.random.uniform(seeds[3], (1,), jnp.float32, 1.6, 2.4), 1.6, 2.4)
    logit_bias = jnp.clip(jax.random.uniform(seeds[4], (1,), jnp.float32, -7.0, -4.0), -7.0, -4.0)
    return dict(image_feats=image_feats, proj_weight=proj_weight, text_embed=text_embed, log_scale=log_scale, logit_bias=logit_bias)


def unit_rows(values):
    inverse = lax.rsqrt(lax.optimization_barrier(jnp.sum(values * values, axis=1, keepdims=True)) + 1e-06)
    return (values * inverse, inverse)

def reference(image_feats, proj_weight, text_embed, log_scale, logit_bias):
    zproj = jnp.dot(image_feats, proj_weight, preferred_element_type=jnp.float32)
    img_unit, img_inv = unit_rows(zproj)
    img_emb = img_unit.astype(jnp.bfloat16)
    txt_unit, txt_inv = unit_rows(text_embed.astype(jnp.float32))
    txt_emb = txt_unit.astype(jnp.bfloat16)
    logit_scale = jnp.exp(log_scale[0])
    logit_shift = logit_bias[0]
    batch_rows = image_feats.shape[0]
    width = image_feats.shape[1]
    block_rows = math.gcd(batch_rows, 512)
    block_total = batch_rows // block_rows
    caption_idx = jnp.arange(batch_rows, dtype=jnp.int32)

    def one_block(caption_grad, block_id):
        row_start = (block_id * block_rows).astype(jnp.int32)
        rows_img = lax.dynamic_slice_in_dim(img_emb, row_start, block_rows, 0)
        products = jnp.dot(rows_img, txt_emb.T, preferred_element_type=jnp.float32)
        logits = logit_scale * products + logit_shift
        image_idx = row_start + jnp.arange(block_rows, dtype=jnp.int32)
        label_sign = jnp.where(image_idx[:, None] == caption_idx[None, :], 1.0, -1.0).astype(logits.dtype)
        loss_rows = lax.optimization_barrier(jnp.sum(jax.nn.softplus(-label_sign * logits), axis=1))
        grad_tile = (-logit_scale * label_sign * jax.nn.sigmoid(-label_sign * logits)).astype(jnp.bfloat16)
        d_img = jnp.dot(grad_tile, txt_emb, preferred_element_type=jnp.float32)
        caption_grad = caption_grad + jnp.dot(grad_tile.T, rows_img, preferred_element_type=jnp.float32)
        return (caption_grad, (loss_rows, d_img))
    start_grad = jnp.zeros((batch_rows, width), jnp.float32)
    caption_grad, (loss_blocks, d_img_blocks) = lax.scan(one_block, start_grad, jnp.arange(block_total, dtype=jnp.int32))
    image_loss = loss_blocks.reshape(batch_rows)
    d_img = d_img_blocks.reshape(batch_rows, width)
    d_zproj = (img_inv * (d_img - img_unit * lax.optimization_barrier(jnp.sum(img_unit * d_img, axis=1, keepdims=True)))).astype(jnp.bfloat16)
    d_proj = jnp.dot(image_feats.T, d_zproj, preferred_element_type=jnp.float32)
    return (image_loss, caption_grad, d_proj)
```

```python
import functools

import jax
import jax.numpy as jnp
from jax import lax
from jax.experimental import pallas as pl
from jax.experimental.pallas import tpu as pltpu
from jax.sharding import PartitionSpec as P

AXES = ("wide", "narrow")
F32 = jnp.float32
BF16 = jnp.bfloat16
LANES = 128
STAT_ROWS = 16
VMEM = pl.BlockSpec(memory_space=pltpu.VMEM)
SMEM = pl.BlockSpec(memory_space=pltpu.SMEM)
NT = (((1,), (1,)), ((), ()))
TN = (((0,), (0,)), ((), ()))
PARAMS = pltpu.CompilerParams(vmem_limit_bytes=40 * 1024 * 1024)


def swapped(value, total, mask):
    return lax.ppermute(value, AXES, [(source, source ^ mask) for source in range(total)])


def split_pair(values):
    high = values.astype(BF16)
    return high, (values - high.astype(F32)).astype(BF16)


def column_block(member, narrow):
    return (member % narrow) * 2 + member // narrow


def pair_kernel(narrow, group, spread, *refs):
    member_ref, log_scale_ref, bias_ref, weight_ref = refs[:4]
    feats = refs[4 : 4 + group]
    texts = refs[4 + group : 4 + group + spread]
    outs = refs[4 + group + spread :]
    feats_out, unit_out, inv_out, emb_out, grad_out, own_out = outs[:6]
    send_out = outs[6 : 5 + group]
    unit_all, text_all, d_all = outs[5 + group :]
    rows, width = feats[0].shape
    images = group * rows
    share = width // group
    member = member_ref[0]

    for step in range(group):
        place = pl.multiple_of((member ^ step) * rows, rows)
        feats_out[pl.ds(place, rows), :] = feats[step][...]
    for start in range(0, images, LANES):
        cols = slice(start, start + LANES)
        proj = jnp.dot(feats_out[cols, :], weight_ref[...], preferred_element_type=F32)
        turned = proj.T
        inverse = lax.rsqrt(jnp.sum(turned * turned, axis=0, keepdims=True) + 1e-06)
        unit = turned * inverse
        inv_out[:, cols] = inverse
        unit_all[:, cols] = unit
        emb_out[:, cols] = unit.astype(BF16)
    block = pl.multiple_of(column_block(member, narrow) * share, share)
    unit_out[...] = unit_all[pl.ds(block, share), :]

    for step in range(spread):
        values = texts[step][...].astype(F32)
        inverse = lax.rsqrt(jnp.sum(values * values, axis=1, keepdims=True) + 1e-06)
        text_all[step * rows : (step + 1) * rows, :] = (values * inverse).astype(BF16)

    scale = jnp.exp(jnp.full((1, 1), log_scale_ref[0], F32))
    shift = bias_ref[0]
    count = 4 * rows if spread % 4 == 0 else rows
    chunks = spread * rows // count

    def one_chunk(chunk, loss_sum, dot_sum, first):
        here = pl.ds(pl.multiple_of(chunk * count, count), count)
        text = text_all[here, :]
        products = jnp.dot(text, emb_out[...], preferred_element_type=F32)
        logits = scale * products + shift
        caption = lax.broadcasted_iota(jnp.int32, (count, images), 0) + chunk * count
        image = lax.broadcasted_iota(jnp.int32, (count, images), 1)
        own = jnp.logical_and(caption < rows, image == member * rows + caption)
        sign = jnp.where(own, 1.0, -1.0).astype(F32)
        away = -sign * logits
        small = jnp.exp(-jnp.abs(away))
        loss = jnp.maximum(away, 0.0) + jnp.log1p(small)
        chance = jnp.where(away >= 0.0, 1.0, small) / (1.0 + small)
        grad = (-scale * sign * chance).astype(BF16)
        grad_out[here, :] = grad
        loss_sum = loss_sum + jnp.sum(loss, axis=0, keepdims=True)
        dot_sum = dot_sum + jnp.sum(grad.astype(F32) * products, axis=0, keepdims=True)
        d_img = lax.dot_general(text, grad, TN, preferred_element_type=F32)
        if first:
            d_all[...] = d_img
        else:
            d_all[...] += d_img
        return loss_sum, dot_sum

    zero = jnp.zeros((1, images), F32)
    sums = one_chunk(0, zero, zero, True)
    if chunks > 1:
        sums = lax.fori_loop(1, chunks, lambda c, s: one_chunk(c, *s, False), sums)
    loss_sum, dot_sum = sums

    own_out[:share, :] = d_all[pl.ds(block, share), :]
    own_out[share : share + 1, :] = loss_sum
    own_out[share + 1 : share + 2, :] = dot_sum
    loss_high, loss_low = split_pair(loss_sum)
    dot_high, dot_low = split_pair(dot_sum)
    row = lax.broadcasted_iota(jnp.int32, (STAT_ROWS, images), 0)
    stats = jnp.zeros((STAT_ROWS, images), F32)
    for place, line in enumerate((loss_high, loss_low, dot_high, dot_low)):
        stats = jnp.where(row == place, line.astype(F32), stats)
    stats = stats.astype(BF16)
    for step in range(1, group):
        part = pl.multiple_of(column_block(member ^ step, narrow) * share, share)
        send_out[step - 1][:share, :] = d_all[pl.ds(part, share), :].astype(BF16)
        send_out[step - 1][share:, :] = stats


def caption_kernel(rows, grad_ref, emb_ref, feats_ref, *outs):
    feats_t, own_out = outs[:2]
    for step in range(len(outs) - 1):
        grad = grad_ref[step * rows : (step + 1) * rows, :]
        product = lax.dot_general(grad, emb_ref[...], NT, preferred_element_type=F32)
        target = outs[1 + step]
        target[...] = product.astype(target.dtype)
    for start in range(0, feats_ref.shape[0], LANES):
        cols = slice(start, start + LANES)
        feats_t[:, cols] = feats_ref[cols, :].astype(F32).T.astype(BF16)


def gathered_gradient(own_ref, got, unit_ref, inv_ref, loss_out):
    share = unit_ref.shape[0]
    total = own_ref[:share, :]
    loss = own_ref[share : share + 1, :]
    along = own_ref[share + 1 : share + 2, :]
    for block in got:
        total = total + block[:share, :].astype(F32)
        stats = block[share:, :].astype(F32)
        loss = loss + (stats[0:1, :] + stats[1:2, :])
        along = along + (stats[2:3, :] + stats[3:4, :])
    loss_out[...] = loss
    return inv_ref[...] * (total - unit_ref[...] * along)


def weight_kernel(group, wide, *refs):
    wide_ref, own_ref = refs[:2]
    got = refs[2 : 1 + group]
    unit_ref, inv_ref, feats_ref, feats_t_ref = refs[1 + group : 5 + group]
    loss_out, own_out = refs[5 + group : 7 + group]
    send_out = refs[7 + group : 6 + group + wide]
    main_all, rest_all = refs[6 + group + wide :]
    share = unit_ref.shape[0]
    rest = share - LANES
    rows = feats_t_ref.shape[0] // wide
    d_zproj = gathered_gradient(own_ref, got, unit_ref, inv_ref, loss_out)
    high, low = split_pair(d_zproj)
    main_all[...] = lax.dot_general(
        feats_t_ref[...], high[:LANES, :], NT, preferred_element_type=F32
    ) + lax.dot_general(feats_t_ref[...], low[:LANES, :], NT, preferred_element_type=F32)
    tail = jnp.dot(high[LANES:, :], feats_ref[...], preferred_element_type=F32) + jnp.dot(
        low[LANES:, :], feats_ref[...], preferred_element_type=F32
    )
    rest_all[...] = jnp.zeros_like(rest_all)
    for place in range(wide):
        begin = place * rows
        rest_all[place, :rest, :] = tail[:, begin : begin + LANES]
        rest_all[place, rest:, : rows - LANES] = tail[:, begin + LANES : begin + rows]
    here = wide_ref[0]
    for step in range(wide):
        place = here ^ step
        begin = pl.multiple_of(place * rows, rows)
        target = own_out if step == 0 else send_out[step - 1]
        target[:rows, :] = main_all[pl.ds(begin, rows), :].astype(target.dtype)
        target[rows:, :] = rest_all[place].astype(target.dtype)


def total_kernel(rest, wide_ref, *refs):
    blocks, out = refs[:-1], refs[-1]
    rows = out.shape[0]
    even = blocks[0][...]
    for block in blocks[2::2]:
        even = even + block[...].astype(F32)
    odd = blocks[1][...].astype(F32)
    for block in blocks[3::2]:
        odd = odd + block[...].astype(F32)
    mine = (wide_ref[0] & 1) == 0
    halves = (jnp.where(mine, even, odd), jnp.where(mine, odd, even))
    for side, half in enumerate(halves):
        left = side * (LANES + rest)
        out[:, left : left + LANES] = half[:rows, :]
        upper = half[rows : rows + rest, :].T
        lower = half[rows + rest :, :].T
        out[:LANES, left + LANES : left + LANES + rest] = upper
        out[LANES:, left + LANES : left + LANES + rest] = lower[: rows - LANES, :]


def sum_kernel(*refs):
    total = refs[0][...]
    for block in refs[1:-1]:
        total = total + block[...].astype(F32)
    refs[-1][...] = total


def local(wide, narrow, image_feats, proj_weight, text_embed, log_scale, logit_bias):
    rows, width = image_feats.shape
    total = wide * narrow
    group = 2 * narrow
    spread = wide // 2
    share = width // group
    images = group * rows
    wide_pos = lax.axis_index("wide").astype(jnp.int32)
    member = (wide_pos & 1) * narrow + lax.axis_index("narrow").astype(jnp.int32)
    wide_pos, member = wide_pos.reshape(1), member.reshape(1)

    feats = [image_feats] + [swapped(image_feats, total, step) for step in range(1, group)]
    texts = [text_embed] + [swapped(text_embed, total, step * group) for step in range(1, spread)]

    sent = jax.ShapeDtypeStruct((share + STAT_ROWS, images), BF16)
    results = pl.pallas_call(
        functools.partial(pair_kernel, narrow, group, spread),
        in_specs=[SMEM] * 3 + [VMEM] * (1 + group + spread),
        out_specs=[VMEM] * (5 + group),
        out_shape=[
            jax.ShapeDtypeStruct((images, width), BF16),
            jax.ShapeDtypeStruct((share, images), F32),
            jax.ShapeDtypeStruct((1, images), F32),
            jax.ShapeDtypeStruct((width, images), BF16),
            jax.ShapeDtypeStruct((spread * rows, images), BF16),
            jax.ShapeDtypeStruct((share + 8, images), F32),
        ]
        + [sent] * (group - 1),
        scratch_shapes=[
            pltpu.VMEM((width, images), F32),
            pltpu.VMEM((spread * rows, width), BF16),
            pltpu.VMEM((width, images), F32),
        ],
        compiler_params=PARAMS,
        name="pairs",
    )(member, log_scale, logit_bias, proj_weight, *feats, *texts)
    all_feats, unit_part, inv_part, img_emb, grad_tile, own_part = results[:6]
    got = [swapped(value, total, step) for step, value in enumerate(results[6:], 1)]

    results = pl.pallas_call(
        functools.partial(caption_kernel, rows),
        in_specs=[VMEM] * 3,
        out_specs=[VMEM] * (1 + spread),
        out_shape=[jax.ShapeDtypeStruct((width, images), BF16), jax.ShapeDtypeStruct((rows, width), F32)]
        + [jax.ShapeDtypeStruct((rows, width), BF16)] * (spread - 1),
        compiler_params=PARAMS,
        name="captions",
    )(grad_tile, img_emb, all_feats)
    feats_t, own_text = results[:2]
    got_text = [swapped(value, total, step * group) for step, value in enumerate(results[2:], 1)]

    out_rows = width // wide
    rest = share - LANES
    packed = out_rows + 2 * rest
    direct = LANES < out_rows <= 2 * LANES and out_rows % 16 == 0 and rest % 16 == 0
    if direct:
        results = pl.pallas_call(
            functools.partial(weight_kernel, group, wide),
            in_specs=[SMEM] + [VMEM] * (4 + group),
            out_specs=[VMEM] * (1 + wide),
            out_shape=[
                jax.ShapeDtypeStruct((1, images), F32),
                jax.ShapeDtypeStruct((packed, LANES), F32),
            ]
            + [jax.ShapeDtypeStruct((packed, LANES), BF16)] * (wide - 1),
            scratch_shapes=[
                pltpu.VMEM((width, LANES), F32),
                pltpu.VMEM((wide, 2 * rest, LANES), F32),
            ],
            compiler_params=PARAMS,
            name="weights",
        )(wide_pos, own_part, *got, unit_part, inv_part, all_feats, feats_t)
        loss_line, own_weight = results[:2]
        got_weight = [swapped(value, total, step * narrow) for step, value in enumerate(results[2:], 1)]
        d_proj = pl.pallas_call(
            functools.partial(total_kernel, rest),
            in_specs=[SMEM] + [VMEM] * wide,
            out_specs=VMEM,
            out_shape=jax.ShapeDtypeStruct((out_rows, 2 * share), F32),
            compiler_params=PARAMS,
            name="weight_total",
        )(wide_pos, own_weight, *got_weight)
    else:

        def gradient_kernel(*refs):
            own_ref, blocks = refs[0], refs[1:group]
            unit_ref, inv_ref, loss_out, d_out = refs[group:]
            d_out[...] = gathered_gradient(own_ref, blocks, unit_ref, inv_ref, loss_out)

        loss_line, d_zproj = pl.pallas_call(
            gradient_kernel,
            in_specs=[VMEM] * (2 + group),
            out_specs=[VMEM] * 2,
            out_shape=[jax.ShapeDtypeStruct((1, images), F32), jax.ShapeDtypeStruct((share, images), F32)],
            compiler_params=PARAMS,
            name="gradient",
        )(own_part, *got, unit_part, inv_part)
        partial = sum(
            lax.dot_general(feats_t, part, NT, preferred_element_type=F32) for part in split_pair(d_zproj)
        )
        left = (wide_pos[0] & 1) == 0
        both = jnp.concatenate([jnp.where(left, partial, 0.0), jnp.where(left, 0.0, partial)], axis=1)
        d_proj = lax.psum_scatter(both, "wide", scatter_dimension=0, tiled=True)

    d_text_unit = pl.pallas_call(
        sum_kernel,
        in_specs=[VMEM] * spread,
        out_specs=VMEM,
        out_shape=jax.ShapeDtypeStruct((rows, width), F32),
        compiler_params=PARAMS,
        name="caption_total",
    )(own_text, *got_text)
    image_loss = lax.dynamic_slice_in_dim(loss_line[0], member[0] * rows, rows, 0)
    return (image_loss, d_text_unit, d_proj)


def solution(mesh):
    placed = (P(AXES, None), P(), P(AXES, None), P(), P())
    return jax.shard_map(
        functools.partial(local, mesh.shape["wide"], mesh.shape["narrow"]),
        mesh=mesh,
        in_specs=placed,
        out_specs=(P(AXES), P(AXES, None), P("wide", "narrow")),
        check_vma=False,
    )
```

```python
import functools

import jax
import jax.numpy as jnp
from jax import lax
from jax.experimental import pallas as pl
from jax.experimental.pallas import tpu as pltpu
from jax.sharding import PartitionSpec as P

AXES = ("outer", "inner", "narrow")
F32 = jnp.float32
BF16 = jnp.bfloat16
LANES = 128
STAT_ROWS = 16
VMEM = pl.BlockSpec(memory_space=pltpu.VMEM)
SMEM = pl.BlockSpec(memory_space=pltpu.SMEM)
NT = (((1,), (1,)), ((), ()))
TN = (((0,), (0,)), ((), ()))
PARAMS = pltpu.CompilerParams(vmem_limit_bytes=40 * 1024 * 1024)


def split_pair(values):
    high = values.astype(BF16)
    return high, (values - high.astype(F32)).astype(BF16)


def column_block(member, narrow):
    return (member % narrow) * 2 + member // narrow


def pair_kernel(
    narrow,
    rows,
    place_ref,
    log_scale_ref,
    bias_ref,
    weight_ref,
    feats_ref,
    texts_ref,
    unit_out,
    inv_out,
    emb_out,
    grad_out,
    send_out,
    unit_all,
    text_all,
    d_all,
):
    images, width = feats_ref.shape
    group, spread = images // rows, texts_ref.shape[0] // rows
    share = width // group
    line, member = place_ref[0], place_ref[1]

    for start in range(0, images, LANES):
        cols = slice(start, start + LANES)
        proj = jnp.dot(feats_ref[cols, :], weight_ref[...], preferred_element_type=F32)
        turned = proj.T
        inverse = lax.rsqrt(jnp.sum(turned * turned, axis=0, keepdims=True) + 1e-06)
        unit = turned * inverse
        inv_out[:, cols] = inverse
        unit_all[:, cols] = unit
        emb_out[:, cols] = unit.astype(BF16)
    block = pl.multiple_of(column_block(member, narrow) * share, share)
    unit_out[...] = unit_all[pl.ds(block, share), :]

    for step in range(spread):
        here = slice(step * rows, (step + 1) * rows)
        values = texts_ref[here, :].astype(F32)
        inverse = lax.rsqrt(jnp.sum(values * values, axis=1, keepdims=True) + 1e-06)
        text_all[here, :] = (values * inverse).astype(BF16)

    scale = jnp.exp(jnp.full((1, 1), log_scale_ref[0], F32))
    shift = bias_ref[0]
    count = 4 * rows if spread % 4 == 0 else rows
    chunks = spread * rows // count

    def one_chunk(chunk, loss_sum, dot_sum, first):
        here = pl.ds(pl.multiple_of(chunk * count, count), count)
        text = text_all[here, :]
        products = jnp.dot(text, emb_out[...], preferred_element_type=F32)
        logits = scale * products + shift
        caption = lax.broadcasted_iota(jnp.int32, (count, images), 0) + (chunk * count - line * rows)
        image = lax.broadcasted_iota(jnp.int32, (count, images), 1)
        here_too = jnp.logical_and(caption >= 0, caption < rows)
        own = jnp.logical_and(here_too, image == member * rows + caption)
        sign = jnp.where(own, 1.0, -1.0).astype(F32)
        away = -sign * logits
        small = jnp.exp(-jnp.abs(away))
        loss = jnp.maximum(away, 0.0) + jnp.log1p(small)
        chance = jnp.where(away >= 0.0, 1.0, small) / (1.0 + small)
        grad = (-scale * sign * chance).astype(BF16)
        grad_out[here, :] = grad
        loss_sum = loss_sum + jnp.sum(loss, axis=0, keepdims=True)
        dot_sum = dot_sum + jnp.sum(grad.astype(F32) * products, axis=0, keepdims=True)
        d_img = lax.dot_general(text, grad, TN, preferred_element_type=F32)
        if first:
            d_all[...] = d_img
        else:
            d_all[...] += d_img
        return loss_sum, dot_sum

    zero = jnp.zeros((1, images), F32)
    sums = one_chunk(0, zero, zero, True)
    if chunks > 1:
        sums = lax.fori_loop(1, chunks, lambda c, s: one_chunk(c, *s, False), sums)
    loss_sum, dot_sum = sums

    loss_high, loss_low = split_pair(loss_sum)
    dot_high, dot_low = split_pair(dot_sum)
    row = lax.broadcasted_iota(jnp.int32, (STAT_ROWS, images), 0)
    stats = jnp.zeros((STAT_ROWS, images), F32)
    for place, line in enumerate((loss_high, loss_low, dot_high, dot_low)):
        stats = jnp.where(row == place, line.astype(F32), stats)
    stats = stats.astype(BF16)
    for place in range(group):
        part = column_block(place, narrow) * share
        send_out[place, :share, :] = d_all[part : part + share, :].astype(BF16)
        send_out[place, share:, :] = stats


def caption_kernel(rows, grad_ref, emb_ref, feats_ref, feats_t, send_out):
    for step in range(send_out.shape[0]):
        grad = grad_ref[step * rows : (step + 1) * rows, :]
        product = lax.dot_general(grad, emb_ref[...], NT, preferred_element_type=F32)
        send_out[step] = product.astype(BF16)
    for start in range(0, feats_ref.shape[0], LANES):
        cols = slice(start, start + LANES)
        feats_t[:, cols] = feats_ref[cols, :].astype(F32).T.astype(BF16)


def gathered_gradient(got_ref, unit_ref, inv_ref, loss_out):
    share = unit_ref.shape[0]
    total = got_ref[0].astype(F32)
    for place in range(1, got_ref.shape[0]):
        total = total + got_ref[place].astype(F32)
    loss_out[...] = total[share : share + 1, :] + total[share + 1 : share + 2, :]
    along = total[share + 2 : share + 3, :] + total[share + 3 : share + 4, :]
    return inv_ref[...] * (total[:share, :] - unit_ref[...] * along)


def weight_kernel(wide, got_ref, unit_ref, inv_ref, feats_ref, feats_t_ref, loss_out, send_out):
    share = unit_ref.shape[0]
    rest = share - LANES
    rows = feats_t_ref.shape[0] // wide
    high, low = split_pair(gathered_gradient(got_ref, unit_ref, inv_ref, loss_out))
    main = lax.dot_general(
        feats_t_ref[...], high[:LANES, :], NT, preferred_element_type=F32
    ) + lax.dot_general(feats_t_ref[...], low[:LANES, :], NT, preferred_element_type=F32)
    tail = jnp.dot(high[LANES:, :], feats_ref[...], preferred_element_type=F32) + jnp.dot(
        low[LANES:, :], feats_ref[...], preferred_element_type=F32
    )
    main, tail = main.astype(BF16), tail.astype(BF16)
    for place in range(wide):
        begin = place * rows
        send_out[place, :rows, :] = main[begin : begin + rows, :]
        send_out[place, rows : rows + rest, :] = tail[:, begin : begin + LANES]
        send_out[place, rows + rest :, :] = jnp.zeros((rest, LANES), BF16)
        send_out[place, rows + rest :, : rows - LANES] = tail[:, begin + LANES : begin + rows]


def total_kernel(rest, got_ref, out):
    rows = out.shape[0]
    for side in range(2):
        half = got_ref[side].astype(F32)
        for place in range(side + 2, got_ref.shape[0], 2):
            half = half + got_ref[place].astype(F32)
        left = side * (LANES + rest)
        out[:, left : left + LANES] = half[:rows, :]
        out[:LANES, left + LANES : left + LANES + rest] = half[rows : rows + rest, :].T
        out[LANES:, left + LANES : left + LANES + rest] = half[rows + rest :, :].T[: rows - LANES, :]


def sum_kernel(got_ref, out):
    total = got_ref[0].astype(F32)
    for place in range(1, got_ref.shape[0]):
        total = total + got_ref[place].astype(F32)
    out[...] = total


def local(wide, narrow, image_feats, proj_weight, text_embed, log_scale, logit_bias):
    rows, width = image_feats.shape
    group = 2 * narrow
    spread = wide // 2
    share = width // group
    images = group * rows
    line = lax.axis_index("outer").astype(jnp.int32)
    member = lax.axis_index(("inner", "narrow")).astype(jnp.int32)

    all_feats = lax.all_gather(image_feats, ("inner", "narrow"), axis=0, tiled=True)
    texts = lax.all_gather(text_embed, "outer", axis=0, tiled=True)

    unit_part, inv_part, img_emb, grad_tile, sent = pl.pallas_call(
        functools.partial(pair_kernel, narrow, rows),
        in_specs=[SMEM] * 3 + [VMEM] * 3,
        out_specs=[VMEM] * 5,
        out_shape=[
            jax.ShapeDtypeStruct((share, images), F32),
            jax.ShapeDtypeStruct((1, images), F32),
            jax.ShapeDtypeStruct((width, images), BF16),
            jax.ShapeDtypeStruct((spread * rows, images), BF16),
            jax.ShapeDtypeStruct((group, share + STAT_ROWS, images), BF16),
        ],
        scratch_shapes=[
            pltpu.VMEM((width, images), F32),
            pltpu.VMEM((spread * rows, width), BF16),
            pltpu.VMEM((width, images), F32),
        ],
        compiler_params=PARAMS,
        name="pairs",
    )(jnp.stack([line, member]), log_scale, logit_bias, proj_weight, all_feats, texts)
    got = lax.all_to_all(sent, ("inner", "narrow"), 0, 0)

    feats_t, sent_text = pl.pallas_call(
        functools.partial(caption_kernel, rows),
        in_specs=[VMEM] * 3,
        out_specs=[VMEM] * 2,
        out_shape=[
            jax.ShapeDtypeStruct((width, images), BF16),
            jax.ShapeDtypeStruct((spread, rows, width), BF16),
        ],
        compiler_params=PARAMS,
        name="captions",
    )(grad_tile, img_emb, all_feats)
    got_text = lax.all_to_all(sent_text, "outer", 0, 0)

    out_rows = width // wide
    rest = share - LANES
    if LANES < out_rows <= 2 * LANES and out_rows % 16 == 0 and rest % 16 == 0:
        loss_line, sent_weight = pl.pallas_call(
            functools.partial(weight_kernel, wide),
            in_specs=[VMEM] * 5,
            out_specs=[VMEM] * 2,
            out_shape=[
                jax.ShapeDtypeStruct((1, images), F32),
                jax.ShapeDtypeStruct((wide, out_rows + 2 * rest, LANES), BF16),
            ],
            compiler_params=PARAMS,
            name="weights",
        )(got, unit_part, inv_part, all_feats, feats_t)
        got_weight = lax.all_to_all(sent_weight, ("outer", "inner"), 0, 0)
        d_proj = pl.pallas_call(
            functools.partial(total_kernel, rest),
            in_specs=[VMEM],
            out_specs=VMEM,
            out_shape=jax.ShapeDtypeStruct((out_rows, 2 * share), F32),
            compiler_params=PARAMS,
            name="weight_total",
        )(got_weight)
    else:

        def gradient_kernel(got_ref, unit_ref, inv_ref, loss_out, d_out):
            d_out[...] = gathered_gradient(got_ref, unit_ref, inv_ref, loss_out)

        loss_line, d_zproj = pl.pallas_call(
            gradient_kernel,
            in_specs=[VMEM] * 3,
            out_specs=[VMEM] * 2,
            out_shape=[jax.ShapeDtypeStruct((1, images), F32), jax.ShapeDtypeStruct((share, images), F32)],
            compiler_params=PARAMS,
            name="gradient",
        )(got, unit_part, inv_part)
        partial = sum(
            lax.dot_general(feats_t, part, NT, preferred_element_type=F32) for part in split_pair(d_zproj)
        )
        left = lax.axis_index("inner") == 0
        both = jnp.concatenate([jnp.where(left, partial, 0.0), jnp.where(left, 0.0, partial)], axis=1)
        d_proj = lax.psum_scatter(both, ("outer", "inner"), scatter_dimension=0, tiled=True)

    d_text_unit = pl.pallas_call(
        sum_kernel,
        in_specs=[VMEM],
        out_specs=VMEM,
        out_shape=jax.ShapeDtypeStruct((rows, width), F32),
        compiler_params=PARAMS,
        name="caption_total",
    )(got_text)
    image_loss = lax.dynamic_slice_in_dim(loss_line[0], member * rows, rows, 0)
    return (image_loss, d_text_unit, d_proj)


def solution(mesh):
    wide, narrow = mesh.shape["wide"], mesh.shape["narrow"]
    cut = jax.sharding.Mesh(mesh.devices.reshape(wide // 2, 2, narrow), AXES)
    placed = (P(AXES, None), P(), P(AXES, None), P(), P())
    return jax.shard_map(
        functools.partial(local, wide, narrow),
        mesh=cut,
        in_specs=placed,
        out_specs=(P(AXES), P(AXES, None), P(AXES[:2], "narrow")),
        check_vma=False,
    )
```

```python
import functools

import jax
import jax.numpy as jnp
from jax import lax
from jax.experimental import pallas as pl
from jax.experimental.pallas import tpu as pltpu
from jax.sharding import PartitionSpec as P

AXES = ("outer", "inner", "narrow")
F32 = jnp.float32
BF16 = jnp.bfloat16
LANES = 128
STAT_ROWS = 16
VMEM = pl.BlockSpec(memory_space=pltpu.VMEM)
SMEM = pl.BlockSpec(memory_space=pltpu.SMEM)
NT = (((1,), (1,)), ((), ()))
TN = (((0,), (0,)), ((), ()))
PARAMS = pltpu.CompilerParams(vmem_limit_bytes=40 * 1024 * 1024)


def swapped(value, total, mask):
    return lax.ppermute(value, AXES, [(source, source ^ mask) for source in range(total)])


def split_pair(values):
    high = values.astype(BF16)
    return high, (values - high.astype(F32)).astype(BF16)


def column_block(member, narrow):
    return (member % narrow) * 2 + member // narrow


def load_kernel(weight_ref, out):
    pltpu.sync_copy(weight_ref, out)


def pair_kernel(narrow, group, spread, *refs):
    member_ref, log_scale_ref, bias_ref, weight_ref, feats_ref = refs[:5]
    texts = refs[5 : 5 + spread]
    outs = refs[5 + spread :]
    unit_out, inv_out, emb_out, grad_out, own_out = outs[:5]
    send_out = outs[5 : 4 + group]
    unit_all, text_all, d_all = outs[4 + group :]
    rows, width = texts[0].shape
    images = group * rows
    share = width // group
    member = member_ref[0]

    for start in range(0, images, LANES):
        cols = slice(start, start + LANES)
        proj = jnp.dot(feats_ref[cols, :], weight_ref[...], preferred_element_type=F32)
        turned = proj.T
        inverse = lax.rsqrt(jnp.sum(turned * turned, axis=0, keepdims=True) + 1e-06)
        unit = turned * inverse
        inv_out[:, cols] = inverse
        unit_all[:, cols] = unit
        emb_out[:, cols] = unit.astype(BF16)
    block = pl.multiple_of(column_block(member, narrow) * share, share)
    unit_out[...] = unit_all[pl.ds(block, share), :]

    for step in range(spread):
        values = texts[step][...].astype(F32)
        inverse = lax.rsqrt(jnp.sum(values * values, axis=1, keepdims=True) + 1e-06)
        text_all[step * rows : (step + 1) * rows, :] = (values * inverse).astype(BF16)

    scale = jnp.exp(jnp.full((1, 1), log_scale_ref[0], F32))
    shift = bias_ref[0]
    count = 4 * rows if spread % 4 == 0 else rows
    chunks = spread * rows // count

    def one_chunk(chunk, loss_sum, dot_sum, first):
        here = pl.ds(pl.multiple_of(chunk * count, count), count)
        text = text_all[here, :]
        products = jnp.dot(text, emb_out[...], preferred_element_type=F32)
        logits = scale * products + shift
        caption = lax.broadcasted_iota(jnp.int32, (count, images), 0) + chunk * count
        image = lax.broadcasted_iota(jnp.int32, (count, images), 1)
        own = jnp.logical_and(caption < rows, image == member * rows + caption)
        sign = jnp.where(own, 1.0, -1.0).astype(F32)
        away = -sign * logits
        small = jnp.exp(-jnp.abs(away))
        loss = jnp.maximum(away, 0.0) + jnp.log1p(small)
        chance = jnp.where(away >= 0.0, 1.0, small) / (1.0 + small)
        grad = (-scale * sign * chance).astype(BF16)
        grad_out[here, :] = grad
        loss_sum = loss_sum + jnp.sum(loss, axis=0, keepdims=True)
        dot_sum = dot_sum + jnp.sum(grad.astype(F32) * products, axis=0, keepdims=True)
        d_img = lax.dot_general(text, grad, TN, preferred_element_type=F32)
        if first:
            d_all[...] = d_img
        else:
            d_all[...] += d_img
        return loss_sum, dot_sum

    zero = jnp.zeros((1, images), F32)
    sums = one_chunk(0, zero, zero, True)
    if chunks > 1:
        sums = lax.fori_loop(1, chunks, lambda c, s: one_chunk(c, *s, False), sums)
    loss_sum, dot_sum = sums

    own_out[:share, :] = d_all[pl.ds(block, share), :]
    own_out[share : share + 1, :] = loss_sum
    own_out[share + 1 : share + 2, :] = dot_sum
    loss_high, loss_low = split_pair(loss_sum)
    dot_high, dot_low = split_pair(dot_sum)
    row = lax.broadcasted_iota(jnp.int32, (STAT_ROWS, images), 0)
    stats = jnp.zeros((STAT_ROWS, images), F32)
    for place, line in enumerate((loss_high, loss_low, dot_high, dot_low)):
        stats = jnp.where(row == place, line.astype(F32), stats)
    stats = stats.astype(BF16)
    for step in range(1, group):
        part = pl.multiple_of(column_block(member ^ step, narrow) * share, share)
        send_out[step - 1][:share, :] = d_all[pl.ds(part, share), :].astype(BF16)
        send_out[step - 1][share:, :] = stats


def caption_kernel(rows, grad_ref, emb_ref, feats_ref, *outs):
    feats_t, own_out = outs[:2]
    for step in range(len(outs) - 1):
        grad = grad_ref[step * rows : (step + 1) * rows, :]
        product = lax.dot_general(grad, emb_ref[...], NT, preferred_element_type=F32)
        target = outs[1 + step]
        target[...] = product.astype(target.dtype)
    for start in range(0, feats_ref.shape[0], LANES):
        cols = slice(start, start + LANES)
        feats_t[:, cols] = feats_ref[cols, :].astype(F32).T.astype(BF16)


def gathered_gradient(own_ref, got, unit_ref, inv_ref, loss_out):
    share = unit_ref.shape[0]
    total = own_ref[:share, :]
    loss = own_ref[share : share + 1, :]
    along = own_ref[share + 1 : share + 2, :]
    for block in got:
        total = total + block[:share, :].astype(F32)
        stats = block[share:, :].astype(F32)
        loss = loss + (stats[0:1, :] + stats[1:2, :])
        along = along + (stats[2:3, :] + stats[3:4, :])
    loss_out[...] = loss
    return inv_ref[...] * (total - unit_ref[...] * along)


def weight_kernel(group, wide, *refs):
    wide_ref, own_ref = refs[:2]
    got = refs[2 : 1 + group]
    unit_ref, inv_ref, feats_ref, feats_t_ref = refs[1 + group : 5 + group]
    loss_out, own_out = refs[5 + group : 7 + group]
    send_out = refs[7 + group : 6 + group + wide]
    main_all, rest_all = refs[6 + group + wide :]
    share = unit_ref.shape[0]
    rest = share - LANES
    rows = feats_t_ref.shape[0] // wide
    d_zproj = gathered_gradient(own_ref, got, unit_ref, inv_ref, loss_out)
    high, low = split_pair(d_zproj)
    main_all[...] = lax.dot_general(
        feats_t_ref[...], high[:LANES, :], NT, preferred_element_type=F32
    ) + lax.dot_general(feats_t_ref[...], low[:LANES, :], NT, preferred_element_type=F32)
    tail = jnp.dot(high[LANES:, :], feats_ref[...], preferred_element_type=F32) + jnp.dot(
        low[LANES:, :], feats_ref[...], preferred_element_type=F32
    )
    rest_all[...] = jnp.zeros_like(rest_all)
    for place in range(wide):
        begin = place * rows
        rest_all[place, :rest, :] = tail[:, begin : begin + LANES]
        rest_all[place, rest:, : rows - LANES] = tail[:, begin + LANES : begin + rows]
    here = wide_ref[0]
    for step in range(wide):
        place = here ^ step
        begin = pl.multiple_of(place * rows, rows)
        target = own_out if step == 0 else send_out[step - 1]
        target[:rows, :] = main_all[pl.ds(begin, rows), :].astype(target.dtype)
        target[rows:, :] = rest_all[place].astype(target.dtype)


def total_kernel(rest, wide_ref, *refs):
    blocks, out = refs[:-1], refs[-1]
    rows = out.shape[0]
    even = blocks[0][...]
    for block in blocks[2::2]:
        even = even + block[...].astype(F32)
    odd = blocks[1][...].astype(F32)
    for block in blocks[3::2]:
        odd = odd + block[...].astype(F32)
    mine = (wide_ref[0] & 1) == 0
    halves = (jnp.where(mine, even, odd), jnp.where(mine, odd, even))
    for side, half in enumerate(halves):
        left = side * (LANES + rest)
        out[:, left : left + LANES] = half[:rows, :]
        upper = half[rows : rows + rest, :].T
        lower = half[rows + rest :, :].T
        out[:LANES, left + LANES : left + LANES + rest] = upper
        out[LANES:, left + LANES : left + LANES + rest] = lower[: rows - LANES, :]


def sum_kernel(*refs):
    total = refs[0][...]
    for block in refs[1:-1]:
        total = total + block[...].astype(F32)
    refs[-1][...] = total


def local(wide, narrow, image_feats, proj_weight, text_embed, log_scale, logit_bias):
    rows, width = image_feats.shape
    total = wide * narrow
    group = 2 * narrow
    spread = wide // 2
    share = width // group
    images = group * rows
    wide_pos = lax.axis_index(AXES[:2]).astype(jnp.int32)
    member = lax.axis_index(AXES[1:]).astype(jnp.int32)
    wide_pos, member = wide_pos.reshape(1), member.reshape(1)

    texts = [text_embed] + [swapped(text_embed, total, step * group) for step in range(1, spread)]

    all_feats = lax.all_gather(image_feats, AXES[1:], axis=0, tiled=True)
    weight = pl.pallas_call(
        load_kernel,
        in_specs=[pl.BlockSpec(memory_space=pl.ANY)],
        out_specs=VMEM,
        out_shape=jax.ShapeDtypeStruct((width, width), BF16),
        compiler_params=PARAMS,
        name="load_weight",
    )(proj_weight)

    sent = jax.ShapeDtypeStruct((share + STAT_ROWS, images), BF16)
    results = pl.pallas_call(
        functools.partial(pair_kernel, narrow, group, spread),
        in_specs=[SMEM] * 3 + [VMEM] * (2 + spread),
        out_specs=[VMEM] * (4 + group),
        out_shape=[
            jax.ShapeDtypeStruct((share, images), F32),
            jax.ShapeDtypeStruct((1, images), F32),
            jax.ShapeDtypeStruct((width, images), BF16),
            jax.ShapeDtypeStruct((spread * rows, images), BF16),
            jax.ShapeDtypeStruct((share + 8, images), F32),
        ]
        + [sent] * (group - 1),
        scratch_shapes=[
            pltpu.VMEM((width, images), F32),
            pltpu.VMEM((spread * rows, width), BF16),
            pltpu.VMEM((width, images), F32),
        ],
        compiler_params=PARAMS,
        name="pairs",
    )(member, log_scale, logit_bias, weight, all_feats, *texts)
    unit_part, inv_part, img_emb, grad_tile, own_part = results[:5]
    got = [swapped(value, total, step) for step, value in enumerate(results[5:], 1)]

    results = pl.pallas_call(
        functools.partial(caption_kernel, rows),
        in_specs=[VMEM] * 3,
        out_specs=[VMEM] * (1 + spread),
        out_shape=[jax.ShapeDtypeStruct((width, images), BF16), jax.ShapeDtypeStruct((rows, width), F32)]
        + [jax.ShapeDtypeStruct((rows, width), BF16)] * (spread - 1),
        compiler_params=PARAMS,
        name="captions",
    )(grad_tile, img_emb, all_feats)
    feats_t, own_text = results[:2]
    got_text = [swapped(value, total, step * group) for step, value in enumerate(results[2:], 1)]

    out_rows = width // wide
    rest = share - LANES
    packed = out_rows + 2 * rest
    direct = LANES < out_rows <= 2 * LANES and out_rows % 16 == 0 and rest % 16 == 0
    if direct:
        results = pl.pallas_call(
            functools.partial(weight_kernel, group, wide),
            in_specs=[SMEM] + [VMEM] * (4 + group),
            out_specs=[VMEM] * (1 + wide),
            out_shape=[
                jax.ShapeDtypeStruct((1, images), F32),
                jax.ShapeDtypeStruct((packed, LANES), F32),
            ]
            + [jax.ShapeDtypeStruct((packed, LANES), BF16)] * (wide - 1),
            scratch_shapes=[
                pltpu.VMEM((width, LANES), F32),
                pltpu.VMEM((wide, 2 * rest, LANES), F32),
            ],
            compiler_params=PARAMS,
            name="weights",
        )(wide_pos, own_part, *got, unit_part, inv_part, all_feats, feats_t)
        loss_line, own_weight = results[:2]
        got_weight = [swapped(value, total, step * narrow) for step, value in enumerate(results[2:], 1)]
        d_proj = pl.pallas_call(
            functools.partial(total_kernel, rest),
            in_specs=[SMEM] + [VMEM] * wide,
            out_specs=VMEM,
            out_shape=jax.ShapeDtypeStruct((out_rows, 2 * share), F32),
            compiler_params=PARAMS,
            name="weight_total",
        )(wide_pos, own_weight, *got_weight)
    else:

        def gradient_kernel(*refs):
            own_ref, blocks = refs[0], refs[1:group]
            unit_ref, inv_ref, loss_out, d_out = refs[group:]
            d_out[...] = gathered_gradient(own_ref, blocks, unit_ref, inv_ref, loss_out)

        loss_line, d_zproj = pl.pallas_call(
            gradient_kernel,
            in_specs=[VMEM] * (2 + group),
            out_specs=[VMEM] * 2,
            out_shape=[jax.ShapeDtypeStruct((1, images), F32), jax.ShapeDtypeStruct((share, images), F32)],
            compiler_params=PARAMS,
            name="gradient",
        )(own_part, *got, unit_part, inv_part)
        partial = sum(
            lax.dot_general(feats_t, part, NT, preferred_element_type=F32) for part in split_pair(d_zproj)
        )
        left = (wide_pos[0] & 1) == 0
        both = jnp.concatenate([jnp.where(left, partial, 0.0), jnp.where(left, 0.0, partial)], axis=1)
        d_proj = lax.psum_scatter(both, AXES[:2], scatter_dimension=0, tiled=True)

    d_text_unit = pl.pallas_call(
        sum_kernel,
        in_specs=[VMEM] * spread,
        out_specs=VMEM,
        out_shape=jax.ShapeDtypeStruct((rows, width), F32),
        compiler_params=PARAMS,
        name="caption_total",
    )(own_text, *got_text)
    image_loss = lax.dynamic_slice_in_dim(loss_line[0], member[0] * rows, rows, 0)
    return (image_loss, d_text_unit, d_proj)


def solution(mesh):
    wide, narrow = mesh.shape["wide"], mesh.shape["narrow"]
    cut = jax.sharding.Mesh(mesh.devices.reshape(wide // 2, 2, narrow), AXES)
    placed = (P(AXES, None), P(), P(AXES, None), P(), P())
    return jax.shard_map(
        functools.partial(local, wide, narrow),
        mesh=cut,
        in_specs=placed,
        out_specs=(P(AXES), P(AXES, None), P(AXES[:2], "narrow")),
        check_vma=False,
    )
```

```python
import functools

import jax
import jax.numpy as jnp
from jax import lax
from jax.experimental import pallas as pl
from jax.experimental.pallas import tpu as pltpu
from jax.sharding import PartitionSpec as P

AXES = ("outer", "inner", "narrow")
F32 = jnp.float32
BF16 = jnp.bfloat16
LANES = 128
STAT_ROWS = 16
VMEM = pl.BlockSpec(memory_space=pltpu.VMEM)
SMEM = pl.BlockSpec(memory_space=pltpu.SMEM)
NT = (((1,), (1,)), ((), ()))
TN = (((0,), (0,)), ((), ()))
ANY = pl.BlockSpec(memory_space=pl.ANY)
MIB = 1024 * 1024


def limit(mebibytes):
    return pltpu.CompilerParams(vmem_limit_bytes=mebibytes * MIB)


def swapped(value, total, mask):
    return lax.ppermute(value, AXES, [(source, source ^ mask) for source in range(total)])


def split_pair(values):
    high = values.astype(BF16)
    return high, (values - high.astype(F32)).astype(BF16)


def column_block(member, narrow):
    return (member % narrow) * 2 + member // narrow


def pair_kernel(narrow, group, spread, *refs):
    member_ref, log_scale_ref, bias_ref, weight_ref, feats_ref = refs[:5]
    texts = refs[5 : 5 + spread]
    outs = refs[5 + spread :]
    unit_out, inv_out, emb_out, grad_out, own_out = outs[:5]
    send_out = outs[5 : 4 + group]
    unit_all, text_all, d_all, weight, own_text, sems = outs[4 + group :]
    rows, width = texts[0].shape
    images = group * rows
    share = width // group
    member = member_ref[0]
    text_copy = pltpu.make_async_copy(texts[0], own_text, sems.at[0])
    weight_copy = pltpu.make_async_copy(weight_ref, weight, sems.at[1])
    text_copy.start()
    weight_copy.start()

    for step in [*range(1, spread), 0]:
        if step == 0:
            text_copy.wait()
        values = (texts[step] if step else own_text)[...].astype(F32)
        inverse = lax.rsqrt(jnp.sum(values * values, axis=1, keepdims=True) + 1e-06)
        text_all[step * rows : (step + 1) * rows, :] = (values * inverse).astype(BF16)

    weight_copy.wait()
    for start in range(0, images, LANES):
        cols = slice(start, start + LANES)
        proj = jnp.dot(feats_ref[cols, :], weight[...], preferred_element_type=F32)
        turned = proj.T
        inverse = lax.rsqrt(jnp.sum(turned * turned, axis=0, keepdims=True) + 1e-06)
        unit = turned * inverse
        inv_out[:, cols] = inverse
        unit_all[:, cols] = unit
        emb_out[:, cols] = unit.astype(BF16)
    block = pl.multiple_of(column_block(member, narrow) * share, share)
    unit_out[...] = unit_all[pl.ds(block, share), :]

    scale = jnp.exp(jnp.full((1, 1), log_scale_ref[0], F32))
    shift = bias_ref[0]
    count = 4 * rows if spread % 4 == 0 else rows
    chunks = spread * rows // count

    def one_chunk(chunk, loss_sum, dot_sum, first):
        here = pl.ds(pl.multiple_of(chunk * count, count), count)
        text = text_all[here, :]
        products = jnp.dot(text, emb_out[...], preferred_element_type=F32)
        logits = scale * products + shift
        caption = lax.broadcasted_iota(jnp.int32, (count, images), 0) + chunk * count
        image = lax.broadcasted_iota(jnp.int32, (count, images), 1)
        own = jnp.logical_and(caption < rows, image == member * rows + caption)
        sign = jnp.where(own, 1.0, -1.0).astype(F32)
        away = -sign * logits
        small = jnp.exp(-jnp.abs(away))
        loss = jnp.maximum(away, 0.0) + jnp.log1p(small)
        chance = jnp.where(away >= 0.0, 1.0, small) / (1.0 + small)
        grad = (-scale * sign * chance).astype(BF16)
        grad_out[here, :] = grad
        loss_sum = loss_sum + jnp.sum(loss, axis=0, keepdims=True)
        dot_sum = dot_sum + jnp.sum(grad.astype(F32) * products, axis=0, keepdims=True)
        d_img = lax.dot_general(text, grad, TN, preferred_element_type=F32)
        if first:
            d_all[...] = d_img
        else:
            d_all[...] += d_img
        return loss_sum, dot_sum

    zero = jnp.zeros((1, images), F32)
    sums = one_chunk(0, zero, zero, True)
    if chunks > 1:
        sums = lax.fori_loop(1, chunks, lambda c, s: one_chunk(c, *s, False), sums)
    loss_sum, dot_sum = sums

    own_out[:share, :] = d_all[pl.ds(block, share), :]
    own_out[share : share + 1, :] = loss_sum
    own_out[share + 1 : share + 2, :] = dot_sum
    loss_high, loss_low = split_pair(loss_sum)
    dot_high, dot_low = split_pair(dot_sum)
    row = lax.broadcasted_iota(jnp.int32, (STAT_ROWS, images), 0)
    stats = jnp.zeros((STAT_ROWS, images), F32)
    for place, line in enumerate((loss_high, loss_low, dot_high, dot_low)):
        stats = jnp.where(row == place, line.astype(F32), stats)
    stats = stats.astype(BF16)
    for step in range(1, group):
        part = pl.multiple_of(column_block(member ^ step, narrow) * share, share)
        send_out[step - 1][:share, :] = d_all[pl.ds(part, share), :].astype(BF16)
        send_out[step - 1][share:, :] = stats


def caption_kernel(rows, grad_ref, emb_ref, feats_ref, *outs):
    feats_t, own_out = outs[:2]
    for step in range(len(outs) - 1):
        grad = grad_ref[step * rows : (step + 1) * rows, :]
        product = lax.dot_general(grad, emb_ref[...], NT, preferred_element_type=F32)
        target = outs[1 + step]
        target[...] = product.astype(target.dtype)
    for start in range(0, feats_ref.shape[0], LANES):
        cols = slice(start, start + LANES)
        feats_t[:, cols] = feats_ref[cols, :].astype(F32).T.astype(BF16)


def gathered_gradient(own_ref, got, unit_ref, inv_ref, loss_out):
    share = unit_ref.shape[0]
    total = own_ref[:share, :]
    loss = own_ref[share : share + 1, :]
    along = own_ref[share + 1 : share + 2, :]
    for block in got:
        total = total + block[:share, :].astype(F32)
        stats = block[share:, :].astype(F32)
        loss = loss + (stats[0:1, :] + stats[1:2, :])
        along = along + (stats[2:3, :] + stats[3:4, :])
    loss_out[...] = loss
    return inv_ref[...] * (total - unit_ref[...] * along)


def weight_kernel(group, wide, *refs):
    own_ref = refs[0]
    got = refs[1:group]
    unit_ref, inv_ref, feats_ref, feats_t_ref, loss_out, send_out = refs[group:]
    share = unit_ref.shape[0]
    rest = share - LANES
    rows = feats_t_ref.shape[0] // wide
    high, low = split_pair(gathered_gradient(own_ref, got, unit_ref, inv_ref, loss_out))
    main = lax.dot_general(
        feats_t_ref[...], high[:LANES, :], NT, preferred_element_type=F32
    ) + lax.dot_general(feats_t_ref[...], low[:LANES, :], NT, preferred_element_type=F32)
    tail = jnp.dot(high[LANES:, :], feats_ref[...], preferred_element_type=F32) + jnp.dot(
        low[LANES:, :], feats_ref[...], preferred_element_type=F32
    )
    main, tail = main.astype(BF16), tail.astype(BF16)
    for place in range(wide):
        begin = place * rows
        send_out[place, :rows, :] = main[begin : begin + rows, :]
        send_out[place, rows : rows + rest, :] = tail[:, begin : begin + LANES]
        send_out[place, rows + rest :, :] = jnp.zeros((rest, LANES), BF16)
        send_out[place, rows + rest :, : rows - LANES] = tail[:, begin + LANES : begin + rows]


def total_kernel(rest, got_ref, out):
    rows = out.shape[0]
    for side in range(2):
        half = got_ref[side].astype(F32)
        for place in range(side + 2, got_ref.shape[0], 2):
            half = half + got_ref[place].astype(F32)
        left = side * (LANES + rest)
        out[:, left : left + LANES] = half[:rows, :]
        out[:LANES, left + LANES : left + LANES + rest] = half[rows : rows + rest, :].T
        out[LANES:, left + LANES : left + LANES + rest] = half[rows + rest :, :].T[: rows - LANES, :]


def sum_kernel(*refs):
    total = refs[0][...]
    for block in refs[1:-1]:
        total = total + block[...].astype(F32)
    refs[-1][...] = total


def local(wide, narrow, image_feats, proj_weight, text_embed, log_scale, logit_bias):
    rows, width = image_feats.shape
    total = wide * narrow
    group = 2 * narrow
    spread = wide // 2
    share = width // group
    images = group * rows
    member = lax.axis_index(AXES[1:]).astype(jnp.int32).reshape(1)

    texts = [text_embed] + [swapped(text_embed, total, step * group) for step in range(1, spread)]

    all_feats = lax.all_gather(image_feats, AXES[1:], axis=0, tiled=True)
    sent = jax.ShapeDtypeStruct((share + STAT_ROWS, images), BF16)
    results = pl.pallas_call(
        functools.partial(pair_kernel, narrow, group, spread),
        in_specs=[SMEM] * 3 + [ANY, VMEM, ANY] + [VMEM] * (spread - 1),
        out_specs=[VMEM] * (4 + group),
        out_shape=[
            jax.ShapeDtypeStruct((share, images), F32),
            jax.ShapeDtypeStruct((1, images), F32),
            jax.ShapeDtypeStruct((width, images), BF16),
            jax.ShapeDtypeStruct((spread * rows, images), BF16),
            jax.ShapeDtypeStruct((share + 8, images), F32),
        ]
        + [sent] * (group - 1),
        scratch_shapes=[
            pltpu.VMEM((width, images), F32),
            pltpu.VMEM((spread * rows, width), BF16),
            pltpu.VMEM((width, images), F32),
            pltpu.VMEM((width, width), BF16),
            pltpu.VMEM((rows, width), BF16),
            pltpu.SemaphoreType.DMA((2,)),
        ],
        compiler_params=limit(24 if spread <= 4 else 40),
        name="pairs",
    )(member, log_scale, logit_bias, proj_weight, all_feats, *texts)
    unit_part, inv_part, img_emb, grad_tile, own_part = results[:5]
    got = [swapped(value, total, step) for step, value in enumerate(results[5:], 1)]

    results = pl.pallas_call(
        functools.partial(caption_kernel, rows),
        in_specs=[VMEM] * 3,
        out_specs=[VMEM] * (1 + spread),
        out_shape=[jax.ShapeDtypeStruct((width, images), BF16), jax.ShapeDtypeStruct((rows, width), F32)]
        + [jax.ShapeDtypeStruct((rows, width), BF16)] * (spread - 1),
        compiler_params=limit(12 if spread <= 4 else 24),
        name="captions",
    )(grad_tile, img_emb, all_feats)
    feats_t, own_text = results[:2]
    got_text = [swapped(value, total, step * group) for step, value in enumerate(results[2:], 1)]

    out_rows = width // wide
    rest = share - LANES
    packed = out_rows + 2 * rest
    direct = LANES < out_rows <= 2 * LANES and out_rows % 16 == 0 and rest % 16 == 0
    if direct:
        loss_line, sent_weight = pl.pallas_call(
            functools.partial(weight_kernel, group, wide),
            in_specs=[VMEM] * (4 + group),
            out_specs=[VMEM] * 2,
            out_shape=[
                jax.ShapeDtypeStruct((1, images), F32),
                jax.ShapeDtypeStruct((wide, packed, LANES), BF16),
            ],
            compiler_params=limit(12),
            name="weights",
        )(own_part, *got, unit_part, inv_part, all_feats, feats_t)
        got_weight = lax.all_to_all(sent_weight, AXES[:2], 0, 0)
        d_proj = pl.pallas_call(
            functools.partial(total_kernel, rest),
            in_specs=[VMEM],
            out_specs=VMEM,
            out_shape=jax.ShapeDtypeStruct((out_rows, 2 * share), F32),
            compiler_params=limit(4),
            name="weight_total",
        )(got_weight)
    else:

        def gradient_kernel(*refs):
            own_ref, blocks = refs[0], refs[1:group]
            unit_ref, inv_ref, loss_out, d_out = refs[group:]
            d_out[...] = gathered_gradient(own_ref, blocks, unit_ref, inv_ref, loss_out)

        loss_line, d_zproj = pl.pallas_call(
            gradient_kernel,
            in_specs=[VMEM] * (2 + group),
            out_specs=[VMEM] * 2,
            out_shape=[jax.ShapeDtypeStruct((1, images), F32), jax.ShapeDtypeStruct((share, images), F32)],
            compiler_params=limit(12),
            name="gradient",
        )(own_part, *got, unit_part, inv_part)
        partial = sum(
            lax.dot_general(feats_t, part, NT, preferred_element_type=F32) for part in split_pair(d_zproj)
        )
        left = lax.axis_index("inner") == 0
        both = jnp.concatenate([jnp.where(left, partial, 0.0), jnp.where(left, 0.0, partial)], axis=1)
        d_proj = lax.psum_scatter(both, AXES[:2], scatter_dimension=0, tiled=True)

    d_text_unit = pl.pallas_call(
        sum_kernel,
        in_specs=[VMEM] * spread,
        out_specs=VMEM,
        out_shape=jax.ShapeDtypeStruct((rows, width), F32),
        compiler_params=limit(4 if spread <= 4 else 12),
        name="caption_total",
    )(own_text, *got_text)
    image_loss = lax.dynamic_slice_in_dim(loss_line[0], member[0] * rows, rows, 0)
    return (image_loss, d_text_unit, d_proj)


def solution(mesh):
    wide, narrow = mesh.shape["wide"], mesh.shape["narrow"]
    cut = jax.sharding.Mesh(mesh.devices.reshape(wide // 2, 2, narrow), AXES)
    placed = (P(AXES, None), P(), P(AXES, None), P(), P())
    return jax.shard_map(
        functools.partial(local, wide, narrow),
        mesh=cut,
        in_specs=placed,
        out_specs=(P(AXES), P(AXES, None), P(AXES[:2], "narrow")),
        check_vma=False,
    )
```

```python
import functools

import jax
import jax.numpy as jnp
from jax import lax
from jax.experimental import pallas as pl
from jax.experimental.pallas import tpu as pltpu
from jax.sharding import PartitionSpec as P

AXES = ("outer", "inner", "narrow")
F32 = jnp.float32
BF16 = jnp.bfloat16
LANES = 128
STAT_ROWS = 16
VMEM = pl.BlockSpec(memory_space=pltpu.VMEM)
SMEM = pl.BlockSpec(memory_space=pltpu.SMEM)
NT = (((1,), (1,)), ((), ()))
TN = (((0,), (0,)), ((), ()))
HBM = pl.BlockSpec(memory_space=pltpu.HBM)
MIB = 1024 * 1024


def limit(mebibytes):
    return pltpu.CompilerParams(vmem_limit_bytes=mebibytes * MIB)


def swapped(value, total, mask):
    return lax.ppermute(value, AXES, [(source, source ^ mask) for source in range(total)])


def split_pair(values):
    high = values.astype(BF16)
    return high, (values - high.astype(F32)).astype(BF16)


def stat_rows(loss, along):
    row = lax.broadcasted_iota(jnp.int32, (STAT_ROWS, loss.shape[1]), 0)
    stats = jnp.zeros(row.shape, F32)
    for place, line in enumerate(split_pair(loss) + split_pair(along)):
        stats = jnp.where(row == place, line.astype(F32), stats)
    return stats.astype(BF16)


def stat_sums(stats):
    stats = stats.astype(F32)
    return stats[0:1, :] + stats[1:2, :], stats[2:3, :] + stats[3:4, :]


def column_block(member, narrow):
    return (member % narrow) * 2 + member // narrow


def pair_kernel(narrow, group, spread, *refs):
    member_ref, log_scale_ref, bias_ref, weight_ref, feats_ref = refs[:5]
    texts = refs[5 : 5 + spread]
    outs = refs[5 + spread :]
    unit_out, inv_out, emb_out, grad_out, own_out, send_out = outs[:6]
    unit_all, text_all, d_all, weight, own_text, scalars, sems = outs[6:]
    rows, width = texts[0].shape
    images = group * rows
    share = width // group
    member = member_ref[0]
    text_copy = pltpu.make_async_copy(texts[0], own_text, sems.at[0])
    weight_copy = pltpu.make_async_copy(weight_ref, weight, sems.at[1])
    scale_copy = pltpu.make_async_copy(log_scale_ref, scalars.at[0], sems.at[2])
    bias_copy = pltpu.make_async_copy(bias_ref, scalars.at[1], sems.at[3])
    for copy in (text_copy, scale_copy, bias_copy, weight_copy):
        copy.start()

    for step in [*range(1, spread), 0]:
        if step == 0:
            text_copy.wait()
        values = (texts[step] if step else own_text)[...].astype(F32)
        inverse = lax.rsqrt(jnp.sum(values * values, axis=1, keepdims=True) + 1e-06)
        text_all[step * rows : (step + 1) * rows, :] = (values * inverse).astype(BF16)

    weight_copy.wait()
    for start in range(0, images, LANES):
        cols = slice(start, start + LANES)
        proj = jnp.dot(feats_ref[cols, :], weight[...], preferred_element_type=F32)
        turned = proj.T
        inverse = lax.rsqrt(jnp.sum(turned * turned, axis=0, keepdims=True) + 1e-06)
        unit = turned * inverse
        inv_out[:, cols] = inverse
        unit_all[:, cols] = unit
        emb_out[:, cols] = unit.astype(BF16)
    block = pl.multiple_of(column_block(member, narrow) * share, share)
    unit_out[...] = unit_all[pl.ds(block, share), :]

    scale_copy.wait()
    bias_copy.wait()
    scale = jnp.exp(jnp.full((1, 1), scalars[0, 0], F32))
    shift = scalars[1, 0]
    count = 4 * rows if spread % 4 == 0 else rows
    chunks = spread * rows // count

    def one_chunk(chunk, loss_sum, dot_sum, first):
        here = pl.ds(pl.multiple_of(chunk * count, count), count)
        text = text_all[here, :]
        products = jnp.dot(text, emb_out[...], preferred_element_type=F32)
        logits = scale * products + shift
        caption = lax.broadcasted_iota(jnp.int32, (count, images), 0) + chunk * count
        image = lax.broadcasted_iota(jnp.int32, (count, images), 1)
        own = jnp.logical_and(caption < rows, image == member * rows + caption)
        sign = jnp.where(own, 1.0, -1.0).astype(F32)
        away = -sign * logits
        small = jnp.exp(-jnp.abs(away))
        loss = jnp.maximum(away, 0.0) + jnp.log1p(small)
        chance = jnp.where(away >= 0.0, 1.0, small) / (1.0 + small)
        grad = (-scale * sign * chance).astype(BF16)
        grad_out[here, :] = grad
        loss_sum = loss_sum + jnp.sum(loss, axis=0, keepdims=True)
        dot_sum = dot_sum + jnp.sum(grad.astype(F32) * products, axis=0, keepdims=True)
        d_img = lax.dot_general(text, grad, TN, preferred_element_type=F32)
        if first:
            d_all[...] = d_img
        else:
            d_all[...] += d_img
        return loss_sum, dot_sum

    zero = jnp.zeros((1, images), F32)
    sums = one_chunk(0, zero, zero, True)
    if chunks > 1:
        sums = lax.fori_loop(1, chunks, lambda c, s: one_chunk(c, *s, False), sums)
    loss_sum, dot_sum = sums

    stats = stat_rows(loss_sum, dot_sum)
    for index in range(group // 2):
        part = pl.multiple_of(column_block(member ^ (2 * index), narrow) * share, share)
        own_out[index, :share, :] = d_all[pl.ds(part, share), :]
        part = pl.multiple_of(column_block(member ^ (2 * index + 1), narrow) * share, share)
        send_out[index, :share, :] = d_all[pl.ds(part, share), :].astype(BF16)
        send_out[index, share:, :] = stats
    own_out[0, share : share + 1, :] = loss_sum
    own_out[0, share + 1 : share + 2, :] = dot_sum


def chip_kernel(own_ref, got_ref, own_out, *send_out):
    share = own_out.shape[0] - 8
    loss, along = stat_sums(got_ref[0, share:, :])
    loss = loss + own_ref[0, share : share + 1, :]
    along = along + own_ref[0, share + 1 : share + 2, :]
    own_out[:share, :] = own_ref[0, :share, :] + got_ref[0, :share, :].astype(F32)
    own_out[share : share + 1, :] = loss
    own_out[share + 1 : share + 2, :] = along
    stats = stat_rows(loss, along)
    for index, target in enumerate(send_out, 1):
        target[:share, :] = (own_ref[index, :share, :] + got_ref[index, :share, :].astype(F32)).astype(BF16)
        target[share:, :] = stats


def caption_kernel(rows, grad_ref, emb_ref, feats_ref, feats_t, own_out, send_out):
    for step in range(grad_ref.shape[0] // rows):
        grad = grad_ref[step * rows : (step + 1) * rows, :]
        product = lax.dot_general(grad, emb_ref[...], NT, preferred_element_type=F32)
        target = send_out if step & 1 else own_out
        target[step // 2] = product.astype(target.dtype)
    for start in range(0, feats_ref.shape[0], LANES):
        cols = slice(start, start + LANES)
        feats_t[:, cols] = feats_ref[cols, :].astype(F32).T.astype(BF16)


def halving_kernel(own_ref, got_ref, own_out, send_out):
    for step in range(own_ref.shape[0]):
        total = own_ref[step] + got_ref[step].astype(F32)
        target = send_out if step & 1 else own_out
        target[step // 2] = total.astype(target.dtype)


def gathered_gradient(own_ref, got, unit_ref, inv_ref, loss_out):
    share = unit_ref.shape[0]
    total = own_ref[:share, :]
    loss = own_ref[share : share + 1, :]
    along = own_ref[share + 1 : share + 2, :]
    for block in got:
        total = total + block[:share, :].astype(F32)
        more_loss, more_along = stat_sums(block[share:, :])
        loss = loss + more_loss
        along = along + more_along
    loss_out[...] = loss
    return inv_ref[...] * (total - unit_ref[...] * along)


def weight_kernel(group, wide, *refs):
    own_ref = refs[0]
    got = refs[1 : group // 2]
    unit_ref, inv_ref, feats_ref, feats_t_ref, loss_out, send_out = refs[group // 2 :]
    share = unit_ref.shape[0]
    rest = share - LANES
    rows = feats_t_ref.shape[0] // wide
    high, low = split_pair(gathered_gradient(own_ref, got, unit_ref, inv_ref, loss_out))
    main = lax.dot_general(
        feats_t_ref[...], high[:LANES, :], NT, preferred_element_type=F32
    ) + lax.dot_general(feats_t_ref[...], low[:LANES, :], NT, preferred_element_type=F32)
    tail = jnp.dot(high[LANES:, :], feats_ref[...], preferred_element_type=F32) + jnp.dot(
        low[LANES:, :], feats_ref[...], preferred_element_type=F32
    )
    main, tail = main.astype(BF16), tail.astype(BF16)
    for place in range(wide):
        begin = place * rows
        send_out[place, :rows, :] = main[begin : begin + rows, :]
        send_out[place, rows : rows + rest, :] = tail[:, begin : begin + LANES]
        send_out[place, rows + rest :, :] = jnp.zeros((rest, LANES), BF16)
        send_out[place, rows + rest :, : rows - LANES] = tail[:, begin + LANES : begin + rows]


def total_kernel(rest, got_ref, out):
    rows = out.shape[0]
    for side in range(2):
        half = got_ref[side].astype(F32)
        for place in range(side + 2, got_ref.shape[0], 2):
            half = half + got_ref[place].astype(F32)
        left = side * (LANES + rest)
        out[:, left : left + LANES] = half[:rows, :]
        out[:LANES, left + LANES : left + LANES + rest] = half[rows : rows + rest, :].T
        out[LANES:, left + LANES : left + LANES + rest] = half[rows + rest :, :].T[: rows - LANES, :]


def sum_kernel(own_ref, got_ref, out):
    out[...] = own_ref[0] + got_ref[0].astype(F32)


def local(wide, narrow, image_feats, proj_weight, text_embed, log_scale, logit_bias):
    rows, width = image_feats.shape
    total = wide * narrow
    group = 2 * narrow
    spread = wide // 2
    share = width // group
    images = group * rows
    member = lax.axis_index(AXES[1:]).astype(jnp.int32).reshape(1)

    texts = [text_embed] + [swapped(text_embed, total, step * group) for step in range(1, spread)]

    all_feats = lax.all_gather(image_feats, AXES[1:], axis=0, tiled=True)
    results = pl.pallas_call(
        functools.partial(pair_kernel, narrow, group, spread),
        in_specs=[SMEM, HBM, HBM, HBM, VMEM, HBM] + [VMEM] * (spread - 1),
        out_specs=[VMEM] * 6,
        out_shape=[
            jax.ShapeDtypeStruct((share, images), F32),
            jax.ShapeDtypeStruct((1, images), F32),
            jax.ShapeDtypeStruct((width, images), BF16),
            jax.ShapeDtypeStruct((spread * rows, images), BF16),
            jax.ShapeDtypeStruct((group // 2, share + 8, images), F32),
            jax.ShapeDtypeStruct((group // 2, share + STAT_ROWS, images), BF16),
        ],
        scratch_shapes=[
            pltpu.VMEM((width, images), F32),
            pltpu.VMEM((spread * rows, width), BF16),
            pltpu.VMEM((width, images), F32),
            pltpu.VMEM((width, width), BF16),
            pltpu.VMEM((rows, width), BF16),
            pltpu.SMEM((2, 1), F32),
            pltpu.SemaphoreType.DMA((4,)),
        ],
        compiler_params=limit(24 if spread <= 4 else 40),
        name="pairs",
    )(member, log_scale, logit_bias, proj_weight, all_feats, *texts)
    unit_part, inv_part, img_emb, grad_tile, own_part, sent_part = results
    got_part = swapped(sent_part, total, 1)
    feats_t, own_text, sent_text = pl.pallas_call(
        functools.partial(caption_kernel, rows),
        in_specs=[VMEM] * 3,
        out_specs=[VMEM] * 3,
        out_shape=[jax.ShapeDtypeStruct((width, images), BF16)]
        + [jax.ShapeDtypeStruct((spread // 2, rows, width), kind) for kind in (F32, BF16)],
        compiler_params=limit(12 if spread <= 4 else 24),
        name="captions",
    )(grad_tile, img_emb, all_feats)
    own_part, *chip_parts = pl.pallas_call(
        chip_kernel,
        in_specs=[VMEM] * 2,
        out_specs=[VMEM] * (group // 2),
        out_shape=[jax.ShapeDtypeStruct((share + 8, images), F32)]
        + [jax.ShapeDtypeStruct((share + STAT_ROWS, images), BF16)] * (group // 2 - 1),
        compiler_params=limit(12),
        name="chip_sum",
    )(own_part, got_part)
    got = [swapped(value, total, 2 * index) for index, value in enumerate(chip_parts, 1)]

    mask = group
    got_text = swapped(sent_text, total, mask)
    while own_text.shape[0] > 1:
        mask *= 2
        own_text, sent_text = pl.pallas_call(
            halving_kernel,
            in_specs=[VMEM] * 2,
            out_specs=[VMEM] * 2,
            out_shape=[
                jax.ShapeDtypeStruct((own_text.shape[0] // 2, rows, width), kind) for kind in (F32, BF16)
            ],
            compiler_params=limit(6 if spread <= 4 else 24),
            name="caption_half",
        )(own_text, got_text)
        got_text = swapped(sent_text, total, mask)

    out_rows = width // wide
    rest = share - LANES
    packed = out_rows + 2 * rest
    direct = LANES < out_rows <= 2 * LANES and out_rows % 16 == 0 and rest % 16 == 0
    if direct:
        loss_line, sent_weight = pl.pallas_call(
            functools.partial(weight_kernel, group, wide),
            in_specs=[VMEM] * (4 + group // 2),
            out_specs=[VMEM] * 2,
            out_shape=[
                jax.ShapeDtypeStruct((1, images), F32),
                jax.ShapeDtypeStruct((wide, packed, LANES), BF16),
            ],
            compiler_params=limit(12),
            name="weights",
        )(own_part, *got, unit_part, inv_part, all_feats, feats_t)
        got_weight = lax.all_to_all(sent_weight, AXES[:2], 0, 0)
        d_proj = pl.pallas_call(
            functools.partial(total_kernel, rest),
            in_specs=[VMEM],
            out_specs=VMEM,
            out_shape=jax.ShapeDtypeStruct((out_rows, 2 * share), F32),
            compiler_params=limit(4),
            name="weight_total",
        )(got_weight)
    else:

        def gradient_kernel(*refs):
            own_ref, blocks = refs[0], refs[1 : group // 2]
            unit_ref, inv_ref, loss_out, d_out = refs[group // 2 :]
            d_out[...] = gathered_gradient(own_ref, blocks, unit_ref, inv_ref, loss_out)

        loss_line, d_zproj = pl.pallas_call(
            gradient_kernel,
            in_specs=[VMEM] * (2 + group // 2),
            out_specs=[VMEM] * 2,
            out_shape=[jax.ShapeDtypeStruct((1, images), F32), jax.ShapeDtypeStruct((share, images), F32)],
            compiler_params=limit(12),
            name="gradient",
        )(own_part, *got, unit_part, inv_part)
        partial = sum(
            lax.dot_general(feats_t, part, NT, preferred_element_type=F32) for part in split_pair(d_zproj)
        )
        left = lax.axis_index("inner") == 0
        both = jnp.concatenate([jnp.where(left, partial, 0.0), jnp.where(left, 0.0, partial)], axis=1)
        d_proj = lax.psum_scatter(both, AXES[:2], scatter_dimension=0, tiled=True)

    d_text_unit = pl.pallas_call(
        sum_kernel,
        in_specs=[VMEM] * 2,
        out_specs=VMEM,
        out_shape=jax.ShapeDtypeStruct((rows, width), F32),
        compiler_params=limit(4),
        name="caption_total",
    )(own_text, got_text)
    image_loss = lax.dynamic_slice_in_dim(loss_line[0], member[0] * rows, rows, 0)
    return (image_loss, d_text_unit, d_proj)


def solution(mesh):
    wide, narrow = mesh.shape["wide"], mesh.shape["narrow"]
    cut = jax.sharding.Mesh(mesh.devices.reshape(wide // 2, 2, narrow), AXES)
    placed = (P(AXES, None), P(), P(AXES, None), P(), P())
    return jax.shard_map(
        functools.partial(local, wide, narrow),
        mesh=cut,
        in_specs=placed,
        out_specs=(P(AXES), P(AXES, None), P(AXES[:2], "narrow")),
        check_vma=False,
    )
```

```python
import functools

import jax
import jax.numpy as jnp
from jax import lax
from jax.experimental import pallas as pl
from jax.experimental.pallas import tpu as pltpu
from jax.sharding import PartitionSpec as P

AXES = ("outer", "inner", "narrow")
F32 = jnp.float32
BF16 = jnp.bfloat16
LANES = 128
STAT_ROWS = 16
VMEM = pl.BlockSpec(memory_space=pltpu.VMEM)
SMEM = pl.BlockSpec(memory_space=pltpu.SMEM)
NT = (((1,), (1,)), ((), ()))
TN = (((0,), (0,)), ((), ()))
MIB = 1024 * 1024


def limit(mebibytes):
    return pltpu.CompilerParams(vmem_limit_bytes=mebibytes * MIB)


def swapped(value, total, mask):
    return lax.ppermute(value, AXES, [(source, source ^ mask) for source in range(total)])


def split_pair(values):
    high = values.astype(BF16)
    return high, (values - high.astype(F32)).astype(BF16)


def stat_rows(loss, along):
    row = lax.broadcasted_iota(jnp.int32, (STAT_ROWS, loss.shape[1]), 0)
    stats = jnp.zeros(row.shape, F32)
    for place, line in enumerate(split_pair(loss) + split_pair(along)):
        stats = jnp.where(row == place, line.astype(F32), stats)
    return stats.astype(BF16)


def stat_sums(stats):
    stats = stats.astype(F32)
    return stats[0:1, :] + stats[1:2, :], stats[2:3, :] + stats[3:4, :]


def column_block(member, narrow):
    return (member % narrow) * 2 + member // narrow


def pair_kernel(narrow, group, spread, *refs):
    member_ref, log_scale_ref, bias_ref, proj_ref = refs[:4]
    texts = refs[4 : 4 + spread]
    outs = refs[4 + spread :]
    unit_out, inv_out, emb_out, grad_out, own_out, send_out = outs[:6]
    unit_all, text_all, d_all = outs[6:]
    rows, width = texts[0].shape
    images = group * rows
    share = width // group
    member = member_ref[0]

    for step in range(spread):
        values = texts[step][...].astype(F32)
        inverse = lax.rsqrt(jnp.sum(values * values, axis=1, keepdims=True) + 1e-06)
        text_all[step * rows : (step + 1) * rows, :] = (values * inverse).astype(BF16)
    for start in range(0, images, LANES):
        cols = slice(start, start + LANES)
        turned = proj_ref[cols, :].T
        inverse = lax.rsqrt(jnp.sum(turned * turned, axis=0, keepdims=True) + 1e-06)
        unit = turned * inverse
        inv_out[:, cols] = inverse
        unit_all[:, cols] = unit
        emb_out[:, cols] = unit.astype(BF16)
    block = pl.multiple_of(column_block(member, narrow) * share, share)
    unit_out[...] = unit_all[pl.ds(block, share), :]

    scale = jnp.exp(jnp.full((1, 1), log_scale_ref[0], F32))
    shift = bias_ref[0]
    count = 4 * rows if spread % 4 == 0 else rows
    chunks = spread * rows // count

    def one_chunk(chunk, loss_sum, dot_sum, first):
        here = pl.ds(pl.multiple_of(chunk * count, count), count)
        text = text_all[here, :]
        products = jnp.dot(text, emb_out[...], preferred_element_type=F32)
        logits = scale * products + shift
        caption = lax.broadcasted_iota(jnp.int32, (count, images), 0) + chunk * count
        image = lax.broadcasted_iota(jnp.int32, (count, images), 1)
        own = jnp.logical_and(caption < rows, image == member * rows + caption)
        sign = jnp.where(own, 1.0, -1.0).astype(F32)
        away = -sign * logits
        small = jnp.exp(-jnp.abs(away))
        loss = jnp.maximum(away, 0.0) + jnp.log1p(small)
        chance = jnp.where(away >= 0.0, 1.0, small) / (1.0 + small)
        grad = (-scale * sign * chance).astype(BF16)
        grad_out[here, :] = grad
        loss_sum = loss_sum + jnp.sum(loss, axis=0, keepdims=True)
        dot_sum = dot_sum + jnp.sum(grad.astype(F32) * products, axis=0, keepdims=True)
        d_img = lax.dot_general(text, grad, TN, preferred_element_type=F32)
        if first:
            d_all[...] = d_img
        else:
            d_all[...] += d_img
        return loss_sum, dot_sum

    zero = jnp.zeros((1, images), F32)
    sums = one_chunk(0, zero, zero, True)
    if chunks > 1:
        sums = lax.fori_loop(1, chunks, lambda c, s: one_chunk(c, *s, False), sums)
    loss_sum, dot_sum = sums

    stats = stat_rows(loss_sum, dot_sum)
    for index in range(group // 2):
        part = pl.multiple_of(column_block(member ^ (2 * index), narrow) * share, share)
        own_out[index, :share, :] = d_all[pl.ds(part, share), :]
        part = pl.multiple_of(column_block(member ^ (2 * index + 1), narrow) * share, share)
        send_out[index, :share, :] = d_all[pl.ds(part, share), :].astype(BF16)
        send_out[index, share:, :] = stats
    own_out[0, share : share + 1, :] = loss_sum
    own_out[0, share + 1 : share + 2, :] = dot_sum


def chip_kernel(own_ref, got_ref, own_out, *send_out):
    share = own_out.shape[0] - 8
    loss, along = stat_sums(got_ref[0, share:, :])
    loss = loss + own_ref[0, share : share + 1, :]
    along = along + own_ref[0, share + 1 : share + 2, :]
    own_out[:share, :] = own_ref[0, :share, :] + got_ref[0, :share, :].astype(F32)
    own_out[share : share + 1, :] = loss
    own_out[share + 1 : share + 2, :] = along
    stats = stat_rows(loss, along)
    for index, target in enumerate(send_out, 1):
        target[:share, :] = (own_ref[index, :share, :] + got_ref[index, :share, :].astype(F32)).astype(BF16)
        target[share:, :] = stats


def caption_kernel(rows, grad_ref, emb_ref, feats_ref, feats_t, own_out, send_out):
    for step in range(grad_ref.shape[0] // rows):
        grad = grad_ref[step * rows : (step + 1) * rows, :]
        product = lax.dot_general(grad, emb_ref[...], NT, preferred_element_type=F32)
        target = send_out if step & 1 else own_out
        target[step // 2] = product.astype(target.dtype)
    for start in range(0, feats_ref.shape[0], LANES):
        cols = slice(start, start + LANES)
        feats_t[:, cols] = feats_ref[cols, :].astype(F32).T.astype(BF16)


def halving_kernel(own_ref, got_ref, own_out, send_out):
    for step in range(own_ref.shape[0]):
        total = own_ref[step] + got_ref[step].astype(F32)
        target = send_out if step & 1 else own_out
        target[step // 2] = total.astype(target.dtype)


def gathered_gradient(own_ref, got, unit_ref, inv_ref, loss_out):
    share = unit_ref.shape[0]
    total = own_ref[:share, :]
    loss = own_ref[share : share + 1, :]
    along = own_ref[share + 1 : share + 2, :]
    for block in got:
        total = total + block[:share, :].astype(F32)
        more_loss, more_along = stat_sums(block[share:, :])
        loss = loss + more_loss
        along = along + more_along
    loss_out[...] = loss
    return inv_ref[...] * (total - unit_ref[...] * along)


def weight_kernel(group, wide, *refs):
    own_ref = refs[0]
    got = refs[1 : group // 2]
    unit_ref, inv_ref, feats_ref, feats_t_ref, loss_out, send_out = refs[group // 2 :]
    share = unit_ref.shape[0]
    rest = share - LANES
    rows = feats_t_ref.shape[0] // wide
    high, low = split_pair(gathered_gradient(own_ref, got, unit_ref, inv_ref, loss_out))
    main = lax.dot_general(
        feats_t_ref[...], high[:LANES, :], NT, preferred_element_type=F32
    ) + lax.dot_general(feats_t_ref[...], low[:LANES, :], NT, preferred_element_type=F32)
    tail = jnp.dot(high[LANES:, :], feats_ref[...], preferred_element_type=F32) + jnp.dot(
        low[LANES:, :], feats_ref[...], preferred_element_type=F32
    )
    main, tail = main.astype(BF16), tail.astype(BF16)
    for place in range(wide):
        begin = place * rows
        send_out[place, :rows, :] = main[begin : begin + rows, :]
        send_out[place, rows : rows + rest, :] = tail[:, begin : begin + LANES]
        send_out[place, rows + rest :, :] = jnp.zeros((rest, LANES), BF16)
        send_out[place, rows + rest :, : rows - LANES] = tail[:, begin + LANES : begin + rows]


def total_kernel(rest, got_ref, out):
    rows = out.shape[0]
    for side in range(2):
        half = got_ref[side].astype(F32)
        for place in range(side + 2, got_ref.shape[0], 2):
            half = half + got_ref[place].astype(F32)
        left = side * (LANES + rest)
        out[:, left : left + LANES] = half[:rows, :]
        out[:LANES, left + LANES : left + LANES + rest] = half[rows : rows + rest, :].T
        out[LANES:, left + LANES : left + LANES + rest] = half[rows + rest :, :].T[: rows - LANES, :]


def sum_kernel(own_ref, got_ref, out):
    out[...] = own_ref[0] + got_ref[0].astype(F32)


def local(wide, narrow, image_feats, proj_weight, text_embed, log_scale, logit_bias):
    rows, width = image_feats.shape
    total = wide * narrow
    group = 2 * narrow
    spread = wide // 2
    share = width // group
    images = group * rows
    member = lax.axis_index(AXES[1:]).astype(jnp.int32).reshape(1)

    texts = [text_embed] + [swapped(text_embed, total, step * group) for step in range(1, spread)]

    all_feats = lax.all_gather(image_feats, AXES[1:], axis=0, tiled=True)
    zproj = jnp.dot(all_feats, proj_weight, preferred_element_type=F32)
    results = pl.pallas_call(
        functools.partial(pair_kernel, narrow, group, spread),
        in_specs=[SMEM] * 3 + [VMEM] * (1 + spread),
        out_specs=[VMEM] * 6,
        out_shape=[
            jax.ShapeDtypeStruct((share, images), F32),
            jax.ShapeDtypeStruct((1, images), F32),
            jax.ShapeDtypeStruct((width, images), BF16),
            jax.ShapeDtypeStruct((spread * rows, images), BF16),
            jax.ShapeDtypeStruct((group // 2, share + 8, images), F32),
            jax.ShapeDtypeStruct((group // 2, share + STAT_ROWS, images), BF16),
        ],
        scratch_shapes=[
            pltpu.VMEM((width, images), F32),
            pltpu.VMEM((spread * rows, width), BF16),
            pltpu.VMEM((width, images), F32),
        ],
        compiler_params=limit(24 if spread <= 4 else 40),
        name="pairs",
    )(member, log_scale, logit_bias, zproj, *texts)
    unit_part, inv_part, img_emb, grad_tile, own_part, sent_part = results
    got_part = swapped(sent_part, total, 1)
    feats_t, own_text, sent_text = pl.pallas_call(
        functools.partial(caption_kernel, rows),
        in_specs=[VMEM] * 3,
        out_specs=[VMEM] * 3,
        out_shape=[jax.ShapeDtypeStruct((width, images), BF16)]
        + [jax.ShapeDtypeStruct((spread // 2, rows, width), kind) for kind in (F32, BF16)],
        compiler_params=limit(12 if spread <= 4 else 24),
        name="captions",
    )(grad_tile, img_emb, all_feats)
    own_part, got_part, sent_text = lax.optimization_barrier((own_part, got_part, sent_text))
    got_text = swapped(sent_text, total, group)
    own_part, *chip_parts = pl.pallas_call(
        chip_kernel,
        in_specs=[VMEM] * 2,
        out_specs=[VMEM] * (group // 2),
        out_shape=[jax.ShapeDtypeStruct((share + 8, images), F32)]
        + [jax.ShapeDtypeStruct((share + STAT_ROWS, images), BF16)] * (group // 2 - 1),
        compiler_params=limit(12),
        name="chip_sum",
    )(own_part, got_part)
    got = [swapped(value, total, 2 * index) for index, value in enumerate(chip_parts, 1)]
    got, got_text = lax.optimization_barrier((got, got_text))

    mask = group
    while own_text.shape[0] > 1:
        mask *= 2
        own_text, sent_text = pl.pallas_call(
            halving_kernel,
            in_specs=[VMEM] * 2,
            out_specs=[VMEM] * 2,
            out_shape=[
                jax.ShapeDtypeStruct((own_text.shape[0] // 2, rows, width), kind) for kind in (F32, BF16)
            ],
            compiler_params=limit(6 if spread <= 4 else 24),
            name="caption_half",
        )(own_text, got_text)
        got_text = swapped(sent_text, total, mask)

    out_rows = width // wide
    rest = share - LANES
    packed = out_rows + 2 * rest
    direct = LANES < out_rows <= 2 * LANES and out_rows % 16 == 0 and rest % 16 == 0
    if direct:
        loss_line, sent_weight = pl.pallas_call(
            functools.partial(weight_kernel, group, wide),
            in_specs=[VMEM] * (4 + group // 2),
            out_specs=[VMEM] * 2,
            out_shape=[
                jax.ShapeDtypeStruct((1, images), F32),
                jax.ShapeDtypeStruct((wide, packed, LANES), BF16),
            ],
            compiler_params=limit(12),
            name="weights",
        )(own_part, *got, unit_part, inv_part, all_feats, feats_t)
        got_weight = lax.all_to_all(sent_weight, AXES[:2], 0, 0)
        d_proj = pl.pallas_call(
            functools.partial(total_kernel, rest),
            in_specs=[VMEM],
            out_specs=VMEM,
            out_shape=jax.ShapeDtypeStruct((out_rows, 2 * share), F32),
            compiler_params=limit(4),
            name="weight_total",
        )(got_weight)
    else:

        def gradient_kernel(*refs):
            own_ref, blocks = refs[0], refs[1 : group // 2]
            unit_ref, inv_ref, loss_out, d_out = refs[group // 2 :]
            d_out[...] = gathered_gradient(own_ref, blocks, unit_ref, inv_ref, loss_out)

        loss_line, d_zproj = pl.pallas_call(
            gradient_kernel,
            in_specs=[VMEM] * (2 + group // 2),
            out_specs=[VMEM] * 2,
            out_shape=[jax.ShapeDtypeStruct((1, images), F32), jax.ShapeDtypeStruct((share, images), F32)],
            compiler_params=limit(12),
            name="gradient",
        )(own_part, *got, unit_part, inv_part)
        partial = sum(
            lax.dot_general(feats_t, part, NT, preferred_element_type=F32) for part in split_pair(d_zproj)
        )
        left = lax.axis_index("inner") == 0
        both = jnp.concatenate([jnp.where(left, partial, 0.0), jnp.where(left, 0.0, partial)], axis=1)
        d_proj = lax.psum_scatter(both, AXES[:2], scatter_dimension=0, tiled=True)

    d_text_unit = pl.pallas_call(
        sum_kernel,
        in_specs=[VMEM] * 2,
        out_specs=VMEM,
        out_shape=jax.ShapeDtypeStruct((rows, width), F32),
        compiler_params=limit(4),
        name="caption_total",
    )(own_text, got_text)
    image_loss = lax.dynamic_slice_in_dim(loss_line[0], member[0] * rows, rows, 0)
    return (image_loss, d_text_unit, d_proj)


def solution(mesh):
    wide, narrow = mesh.shape["wide"], mesh.shape["narrow"]
    cut = jax.sharding.Mesh(mesh.devices.reshape(wide // 2, 2, narrow), AXES)
    placed = (P(AXES, None), P(), P(AXES, None), P(), P())
    return jax.shard_map(
        functools.partial(local, wide, narrow),
        mesh=cut,
        in_specs=placed,
        out_specs=(P(AXES), P(AXES, None), P(AXES[:2], "narrow")),
        check_vma=False,
    )
```

```python
import functools

import jax
import jax.numpy as jnp
from jax import lax
from jax.experimental import pallas as pl
from jax.experimental.pallas import tpu as pltpu
from jax.sharding import PartitionSpec as P

AXES = ("outer", "inner", "narrow")
F32 = jnp.float32
BF16 = jnp.bfloat16
LANES = 128
STAT_ROWS = 16
VMEM = pl.BlockSpec(memory_space=pltpu.VMEM)
SMEM = pl.BlockSpec(memory_space=pltpu.SMEM)
NT = (((1,), (1,)), ((), ()))
TN = (((0,), (0,)), ((), ()))
MIB = 1024 * 1024


def limit(mebibytes):
    return pltpu.CompilerParams(vmem_limit_bytes=mebibytes * MIB)


def swapped(value, total, mask):
    return lax.ppermute(value, AXES, [(source, source ^ mask) for source in range(total)])


def split_pair(values):
    high = values.astype(BF16)
    return high, (values - high.astype(F32)).astype(BF16)


def stat_rows(loss, along):
    row = lax.broadcasted_iota(jnp.int32, (STAT_ROWS, loss.shape[1]), 0)
    stats = jnp.zeros(row.shape, F32)
    for place, line in enumerate(split_pair(loss) + split_pair(along)):
        stats = jnp.where(row == place, line.astype(F32), stats)
    return stats.astype(BF16)


def stat_sums(stats):
    stats = stats.astype(F32)
    return stats[0:1, :] + stats[1:2, :], stats[2:3, :] + stats[3:4, :]


def column_block(member, narrow):
    return (member % narrow) * 2 + member // narrow


def load_kernel(log_scale_ref, bias_ref, weight_ref, feats_ref, text_ref, weight_out, feats_out, text_out, scalars_out):
    weight_out[...] = weight_ref[...]
    feats_out[...] = feats_ref[...]
    text_out[...] = text_ref[...]
    row = lax.broadcasted_iota(jnp.int32, scalars_out.shape, 0)
    scale = jnp.exp(jnp.full(scalars_out.shape, log_scale_ref[0], F32))
    scalars_out[...] = jnp.where(row == 0, scale, bias_ref[0])


def stack_kernel(member_ref, *refs):
    blocks, out = refs[:-1], refs[-1]
    rows = blocks[0].shape[0]
    chip = member_ref[0] // 2
    for step, block in enumerate(blocks):
        place = pl.multiple_of((chip ^ step) * rows, rows)
        out[pl.ds(place, rows), :] = block[...]


def text_kernel(*refs):
    texts, out = refs[:-1], refs[-1]
    rows = texts[0].shape[0]
    for step, text in enumerate(texts):
        values = text[...].astype(F32)
        inverse = lax.rsqrt(jnp.sum(values * values, axis=1, keepdims=True) + 1e-06)
        out[step * rows : (step + 1) * rows, :] = (values * inverse).astype(BF16)


def first_image(member, rows, group):
    return (member % 2) * (group // 2 * rows) + (member // 2) * rows


def pair_kernel(
    narrow,
    group,
    member_ref,
    scalars_ref,
    weight,
    own_half,
    got_half,
    text_all,
    feats_ref,
    unit_out,
    inv_out,
    emb_out,
    grad_out,
    own_out,
    send_out,
    unit_all,
    d_all,
):
    images, width = feats_ref.shape
    rows = images // group
    spread = text_all.shape[0] // rows
    half = images // 2
    share = width // group
    member = member_ref[0]

    place = pl.multiple_of((member % 2) * half, half)
    feats_ref[pl.ds(place, half), :] = own_half[...]
    place = pl.multiple_of((1 - member % 2) * half, half)
    feats_ref[pl.ds(place, half), :] = got_half[...]
    for start in range(0, images, LANES):
        cols = slice(start, start + LANES)
        proj = jnp.dot(feats_ref[cols, :], weight[...], preferred_element_type=F32)
        turned = proj.T
        inverse = lax.rsqrt(jnp.sum(turned * turned, axis=0, keepdims=True) + 1e-06)
        unit = turned * inverse
        inv_out[:, cols] = inverse
        unit_all[:, cols] = unit
        emb_out[:, cols] = unit.astype(BF16)
    block = pl.multiple_of(column_block(member, narrow) * share, share)
    unit_out[...] = unit_all[pl.ds(block, share), :]

    scale = scalars_ref[0:1, 0:1]
    shift = scalars_ref[1:2, 0:1]
    count = 4 * rows if spread % 4 == 0 else rows
    chunks = spread * rows // count

    def one_chunk(chunk, loss_sum, dot_sum, first):
        here = pl.ds(pl.multiple_of(chunk * count, count), count)
        text = text_all[here, :]
        products = jnp.dot(text, emb_out[...], preferred_element_type=F32)
        logits = scale * products + shift
        caption = lax.broadcasted_iota(jnp.int32, (count, images), 0) + chunk * count
        image = lax.broadcasted_iota(jnp.int32, (count, images), 1)
        own = jnp.logical_and(caption < rows, image == first_image(member, rows, group) + caption)
        sign = jnp.where(own, 1.0, -1.0).astype(F32)
        away = -sign * logits
        small = jnp.exp(-jnp.abs(away))
        loss = jnp.maximum(away, 0.0) + jnp.log1p(small)
        chance = jnp.where(away >= 0.0, 1.0, small) / (1.0 + small)
        grad = (-scale * sign * chance).astype(BF16)
        grad_out[here, :] = grad
        loss_sum = loss_sum + jnp.sum(loss, axis=0, keepdims=True)
        dot_sum = dot_sum + jnp.sum(grad.astype(F32) * products, axis=0, keepdims=True)
        d_img = lax.dot_general(text, grad, TN, preferred_element_type=F32)
        if first:
            d_all[...] = d_img
        else:
            d_all[...] += d_img
        return loss_sum, dot_sum

    zero = jnp.zeros((1, images), F32)
    sums = one_chunk(0, zero, zero, True)
    if chunks > 1:
        sums = lax.fori_loop(1, chunks, lambda c, s: one_chunk(c, *s, False), sums)
    loss_sum, dot_sum = sums

    stats = stat_rows(loss_sum, dot_sum)
    for index in range(group // 2):
        part = pl.multiple_of(column_block(member ^ (2 * index), narrow) * share, share)
        own_out[index, :share, :] = d_all[pl.ds(part, share), :]
        part = pl.multiple_of(column_block(member ^ (2 * index + 1), narrow) * share, share)
        send_out[index, :share, :] = d_all[pl.ds(part, share), :].astype(BF16)
        send_out[index, share:, :] = stats
    own_out[0, share : share + 1, :] = loss_sum
    own_out[0, share + 1 : share + 2, :] = dot_sum


def chip_kernel(own_ref, got_ref, own_out, *send_out):
    share = own_out.shape[0] - 8
    loss, along = stat_sums(got_ref[0, share:, :])
    loss = loss + own_ref[0, share : share + 1, :]
    along = along + own_ref[0, share + 1 : share + 2, :]
    own_out[:share, :] = own_ref[0, :share, :] + got_ref[0, :share, :].astype(F32)
    own_out[share : share + 1, :] = loss
    own_out[share + 1 : share + 2, :] = along
    stats = stat_rows(loss, along)
    for index, target in enumerate(send_out, 1):
        target[:share, :] = (own_ref[index, :share, :] + got_ref[index, :share, :].astype(F32)).astype(BF16)
        target[share:, :] = stats


def caption_kernel(rows, grad_ref, emb_ref, feats_ref, feats_t, *outs):
    for step, target in enumerate(outs):
        grad = grad_ref[step * rows : (step + 1) * rows, :]
        product = lax.dot_general(grad, emb_ref[...], NT, preferred_element_type=F32)
        target[...] = product.astype(target.dtype)
    for start in range(0, feats_ref.shape[0], LANES):
        cols = slice(start, start + LANES)
        feats_t[:, cols] = feats_ref[cols, :].astype(F32).T.astype(BF16)


def gathered_gradient(own_ref, got, unit_ref, inv_ref, loss_out):
    share = unit_ref.shape[0]
    total = own_ref[:share, :]
    loss = own_ref[share : share + 1, :]
    along = own_ref[share + 1 : share + 2, :]
    for block in got:
        total = total + block[:share, :].astype(F32)
        more_loss, more_along = stat_sums(block[share:, :])
        loss = loss + more_loss
        along = along + more_along
    loss_out[...] = loss
    return inv_ref[...] * (total - unit_ref[...] * along)


def weight_kernel(group, wide, *refs):
    own_ref = refs[0]
    got = refs[1 : group // 2]
    unit_ref, inv_ref, feats_ref, feats_t_ref, loss_out, send_out = refs[group // 2 :]
    share = unit_ref.shape[0]
    rest = share - LANES
    rows = feats_t_ref.shape[0] // wide
    high, low = split_pair(gathered_gradient(own_ref, got, unit_ref, inv_ref, loss_out))
    main = lax.dot_general(
        feats_t_ref[...], high[:LANES, :], NT, preferred_element_type=F32
    ) + lax.dot_general(feats_t_ref[...], low[:LANES, :], NT, preferred_element_type=F32)
    tail = jnp.dot(high[LANES:, :], feats_ref[...], preferred_element_type=F32) + jnp.dot(
        low[LANES:, :], feats_ref[...], preferred_element_type=F32
    )
    main, tail = main.astype(BF16), tail.astype(BF16)
    for place in range(wide):
        begin = place * rows
        send_out[place, :rows, :] = main[begin : begin + rows, :]
        send_out[place, rows : rows + rest, :] = tail[:, begin : begin + LANES]
        send_out[place, rows + rest :, :] = jnp.zeros((rest, LANES), BF16)
        send_out[place, rows + rest :, : rows - LANES] = tail[:, begin + LANES : begin + rows]


def total_text(refs, out):
    total = refs[0][...]
    for block in refs[1:]:
        total = total + block[...].astype(F32)
    out[...] = total


def total_kernel(rest, *refs):
    got_ref, out, text_out = refs[0], refs[-2], refs[-1]
    total_text(refs[1:-2], text_out)
    rows = out.shape[0]
    for side in range(2):
        half = got_ref[side].astype(F32)
        for place in range(side + 2, got_ref.shape[0], 2):
            half = half + got_ref[place].astype(F32)
        left = side * (LANES + rest)
        out[:, left : left + LANES] = half[:rows, :]
        out[:LANES, left + LANES : left + LANES + rest] = half[rows : rows + rest, :].T
        out[LANES:, left + LANES : left + LANES + rest] = half[rows + rest :, :].T[: rows - LANES, :]


def sum_kernel(*refs):
    total_text(refs[:-1], refs[-1])


def local(wide, narrow, image_feats, proj_weight, text_embed, log_scale, logit_bias):
    rows, width = image_feats.shape
    total = wide * narrow
    group = 2 * narrow
    spread = wide // 2
    share = width // group
    images = group * rows
    member = lax.axis_index(AXES[1:]).astype(jnp.int32).reshape(1)

    texts = [swapped(text_embed, total, step * group) for step in range(1, spread)]
    got_feats = [swapped(image_feats, total, 2 * step) for step in range(1, group // 2)]
    arrived = lax.optimization_barrier([got_feats[0], *texts[:0:-1], got_feats[-1], texts[0], *got_feats[1:-1]])
    got_feats = [arrived[0], *arrived[spread + 1 :], arrived[spread - 1]]
    texts = [arrived[spread], *arrived[spread - 2 : 0 : -1]]
    weight, own_feats, own_text, scalars = pl.pallas_call(
        load_kernel,
        in_specs=[SMEM] * 2 + [VMEM] * 3,
        out_specs=[VMEM] * 4,
        out_shape=[
            jax.ShapeDtypeStruct((width, width), BF16),
            jax.ShapeDtypeStruct((rows, width), BF16),
            jax.ShapeDtypeStruct((rows, width), BF16),
            jax.ShapeDtypeStruct((8, LANES), F32),
        ],
        compiler_params=limit(8),
        name="load",
    )(log_scale, logit_bias, proj_weight, image_feats, text_embed)
    own_half = pl.pallas_call(
        stack_kernel,
        in_specs=[SMEM] + [VMEM] * (group // 2),
        out_specs=VMEM,
        out_shape=jax.ShapeDtypeStruct((images // 2, width), BF16),
        compiler_params=limit(4),
        name="stack",
    )(member, own_feats, *got_feats)
    got_half = swapped(own_half, total, 1)
    text_emb = pl.pallas_call(
        text_kernel,
        in_specs=[VMEM] * spread,
        out_specs=VMEM,
        out_shape=jax.ShapeDtypeStruct((spread * rows, width), BF16),
        compiler_params=limit(4 if spread <= 4 else 16),
        name="text_unit",
    )(own_text, *texts)

    results = pl.pallas_call(
        functools.partial(pair_kernel, narrow, group),
        in_specs=[SMEM] + [VMEM] * 5,
        out_specs=[VMEM] * 7,
        out_shape=[
            jax.ShapeDtypeStruct((images, width), BF16),
            jax.ShapeDtypeStruct((share, images), F32),
            jax.ShapeDtypeStruct((1, images), F32),
            jax.ShapeDtypeStruct((width, images), BF16),
            jax.ShapeDtypeStruct((spread * rows, images), BF16),
            jax.ShapeDtypeStruct((group // 2, share + 8, images), F32),
            jax.ShapeDtypeStruct((group // 2, share + STAT_ROWS, images), BF16),
        ],
        scratch_shapes=[
            pltpu.VMEM((width, images), F32),
            pltpu.VMEM((width, images), F32),
        ],
        compiler_params=limit(24 if spread <= 4 else 40),
        name="pairs",
    )(member, scalars, weight, own_half, got_half, text_emb)
    all_feats, unit_part, inv_part, img_emb, grad_tile, own_part, sent_part = results
    got_part = swapped(sent_part, total, 1)
    feats_t, own_text, *sent_text = pl.pallas_call(
        functools.partial(caption_kernel, rows),
        in_specs=[VMEM] * 3,
        out_specs=[VMEM] * (1 + spread),
        out_shape=[jax.ShapeDtypeStruct((width, images), BF16), jax.ShapeDtypeStruct((rows, width), F32)]
        + [jax.ShapeDtypeStruct((rows, width), BF16)] * (spread - 1),
        compiler_params=limit(12 if spread <= 4 else 24),
        name="captions",
    )(grad_tile, img_emb, all_feats)
    own_part, got_part, sent_text = lax.optimization_barrier((own_part, got_part, sent_text))
    got_text = [swapped(value, total, step * group) for step, value in enumerate(sent_text, 1)]
    own_part, *chip_parts = pl.pallas_call(
        chip_kernel,
        in_specs=[VMEM] * 2,
        out_specs=[VMEM] * (group // 2),
        out_shape=[jax.ShapeDtypeStruct((share + 8, images), F32)]
        + [jax.ShapeDtypeStruct((share + STAT_ROWS, images), BF16)] * (group // 2 - 1),
        compiler_params=limit(12),
        name="chip_sum",
    )(own_part, got_part)
    got = [swapped(value, total, 2 * index) for index, value in enumerate(chip_parts, 1)]

    out_rows = width // wide
    rest = share - LANES
    packed = out_rows + 2 * rest
    direct = LANES < out_rows <= 2 * LANES and out_rows % 16 == 0 and rest % 16 == 0
    if direct:
        loss_line, sent_weight = pl.pallas_call(
            functools.partial(weight_kernel, group, wide),
            in_specs=[VMEM] * (4 + group // 2),
            out_specs=[VMEM] * 2,
            out_shape=[
                jax.ShapeDtypeStruct((1, images), F32),
                jax.ShapeDtypeStruct((wide, packed, LANES), BF16),
            ],
            compiler_params=limit(12),
            name="weights",
        )(own_part, *got, unit_part, inv_part, all_feats, feats_t)
        got_weight = lax.all_to_all(sent_weight, AXES[:2], 0, 0)
        got_weight, got_text = lax.optimization_barrier((got_weight, got_text))
        d_proj, d_text_unit = pl.pallas_call(
            functools.partial(total_kernel, rest),
            in_specs=[VMEM] * (1 + spread),
            out_specs=[VMEM] * 2,
            out_shape=[
                jax.ShapeDtypeStruct((out_rows, 2 * share), F32),
                jax.ShapeDtypeStruct((rows, width), F32),
            ],
            compiler_params=limit(6),
            name="totals",
        )(got_weight, own_text, *got_text)
    else:

        def gradient_kernel(*refs):
            own_ref, blocks = refs[0], refs[1 : group // 2]
            unit_ref, inv_ref, loss_out, d_out = refs[group // 2 :]
            d_out[...] = gathered_gradient(own_ref, blocks, unit_ref, inv_ref, loss_out)

        loss_line, d_zproj = pl.pallas_call(
            gradient_kernel,
            in_specs=[VMEM] * (2 + group // 2),
            out_specs=[VMEM] * 2,
            out_shape=[jax.ShapeDtypeStruct((1, images), F32), jax.ShapeDtypeStruct((share, images), F32)],
            compiler_params=limit(12),
            name="gradient",
        )(own_part, *got, unit_part, inv_part)
        partial = sum(
            lax.dot_general(feats_t, part, NT, preferred_element_type=F32) for part in split_pair(d_zproj)
        )
        left = lax.axis_index("inner") == 0
        both = jnp.concatenate([jnp.where(left, partial, 0.0), jnp.where(left, 0.0, partial)], axis=1)
        d_proj = lax.psum_scatter(both, AXES[:2], scatter_dimension=0, tiled=True)
        d_text_unit = pl.pallas_call(
            sum_kernel,
            in_specs=[VMEM] * spread,
            out_specs=VMEM,
            out_shape=jax.ShapeDtypeStruct((rows, width), F32),
            compiler_params=limit(12),
            name="caption_total",
        )(own_text, *got_text)
    image_loss = lax.dynamic_slice_in_dim(loss_line[0], first_image(member[0], rows, group), rows, 0)
    return (image_loss, d_text_unit, d_proj)


def solution(mesh):
    wide, narrow = mesh.shape["wide"], mesh.shape["narrow"]
    cut = jax.sharding.Mesh(mesh.devices.reshape(wide // 2, 2, narrow), AXES)
    placed = (P(AXES, None), P(), P(AXES, None), P(), P())
    return jax.shard_map(
        functools.partial(local, wide, narrow),
        mesh=cut,
        in_specs=placed,
        out_specs=(P(AXES), P(AXES, None), P(AXES[:2], "narrow")),
        check_vma=False,
    )
```

```python
import functools

import jax
import jax.numpy as jnp
from jax import lax
from jax.experimental import pallas as pl
from jax.experimental.pallas import tpu as pltpu
from jax.sharding import PartitionSpec as P

AXES = ("outer", "inner", "narrow")
F32 = jnp.float32
BF16 = jnp.bfloat16
LANES = 128
STAT_ROWS = 16
VMEM = pl.BlockSpec(memory_space=pltpu.VMEM)
SMEM = pl.BlockSpec(memory_space=pltpu.SMEM)
NT = (((1,), (1,)), ((), ()))
TN = (((0,), (0,)), ((), ()))
MIB = 1024 * 1024


def limit(mebibytes):
    return pltpu.CompilerParams(vmem_limit_bytes=mebibytes * MIB)


def swapped(value, total, mask):
    return lax.ppermute(value, AXES, [(source, source ^ mask) for source in range(total)])


def split_pair(values):
    high = values.astype(BF16)
    return high, (values - high.astype(F32)).astype(BF16)


def stat_rows(loss, along):
    row = lax.broadcasted_iota(jnp.int32, (STAT_ROWS, loss.shape[1]), 0)
    stats = jnp.zeros(row.shape, F32)
    for place, line in enumerate(split_pair(loss) + split_pair(along)):
        stats = jnp.where(row == place, line.astype(F32), stats)
    return stats.astype(BF16)


def stat_sums(stats):
    stats = stats.astype(F32)
    return stats[0:1, :] + stats[1:2, :], stats[2:3, :] + stats[3:4, :]


def column_block(member, narrow):
    return (member % narrow) * 2 + member // narrow


def load_kernel(log_scale_ref, bias_ref, weight_ref, feats_ref, text_ref, weight_out, feats_out, text_out, scalars_out):
    weight_out[...] = weight_ref[...]
    feats_out[...] = feats_ref[...]
    text_out[...] = text_ref[...]
    row = lax.broadcasted_iota(jnp.int32, scalars_out.shape, 0)
    scale = jnp.exp(jnp.full(scalars_out.shape, log_scale_ref[0], F32))
    scalars_out[...] = jnp.where(row == 0, scale, bias_ref[0])


def stack_kernel(member_ref, *refs):
    blocks, out = refs[:-1], refs[-1]
    rows = blocks[0].shape[0]
    chip = member_ref[0] // 2
    for step, block in enumerate(blocks):
        place = pl.multiple_of((chip ^ step) * rows, rows)
        out[pl.ds(place, rows), :] = block[...]


def text_kernel(*refs):
    texts, out = refs[:-1], refs[-1]
    rows = texts[0].shape[0]
    for step, text in enumerate(texts):
        values = text[...].astype(F32)
        inverse = lax.rsqrt(jnp.sum(values * values, axis=1, keepdims=True) + 1e-06)
        out[step * rows : (step + 1) * rows, :] = (values * inverse).astype(BF16)


def first_image(member, rows, group):
    return (member % 2) * (group // 2 * rows) + (member // 2) * rows


def pair_kernel(
    narrow,
    group,
    member_ref,
    scalars_ref,
    weight,
    own_half,
    got_half,
    text_all,
    feats_ref,
    unit_out,
    inv_out,
    emb_out,
    grad_out,
    own_out,
    send_out,
    unit_all,
    d_all,
):
    images, width = feats_ref.shape
    rows = images // group
    spread = text_all.shape[0] // rows
    half = images // 2
    share = width // group
    member = member_ref[0]

    place = pl.multiple_of((member % 2) * half, half)
    feats_ref[pl.ds(place, half), :] = own_half[...]
    place = pl.multiple_of((1 - member % 2) * half, half)
    feats_ref[pl.ds(place, half), :] = got_half[...]
    for start in range(0, images, LANES):
        cols = slice(start, start + LANES)
        proj = jnp.dot(feats_ref[cols, :], weight[...], preferred_element_type=F32)
        turned = proj.T
        inverse = lax.rsqrt(jnp.sum(turned * turned, axis=0, keepdims=True) + 1e-06)
        unit = turned * inverse
        inv_out[:, cols] = inverse
        unit_all[:, cols] = unit
        emb_out[:, cols] = unit.astype(BF16)
    block = pl.multiple_of(column_block(member, narrow) * share, share)
    unit_out[...] = unit_all[pl.ds(block, share), :]

    scale = scalars_ref[0:1, 0:1]
    shift = scalars_ref[1:2, 0:1]
    count = 4 * rows if spread % 4 == 0 else rows
    chunks = spread * rows // count

    def one_chunk(chunk, loss_sum, dot_sum, first):
        here = pl.ds(pl.multiple_of(chunk * count, count), count)
        text = text_all[here, :]
        products = jnp.dot(text, emb_out[...], preferred_element_type=F32)
        logits = scale * products + shift
        caption = lax.broadcasted_iota(jnp.int32, (count, images), 0) + chunk * count
        image = lax.broadcasted_iota(jnp.int32, (count, images), 1)
        own = jnp.logical_and(caption < rows, image == first_image(member, rows, group) + caption)
        sign = jnp.where(own, 1.0, -1.0).astype(F32)
        away = -sign * logits
        small = jnp.exp(-jnp.abs(away))
        loss = jnp.maximum(away, 0.0) + jnp.log1p(small)
        chance = jnp.where(away >= 0.0, 1.0, small) / (1.0 + small)
        grad = (-scale * sign * chance).astype(BF16)
        grad_out[here, :] = grad
        loss_sum = loss_sum + jnp.sum(loss, axis=0, keepdims=True)
        dot_sum = dot_sum + jnp.sum(grad.astype(F32) * products, axis=0, keepdims=True)
        d_img = lax.dot_general(text, grad, TN, preferred_element_type=F32)
        if first:
            d_all[...] = d_img
        else:
            d_all[...] += d_img
        return loss_sum, dot_sum

    zero = jnp.zeros((1, images), F32)
    sums = one_chunk(0, zero, zero, True)
    if chunks > 1:
        sums = lax.fori_loop(1, chunks, lambda c, s: one_chunk(c, *s, False), sums)
    loss_sum, dot_sum = sums

    stats = stat_rows(loss_sum, dot_sum)
    for index in range(group // 2):
        part = pl.multiple_of(column_block(member ^ (2 * index), narrow) * share, share)
        own_out[index, :share, :] = d_all[pl.ds(part, share), :]
        part = pl.multiple_of(column_block(member ^ (2 * index + 1), narrow) * share, share)
        send_out[index, :share, :] = d_all[pl.ds(part, share), :].astype(BF16)
        send_out[index, share:, :] = stats
    own_out[0, share : share + 1, :] = loss_sum
    own_out[0, share + 1 : share + 2, :] = dot_sum


def chip_kernel(own_ref, got_ref, own_out, *send_out):
    share = own_out.shape[0] - 8
    loss, along = stat_sums(got_ref[0, share:, :])
    loss = loss + own_ref[0, share : share + 1, :]
    along = along + own_ref[0, share + 1 : share + 2, :]
    own_out[:share, :] = own_ref[0, :share, :] + got_ref[0, :share, :].astype(F32)
    own_out[share : share + 1, :] = loss
    own_out[share + 1 : share + 2, :] = along
    stats = stat_rows(loss, along)
    for index, target in enumerate(send_out, 1):
        target[:share, :] = (own_ref[index, :share, :] + got_ref[index, :share, :].astype(F32)).astype(BF16)
        target[share:, :] = stats


def caption_kernel(rows, grad_ref, emb_ref, feats_ref, feats_t, *outs):
    for step, target in enumerate(outs):
        grad = grad_ref[step * rows : (step + 1) * rows, :]
        product = lax.dot_general(grad, emb_ref[...], NT, preferred_element_type=F32)
        target[...] = product.astype(target.dtype)
    for start in range(0, feats_ref.shape[0], LANES):
        cols = slice(start, start + LANES)
        feats_t[:, cols] = feats_ref[cols, :].astype(F32).T.astype(BF16)


def gathered_gradient(own_ref, got, unit_ref, inv_ref, loss_out):
    share = unit_ref.shape[0]
    total = own_ref[:share, :]
    loss = own_ref[share : share + 1, :]
    along = own_ref[share + 1 : share + 2, :]
    for block in got:
        total = total + block[:share, :].astype(F32)
        more_loss, more_along = stat_sums(block[share:, :])
        loss = loss + more_loss
        along = along + more_along
    loss_out[...] = loss
    return inv_ref[...] * (total - unit_ref[...] * along)


def weight_kernel(group, wide, *refs):
    own_ref = refs[0]
    got = refs[1 : group // 2]
    unit_ref, inv_ref, feats_ref, feats_t_ref, loss_out, send_out = refs[group // 2 :]
    share = unit_ref.shape[0]
    rest = share - LANES
    rows = feats_t_ref.shape[0] // wide
    high, low = split_pair(gathered_gradient(own_ref, got, unit_ref, inv_ref, loss_out))
    main = lax.dot_general(
        feats_t_ref[...], high[:LANES, :], NT, preferred_element_type=F32
    ) + lax.dot_general(feats_t_ref[...], low[:LANES, :], NT, preferred_element_type=F32)
    tail = jnp.dot(high[LANES:, :], feats_ref[...], preferred_element_type=F32) + jnp.dot(
        low[LANES:, :], feats_ref[...], preferred_element_type=F32
    )
    main, tail = main.astype(BF16), tail.astype(BF16)
    for place in range(wide):
        begin = place * rows
        send_out[place, :rows, :] = main[begin : begin + rows, :]
        send_out[place, rows : rows + rest, :] = tail[:, begin : begin + LANES]
        send_out[place, rows + rest :, :] = jnp.zeros((rest, LANES), BF16)
        send_out[place, rows + rest :, : rows - LANES] = tail[:, begin + LANES : begin + rows]


def total_kernel(rest, got_ref, out):
    rows = out.shape[0]
    for side in range(2):
        half = got_ref[side].astype(F32)
        for place in range(side + 2, got_ref.shape[0], 2):
            half = half + got_ref[place].astype(F32)
        left = side * (LANES + rest)
        out[:, left : left + LANES] = half[:rows, :]
        out[:LANES, left + LANES : left + LANES + rest] = half[rows : rows + rest, :].T
        out[LANES:, left + LANES : left + LANES + rest] = half[rows + rest :, :].T[: rows - LANES, :]


def sum_kernel(*refs):
    total = refs[0][...]
    for block in refs[1:-1]:
        total = total + block[...].astype(F32)
    refs[-1][...] = total


def local(wide, narrow, image_feats, proj_weight, text_embed, log_scale, logit_bias):
    rows, width = image_feats.shape
    total = wide * narrow
    group = 2 * narrow
    spread = wide // 2
    share = width // group
    images = group * rows
    member = lax.axis_index(AXES[1:]).astype(jnp.int32).reshape(1)

    texts = [swapped(text_embed, total, step * group) for step in range(1, spread)]
    got_feats = [swapped(image_feats, total, 2 * step) for step in range(1, group // 2)]
    arrived = lax.optimization_barrier([got_feats[0], *texts[:0:-1], got_feats[-1], texts[0], *got_feats[1:-1]])
    got_feats = [arrived[0], *arrived[spread + 1 :], arrived[spread - 1]]
    texts = [arrived[spread], *arrived[spread - 2 : 0 : -1]]
    weight, own_feats, own_text, scalars = pl.pallas_call(
        load_kernel,
        in_specs=[SMEM] * 2 + [VMEM] * 3,
        out_specs=[VMEM] * 4,
        out_shape=[
            jax.ShapeDtypeStruct((width, width), BF16),
            jax.ShapeDtypeStruct((rows, width), BF16),
            jax.ShapeDtypeStruct((rows, width), BF16),
            jax.ShapeDtypeStruct((8, LANES), F32),
        ],
        compiler_params=limit(8),
        name="load",
    )(log_scale, logit_bias, proj_weight, image_feats, text_embed)
    own_half = pl.pallas_call(
        stack_kernel,
        in_specs=[SMEM] + [VMEM] * (group // 2),
        out_specs=VMEM,
        out_shape=jax.ShapeDtypeStruct((images // 2, width), BF16),
        compiler_params=limit(4),
        name="stack",
    )(member, own_feats, *got_feats)
    got_half = swapped(own_half, total, 1)
    text_emb = pl.pallas_call(
        text_kernel,
        in_specs=[VMEM] * spread,
        out_specs=VMEM,
        out_shape=jax.ShapeDtypeStruct((spread * rows, width), BF16),
        compiler_params=limit(4 if spread <= 4 else 16),
        name="text_unit",
    )(own_text, *texts)

    results = pl.pallas_call(
        functools.partial(pair_kernel, narrow, group),
        in_specs=[SMEM] + [VMEM] * 5,
        out_specs=[VMEM] * 7,
        out_shape=[
            jax.ShapeDtypeStruct((images, width), BF16),
            jax.ShapeDtypeStruct((share, images), F32),
            jax.ShapeDtypeStruct((1, images), F32),
            jax.ShapeDtypeStruct((width, images), BF16),
            jax.ShapeDtypeStruct((spread * rows, images), BF16),
            jax.ShapeDtypeStruct((group // 2, share + 8, images), F32),
            jax.ShapeDtypeStruct((group // 2, share + STAT_ROWS, images), BF16),
        ],
        scratch_shapes=[
            pltpu.VMEM((width, images), F32),
            pltpu.VMEM((width, images), F32),
        ],
        compiler_params=limit(24 if spread <= 4 else 40),
        name="pairs",
    )(member, scalars, weight, own_half, got_half, text_emb)
    all_feats, unit_part, inv_part, img_emb, grad_tile, own_part, sent_part = results
    got_part = swapped(sent_part, total, 1)
    feats_t, own_text, *sent_text = pl.pallas_call(
        functools.partial(caption_kernel, rows),
        in_specs=[VMEM] * 3,
        out_specs=[VMEM] * (1 + spread),
        out_shape=[jax.ShapeDtypeStruct((width, images), BF16), jax.ShapeDtypeStruct((rows, width), F32)]
        + [jax.ShapeDtypeStruct((rows, width), BF16)] * (spread - 1),
        compiler_params=limit(12 if spread <= 4 else 24),
        name="captions",
    )(grad_tile, img_emb, all_feats)
    own_part, got_part, sent_text = lax.optimization_barrier((own_part, got_part, sent_text))
    got_text = [swapped(value, total, step * group) for step, value in enumerate(sent_text, 1)]
    own_part, *chip_parts = pl.pallas_call(
        chip_kernel,
        in_specs=[VMEM] * 2,
        out_specs=[VMEM] * (group // 2),
        out_shape=[jax.ShapeDtypeStruct((share + 8, images), F32)]
        + [jax.ShapeDtypeStruct((share + STAT_ROWS, images), BF16)] * (group // 2 - 1),
        compiler_params=limit(12),
        name="chip_sum",
    )(own_part, got_part)
    got = [swapped(value, total, 2 * index) for index, value in enumerate(chip_parts, 1)]

    out_rows = width // wide
    rest = share - LANES
    packed = out_rows + 2 * rest
    direct = LANES < out_rows <= 2 * LANES and out_rows % 16 == 0 and rest % 16 == 0
    if direct:
        loss_line, sent_weight = pl.pallas_call(
            functools.partial(weight_kernel, group, wide),
            in_specs=[VMEM] * (4 + group // 2),
            out_specs=[VMEM] * 2,
            out_shape=[
                jax.ShapeDtypeStruct((1, images), F32),
                jax.ShapeDtypeStruct((wide, packed, LANES), BF16),
            ],
            compiler_params=limit(12),
            name="weights",
        )(own_part, *got, unit_part, inv_part, all_feats, feats_t)
        order = [*got_text[1:], got_text[0]]
        sent_weight, *order = lax.optimization_barrier((sent_weight, *order))
        got_text = [order[-1], *order[:-1]]
        got_weight = lax.all_to_all(sent_weight, AXES[:2], 0, 0)
        d_proj = pl.pallas_call(
            functools.partial(total_kernel, rest),
            in_specs=[VMEM],
            out_specs=VMEM,
            out_shape=jax.ShapeDtypeStruct((out_rows, 2 * share), F32),
            compiler_params=limit(4),
            name="weight_total",
        )(got_weight)
    else:

        def gradient_kernel(*refs):
            own_ref, blocks = refs[0], refs[1 : group // 2]
            unit_ref, inv_ref, loss_out, d_out = refs[group // 2 :]
            d_out[...] = gathered_gradient(own_ref, blocks, unit_ref, inv_ref, loss_out)

        loss_line, d_zproj = pl.pallas_call(
            gradient_kernel,
            in_specs=[VMEM] * (2 + group // 2),
            out_specs=[VMEM] * 2,
            out_shape=[jax.ShapeDtypeStruct((1, images), F32), jax.ShapeDtypeStruct((share, images), F32)],
            compiler_params=limit(12),
            name="gradient",
        )(own_part, *got, unit_part, inv_part)
        partial = sum(
            lax.dot_general(feats_t, part, NT, preferred_element_type=F32) for part in split_pair(d_zproj)
        )
        left = lax.axis_index("inner") == 0
        both = jnp.concatenate([jnp.where(left, partial, 0.0), jnp.where(left, 0.0, partial)], axis=1)
        d_proj = lax.psum_scatter(both, AXES[:2], scatter_dimension=0, tiled=True)

    d_text_unit = pl.pallas_call(
        sum_kernel,
        in_specs=[VMEM] * spread,
        out_specs=VMEM,
        out_shape=jax.ShapeDtypeStruct((rows, width), F32),
        compiler_params=limit(12),
        name="caption_total",
    )(own_text, *got_text)
    image_loss = lax.dynamic_slice_in_dim(loss_line[0], first_image(member[0], rows, group), rows, 0)
    return (image_loss, d_text_unit, d_proj)


def solution(mesh):
    wide, narrow = mesh.shape["wide"], mesh.shape["narrow"]
    cut = jax.sharding.Mesh(mesh.devices.reshape(wide // 2, 2, narrow), AXES)
    placed = (P(AXES, None), P(), P(AXES, None), P(), P())
    return jax.shard_map(
        functools.partial(local, wide, narrow),
        mesh=cut,
        in_specs=placed,
        out_specs=(P(AXES), P(AXES, None), P(AXES[:2], "narrow")),
        check_vma=False,
    )
```

```python
import functools

import jax
import jax.numpy as jnp
from jax import lax
from jax.experimental import pallas as pl
from jax.experimental.pallas import tpu as pltpu
from jax.sharding import PartitionSpec as P

AXES = ("outer", "inner", "narrow")
F32 = jnp.float32
BF16 = jnp.bfloat16
LANES = 128
STAT_ROWS = 16
VMEM = pl.BlockSpec(memory_space=pltpu.VMEM)
SMEM = pl.BlockSpec(memory_space=pltpu.SMEM)
NT = (((1,), (1,)), ((), ()))
TN = (((0,), (0,)), ((), ()))
MIB = 1024 * 1024


def limit(mebibytes):
    return pltpu.CompilerParams(vmem_limit_bytes=mebibytes * MIB)


def swapped(value, total, mask):
    return lax.ppermute(value, AXES, [(source, source ^ mask) for source in range(total)])


def split_pair(values):
    high = values.astype(BF16)
    return high, (values - high.astype(F32)).astype(BF16)


def stat_rows(loss, along):
    row = lax.broadcasted_iota(jnp.int32, (STAT_ROWS, loss.shape[1]), 0)
    stats = jnp.zeros(row.shape, F32)
    for place, line in enumerate(split_pair(loss) + split_pair(along)):
        stats = jnp.where(row == place, line.astype(F32), stats)
    return stats.astype(BF16)


def stat_sums(stats):
    stats = stats.astype(F32)
    return stats[0:1, :] + stats[1:2, :], stats[2:3, :] + stats[3:4, :]


def column_block(member, narrow):
    return (member % narrow) * 2 + member // narrow


def load_kernel(log_scale_ref, bias_ref, weight_ref, feats_ref, text_ref, weight_out, feats_out, text_out, scalars_out):
    weight_out[...] = weight_ref[...]
    feats_out[...] = feats_ref[...]
    text_out[...] = text_ref[...]
    row = lax.broadcasted_iota(jnp.int32, scalars_out.shape, 0)
    scale = jnp.exp(jnp.full(scalars_out.shape, log_scale_ref[0], F32))
    scalars_out[...] = jnp.where(row == 0, scale, bias_ref[0])


def stack_kernel(member_ref, *refs):
    blocks, out = refs[:-1], refs[-1]
    rows = blocks[0].shape[0]
    chip = member_ref[0] // 2
    for step, block in enumerate(blocks):
        place = pl.multiple_of((chip ^ step) * rows, rows)
        out[pl.ds(place, rows), :] = block[...]


def text_kernel(*refs):
    texts, out = refs[:-1], refs[-1]
    rows = texts[0].shape[0]
    for step, text in enumerate(texts):
        values = text[...].astype(F32)
        inverse = lax.rsqrt(jnp.sum(values * values, axis=1, keepdims=True) + 1e-06)
        out[step * rows : (step + 1) * rows, :] = (values * inverse).astype(BF16)


def project_kernel(feats_ref, weight_ref, out):
    out[...] = jnp.dot(feats_ref[...], weight_ref[...], preferred_element_type=F32)


def first_image(member, rows, group):
    return (member % 2) * (group // 2 * rows) + (member // 2) * rows


def pair_kernel(
    narrow,
    group,
    member_ref,
    scalars_ref,
    weight,
    own_half,
    own_proj,
    got_half,
    text_all,
    feats_ref,
    unit_out,
    inv_out,
    emb_out,
    grad_out,
    own_out,
    send_out,
    unit_all,
    d_all,
    proj_all,
):
    images, width = feats_ref.shape
    rows = images // group
    spread = text_all.shape[0] // rows
    half = images // 2
    share = width // group
    member = member_ref[0]

    place = pl.multiple_of((member % 2) * half, half)
    feats_ref[pl.ds(place, half), :] = own_half[...]
    proj_all[pl.ds(place, half), :] = own_proj[...]
    place = pl.multiple_of((1 - member % 2) * half, half)
    feats_ref[pl.ds(place, half), :] = got_half[...]
    proj_all[pl.ds(place, half), :] = jnp.dot(got_half[...], weight[...], preferred_element_type=F32)
    for start in range(0, images, LANES):
        cols = slice(start, start + LANES)
        turned = proj_all[cols, :].T
        inverse = lax.rsqrt(jnp.sum(turned * turned, axis=0, keepdims=True) + 1e-06)
        unit = turned * inverse
        inv_out[:, cols] = inverse
        unit_all[:, cols] = unit
        emb_out[:, cols] = unit.astype(BF16)
    block = pl.multiple_of(column_block(member, narrow) * share, share)
    unit_out[...] = unit_all[pl.ds(block, share), :]

    scale = scalars_ref[0:1, 0:1]
    shift = scalars_ref[1:2, 0:1]
    count = 4 * rows if spread % 4 == 0 else rows
    chunks = spread * rows // count

    def one_chunk(chunk, loss_sum, dot_sum, first):
        here = pl.ds(pl.multiple_of(chunk * count, count), count)
        text = text_all[here, :]
        products = jnp.dot(text, emb_out[...], preferred_element_type=F32)
        logits = scale * products + shift
        caption = lax.broadcasted_iota(jnp.int32, (count, images), 0) + chunk * count
        image = lax.broadcasted_iota(jnp.int32, (count, images), 1)
        own = jnp.logical_and(caption < rows, image == first_image(member, rows, group) + caption)
        sign = jnp.where(own, 1.0, -1.0).astype(F32)
        away = -sign * logits
        small = jnp.exp(-jnp.abs(away))
        loss = jnp.maximum(away, 0.0) + jnp.log1p(small)
        chance = jnp.where(away >= 0.0, 1.0, small) / (1.0 + small)
        grad = (-scale * sign * chance).astype(BF16)
        grad_out[here, :] = grad
        loss_sum = loss_sum + jnp.sum(loss, axis=0, keepdims=True)
        dot_sum = dot_sum + jnp.sum(grad.astype(F32) * products, axis=0, keepdims=True)
        d_img = lax.dot_general(text, grad, TN, preferred_element_type=F32)
        if first:
            d_all[...] = d_img
        else:
            d_all[...] += d_img
        return loss_sum, dot_sum

    zero = jnp.zeros((1, images), F32)
    sums = one_chunk(0, zero, zero, True)
    if chunks > 1:
        sums = lax.fori_loop(1, chunks, lambda c, s: one_chunk(c, *s, False), sums)
    loss_sum, dot_sum = sums

    stats = stat_rows(loss_sum, dot_sum)
    for index in range(group // 2):
        part = pl.multiple_of(column_block(member ^ (2 * index), narrow) * share, share)
        own_out[index, :share, :] = d_all[pl.ds(part, share), :]
        part = pl.multiple_of(column_block(member ^ (2 * index + 1), narrow) * share, share)
        send_out[index, :share, :] = d_all[pl.ds(part, share), :].astype(BF16)
        send_out[index, share:, :] = stats
    own_out[0, share : share + 1, :] = loss_sum
    own_out[0, share + 1 : share + 2, :] = dot_sum


def chip_kernel(own_ref, got_ref, own_out, *send_out):
    share = own_out.shape[0] - 8
    loss, along = stat_sums(got_ref[0, share:, :])
    loss = loss + own_ref[0, share : share + 1, :]
    along = along + own_ref[0, share + 1 : share + 2, :]
    own_out[:share, :] = own_ref[0, :share, :] + got_ref[0, :share, :].astype(F32)
    own_out[share : share + 1, :] = loss
    own_out[share + 1 : share + 2, :] = along
    stats = stat_rows(loss, along)
    for index, target in enumerate(send_out, 1):
        target[:share, :] = (own_ref[index, :share, :] + got_ref[index, :share, :].astype(F32)).astype(BF16)
        target[share:, :] = stats


def caption_kernel(rows, grad_ref, emb_ref, feats_ref, feats_t, *outs):
    for step, target in enumerate(outs):
        grad = grad_ref[step * rows : (step + 1) * rows, :]
        product = lax.dot_general(grad, emb_ref[...], NT, preferred_element_type=F32)
        target[...] = product.astype(target.dtype)
    for start in range(0, feats_ref.shape[0], LANES):
        cols = slice(start, start + LANES)
        feats_t[:, cols] = feats_ref[cols, :].astype(F32).T.astype(BF16)


def gathered_gradient(own_ref, got, unit_ref, inv_ref, loss_out):
    share = unit_ref.shape[0]
    total = own_ref[:share, :]
    loss = own_ref[share : share + 1, :]
    along = own_ref[share + 1 : share + 2, :]
    for block in got:
        total = total + block[:share, :].astype(F32)
        more_loss, more_along = stat_sums(block[share:, :])
        loss = loss + more_loss
        along = along + more_along
    loss_out[...] = loss
    return inv_ref[...] * (total - unit_ref[...] * along)


def weight_kernel(group, wide, *refs):
    own_ref = refs[0]
    got = refs[1 : group // 2]
    unit_ref, inv_ref, feats_ref, feats_t_ref, loss_out, send_out = refs[group // 2 :]
    share = unit_ref.shape[0]
    rest = share - LANES
    rows = feats_t_ref.shape[0] // wide
    high, low = split_pair(gathered_gradient(own_ref, got, unit_ref, inv_ref, loss_out))
    main = lax.dot_general(
        feats_t_ref[...], high[:LANES, :], NT, preferred_element_type=F32
    ) + lax.dot_general(feats_t_ref[...], low[:LANES, :], NT, preferred_element_type=F32)
    tail = jnp.dot(high[LANES:, :], feats_ref[...], preferred_element_type=F32) + jnp.dot(
        low[LANES:, :], feats_ref[...], preferred_element_type=F32
    )
    main, tail = main.astype(BF16), tail.astype(BF16)
    for place in range(wide):
        begin = place * rows
        send_out[place, :rows, :] = main[begin : begin + rows, :]
        send_out[place, rows : rows + rest, :] = tail[:, begin : begin + LANES]
        send_out[place, rows + rest :, :] = jnp.zeros((rest, LANES), BF16)
        send_out[place, rows + rest :, : rows - LANES] = tail[:, begin + LANES : begin + rows]


def total_kernel(rest, got_ref, out):
    rows = out.shape[0]
    for side in range(2):
        half = got_ref[side].astype(F32)
        for place in range(side + 2, got_ref.shape[0], 2):
            half = half + got_ref[place].astype(F32)
        left = side * (LANES + rest)
        out[:, left : left + LANES] = half[:rows, :]
        out[:LANES, left + LANES : left + LANES + rest] = half[rows : rows + rest, :].T
        out[LANES:, left + LANES : left + LANES + rest] = half[rows + rest :, :].T[: rows - LANES, :]


def sum_kernel(*refs):
    total = refs[0][...]
    for block in refs[1:-1]:
        total = total + block[...].astype(F32)
    refs[-1][...] = total


def local(wide, narrow, image_feats, proj_weight, text_embed, log_scale, logit_bias):
    rows, width = image_feats.shape
    total = wide * narrow
    group = 2 * narrow
    spread = wide // 2
    share = width // group
    images = group * rows
    member = lax.axis_index(AXES[1:]).astype(jnp.int32).reshape(1)

    far = swapped(text_embed, total, 2 * group)
    near = swapped(text_embed, total, group)
    got_feats = [swapped(image_feats, total, 2 * step) for step in range(1, group // 2)]
    far, last, near, *rest_feats = lax.optimization_barrier([far, got_feats[-1], near, *got_feats[-2::-1]])
    got_feats = [*rest_feats[::-1], last]
    texts = [near, far, swapped(far, total, group)]
    while len(texts) + 1 < spread:
        mask = (len(texts) + 1) * group
        texts += [swapped(text, total, mask) for text in [text_embed, *texts]]
    weight, own_feats, own_text, scalars = pl.pallas_call(
        load_kernel,
        in_specs=[SMEM] * 2 + [VMEM] * 3,
        out_specs=[VMEM] * 4,
        out_shape=[
            jax.ShapeDtypeStruct((width, width), BF16),
            jax.ShapeDtypeStruct((rows, width), BF16),
            jax.ShapeDtypeStruct((rows, width), BF16),
            jax.ShapeDtypeStruct((8, LANES), F32),
        ],
        compiler_params=limit(8),
        name="load",
    )(log_scale, logit_bias, proj_weight, image_feats, text_embed)
    own_half = pl.pallas_call(
        stack_kernel,
        in_specs=[SMEM] + [VMEM] * (group // 2),
        out_specs=VMEM,
        out_shape=jax.ShapeDtypeStruct((images // 2, width), BF16),
        compiler_params=limit(4),
        name="stack",
    )(member, own_feats, *got_feats)
    got_half = swapped(own_half, total, 1)
    own_proj = pl.pallas_call(
        project_kernel,
        in_specs=[VMEM] * 2,
        out_specs=VMEM,
        out_shape=jax.ShapeDtypeStruct((images // 2, width), F32),
        compiler_params=limit(8),
        name="own_projection",
    )(own_half, weight)
    text_emb = pl.pallas_call(
        text_kernel,
        in_specs=[VMEM] * spread,
        out_specs=VMEM,
        out_shape=jax.ShapeDtypeStruct((spread * rows, width), BF16),
        compiler_params=limit(4 if spread <= 4 else 16),
        name="text_unit",
    )(own_text, *texts)

    results = pl.pallas_call(
        functools.partial(pair_kernel, narrow, group),
        in_specs=[SMEM] + [VMEM] * 6,
        out_specs=[VMEM] * 7,
        out_shape=[
            jax.ShapeDtypeStruct((images, width), BF16),
            jax.ShapeDtypeStruct((share, images), F32),
            jax.ShapeDtypeStruct((1, images), F32),
            jax.ShapeDtypeStruct((width, images), BF16),
            jax.ShapeDtypeStruct((spread * rows, images), BF16),
            jax.ShapeDtypeStruct((group // 2, share + 8, images), F32),
            jax.ShapeDtypeStruct((group // 2, share + STAT_ROWS, images), BF16),
        ],
        scratch_shapes=[
            pltpu.VMEM((width, images), F32),
            pltpu.VMEM((width, images), F32),
            pltpu.VMEM((images, width), F32),
        ],
        compiler_params=limit(24 if spread <= 4 else 40),
        name="pairs",
    )(member, scalars, weight, own_half, own_proj, got_half, text_emb)
    all_feats, unit_part, inv_part, img_emb, grad_tile, own_part, sent_part = results
    got_part = swapped(sent_part, total, 1)
    feats_t, own_text, *sent_text = pl.pallas_call(
        functools.partial(caption_kernel, rows),
        in_specs=[VMEM] * 3,
        out_specs=[VMEM] * (1 + spread),
        out_shape=[jax.ShapeDtypeStruct((width, images), BF16), jax.ShapeDtypeStruct((rows, width), F32)]
        + [jax.ShapeDtypeStruct((rows, width), BF16)] * (spread - 1),
        compiler_params=limit(12 if spread <= 4 else 24),
        name="captions",
    )(grad_tile, img_emb, all_feats)
    own_part, got_part, sent_text = lax.optimization_barrier((own_part, got_part, sent_text))
    got_text = [swapped(value, total, step * group) for step, value in enumerate(sent_text, 1)]
    own_part, *chip_parts = pl.pallas_call(
        chip_kernel,
        in_specs=[VMEM] * 2,
        out_specs=[VMEM] * (group // 2),
        out_shape=[jax.ShapeDtypeStruct((share + 8, images), F32)]
        + [jax.ShapeDtypeStruct((share + STAT_ROWS, images), BF16)] * (group // 2 - 1),
        compiler_params=limit(12),
        name="chip_sum",
    )(own_part, got_part)
    got = [swapped(value, total, 2 * index) for index, value in enumerate(chip_parts, 1)]
    got_text[1], got = lax.optimization_barrier((got_text[1], got))

    out_rows = width // wide
    rest = share - LANES
    packed = out_rows + 2 * rest
    direct = LANES < out_rows <= 2 * LANES and out_rows % 16 == 0 and rest % 16 == 0
    if direct:
        loss_line, sent_weight = pl.pallas_call(
            functools.partial(weight_kernel, group, wide),
            in_specs=[VMEM] * (4 + group // 2),
            out_specs=[VMEM] * 2,
            out_shape=[
                jax.ShapeDtypeStruct((1, images), F32),
                jax.ShapeDtypeStruct((wide, packed, LANES), BF16),
            ],
            compiler_params=limit(12),
            name="weights",
        )(own_part, *got, unit_part, inv_part, all_feats, feats_t)
        order = [*got_text[1:], got_text[0]]
        sent_weight, *order = lax.optimization_barrier((sent_weight, *order))
        got_text = [order[-1], *order[:-1]]
        got_weight = lax.all_to_all(sent_weight, AXES[:2], 0, 0)
        d_proj = pl.pallas_call(
            functools.partial(total_kernel, rest),
            in_specs=[VMEM],
            out_specs=VMEM,
            out_shape=jax.ShapeDtypeStruct((out_rows, 2 * share), F32),
            compiler_params=limit(4),
            name="weight_total",
        )(got_weight)
    else:

        def gradient_kernel(*refs):
            own_ref, blocks = refs[0], refs[1 : group // 2]
            unit_ref, inv_ref, loss_out, d_out = refs[group // 2 :]
            d_out[...] = gathered_gradient(own_ref, blocks, unit_ref, inv_ref, loss_out)

        loss_line, d_zproj = pl.pallas_call(
            gradient_kernel,
            in_specs=[VMEM] * (2 + group // 2),
            out_specs=[VMEM] * 2,
            out_shape=[jax.ShapeDtypeStruct((1, images), F32), jax.ShapeDtypeStruct((share, images), F32)],
            compiler_params=limit(12),
            name="gradient",
        )(own_part, *got, unit_part, inv_part)
        partial = sum(
            lax.dot_general(feats_t, part, NT, preferred_element_type=F32) for part in split_pair(d_zproj)
        )
        left = lax.axis_index("inner") == 0
        both = jnp.concatenate([jnp.where(left, partial, 0.0), jnp.where(left, 0.0, partial)], axis=1)
        d_proj = lax.psum_scatter(both, AXES[:2], scatter_dimension=0, tiled=True)

    d_text_unit = pl.pallas_call(
        sum_kernel,
        in_specs=[VMEM] * spread,
        out_specs=VMEM,
        out_shape=jax.ShapeDtypeStruct((rows, width), F32),
        compiler_params=limit(12),
        name="caption_total",
    )(own_text, *got_text)
    image_loss = lax.dynamic_slice_in_dim(loss_line[0], first_image(member[0], rows, group), rows, 0)
    return (image_loss, d_text_unit, d_proj)


def solution(mesh):
    wide, narrow = mesh.shape["wide"], mesh.shape["narrow"]
    cut = jax.sharding.Mesh(mesh.devices.reshape(wide // 2, 2, narrow), AXES)
    placed = (P(AXES, None), P(), P(AXES, None), P(), P())
    return jax.shard_map(
        functools.partial(local, wide, narrow),
        mesh=cut,
        in_specs=placed,
        out_specs=(P(AXES), P(AXES, None), P(AXES[:2], "narrow")),
        check_vma=False,
    )
```

```python
import functools

import jax
import jax.numpy as jnp
from jax import lax
from jax.experimental import pallas as pl
from jax.experimental.pallas import tpu as pltpu
from jax.sharding import PartitionSpec as P

AXES = ("outer", "inner", "narrow")
F32 = jnp.float32
BF16 = jnp.bfloat16
LANES = 128
STAT_ROWS = 16
VMEM = pl.BlockSpec(memory_space=pltpu.VMEM)
SMEM = pl.BlockSpec(memory_space=pltpu.SMEM)
NT = (((1,), (1,)), ((), ()))
TN = (((0,), (0,)), ((), ()))
MIB = 1024 * 1024


def limit(mebibytes):
    return pltpu.CompilerParams(vmem_limit_bytes=mebibytes * MIB)


def hint(flops):
    return pl.CostEstimate(flops=flops, bytes_accessed=0, transcendentals=0)


def swapped(value, total, mask):
    return lax.ppermute(value, AXES, [(source, source ^ mask) for source in range(total)])


def split_pair(values):
    high = values.astype(BF16)
    return high, (values - high.astype(F32)).astype(BF16)


def stat_rows(loss, along):
    row = lax.broadcasted_iota(jnp.int32, (STAT_ROWS, loss.shape[1]), 0)
    stats = jnp.zeros(row.shape, F32)
    for place, line in enumerate(split_pair(loss) + split_pair(along)):
        stats = jnp.where(row == place, line.astype(F32), stats)
    return stats.astype(BF16)


def stat_sums(stats):
    stats = stats.astype(F32)
    return stats[0:1, :] + stats[1:2, :], stats[2:3, :] + stats[3:4, :]


def column_block(member, narrow):
    return (member % narrow) * 2 + member // narrow


def unit_text(text):
    values = text.astype(F32)
    inverse = lax.rsqrt(jnp.sum(values * values, axis=1, keepdims=True) + 1e-06)
    return (values * inverse).astype(BF16)


def own_kernel(log_scale_ref, bias_ref, text_ref, text_out, scalars_out):
    text_out[...] = unit_text(text_ref[...])
    row = lax.broadcasted_iota(jnp.int32, scalars_out.shape, 0)
    scale = jnp.exp(jnp.full(scalars_out.shape, log_scale_ref[0], F32))
    scalars_out[...] = jnp.where(row == 0, scale, bias_ref[0])


def stack_kernel(member_ref, *refs):
    blocks, half_out = refs[:-1], refs[-1]
    rows = blocks[0].shape[0]
    chip = member_ref[0] // 2
    for step, block in enumerate(blocks):
        place = pl.multiple_of((chip ^ step) * rows, rows)
        half_out[pl.ds(place, rows), :] = block[...]


def text_kernel(*refs):
    texts, out = refs[:-1], refs[-1]
    rows = texts[0].shape[0]
    out[:rows, :] = texts[0][...]
    for place, text in enumerate(texts[1:], 1):
        step = len(texts) - place
        out[step * rows : (step + 1) * rows, :] = unit_text(text[...])


def project_kernel(feats_ref, weight_ref, out):
    out[...] = jnp.dot(feats_ref[...], weight_ref[...], preferred_element_type=F32)


def first_image(member, rows, group):
    return (member % 2) * (group // 2 * rows) + (member // 2) * rows


def pair_kernel(
    narrow,
    group,
    member_ref,
    scalars_ref,
    weight,
    own_half,
    own_proj,
    got_half,
    text_all,
    feats_ref,
    unit_out,
    inv_out,
    emb_out,
    grad_out,
    own_out,
    send_out,
    unit_all,
    d_all,
    proj_all,
):
    images, width = feats_ref.shape
    rows = images // group
    spread = text_all.shape[0] // rows
    half = images // 2
    share = width // group
    member = member_ref[0]

    place = pl.multiple_of((member % 2) * half, half)
    feats_ref[pl.ds(place, half), :] = own_half[...]
    proj_all[pl.ds(place, half), :] = own_proj[...]
    place = pl.multiple_of((1 - member % 2) * half, half)
    feats_ref[pl.ds(place, half), :] = got_half[...]
    proj_all[pl.ds(place, half), :] = jnp.dot(got_half[...], weight[...], preferred_element_type=F32)
    for start in range(0, images, LANES):
        cols = slice(start, start + LANES)
        turned = proj_all[cols, :].T
        inverse = lax.rsqrt(jnp.sum(turned * turned, axis=0, keepdims=True) + 1e-06)
        unit = turned * inverse
        inv_out[:, cols] = inverse
        unit_all[:, cols] = unit
        emb_out[:, cols] = unit.astype(BF16)
    block = pl.multiple_of(column_block(member, narrow) * share, share)
    unit_out[...] = unit_all[pl.ds(block, share), :]

    scale = scalars_ref[0:1, 0:1]
    shift = scalars_ref[1:2, 0:1]
    count = 4 * rows if spread % 4 == 0 else rows
    chunks = spread * rows // count

    def one_chunk(chunk, loss_sum, dot_sum, first):
        here = pl.ds(pl.multiple_of(chunk * count, count), count)
        text = text_all[here, :]
        products = jnp.dot(text, emb_out[...], preferred_element_type=F32)
        logits = scale * products + shift
        caption = lax.broadcasted_iota(jnp.int32, (count, images), 0) + chunk * count
        image = lax.broadcasted_iota(jnp.int32, (count, images), 1)
        own = jnp.logical_and(caption < rows, image == first_image(member, rows, group) + caption)
        sign = jnp.where(own, 1.0, -1.0).astype(F32)
        away = -sign * logits
        small = jnp.exp(-jnp.abs(away))
        loss = jnp.maximum(away, 0.0) + jnp.log1p(small)
        chance = jnp.where(away >= 0.0, 1.0, small) / (1.0 + small)
        grad = (-scale * sign * chance).astype(BF16)
        grad_out[here, :] = grad
        loss_sum = loss_sum + jnp.sum(loss, axis=0, keepdims=True)
        dot_sum = dot_sum + jnp.sum(grad.astype(F32) * products, axis=0, keepdims=True)
        d_img = lax.dot_general(text, grad, TN, preferred_element_type=F32)
        if first:
            d_all[...] = d_img
        else:
            d_all[...] += d_img
        return loss_sum, dot_sum

    zero = jnp.zeros((1, images), F32)
    sums = one_chunk(0, zero, zero, True)
    if chunks > 1:
        sums = lax.fori_loop(1, chunks, lambda c, s: one_chunk(c, *s, False), sums)
    loss_sum, dot_sum = sums

    stats = stat_rows(loss_sum, dot_sum)
    for index in range(group // 2):
        part = pl.multiple_of(column_block(member ^ (2 * index), narrow) * share, share)
        own_out[index, :share, :] = d_all[pl.ds(part, share), :]
        part = pl.multiple_of(column_block(member ^ (2 * index + 1), narrow) * share, share)
        send_out[index, :share, :] = d_all[pl.ds(part, share), :].astype(BF16)
        send_out[index, share:, :] = stats
    own_out[0, share : share + 1, :] = loss_sum
    own_out[0, share + 1 : share + 2, :] = dot_sum


def chip_kernel(own_ref, got_ref, own_out, *send_out):
    share = own_out.shape[0] - 8
    loss, along = stat_sums(got_ref[0, share:, :])
    loss = loss + own_ref[0, share : share + 1, :]
    along = along + own_ref[0, share + 1 : share + 2, :]
    own_out[:share, :] = own_ref[0, :share, :] + got_ref[0, :share, :].astype(F32)
    own_out[share : share + 1, :] = loss
    own_out[share + 1 : share + 2, :] = along
    stats = stat_rows(loss, along)
    for index, target in enumerate(send_out, 1):
        target[:share, :] = (own_ref[index, :share, :] + got_ref[index, :share, :].astype(F32)).astype(BF16)
        target[share:, :] = stats


def caption_kernel(rows, grad_ref, emb_ref, feats_ref, feats_t, *outs):
    for step, target in enumerate(outs):
        grad = grad_ref[step * rows : (step + 1) * rows, :]
        product = lax.dot_general(grad, emb_ref[...], NT, preferred_element_type=F32)
        target[...] = product.astype(target.dtype)
    for start in range(0, feats_ref.shape[0], LANES):
        cols = slice(start, start + LANES)
        feats_t[:, cols] = feats_ref[cols, :].astype(F32).T.astype(BF16)


def gathered_gradient(own_ref, got, unit_ref, inv_ref, loss_out):
    share = unit_ref.shape[0]
    total = own_ref[:share, :]
    loss = own_ref[share : share + 1, :]
    along = own_ref[share + 1 : share + 2, :]
    for block in got:
        total = total + block[:share, :].astype(F32)
        more_loss, more_along = stat_sums(block[share:, :])
        loss = loss + more_loss
        along = along + more_along
    loss_out[...] = loss
    return inv_ref[...] * (total - unit_ref[...] * along)


def weight_kernel(group, wide, *refs):
    own_ref = refs[0]
    got = refs[1 : group // 2]
    unit_ref, inv_ref, feats_ref, feats_t_ref, loss_out, send_out = refs[group // 2 :]
    share = unit_ref.shape[0]
    rest = share - LANES
    rows = feats_t_ref.shape[0] // wide
    high, low = split_pair(gathered_gradient(own_ref, got, unit_ref, inv_ref, loss_out))
    main = lax.dot_general(
        feats_t_ref[...], high[:LANES, :], NT, preferred_element_type=F32
    ) + lax.dot_general(feats_t_ref[...], low[:LANES, :], NT, preferred_element_type=F32)
    tail = jnp.dot(high[LANES:, :], feats_ref[...], preferred_element_type=F32) + jnp.dot(
        low[LANES:, :], feats_ref[...], preferred_element_type=F32
    )
    main, tail = main.astype(BF16), tail.astype(BF16)
    for place in range(wide):
        begin = place * rows
        send_out[place, :rows, :] = main[begin : begin + rows, :]
        send_out[place, rows : rows + rest, :] = tail[:, begin : begin + LANES]
        send_out[place, rows + rest :, :] = jnp.zeros((rest, LANES), BF16)
        send_out[place, rows + rest :, : rows - LANES] = tail[:, begin + LANES : begin + rows]


def total_kernel(rest, got_ref, out):
    rows = out.shape[0]
    for side in range(2):
        half = got_ref[side].astype(F32)
        for place in range(side + 2, got_ref.shape[0], 2):
            half = half + got_ref[place].astype(F32)
        left = side * (LANES + rest)
        out[:, left : left + LANES] = half[:rows, :]
        out[:LANES, left + LANES : left + LANES + rest] = half[rows : rows + rest, :].T
        out[LANES:, left + LANES : left + LANES + rest] = half[rows + rest :, :].T[: rows - LANES, :]


def sum_kernel(*refs):
    total = refs[0][...]
    for block in refs[1:-1]:
        total = total + block[...].astype(F32)
    refs[-1][...] = total


def local(wide, narrow, image_feats, proj_weight, text_embed, log_scale, logit_bias):
    rows, width = image_feats.shape
    total = wide * narrow
    group = 2 * narrow
    spread = wide // 2
    share = width // group
    images = group * rows
    member = lax.axis_index(AXES[1:]).astype(jnp.int32).reshape(1)

    texts = [swapped(text_embed, total, step * group) for step in range(1, spread)]
    got_feats = [swapped(image_feats, total, 2 * step) for step in range(1, group // 2)]
    own_text, scalars = pl.pallas_call(
        own_kernel,
        in_specs=[SMEM] * 2 + [VMEM],
        out_specs=[VMEM] * 2,
        out_shape=[jax.ShapeDtypeStruct((rows, width), BF16), jax.ShapeDtypeStruct((8, LANES), F32)],
        compiler_params=limit(4),
        cost_estimate=hint(10**10),
        name="own_text",
    )(log_scale, logit_bias, text_embed)
    own_half = pl.pallas_call(
        stack_kernel,
        in_specs=[SMEM] + [VMEM] * (group // 2),
        out_specs=VMEM,
        out_shape=jax.ShapeDtypeStruct((images // 2, width), BF16),
        compiler_params=limit(4),
        name="stack",
    )(member, image_feats, *got_feats)
    got_half = swapped(own_half, total, 1)
    own_proj = pl.pallas_call(
        project_kernel,
        in_specs=[VMEM] * 2,
        out_specs=VMEM,
        out_shape=jax.ShapeDtypeStruct((images // 2, width), F32),
        compiler_params=limit(8),
        name="own_projection",
    )(own_half, proj_weight)
    own_proj, *texts = lax.optimization_barrier((own_proj, *texts[::-1]))
    text_emb = pl.pallas_call(
        text_kernel,
        in_specs=[VMEM] * spread,
        out_specs=VMEM,
        out_shape=jax.ShapeDtypeStruct((spread * rows, width), BF16),
        compiler_params=limit(4 if spread <= 4 else 16),
        cost_estimate=hint(10**10),
        name="text_unit",
    )(own_text, *texts)

    results = pl.pallas_call(
        functools.partial(pair_kernel, narrow, group),
        in_specs=[SMEM] + [VMEM] * 6,
        out_specs=[VMEM] * 7,
        out_shape=[
            jax.ShapeDtypeStruct((images, width), BF16),
            jax.ShapeDtypeStruct((share, images), F32),
            jax.ShapeDtypeStruct((1, images), F32),
            jax.ShapeDtypeStruct((width, images), BF16),
            jax.ShapeDtypeStruct((spread * rows, images), BF16),
            jax.ShapeDtypeStruct((group // 2, share + 8, images), F32),
            jax.ShapeDtypeStruct((group // 2, share + STAT_ROWS, images), BF16),
        ],
        scratch_shapes=[
            pltpu.VMEM((width, images), F32),
            pltpu.VMEM((width, images), F32),
            pltpu.VMEM((images, width), F32),
        ],
        compiler_params=limit(24 if spread <= 4 else 40),
        name="pairs",
    )(member, scalars, proj_weight, own_half, own_proj, got_half, text_emb)
    all_feats, unit_part, inv_part, img_emb, grad_tile, own_part, sent_part = results
    got_part = swapped(sent_part, total, 1)
    feats_t, own_text, *sent_text = pl.pallas_call(
        functools.partial(caption_kernel, rows),
        in_specs=[VMEM] * 3,
        out_specs=[VMEM] * (1 + spread),
        out_shape=[jax.ShapeDtypeStruct((width, images), BF16), jax.ShapeDtypeStruct((rows, width), F32)]
        + [jax.ShapeDtypeStruct((rows, width), BF16)] * (spread - 1),
        compiler_params=limit(12 if spread <= 4 else 24),
        name="captions",
    )(grad_tile, img_emb, all_feats)
    own_part, got_part, sent_text = lax.optimization_barrier((own_part, got_part, sent_text))
    got_text = [swapped(value, total, step * group) for step, value in enumerate(sent_text, 1)]
    own_part, *chip_parts = pl.pallas_call(
        chip_kernel,
        in_specs=[VMEM] * 2,
        out_specs=[VMEM] * (group // 2),
        out_shape=[jax.ShapeDtypeStruct((share + 8, images), F32)]
        + [jax.ShapeDtypeStruct((share + STAT_ROWS, images), BF16)] * (group // 2 - 1),
        compiler_params=limit(12),
        name="chip_sum",
    )(own_part, got_part)
    got = [swapped(value, total, 2 * index) for index, value in enumerate(chip_parts, 1)]

    out_rows = width // wide
    rest = share - LANES
    packed = out_rows + 2 * rest
    direct = LANES < out_rows <= 2 * LANES and out_rows % 16 == 0 and rest % 16 == 0
    if direct:
        loss_line, sent_weight = pl.pallas_call(
            functools.partial(weight_kernel, group, wide),
            in_specs=[VMEM] * (4 + group // 2),
            out_specs=[VMEM] * 2,
            out_shape=[
                jax.ShapeDtypeStruct((1, images), F32),
                jax.ShapeDtypeStruct((wide, packed, LANES), BF16),
            ],
            compiler_params=limit(12),
            name="weights",
        )(own_part, *got, unit_part, inv_part, all_feats, feats_t)
        got_weight = lax.all_to_all(sent_weight, AXES[:2], 0, 0)
        d_proj = pl.pallas_call(
            functools.partial(total_kernel, rest),
            in_specs=[VMEM],
            out_specs=VMEM,
            out_shape=jax.ShapeDtypeStruct((out_rows, 2 * share), F32),
            compiler_params=limit(4),
            name="weight_total",
        )(got_weight)
    else:

        def gradient_kernel(*refs):
            own_ref, blocks = refs[0], refs[1 : group // 2]
            unit_ref, inv_ref, loss_out, d_out = refs[group // 2 :]
            d_out[...] = gathered_gradient(own_ref, blocks, unit_ref, inv_ref, loss_out)

        loss_line, d_zproj = pl.pallas_call(
            gradient_kernel,
            in_specs=[VMEM] * (2 + group // 2),
            out_specs=[VMEM] * 2,
            out_shape=[jax.ShapeDtypeStruct((1, images), F32), jax.ShapeDtypeStruct((share, images), F32)],
            compiler_params=limit(12),
            name="gradient",
        )(own_part, *got, unit_part, inv_part)
        partial = sum(
            lax.dot_general(feats_t, part, NT, preferred_element_type=F32) for part in split_pair(d_zproj)
        )
        left = lax.axis_index("inner") == 0
        both = jnp.concatenate([jnp.where(left, partial, 0.0), jnp.where(left, 0.0, partial)], axis=1)
        d_proj = lax.psum_scatter(both, AXES[:2], scatter_dimension=0, tiled=True)

    d_text_unit = pl.pallas_call(
        sum_kernel,
        in_specs=[VMEM] * spread,
        out_specs=VMEM,
        out_shape=jax.ShapeDtypeStruct((rows, width), F32),
        compiler_params=limit(12),
        cost_estimate=hint(5 * 10**9),
        name="caption_total",
    )(own_text, *got_text)
    image_loss = lax.dynamic_slice_in_dim(loss_line[0], first_image(member[0], rows, group), rows, 0)
    return (image_loss, d_text_unit, d_proj)


def solution(mesh):
    wide, narrow = mesh.shape["wide"], mesh.shape["narrow"]
    cut = jax.sharding.Mesh(mesh.devices.reshape(wide // 2, 2, narrow), AXES)
    placed = (P(AXES, None), P(), P(AXES, None), P(), P())
    return jax.shard_map(
        functools.partial(local, wide, narrow),
        mesh=cut,
        in_specs=placed,
        out_specs=(P(AXES), P(AXES, None), P(AXES[:2], "narrow")),
        check_vma=False,
    )
```

```python
import functools

import jax
import jax.numpy as jnp
from jax import lax
from jax.experimental import pallas as pl
from jax.experimental.pallas import tpu as pltpu
from jax.sharding import PartitionSpec as P

AXES = ("outer", "inner", "narrow")
F32 = jnp.float32
BF16 = jnp.bfloat16
LANES = 128
STAT_ROWS = 16
VMEM = pl.BlockSpec(memory_space=pltpu.VMEM)
SMEM = pl.BlockSpec(memory_space=pltpu.SMEM)
NT = (((1,), (1,)), ((), ()))
TN = (((0,), (0,)), ((), ()))
MIB = 1024 * 1024


def limit(mebibytes):
    return pltpu.CompilerParams(vmem_limit_bytes=mebibytes * MIB)


def hint(flops):
    return pl.CostEstimate(flops=flops, bytes_accessed=0, transcendentals=0)


def swapped(value, total, mask):
    return lax.ppermute(value, AXES, [(source, source ^ mask) for source in range(total)])


def split_pair(values):
    high = values.astype(BF16)
    return high, (values - high.astype(F32)).astype(BF16)


def stat_rows(loss, along):
    row = lax.broadcasted_iota(jnp.int32, (STAT_ROWS, loss.shape[1]), 0)
    stats = jnp.zeros(row.shape, F32)
    for place, line in enumerate(split_pair(loss) + split_pair(along)):
        stats = jnp.where(row == place, line.astype(F32), stats)
    return stats.astype(BF16)


def stat_sums(stats):
    stats = stats.astype(F32)
    return stats[0:1, :] + stats[1:2, :], stats[2:3, :] + stats[3:4, :]


def column_block(member, narrow):
    return (member % narrow) * 2 + member // narrow


def unit_text(text):
    values = text.astype(F32)
    inverse = lax.rsqrt(jnp.sum(values * values, axis=1, keepdims=True) + 1e-06)
    return (values * inverse).astype(BF16)


def own_kernel(log_scale_ref, bias_ref, text_ref, text_out, scalars_out):
    text_out[...] = unit_text(text_ref[...])
    row = lax.broadcasted_iota(jnp.int32, scalars_out.shape, 0)
    scale = jnp.exp(jnp.full(scalars_out.shape, log_scale_ref[0], F32))
    scalars_out[...] = jnp.where(row == 0, scale, bias_ref[0])


def stack_kernel(member_ref, *refs):
    blocks, half_out = refs[:-1], refs[-1]
    rows = blocks[0].shape[0]
    chip = member_ref[0] // 2
    for step, block in enumerate(blocks):
        place = pl.multiple_of((chip ^ step) * rows, rows)
        half_out[pl.ds(place, rows), :] = block[...]


def text_kernel(*refs):
    texts, out = refs[:-1], refs[-1]
    rows = texts[0].shape[0]
    out[:rows, :] = texts[0][...]
    for place, text in enumerate(texts[1:], 1):
        step = len(texts) - place
        out[step * rows : (step + 1) * rows, :] = unit_text(text[...])


def project_kernel(feats_ref, weight_ref, out):
    out[...] = jnp.dot(feats_ref[...], weight_ref[...], preferred_element_type=F32)


def first_image(member, rows, group):
    return (member % 2) * (group // 2 * rows) + (member // 2) * rows


def pair_kernel(
    narrow,
    group,
    member_ref,
    scalars_ref,
    weight,
    own_half,
    own_proj,
    got_half,
    text_all,
    feats_ref,
    unit_out,
    inv_out,
    emb_out,
    grad_out,
    own_out,
    send_out,
    unit_all,
    d_all,
    proj_all,
):
    images, width = feats_ref.shape
    rows = images // group
    spread = text_all.shape[0] // rows
    half = images // 2
    share = width // group
    member = member_ref[0]

    place = pl.multiple_of((member % 2) * half, half)
    feats_ref[pl.ds(place, half), :] = own_half[...]
    proj_all[pl.ds(place, half), :] = own_proj[...]
    place = pl.multiple_of((1 - member % 2) * half, half)
    feats_ref[pl.ds(place, half), :] = got_half[...]
    proj_all[pl.ds(place, half), :] = jnp.dot(got_half[...], weight[...], preferred_element_type=F32)
    for start in range(0, images, LANES):
        cols = slice(start, start + LANES)
        turned = proj_all[cols, :].T
        inverse = lax.rsqrt(jnp.sum(turned * turned, axis=0, keepdims=True) + 1e-06)
        unit = turned * inverse
        inv_out[:, cols] = inverse
        unit_all[:, cols] = unit
        emb_out[:, cols] = unit.astype(BF16)
    block = pl.multiple_of(column_block(member, narrow) * share, share)
    unit_out[...] = unit_all[pl.ds(block, share), :]

    scale = scalars_ref[0:1, 0:1]
    shift = scalars_ref[1:2, 0:1]
    count = 4 * rows if spread % 4 == 0 else rows
    chunks = spread * rows // count

    def one_chunk(chunk, loss_sum, dot_sum, first):
        here = pl.ds(pl.multiple_of(chunk * count, count), count)
        text = text_all[here, :]
        products = jnp.dot(text, emb_out[...], preferred_element_type=F32)
        logits = scale * products + shift
        caption = lax.broadcasted_iota(jnp.int32, (count, images), 0) + chunk * count
        image = lax.broadcasted_iota(jnp.int32, (count, images), 1)
        own = jnp.logical_and(caption < rows, image == first_image(member, rows, group) + caption)
        sign = jnp.where(own, 1.0, -1.0).astype(F32)
        away = -sign * logits
        small = jnp.exp(-jnp.abs(away))
        loss = jnp.maximum(away, 0.0) + jnp.log1p(small)
        chance = jnp.where(away >= 0.0, 1.0, small) / (1.0 + small)
        grad = (-scale * sign * chance).astype(BF16)
        grad_out[here, :] = grad
        loss_sum = loss_sum + jnp.sum(loss, axis=0, keepdims=True)
        dot_sum = dot_sum + jnp.sum(grad.astype(F32) * products, axis=0, keepdims=True)
        d_img = lax.dot_general(text, grad, TN, preferred_element_type=F32)
        if first:
            d_all[...] = d_img
        else:
            d_all[...] += d_img
        return loss_sum, dot_sum

    zero = jnp.zeros((1, images), F32)
    sums = one_chunk(0, zero, zero, True)
    if chunks > 1:
        sums = lax.fori_loop(1, chunks, lambda c, s: one_chunk(c, *s, False), sums)
    loss_sum, dot_sum = sums

    stats = stat_rows(loss_sum, dot_sum)
    for index in range(group // 2):
        part = pl.multiple_of(column_block(member ^ (2 * index), narrow) * share, share)
        own_out[index, :share, :] = d_all[pl.ds(part, share), :]
        part = pl.multiple_of(column_block(member ^ (2 * index + 1), narrow) * share, share)
        send_out[index, :share, :] = d_all[pl.ds(part, share), :].astype(BF16)
        send_out[index, share:, :] = stats
    own_out[0, share : share + 1, :] = loss_sum
    own_out[0, share + 1 : share + 2, :] = dot_sum


def chip_kernel(own_ref, got_ref, own_out, *send_out):
    share = own_out.shape[0] - 8
    loss, along = stat_sums(got_ref[0, share:, :])
    loss = loss + own_ref[0, share : share + 1, :]
    along = along + own_ref[0, share + 1 : share + 2, :]
    own_out[:share, :] = own_ref[0, :share, :] + got_ref[0, :share, :].astype(F32)
    own_out[share : share + 1, :] = loss
    own_out[share + 1 : share + 2, :] = along
    stats = stat_rows(loss, along)
    for index, target in enumerate(send_out, 1):
        target[:share, :] = (own_ref[index, :share, :] + got_ref[index, :share, :].astype(F32)).astype(BF16)
        target[share:, :] = stats


def caption_kernel(rows, grad_ref, emb_ref, feats_ref, feats_t, *outs):
    for step, target in enumerate(outs):
        grad = grad_ref[step * rows : (step + 1) * rows, :]
        product = lax.dot_general(grad, emb_ref[...], NT, preferred_element_type=F32)
        target[...] = product.astype(target.dtype)
    for start in range(0, feats_ref.shape[0], LANES):
        cols = slice(start, start + LANES)
        feats_t[:, cols] = feats_ref[cols, :].astype(F32).T.astype(BF16)


def gathered_gradient(own_ref, got, unit_ref, inv_ref, loss_out):
    share = unit_ref.shape[0]
    total = own_ref[:share, :]
    loss = own_ref[share : share + 1, :]
    along = own_ref[share + 1 : share + 2, :]
    for block in got:
        total = total + block[:share, :].astype(F32)
        more_loss, more_along = stat_sums(block[share:, :])
        loss = loss + more_loss
        along = along + more_along
    loss_out[...] = loss
    return inv_ref[...] * (total - unit_ref[...] * along)


def weight_kernel(group, wide, *refs):
    wide_ref, own_ref = refs[:2]
    got = refs[2 : 1 + group // 2]
    unit_ref, inv_ref, feats_ref, feats_t_ref, loss_out, own_out = refs[1 + group // 2 : 7 + group // 2]
    send_out = refs[7 + group // 2 : 6 + group // 2 + wide]
    main_all, rest_all = refs[6 + group // 2 + wide :]
    share = unit_ref.shape[0]
    rest = share - LANES
    rows = feats_t_ref.shape[0] // wide
    high, low = split_pair(gathered_gradient(own_ref, got, unit_ref, inv_ref, loss_out))
    both = jnp.concatenate([high[:LANES, :], low[:LANES, :]], axis=0)
    main = lax.dot_general(feats_t_ref[...], both, NT, preferred_element_type=F32)
    main_all[...] = main[:, :LANES] + main[:, LANES:]
    both = jnp.concatenate([high[LANES:, :], low[LANES:, :]], axis=0)
    tail = jnp.dot(both, feats_ref[...], preferred_element_type=F32)
    tail = tail[:rest, :] + tail[rest:, :]
    for place in range(wide):
        begin = place * rows
        rest_all[place, :rest, :] = tail[:, begin : begin + LANES]
        rest_all[place, rest:, :] = jnp.zeros((rest, LANES), F32)
        rest_all[place, rest:, : rows - LANES] = tail[:, begin + LANES : begin + rows]
    for step in range(wide):
        place = wide_ref[0] ^ step
        target = own_out if step == 0 else send_out[step - 1]
        target[:rows, :] = main_all[pl.ds(pl.multiple_of(place * rows, rows), rows), :].astype(target.dtype)
        target[rows:, :] = rest_all[place].astype(target.dtype)


def total_kernel(rest, wide_ref, *refs):
    blocks, out = refs[:-1], refs[-1]
    rows = out.shape[0]
    same, other = blocks[0][...], blocks[1][...].astype(F32)
    for block in blocks[2::2]:
        same = same + block[...].astype(F32)
    for block in blocks[3::2]:
        other = other + block[...].astype(F32)
    left_is_same = wide_ref[0] % 2 == 0
    halves = (jnp.where(left_is_same, same, other), jnp.where(left_is_same, other, same))
    for side, half in enumerate(halves):
        left = side * (LANES + rest)
        out[:, left : left + LANES] = half[:rows, :]
        out[:LANES, left + LANES : left + LANES + rest] = half[rows : rows + rest, :].T
        out[LANES:, left + LANES : left + LANES + rest] = half[rows + rest :, :].T[: rows - LANES, :]


def sum_kernel(*refs):
    total = refs[0][...]
    for block in refs[1:-1]:
        total = total + block[...].astype(F32)
    refs[-1][...] = total


def local(wide, narrow, image_feats, proj_weight, text_embed, log_scale, logit_bias):
    rows, width = image_feats.shape
    total = wide * narrow
    group = 2 * narrow
    spread = wide // 2
    share = width // group
    images = group * rows
    member = lax.axis_index(AXES[1:]).astype(jnp.int32).reshape(1)

    texts = [swapped(text_embed, total, step * group) for step in range(1, spread)]
    got_feats = [swapped(image_feats, total, 2 * step) for step in range(1, group // 2)]
    own_text, scalars = pl.pallas_call(
        own_kernel,
        in_specs=[SMEM] * 2 + [VMEM],
        out_specs=[VMEM] * 2,
        out_shape=[jax.ShapeDtypeStruct((rows, width), BF16), jax.ShapeDtypeStruct((8, LANES), F32)],
        compiler_params=limit(4),
        cost_estimate=hint(10**10),
        name="own_text",
    )(log_scale, logit_bias, text_embed)
    own_half = pl.pallas_call(
        stack_kernel,
        in_specs=[SMEM] + [VMEM] * (group // 2),
        out_specs=VMEM,
        out_shape=jax.ShapeDtypeStruct((images // 2, width), BF16),
        compiler_params=limit(4),
        name="stack",
    )(member, image_feats, *got_feats)
    got_half = swapped(own_half, total, 1)
    own_proj = pl.pallas_call(
        project_kernel,
        in_specs=[VMEM] * 2,
        out_specs=VMEM,
        out_shape=jax.ShapeDtypeStruct((images // 2, width), F32),
        compiler_params=limit(8),
        name="own_projection",
    )(own_half, proj_weight)
    own_proj, *texts = lax.optimization_barrier((own_proj, *texts[::-1]))
    text_emb = pl.pallas_call(
        text_kernel,
        in_specs=[VMEM] * spread,
        out_specs=VMEM,
        out_shape=jax.ShapeDtypeStruct((spread * rows, width), BF16),
        compiler_params=limit(4 if spread <= 4 else 16),
        cost_estimate=hint(10**10),
        name="text_unit",
    )(own_text, *texts)

    results = pl.pallas_call(
        functools.partial(pair_kernel, narrow, group),
        in_specs=[SMEM] + [VMEM] * 6,
        out_specs=[VMEM] * 7,
        out_shape=[
            jax.ShapeDtypeStruct((images, width), BF16),
            jax.ShapeDtypeStruct((share, images), F32),
            jax.ShapeDtypeStruct((1, images), F32),
            jax.ShapeDtypeStruct((width, images), BF16),
            jax.ShapeDtypeStruct((spread * rows, images), BF16),
            jax.ShapeDtypeStruct((group // 2, share + 8, images), F32),
            jax.ShapeDtypeStruct((group // 2, share + STAT_ROWS, images), BF16),
        ],
        scratch_shapes=[
            pltpu.VMEM((width, images), F32),
            pltpu.VMEM((width, images), F32),
            pltpu.VMEM((images, width), F32),
        ],
        compiler_params=limit(24 if spread <= 4 else 40),
        name="pairs",
    )(member, scalars, proj_weight, own_half, own_proj, got_half, text_emb)
    all_feats, unit_part, inv_part, img_emb, grad_tile, own_part, sent_part = results
    got_part = swapped(sent_part, total, 1)
    feats_t, own_text, *sent_text = pl.pallas_call(
        functools.partial(caption_kernel, rows),
        in_specs=[VMEM] * 3,
        out_specs=[VMEM] * (1 + spread),
        out_shape=[jax.ShapeDtypeStruct((width, images), BF16), jax.ShapeDtypeStruct((rows, width), F32)]
        + [jax.ShapeDtypeStruct((rows, width), BF16)] * (spread - 1),
        compiler_params=limit(12 if spread <= 4 else 24),
        name="captions",
    )(grad_tile, img_emb, all_feats)
    own_part, got_part, sent_text = lax.optimization_barrier((own_part, got_part, sent_text))
    got_text = [swapped(value, total, step * group) for step, value in enumerate(sent_text, 1)]
    own_part, *chip_parts = pl.pallas_call(
        chip_kernel,
        in_specs=[VMEM] * 2,
        out_specs=[VMEM] * (group // 2),
        out_shape=[jax.ShapeDtypeStruct((share + 8, images), F32)]
        + [jax.ShapeDtypeStruct((share + STAT_ROWS, images), BF16)] * (group // 2 - 1),
        compiler_params=limit(12),
        name="chip_sum",
    )(own_part, got_part)
    got = [swapped(value, total, 2 * index) for index, value in enumerate(chip_parts, 1)]

    out_rows = width // wide
    rest = share - LANES
    packed = out_rows + 2 * rest
    direct = LANES < out_rows <= 2 * LANES and out_rows % 16 == 0 and rest % 16 == 0
    if direct:
        wide_pos = lax.axis_index(AXES[:2]).astype(jnp.int32).reshape(1)
        loss_line, own_weight, *sent_weight = pl.pallas_call(
            functools.partial(weight_kernel, group, wide),
            in_specs=[SMEM] + [VMEM] * (4 + group // 2),
            out_specs=[VMEM] * (1 + wide),
            out_shape=[jax.ShapeDtypeStruct((1, images), F32), jax.ShapeDtypeStruct((packed, LANES), F32)]
            + [jax.ShapeDtypeStruct((packed, LANES), BF16)] * (wide - 1),
            scratch_shapes=[pltpu.VMEM((width, LANES), F32), pltpu.VMEM((wide, 2 * rest, LANES), F32)],
            compiler_params=limit(12),
            name="weights",
        )(wide_pos, own_part, *got, unit_part, inv_part, all_feats, feats_t)
        got_weight = [swapped(value, total, step * narrow) for step, value in enumerate(sent_weight, 1)]
        got_weight = lax.optimization_barrier(got_weight[::-1])[::-1]
        d_proj = pl.pallas_call(
            functools.partial(total_kernel, rest),
            in_specs=[SMEM] + [VMEM] * wide,
            out_specs=VMEM,
            out_shape=jax.ShapeDtypeStruct((out_rows, 2 * share), F32),
            compiler_params=limit(4),
            name="weight_total",
        )(wide_pos, own_weight, *got_weight)
    else:

        def gradient_kernel(*refs):
            own_ref, blocks = refs[0], refs[1 : group // 2]
            unit_ref, inv_ref, loss_out, d_out = refs[group // 2 :]
            d_out[...] = gathered_gradient(own_ref, blocks, unit_ref, inv_ref, loss_out)

        loss_line, d_zproj = pl.pallas_call(
            gradient_kernel,
            in_specs=[VMEM] * (2 + group // 2),
            out_specs=[VMEM] * 2,
            out_shape=[jax.ShapeDtypeStruct((1, images), F32), jax.ShapeDtypeStruct((share, images), F32)],
            compiler_params=limit(12),
            name="gradient",
        )(own_part, *got, unit_part, inv_part)
        partial = sum(
            lax.dot_general(feats_t, part, NT, preferred_element_type=F32) for part in split_pair(d_zproj)
        )
        left = lax.axis_index("inner") == 0
        both = jnp.concatenate([jnp.where(left, partial, 0.0), jnp.where(left, 0.0, partial)], axis=1)
        d_proj = lax.psum_scatter(both, AXES[:2], scatter_dimension=0, tiled=True)

    d_text_unit = pl.pallas_call(
        sum_kernel,
        in_specs=[VMEM] * spread,
        out_specs=VMEM,
        out_shape=jax.ShapeDtypeStruct((rows, width), F32),
        compiler_params=limit(12),
        cost_estimate=hint(5 * 10**9),
        name="caption_total",
    )(own_text, *got_text[::-1])
    image_loss = lax.dynamic_slice_in_dim(loss_line[0], first_image(member[0], rows, group), rows, 0)
    return (image_loss, d_text_unit, d_proj)


def solution(mesh):
    wide, narrow = mesh.shape["wide"], mesh.shape["narrow"]
    cut = jax.sharding.Mesh(mesh.devices.reshape(wide // 2, 2, narrow), AXES)
    placed = (P(AXES, None), P(), P(AXES, None), P(), P())
    return jax.shard_map(
        functools.partial(local, wide, narrow),
        mesh=cut,
        in_specs=placed,
        out_specs=(P(AXES), P(AXES, None), P(AXES[:2], "narrow")),
        check_vma=False,
    )
```

```python
import functools

import jax
import jax.numpy as jnp
from jax import lax
from jax.experimental import pallas as pl
from jax.experimental.pallas import tpu as pltpu
from jax.sharding import PartitionSpec as P

AXES = ("outer", "inner", "narrow")
F32 = jnp.float32
BF16 = jnp.bfloat16
LANES = 128
STAT_ROWS = 16
VMEM = pl.BlockSpec(memory_space=pltpu.VMEM)
SMEM = pl.BlockSpec(memory_space=pltpu.SMEM)
NT = (((1,), (1,)), ((), ()))
TN = (((0,), (0,)), ((), ()))
MIB = 1024 * 1024


def limit(mebibytes):
    return pltpu.CompilerParams(vmem_limit_bytes=mebibytes * MIB)


def hint(flops):
    return pl.CostEstimate(flops=flops, bytes_accessed=0, transcendentals=0)


def swapped(value, total, mask):
    return lax.ppermute(value, AXES, [(source, source ^ mask) for source in range(total)])


def split_pair(values):
    high = values.astype(BF16)
    return high, (values - high.astype(F32)).astype(BF16)


def loss_rows(loss):
    row = lax.broadcasted_iota(jnp.int32, (STAT_ROWS, loss.shape[1]), 0)
    high, low = split_pair(loss)
    rows = jnp.where(row == 0, high.astype(F32), jnp.where(row == 1, low.astype(F32), 0.0))
    return rows.astype(BF16)


def loss_of(rows):
    rows = rows.astype(F32)
    return rows[0:1, :] + rows[1:2, :]


def column_block(member, narrow):
    return (member % narrow) * 2 + member // narrow


def unit_text(text):
    values = text.astype(F32)
    inverse = lax.rsqrt(jnp.sum(values * values, axis=1, keepdims=True) + 1e-06)
    return (values * inverse).astype(BF16)


def own_kernel(log_scale_ref, bias_ref, text_ref, text_out, scalars_out):
    text_out[...] = unit_text(text_ref[...])
    row = lax.broadcasted_iota(jnp.int32, scalars_out.shape, 0)
    scale = jnp.exp(jnp.full(scalars_out.shape, log_scale_ref[0], F32))
    scalars_out[...] = jnp.where(row == 0, scale, bias_ref[0])


def stack_kernel(member_ref, *refs):
    blocks, half_out = refs[:-1], refs[-1]
    rows = blocks[0].shape[0]
    chip = member_ref[0] // 2
    for step, block in enumerate(blocks):
        place = pl.multiple_of((chip ^ step) * rows, rows)
        half_out[pl.ds(place, rows), :] = block[...]


def text_kernel(*refs):
    texts, out = refs[:-1], refs[-1]
    rows = texts[0].shape[0]
    out[:rows, :] = texts[0][...]
    for place, text in enumerate(texts[1:], 1):
        step = len(texts) - place
        out[step * rows : (step + 1) * rows, :] = unit_text(text[...])


def project_kernel(feats_ref, weight_ref, out):
    out[...] = jnp.dot(feats_ref[...], weight_ref[...], preferred_element_type=F32)


def first_image(member, rows, group):
    return (member % 2) * (group // 2 * rows) + (member // 2) * rows


def pair_kernel(
    narrow,
    group,
    member_ref,
    scalars_ref,
    weight,
    own_half,
    own_proj,
    got_half,
    text_all,
    feats_ref,
    inv_out,
    emb_out,
    grad_out,
    own_out,
    send_out,
    unit_all,
    d_all,
    proj_all,
):
    images, width = feats_ref.shape
    rows = images // group
    spread = text_all.shape[0] // rows
    half = images // 2
    share = width // group
    member = member_ref[0]

    place = pl.multiple_of((member % 2) * half, half)
    feats_ref[pl.ds(place, half), :] = own_half[...]
    proj_all[pl.ds(place, half), :] = own_proj[...]
    place = pl.multiple_of((1 - member % 2) * half, half)
    feats_ref[pl.ds(place, half), :] = got_half[...]
    proj_all[pl.ds(place, half), :] = jnp.dot(got_half[...], weight[...], preferred_element_type=F32)
    for start in range(0, images, LANES):
        cols = slice(start, start + LANES)
        turned = proj_all[cols, :].T
        inverse = lax.rsqrt(jnp.sum(turned * turned, axis=0, keepdims=True) + 1e-06)
        unit = turned * inverse
        inv_out[:, cols] = inverse
        unit_all[:, cols] = unit
        emb_out[:, cols] = unit.astype(BF16)

    scale = scalars_ref[0:1, 0:1]
    shift = scalars_ref[1:2, 0:1]
    count = 4 * rows if spread % 4 == 0 else rows
    chunks = spread * rows // count

    def one_chunk(chunk, loss_sum, dot_sum, first):
        here = pl.ds(pl.multiple_of(chunk * count, count), count)
        text = text_all[here, :]
        products = jnp.dot(text, emb_out[...], preferred_element_type=F32)
        logits = scale * products + shift
        caption = lax.broadcasted_iota(jnp.int32, (count, images), 0) + chunk * count
        image = lax.broadcasted_iota(jnp.int32, (count, images), 1)
        own = jnp.logical_and(caption < rows, image == first_image(member, rows, group) + caption)
        sign = jnp.where(own, 1.0, -1.0).astype(F32)
        away = -sign * logits
        small = jnp.exp(-jnp.abs(away))
        loss = jnp.maximum(away, 0.0) + jnp.log1p(small)
        chance = jnp.where(away >= 0.0, 1.0, small) / (1.0 + small)
        grad = (-scale * sign * chance).astype(BF16)
        grad_out[here, :] = grad
        loss_sum = loss_sum + jnp.sum(loss, axis=0, keepdims=True)
        dot_sum = dot_sum + jnp.sum(grad.astype(F32) * products, axis=0, keepdims=True)
        d_img = lax.dot_general(text, grad, TN, preferred_element_type=F32)
        if first:
            d_all[...] = d_img
        else:
            d_all[...] += d_img
        return loss_sum, dot_sum

    zero = jnp.zeros((1, images), F32)
    sums = one_chunk(0, zero, zero, True)
    if chunks > 1:
        sums = lax.fori_loop(1, chunks, lambda c, s: one_chunk(c, *s, False), sums)
    loss_sum, dot_sum = sums

    def projected(index):
        part = pl.ds(pl.multiple_of(column_block(member ^ index, narrow) * share, share), share)
        return d_all[part, :] - unit_all[part, :] * dot_sum

    losses = loss_rows(loss_sum)
    for index in range(group // 2):
        own_out[index, :share, :] = projected(2 * index)
        send_out[index, :share, :] = projected(2 * index + 1).astype(BF16)
        send_out[index, share:, :] = losses
    own_out[0, share : share + 1, :] = loss_sum


def chip_kernel(own_ref, got_ref, own_out, *send_out):
    share = own_out.shape[0] - 8
    loss = own_ref[0, share : share + 1, :] + loss_of(got_ref[0, share:, :])
    own_out[:share, :] = own_ref[0, :share, :] + got_ref[0, :share, :].astype(F32)
    own_out[share : share + 1, :] = loss
    losses = loss_rows(loss)
    for index, target in enumerate(send_out, 1):
        target[:share, :] = (own_ref[index, :share, :] + got_ref[index, :share, :].astype(F32)).astype(BF16)
        target[share:, :] = losses


def caption_kernel(rows, grad_ref, emb_ref, feats_ref, feats_t, *outs):
    for step, target in enumerate(outs):
        grad = grad_ref[step * rows : (step + 1) * rows, :]
        product = lax.dot_general(grad, emb_ref[...], NT, preferred_element_type=F32)
        target[...] = product.astype(target.dtype)
    for start in range(0, feats_ref.shape[0], LANES):
        cols = slice(start, start + LANES)
        feats_t[:, cols] = feats_ref[cols, :].astype(F32).T.astype(BF16)


def gathered_gradient(own_ref, got, inv_ref, loss_out):
    share = own_ref.shape[0] - 8
    total = own_ref[:share, :]
    loss = own_ref[share : share + 1, :]
    for block in got:
        total = total + block[:share, :].astype(F32)
        loss = loss + loss_of(block[share:, :])
    loss_out[...] = loss
    return inv_ref[...] * total


def weight_kernel(group, spread, *refs):
    wide_ref, own_ref = refs[:2]
    got = refs[2 : 1 + group // 2]
    inv_ref, feats_ref, feats_t_ref, loss_out, own_out = refs[1 + group // 2 : 6 + group // 2]
    send_out = refs[6 + group // 2 : 5 + group // 2 + spread]
    main_all, rest_all = refs[5 + group // 2 + spread :]
    wide = 2 * spread
    rows = feats_t_ref.shape[0] // wide
    high, low = split_pair(gathered_gradient(own_ref, got, inv_ref, loss_out))
    rest = high.shape[0] - LANES
    both = jnp.concatenate([high[:LANES, :], low[:LANES, :]], axis=0)
    main = lax.dot_general(feats_t_ref[...], both, NT, preferred_element_type=F32)
    main_all[...] = main[:, :LANES] + main[:, LANES:]
    both = jnp.concatenate([high[LANES:, :], low[LANES:, :]], axis=0)
    tail = jnp.dot(both, feats_ref[...], preferred_element_type=F32)
    tail = tail[:rest, :] + tail[rest:, :]
    for place in range(wide):
        begin = place * rows
        rest_all[place, :rest, :] = tail[:, begin : begin + LANES]
        rest_all[place, rest:, :] = jnp.zeros((rest, LANES), F32)
        rest_all[place, rest:, : rows - LANES] = tail[:, begin + LANES : begin + rows]
    for step in range(spread):
        target = send_out[step - 1] if step else own_out
        for side in range(2):
            place = wide_ref[0] ^ (2 * step + side)
            begin = side * (rows + 2 * rest)
            part = main_all[pl.ds(pl.multiple_of(place * rows, rows), rows), :]
            target[begin : begin + rows, :] = part.astype(target.dtype)
            target[begin + rows : begin + rows + 2 * rest, :] = rest_all[place].astype(target.dtype)


def line_kernel(*refs):
    blocks, (own_out, send_out) = refs[:-2], refs[-2:]
    total = blocks[0][...]
    for block in blocks[1:]:
        total = total + block[...].astype(F32)
    packed = own_out.shape[0]
    own_out[...] = total[:packed, :]
    send_out[...] = total[packed:, :].astype(BF16)


def total_kernel(rest, wide_ref, same_ref, other_ref, out):
    rows = out.shape[0]
    same, other = same_ref[...], other_ref[...].astype(F32)
    left_is_same = wide_ref[0] % 2 == 0
    halves = (jnp.where(left_is_same, same, other), jnp.where(left_is_same, other, same))
    for side, half in enumerate(halves):
        left = side * (LANES + rest)
        out[:, left : left + LANES] = half[:rows, :]
        out[:LANES, left + LANES : left + LANES + rest] = half[rows : rows + rest, :].T
        out[LANES:, left + LANES : left + LANES + rest] = half[rows + rest :, :].T[: rows - LANES, :]


def sum_kernel(*refs):
    total = refs[0][...]
    for block in refs[1:-1]:
        total = total + block[...].astype(F32)
    refs[-1][...] = total


def local(wide, narrow, image_feats, proj_weight, text_embed, log_scale, logit_bias):
    rows, width = image_feats.shape
    total = wide * narrow
    group = 2 * narrow
    spread = wide // 2
    share = width // group
    images = group * rows
    member = lax.axis_index(AXES[1:]).astype(jnp.int32).reshape(1)

    texts = [swapped(text_embed, total, step * group) for step in range(1, spread)]
    got_feats = [swapped(image_feats, total, 2 * step) for step in range(1, group // 2)]
    own_text, scalars = pl.pallas_call(
        own_kernel,
        in_specs=[SMEM] * 2 + [VMEM],
        out_specs=[VMEM] * 2,
        out_shape=[jax.ShapeDtypeStruct((rows, width), BF16), jax.ShapeDtypeStruct((8, LANES), F32)],
        compiler_params=limit(4),
        cost_estimate=hint(10**10),
        name="own_text",
    )(log_scale, logit_bias, text_embed)
    own_half = pl.pallas_call(
        stack_kernel,
        in_specs=[SMEM] + [VMEM] * (group // 2),
        out_specs=VMEM,
        out_shape=jax.ShapeDtypeStruct((images // 2, width), BF16),
        compiler_params=limit(4),
        name="stack",
    )(member, image_feats, *got_feats)
    got_half = swapped(own_half, total, 1)
    own_proj = pl.pallas_call(
        project_kernel,
        in_specs=[VMEM] * 2,
        out_specs=VMEM,
        out_shape=jax.ShapeDtypeStruct((images // 2, width), F32),
        compiler_params=limit(8),
        name="own_projection",
    )(own_half, proj_weight)
    own_proj, *texts = lax.optimization_barrier((own_proj, *texts[::-1]))
    text_emb = pl.pallas_call(
        text_kernel,
        in_specs=[VMEM] * spread,
        out_specs=VMEM,
        out_shape=jax.ShapeDtypeStruct((spread * rows, width), BF16),
        compiler_params=limit(4 if spread <= 4 else 16),
        cost_estimate=hint(10**10),
        name="text_unit",
    )(own_text, *texts)

    results = pl.pallas_call(
        functools.partial(pair_kernel, narrow, group),
        in_specs=[SMEM] + [VMEM] * 6,
        out_specs=[VMEM] * 6,
        out_shape=[
            jax.ShapeDtypeStruct((images, width), BF16),
            jax.ShapeDtypeStruct((1, images), F32),
            jax.ShapeDtypeStruct((width, images), BF16),
            jax.ShapeDtypeStruct((spread * rows, images), BF16),
            jax.ShapeDtypeStruct((group // 2, share + 8, images), F32),
            jax.ShapeDtypeStruct((group // 2, share + STAT_ROWS, images), BF16),
        ],
        scratch_shapes=[
            pltpu.VMEM((width, images), F32),
            pltpu.VMEM((width, images), F32),
            pltpu.VMEM((images, width), F32),
        ],
        compiler_params=limit(24 if spread <= 4 else 40),
        name="pairs",
    )(member, scalars, proj_weight, own_half, own_proj, got_half, text_emb)
    all_feats, inv_part, img_emb, grad_tile, own_part, sent_part = results
    got_part = swapped(sent_part, total, 1)
    feats_t, own_text, *sent_text = pl.pallas_call(
        functools.partial(caption_kernel, rows),
        in_specs=[VMEM] * 3,
        out_specs=[VMEM] * (1 + spread),
        out_shape=[jax.ShapeDtypeStruct((width, images), BF16), jax.ShapeDtypeStruct((rows, width), F32)]
        + [jax.ShapeDtypeStruct((rows, width), BF16)] * (spread - 1),
        compiler_params=limit(12 if spread <= 4 else 24),
        name="captions",
    )(grad_tile, img_emb, all_feats)
    own_part, got_part, sent_text = lax.optimization_barrier((own_part, got_part, sent_text))
    got_text = [swapped(value, total, step * group) for step, value in enumerate(sent_text, 1)]
    own_part, *chip_parts = pl.pallas_call(
        chip_kernel,
        in_specs=[VMEM] * 2,
        out_specs=[VMEM] * (group // 2),
        out_shape=[jax.ShapeDtypeStruct((share + 8, images), F32)]
        + [jax.ShapeDtypeStruct((share + STAT_ROWS, images), BF16)] * (group // 2 - 1),
        compiler_params=limit(12),
        name="chip_sum",
    )(own_part, got_part)
    got = [swapped(value, total, 2 * index) for index, value in enumerate(chip_parts, 1)]

    out_rows = width // wide
    rest = share - LANES
    packed = out_rows + 2 * rest
    direct = LANES < out_rows <= 2 * LANES and out_rows % 16 == 0 and rest % 16 == 0
    if direct:
        wide_pos = lax.axis_index(AXES[:2]).astype(jnp.int32).reshape(1)
        loss_line, own_weight, *sent_weight = pl.pallas_call(
            functools.partial(weight_kernel, group, spread),
            in_specs=[SMEM] + [VMEM] * (3 + group // 2),
            out_specs=[VMEM] * (1 + spread),
            out_shape=[jax.ShapeDtypeStruct((1, images), F32), jax.ShapeDtypeStruct((2 * packed, LANES), F32)]
            + [jax.ShapeDtypeStruct((2 * packed, LANES), BF16)] * (spread - 1),
            scratch_shapes=[pltpu.VMEM((width, LANES), F32), pltpu.VMEM((wide, 2 * rest, LANES), F32)],
            compiler_params=limit(12),
            name="weights",
        )(wide_pos, own_part, *got, inv_part, all_feats, feats_t)
        got_weight = [swapped(value, total, step * group) for step, value in enumerate(sent_weight, 1)]
        own_weight, sent_weight = pl.pallas_call(
            line_kernel,
            in_specs=[VMEM] * spread,
            out_specs=[VMEM] * 2,
            out_shape=[jax.ShapeDtypeStruct((packed, LANES), kind) for kind in (F32, BF16)],
            compiler_params=limit(4),
            name="weight_line",
        )(own_weight, *got_weight[::-1])
        got_weight = swapped(sent_weight, total, narrow)
        d_proj = pl.pallas_call(
            functools.partial(total_kernel, rest),
            in_specs=[SMEM] + [VMEM] * 2,
            out_specs=VMEM,
            out_shape=jax.ShapeDtypeStruct((out_rows, 2 * share), F32),
            compiler_params=limit(4),
            name="weight_total",
        )(wide_pos, own_weight, got_weight)
    else:

        def gradient_kernel(*refs):
            own_ref, blocks = refs[0], refs[1 : group // 2]
            inv_ref, loss_out, d_out = refs[group // 2 :]
            d_out[...] = gathered_gradient(own_ref, blocks, inv_ref, loss_out)

        loss_line, d_zproj = pl.pallas_call(
            gradient_kernel,
            in_specs=[VMEM] * (1 + group // 2),
            out_specs=[VMEM] * 2,
            out_shape=[jax.ShapeDtypeStruct((1, images), F32), jax.ShapeDtypeStruct((share, images), F32)],
            compiler_params=limit(12),
            name="gradient",
        )(own_part, *got, inv_part)
        partial = sum(
            lax.dot_general(feats_t, part, NT, preferred_element_type=F32) for part in split_pair(d_zproj)
        )
        left = lax.axis_index("inner") == 0
        both = jnp.concatenate([jnp.where(left, partial, 0.0), jnp.where(left, 0.0, partial)], axis=1)
        d_proj = lax.psum_scatter(both, AXES[:2], scatter_dimension=0, tiled=True)

    d_text_unit = pl.pallas_call(
        sum_kernel,
        in_specs=[VMEM] * spread,
        out_specs=VMEM,
        out_shape=jax.ShapeDtypeStruct((rows, width), F32),
        compiler_params=limit(12),
        cost_estimate=hint(5 * 10**9),
        name="caption_total",
    )(own_text, *got_text[::-1])
    image_loss = lax.dynamic_slice_in_dim(loss_line[0], first_image(member[0], rows, group), rows, 0)
    return (image_loss, d_text_unit, d_proj)


def solution(mesh):
    wide, narrow = mesh.shape["wide"], mesh.shape["narrow"]
    cut = jax.sharding.Mesh(mesh.devices.reshape(wide // 2, 2, narrow), AXES)
    placed = (P(AXES, None), P(), P(AXES, None), P(), P())
    return jax.shard_map(
        functools.partial(local, wide, narrow),
        mesh=cut,
        in_specs=placed,
        out_specs=(P(AXES), P(AXES, None), P(AXES[:2], "narrow")),
        check_vma=False,
    )
```

```python
import functools

import jax
import jax.numpy as jnp
from jax import lax
from jax.experimental import pallas as pl
from jax.experimental.pallas import tpu as pltpu
from jax.sharding import PartitionSpec as P

AXES = ("outer", "inner", "narrow")
F32 = jnp.float32
BF16 = jnp.bfloat16
LANES = 128
STAT_ROWS = 16
VMEM = pl.BlockSpec(memory_space=pltpu.VMEM)
SMEM = pl.BlockSpec(memory_space=pltpu.SMEM)
NT = (((1,), (1,)), ((), ()))
TN = (((0,), (0,)), ((), ()))
MIB = 1024 * 1024


def limit(mebibytes):
    return pltpu.CompilerParams(vmem_limit_bytes=mebibytes * MIB)


def hint(flops):
    return pl.CostEstimate(flops=flops, bytes_accessed=0, transcendentals=0)


def swapped(value, total, mask):
    return lax.ppermute(value, AXES, [(source, source ^ mask) for source in range(total)])


def split_pair(values):
    high = values.astype(BF16)
    return high, (values - high.astype(F32)).astype(BF16)


def loss_rows(loss):
    row = lax.broadcasted_iota(jnp.int32, (STAT_ROWS, loss.shape[1]), 0)
    high, low = split_pair(loss)
    rows = jnp.where(row == 0, high.astype(F32), jnp.where(row == 1, low.astype(F32), 0.0))
    return rows.astype(BF16)


def loss_of(rows):
    rows = rows.astype(F32)
    return rows[0:1, :] + rows[1:2, :]


def column_block(member, narrow):
    return (member % narrow) * 2 + member // narrow


def unit_text(text):
    values = text.astype(F32)
    inverse = lax.rsqrt(jnp.sum(values * values, axis=1, keepdims=True) + 1e-06)
    return (values * inverse).astype(BF16)


def own_kernel(log_scale_ref, bias_ref, text_ref, text_out, scalars_out):
    text_out[...] = unit_text(text_ref[...])
    row = lax.broadcasted_iota(jnp.int32, scalars_out.shape, 0)
    scale = jnp.exp(jnp.full(scalars_out.shape, log_scale_ref[0], F32))
    scalars_out[...] = jnp.where(row == 0, scale, bias_ref[0])


def stack_kernel(member_ref, *refs):
    blocks, half_out = refs[:-1], refs[-1]
    rows = blocks[0].shape[0]
    chip = member_ref[0] // 2
    for step, block in enumerate(blocks):
        place = pl.multiple_of((chip ^ step) * rows, rows)
        half_out[pl.ds(place, rows), :] = block[...]


def text_kernel(*refs):
    texts, out = refs[:-1], refs[-1]
    rows = texts[0].shape[0]
    out[:rows, :] = texts[0][...]
    for place, text in enumerate(texts[1:], 1):
        step = len(texts) - place
        out[step * rows : (step + 1) * rows, :] = unit_text(text[...])


def project_kernel(feats_ref, weight_ref, out):
    out[...] = jnp.dot(feats_ref[...], weight_ref[...], preferred_element_type=F32)


def first_image(member, rows, group):
    return (member % 2) * (group // 2 * rows) + (member // 2) * rows


def pair_kernel(
    narrow,
    group,
    member_ref,
    scalars_ref,
    weight,
    own_half,
    own_proj,
    got_half,
    text_all,
    feats_ref,
    inv_out,
    emb_out,
    grad_out,
    own_out,
    send_out,
    unit_all,
    d_all,
    proj_all,
):
    images, width = feats_ref.shape
    rows = images // group
    spread = text_all.shape[0] // rows
    half = images // 2
    share = width // group
    member = member_ref[0]

    place = pl.multiple_of((member % 2) * half, half)
    feats_ref[pl.ds(place, half), :] = own_half[...]
    proj_all[pl.ds(place, half), :] = own_proj[...]
    place = pl.multiple_of((1 - member % 2) * half, half)
    feats_ref[pl.ds(place, half), :] = got_half[...]
    proj_all[pl.ds(place, half), :] = jnp.dot(got_half[...], weight[...], preferred_element_type=F32)
    for start in range(0, images, LANES):
        cols = slice(start, start + LANES)
        turned = proj_all[cols, :].T
        inverse = lax.rsqrt(jnp.sum(turned * turned, axis=0, keepdims=True) + 1e-06)
        unit = turned * inverse
        inv_out[:, cols] = inverse
        unit_all[:, cols] = unit
        emb_out[:, cols] = unit.astype(BF16)

    scale = scalars_ref[0:1, 0:1]
    shift = scalars_ref[1:2, 0:1]
    count = 4 * rows if spread % 4 == 0 else rows
    chunks = spread * rows // count

    def one_chunk(chunk, loss_sum, dot_sum, first):
        here = pl.ds(pl.multiple_of(chunk * count, count), count)
        text = text_all[here, :]
        products = jnp.dot(text, emb_out[...], preferred_element_type=F32)
        logits = scale * products + shift
        caption = lax.broadcasted_iota(jnp.int32, (count, images), 0) + chunk * count
        image = lax.broadcasted_iota(jnp.int32, (count, images), 1)
        own = jnp.logical_and(caption < rows, image == first_image(member, rows, group) + caption)
        sign = jnp.where(own, 1.0, -1.0).astype(F32)
        away = -sign * logits
        small = jnp.exp(-jnp.abs(away))
        loss = jnp.maximum(away, 0.0) + jnp.log1p(small)
        chance = jnp.where(away >= 0.0, 1.0, small) / (1.0 + small)
        grad = (-scale * sign * chance).astype(BF16)
        grad_out[here, :] = grad
        loss_sum = loss_sum + jnp.sum(loss, axis=0, keepdims=True)
        dot_sum = dot_sum + jnp.sum(grad.astype(F32) * products, axis=0, keepdims=True)
        d_img = lax.dot_general(text, grad, TN, preferred_element_type=F32)
        if first:
            d_all[...] = d_img
        else:
            d_all[...] += d_img
        return loss_sum, dot_sum

    zero = jnp.zeros((1, images), F32)
    sums = one_chunk(0, zero, zero, True)
    if chunks > 1:
        sums = lax.fori_loop(1, chunks, lambda c, s: one_chunk(c, *s, False), sums)
    loss_sum, dot_sum = sums

    def projected(index):
        part = pl.ds(pl.multiple_of(column_block(member ^ index, narrow) * share, share), share)
        return d_all[part, :] - unit_all[part, :] * dot_sum

    losses = loss_rows(loss_sum)
    for index in range(group // 2):
        own_out[index, :share, :] = projected(2 * index)
        send_out[index, :share, :] = projected(2 * index + 1).astype(BF16)
        send_out[index, share:, :] = losses
    own_out[0, share : share + 1, :] = loss_sum


def chip_kernel(own_ref, got_ref, own_out, *send_out):
    share = own_out.shape[0] - 8
    loss = own_ref[0, share : share + 1, :] + loss_of(got_ref[0, share:, :])
    own_out[:share, :] = own_ref[0, :share, :] + got_ref[0, :share, :].astype(F32)
    own_out[share : share + 1, :] = loss
    losses = loss_rows(loss)
    for index, target in enumerate(send_out, 1):
        target[:share, :] = (own_ref[index, :share, :] + got_ref[index, :share, :].astype(F32)).astype(BF16)
        target[share:, :] = losses


def caption_kernel(rows, grad_ref, emb_ref, feats_ref, feats_t, *outs):
    for step, target in enumerate(outs):
        grad = grad_ref[step * rows : (step + 1) * rows, :]
        product = lax.dot_general(grad, emb_ref[...], NT, preferred_element_type=F32)
        target[...] = product.astype(target.dtype)
    for start in range(0, feats_ref.shape[0], LANES):
        cols = slice(start, start + LANES)
        feats_t[:, cols] = feats_ref[cols, :].astype(F32).T.astype(BF16)


def gathered_gradient(own_ref, got, inv_ref, loss_out):
    share = own_ref.shape[0] - 8
    total = own_ref[:share, :]
    loss = own_ref[share : share + 1, :]
    for block in got:
        total = total + block[:share, :].astype(F32)
        loss = loss + loss_of(block[share:, :])
    loss_out[...] = loss
    return inv_ref[...] * total


def weight_kernel(group, wide, *refs):
    wide_ref, own_ref = refs[:2]
    got = refs[2 : 1 + group // 2]
    inv_ref, feats_ref, feats_t_ref, loss_out, own_out = refs[1 + group // 2 : 6 + group // 2]
    send_out = refs[6 + group // 2 : 5 + group // 2 + wide]
    main_all, rest_all = refs[5 + group // 2 + wide :]
    rows = feats_t_ref.shape[0] // wide
    high, low = split_pair(gathered_gradient(own_ref, got, inv_ref, loss_out))
    rest = high.shape[0] - LANES
    both = jnp.concatenate([high[:LANES, :], low[:LANES, :]], axis=0)
    main = lax.dot_general(feats_t_ref[...], both, NT, preferred_element_type=F32)
    main_all[...] = main[:, :LANES] + main[:, LANES:]
    both = jnp.concatenate([high[LANES:, :], low[LANES:, :]], axis=0)
    tail = jnp.dot(both, feats_ref[...], preferred_element_type=F32)
    tail = tail[:rest, :] + tail[rest:, :]
    for place in range(wide):
        begin = place * rows
        rest_all[place, :rest, :] = tail[:, begin : begin + LANES]
        rest_all[place, rest:, :] = jnp.zeros((rest, LANES), F32)
        rest_all[place, rest:, : rows - LANES] = tail[:, begin + LANES : begin + rows]
    for step in range(wide):
        place = wide_ref[0] ^ step
        target = own_out if step == 0 else send_out[step - 1]
        target[:rows, :] = main_all[pl.ds(pl.multiple_of(place * rows, rows), rows), :].astype(target.dtype)
        target[rows:, :] = rest_all[place].astype(target.dtype)


def total_kernel(rest, wide_ref, *refs):
    blocks, out = refs[:-1], refs[-1]
    rows = out.shape[0]
    same, other = blocks[0][...], blocks[1][...].astype(F32)
    for block in blocks[2::2]:
        same = same + block[...].astype(F32)
    for block in blocks[3::2]:
        other = other + block[...].astype(F32)
    left_is_same = wide_ref[0] % 2 == 0
    halves = (jnp.where(left_is_same, same, other), jnp.where(left_is_same, other, same))
    for side, half in enumerate(halves):
        left = side * (LANES + rest)
        out[:, left : left + LANES] = half[:rows, :]
        out[:LANES, left + LANES : left + LANES + rest] = half[rows : rows + rest, :].T
        out[LANES:, left + LANES : left + LANES + rest] = half[rows + rest :, :].T[: rows - LANES, :]


def sum_kernel(*refs):
    total = refs[0][...]
    for block in refs[1:-1]:
        total = total + block[...].astype(F32)
    refs[-1][...] = total


def local(wide, narrow, image_feats, proj_weight, text_embed, log_scale, logit_bias):
    rows, width = image_feats.shape
    total = wide * narrow
    group = 2 * narrow
    spread = wide // 2
    share = width // group
    images = group * rows
    member = lax.axis_index(AXES[1:]).astype(jnp.int32).reshape(1)

    texts = [swapped(text_embed, total, step * group) for step in range(1, spread)]
    got_feats = [swapped(image_feats, total, 2 * step) for step in range(1, group // 2)]
    own_text, scalars = pl.pallas_call(
        own_kernel,
        in_specs=[SMEM] * 2 + [VMEM],
        out_specs=[VMEM] * 2,
        out_shape=[jax.ShapeDtypeStruct((rows, width), BF16), jax.ShapeDtypeStruct((8, LANES), F32)],
        compiler_params=limit(4),
        cost_estimate=hint(10**10),
        name="own_text",
    )(log_scale, logit_bias, text_embed)
    own_half = pl.pallas_call(
        stack_kernel,
        in_specs=[SMEM] + [VMEM] * (group // 2),
        out_specs=VMEM,
        out_shape=jax.ShapeDtypeStruct((images // 2, width), BF16),
        compiler_params=limit(4),
        name="stack",
    )(member, image_feats, *got_feats)
    got_half = swapped(own_half, total, 1)
    own_proj = pl.pallas_call(
        project_kernel,
        in_specs=[VMEM] * 2,
        out_specs=VMEM,
        out_shape=jax.ShapeDtypeStruct((images // 2, width), F32),
        compiler_params=limit(8),
        name="own_projection",
    )(own_half, proj_weight)
    own_proj, *texts = lax.optimization_barrier((own_proj, *texts[::-1]))
    text_emb = pl.pallas_call(
        text_kernel,
        in_specs=[VMEM] * spread,
        out_specs=VMEM,
        out_shape=jax.ShapeDtypeStruct((spread * rows, width), BF16),
        compiler_params=limit(4 if spread <= 4 else 16),
        cost_estimate=hint(10**10),
        name="text_unit",
    )(own_text, *texts)

    results = pl.pallas_call(
        functools.partial(pair_kernel, narrow, group),
        in_specs=[SMEM] + [VMEM] * 6,
        out_specs=[VMEM] * 6,
        out_shape=[
            jax.ShapeDtypeStruct((images, width), BF16),
            jax.ShapeDtypeStruct((1, images), F32),
            jax.ShapeDtypeStruct((width, images), BF16),
            jax.ShapeDtypeStruct((spread * rows, images), BF16),
            jax.ShapeDtypeStruct((group // 2, share + 8, images), F32),
            jax.ShapeDtypeStruct((group // 2, share + STAT_ROWS, images), BF16),
        ],
        scratch_shapes=[
            pltpu.VMEM((width, images), F32),
            pltpu.VMEM((width, images), F32),
            pltpu.VMEM((images, width), F32),
        ],
        compiler_params=limit(24 if spread <= 4 else 40),
        name="pairs",
    )(member, scalars, proj_weight, own_half, own_proj, got_half, text_emb)
    all_feats, inv_part, img_emb, grad_tile, own_part, sent_part = results
    got_part = swapped(sent_part, total, 1)
    feats_t, own_text, *sent_text = pl.pallas_call(
        functools.partial(caption_kernel, rows),
        in_specs=[VMEM] * 3,
        out_specs=[VMEM] * (1 + spread),
        out_shape=[jax.ShapeDtypeStruct((width, images), BF16), jax.ShapeDtypeStruct((rows, width), F32)]
        + [jax.ShapeDtypeStruct((rows, width), BF16)] * (spread - 1),
        compiler_params=limit(12 if spread <= 4 else 24),
        name="captions",
    )(grad_tile, img_emb, all_feats)
    own_part, got_part, sent_text = lax.optimization_barrier((own_part, got_part, sent_text))
    got_text = [swapped(value, total, step * group) for step, value in enumerate(sent_text, 1)]
    own_part, *chip_parts = pl.pallas_call(
        chip_kernel,
        in_specs=[VMEM] * 2,
        out_specs=[VMEM] * (group // 2),
        out_shape=[jax.ShapeDtypeStruct((share + 8, images), F32)]
        + [jax.ShapeDtypeStruct((share + STAT_ROWS, images), BF16)] * (group // 2 - 1),
        compiler_params=limit(12),
        name="chip_sum",
    )(own_part, got_part)
    got = [swapped(value, total, 2 * index) for index, value in enumerate(chip_parts, 1)]

    out_rows = width // wide
    rest = share - LANES
    packed = out_rows + 2 * rest
    direct = LANES < out_rows <= 2 * LANES and out_rows % 16 == 0 and rest % 16 == 0
    if direct:
        wide_pos = lax.axis_index(AXES[:2]).astype(jnp.int32).reshape(1)
        loss_line, own_weight, *sent_weight = pl.pallas_call(
            functools.partial(weight_kernel, group, wide),
            in_specs=[SMEM] + [VMEM] * (3 + group // 2),
            out_specs=[VMEM] * (1 + wide),
            out_shape=[jax.ShapeDtypeStruct((1, images), F32), jax.ShapeDtypeStruct((packed, LANES), F32)]
            + [jax.ShapeDtypeStruct((packed, LANES), BF16)] * (wide - 1),
            scratch_shapes=[pltpu.VMEM((width, LANES), F32), pltpu.VMEM((wide, 2 * rest, LANES), F32)],
            compiler_params=limit(12),
            name="weights",
        )(wide_pos, own_part, *got, inv_part, all_feats, feats_t)
        got_weight = [swapped(value, total, step * narrow) for step, value in enumerate(sent_weight, 1)]
        got_weight = lax.optimization_barrier(got_weight[::-1])[::-1]
        d_proj = pl.pallas_call(
            functools.partial(total_kernel, rest),
            in_specs=[SMEM] + [VMEM] * wide,
            out_specs=VMEM,
            out_shape=jax.ShapeDtypeStruct((out_rows, 2 * share), F32),
            compiler_params=limit(4),
            name="weight_total",
        )(wide_pos, own_weight, *got_weight)
    else:

        def gradient_kernel(*refs):
            own_ref, blocks = refs[0], refs[1 : group // 2]
            inv_ref, loss_out, d_out = refs[group // 2 :]
            d_out[...] = gathered_gradient(own_ref, blocks, inv_ref, loss_out)

        loss_line, d_zproj = pl.pallas_call(
            gradient_kernel,
            in_specs=[VMEM] * (1 + group // 2),
            out_specs=[VMEM] * 2,
            out_shape=[jax.ShapeDtypeStruct((1, images), F32), jax.ShapeDtypeStruct((share, images), F32)],
            compiler_params=limit(12),
            name="gradient",
        )(own_part, *got, inv_part)
        partial = sum(
            lax.dot_general(feats_t, part, NT, preferred_element_type=F32) for part in split_pair(d_zproj)
        )
        left = lax.axis_index("inner") == 0
        both = jnp.concatenate([jnp.where(left, partial, 0.0), jnp.where(left, 0.0, partial)], axis=1)
        d_proj = lax.psum_scatter(both, AXES[:2], scatter_dimension=0, tiled=True)

    d_text_unit = pl.pallas_call(
        sum_kernel,
        in_specs=[VMEM] * spread,
        out_specs=VMEM,
        out_shape=jax.ShapeDtypeStruct((rows, width), F32),
        compiler_params=limit(12),
        cost_estimate=hint(5 * 10**9),
        name="caption_total",
    )(own_text, *got_text[::-1])
    image_loss = lax.dynamic_slice_in_dim(loss_line[0], first_image(member[0], rows, group), rows, 0)
    return (image_loss, d_text_unit, d_proj)


def solution(mesh):
    wide, narrow = mesh.shape["wide"], mesh.shape["narrow"]
    cut = jax.sharding.Mesh(mesh.devices.reshape(wide // 2, 2, narrow), AXES)
    placed = (P(AXES, None), P(), P(AXES, None), P(), P())
    return jax.shard_map(
        functools.partial(local, wide, narrow),
        mesh=cut,
        in_specs=placed,
        out_specs=(P(AXES), P(AXES, None), P(AXES[:2], "narrow")),
        check_vma=False,
    )
```

```python
import functools

import jax
import jax.numpy as jnp
from jax import lax
from jax.experimental import pallas as pl
from jax.experimental.pallas import tpu as pltpu
from jax.sharding import PartitionSpec as P

AXES = ("outer", "inner", "narrow")
F32 = jnp.float32
BF16 = jnp.bfloat16
LANES = 128
STAT_ROWS = 16
VMEM = pl.BlockSpec(memory_space=pltpu.VMEM)
SMEM = pl.BlockSpec(memory_space=pltpu.SMEM)
NT = (((1,), (1,)), ((), ()))
TN = (((0,), (0,)), ((), ()))
MIB = 1024 * 1024


def limit(mebibytes):
    return pltpu.CompilerParams(vmem_limit_bytes=mebibytes * MIB)


def hint(flops):
    return pl.CostEstimate(flops=flops, bytes_accessed=0, transcendentals=0)


def swapped(value, total, mask):
    return lax.ppermute(value, AXES, [(source, source ^ mask) for source in range(total)])


def split_pair(values):
    high = values.astype(BF16)
    return high, (values - high.astype(F32)).astype(BF16)


def loss_rows(loss):
    row = lax.broadcasted_iota(jnp.int32, (STAT_ROWS, loss.shape[1]), 0)
    high, low = split_pair(loss)
    rows = jnp.where(row == 0, high.astype(F32), jnp.where(row == 1, low.astype(F32), 0.0))
    return rows.astype(BF16)


def loss_of(rows):
    rows = rows.astype(F32)
    return rows[0:1, :] + rows[1:2, :]


def column_block(member, narrow):
    return (member % narrow) * 2 + member // narrow


def unit_text(text):
    values = text.astype(F32)
    inverse = lax.rsqrt(jnp.sum(values * values, axis=1, keepdims=True) + 1e-06)
    return (values * inverse).astype(BF16)


def own_kernel(log_scale_ref, bias_ref, text_ref, text_out, scalars_out):
    text_out[...] = unit_text(text_ref[...])
    row = lax.broadcasted_iota(jnp.int32, scalars_out.shape, 0)
    scale = jnp.exp(jnp.full(scalars_out.shape, log_scale_ref[0], F32))
    scalars_out[...] = jnp.where(row == 0, scale, bias_ref[0])


def stack_kernel(member_ref, *refs):
    blocks, half_out = refs[:-1], refs[-1]
    rows = blocks[0].shape[0]
    chip = member_ref[0] // 2
    for step, block in enumerate(blocks):
        place = pl.multiple_of((chip ^ step) * rows, rows)
        half_out[pl.ds(place, rows), :] = block[...]


def text_kernel(*refs):
    texts, out = refs[:-1], refs[-1]
    rows = texts[0].shape[0]
    out[:rows, :] = texts[0][...]
    for place, text in enumerate(texts[1:], 1):
        step = len(texts) - place
        out[step * rows : (step + 1) * rows, :] = unit_text(text[...])


def project_kernel(feats_ref, weight_ref, out):
    out[...] = jnp.dot(feats_ref[...], weight_ref[...], preferred_element_type=F32)


def first_image(member, rows, group):
    return (member % 2) * (group // 2 * rows) + (member // 2) * rows


def pair_kernel(
    narrow,
    group,
    member_ref,
    scalars_ref,
    weight,
    own_half,
    own_proj,
    got_half,
    text_all,
    feats_ref,
    inv_out,
    emb_out,
    grad_out,
    own_out,
    send_out,
    unit_all,
    d_all,
    proj_all,
):
    images, width = feats_ref.shape
    rows = images // group
    spread = text_all.shape[0] // rows
    half = images // 2
    share = width // group
    member = member_ref[0]

    place = pl.multiple_of((member % 2) * half, half)
    feats_ref[pl.ds(place, half), :] = own_half[...]
    proj_all[pl.ds(place, half), :] = own_proj[...]
    place = pl.multiple_of((1 - member % 2) * half, half)
    feats_ref[pl.ds(place, half), :] = got_half[...]
    proj_all[pl.ds(place, half), :] = jnp.dot(got_half[...], weight[...], preferred_element_type=F32)
    for start in range(0, images, LANES):
        cols = slice(start, start + LANES)
        turned = proj_all[cols, :].T
        inverse = lax.rsqrt(jnp.sum(turned * turned, axis=0, keepdims=True) + 1e-06)
        unit = turned * inverse
        inv_out[:, cols] = inverse
        unit_all[:, cols] = unit
        emb_out[:, cols] = unit.astype(BF16)

    scale = scalars_ref[0:1, 0:1]
    shift = scalars_ref[1:2, 0:1]
    count = 4 * rows if spread % 4 == 0 else rows
    chunks = spread * rows // count

    def one_chunk(chunk, loss_sum, dot_sum, first):
        here = pl.ds(pl.multiple_of(chunk * count, count), count)
        text = text_all[here, :]
        products = jnp.dot(text, emb_out[...], preferred_element_type=F32)
        logits = scale * products + shift
        caption = lax.broadcasted_iota(jnp.int32, (count, images), 0) + chunk * count
        image = lax.broadcasted_iota(jnp.int32, (count, images), 1)
        own = jnp.logical_and(caption < rows, image == first_image(member, rows, group) + caption)
        sign = jnp.where(own, 1.0, -1.0).astype(F32)
        away = -sign * logits
        small = jnp.exp(-jnp.abs(away))
        loss = jnp.maximum(away, 0.0) + jnp.log1p(small)
        chance = jnp.where(away >= 0.0, 1.0, small) / (1.0 + small)
        grad = (-scale * sign * chance).astype(BF16)
        grad_out[here, :] = grad
        loss_sum = loss_sum + jnp.sum(loss, axis=0, keepdims=True)
        dot_sum = dot_sum + jnp.sum(grad.astype(F32) * products, axis=0, keepdims=True)
        d_img = lax.dot_general(text, grad, TN, preferred_element_type=F32)
        if first:
            d_all[...] = d_img
        else:
            d_all[...] += d_img
        return loss_sum, dot_sum

    zero = jnp.zeros((1, images), F32)
    sums = one_chunk(0, zero, zero, True)
    if chunks > 1:
        sums = lax.fori_loop(1, chunks, lambda c, s: one_chunk(c, *s, False), sums)
    loss_sum, dot_sum = sums

    def projected(index):
        part = pl.ds(pl.multiple_of(column_block(member ^ index, narrow) * share, share), share)
        return d_all[part, :] - unit_all[part, :] * dot_sum

    losses = loss_rows(loss_sum)
    for index in range(group // 2):
        own_out[index, :share, :] = projected(2 * index)
        send_out[index, :share, :] = projected(2 * index + 1).astype(BF16)
        send_out[index, share:, :] = losses
    own_out[0, share : share + 1, :] = loss_sum


def chip_kernel(own_ref, got_ref, own_out, *send_out):
    share = own_out.shape[0] - 8
    loss = own_ref[0, share : share + 1, :] + loss_of(got_ref[0, share:, :])
    own_out[:share, :] = own_ref[0, :share, :] + got_ref[0, :share, :].astype(F32)
    own_out[share : share + 1, :] = loss
    losses = loss_rows(loss)
    for index, target in enumerate(send_out, 1):
        target[:share, :] = (own_ref[index, :share, :] + got_ref[index, :share, :].astype(F32)).astype(BF16)
        target[share:, :] = losses


def caption_kernel(rows, grad_ref, emb_ref, *outs):
    for step, target in enumerate(outs):
        grad = grad_ref[step * rows : (step + 1) * rows, :]
        product = lax.dot_general(grad, emb_ref[...], NT, preferred_element_type=F32)
        target[...] = product.astype(target.dtype)


def turn_kernel(feats_ref, feats_t):
    for start in range(0, feats_ref.shape[0], LANES):
        cols = slice(start, start + LANES)
        feats_t[:, cols] = feats_ref[cols, :].astype(F32).T.astype(BF16)


def gathered_gradient(own_ref, got, inv_ref, loss_out):
    share = own_ref.shape[0] - 8
    total = own_ref[:share, :]
    loss = own_ref[share : share + 1, :]
    for block in got:
        total = total + block[:share, :].astype(F32)
        loss = loss + loss_of(block[share:, :])
    loss_out[...] = loss
    return inv_ref[...] * total


def weight_kernel(group, wide, *refs):
    own_ref, got = refs[0], refs[1 : group // 2]
    inv_ref, feats_ref, feats_t_ref, loss_out, send_out = refs[group // 2 :]
    rows = feats_t_ref.shape[0] // wide
    high, low = split_pair(gathered_gradient(own_ref, got, inv_ref, loss_out))
    rest = high.shape[0] - LANES
    both = jnp.concatenate([high[LANES:, :], low[LANES:, :]], axis=0)
    tail = jnp.dot(both, feats_ref[...], preferred_element_type=F32)
    tail = (tail[:rest, :] + tail[rest:, :]).astype(BF16)
    both = jnp.concatenate([high[:LANES, :], low[:LANES, :]], axis=0)
    main = lax.dot_general(feats_t_ref[...], both, NT, preferred_element_type=F32)
    main = (main[:, :LANES] + main[:, LANES:]).astype(BF16)
    for place in range(wide):
        begin = place * rows
        send_out[place, :rows, :] = main[begin : begin + rows, :]
        send_out[place, rows : rows + rest, :] = tail[:, begin : begin + LANES]
        send_out[place, rows + rest :, :] = jnp.zeros((rest, LANES), BF16)
        send_out[place, rows + rest :, : rows - LANES] = tail[:, begin + LANES : begin + rows]


def total_kernel(rest, got_ref, out):
    rows = out.shape[0]
    for side in range(2):
        half = got_ref[side].astype(F32)
        for place in range(side + 2, got_ref.shape[0], 2):
            half = half + got_ref[place].astype(F32)
        left = side * (LANES + rest)
        out[:, left : left + LANES] = half[:rows, :]
        out[:LANES, left + LANES : left + LANES + rest] = half[rows : rows + rest, :].T
        out[LANES:, left + LANES : left + LANES + rest] = half[rows + rest :, :].T[: rows - LANES, :]


def sum_kernel(*refs):
    total = refs[0][...]
    for block in refs[1:-1]:
        total = total + block[...].astype(F32)
    refs[-1][...] = total


def add_text(own, parts, cost):
    return pl.pallas_call(
        sum_kernel,
        in_specs=[VMEM] * (1 + len(parts)),
        out_specs=VMEM,
        out_shape=jax.ShapeDtypeStruct(own.shape, F32),
        compiler_params=limit(12),
        cost_estimate=cost,
        name="caption_sum",
    )(own, *parts)


def local(wide, narrow, image_feats, proj_weight, text_embed, log_scale, logit_bias):
    rows, width = image_feats.shape
    total = wide * narrow
    group = 2 * narrow
    spread = wide // 2
    share = width // group
    images = group * rows
    member = lax.axis_index(AXES[1:]).astype(jnp.int32).reshape(1)

    texts = [swapped(text_embed, total, step * group) for step in range(1, spread)]
    got_feats = [swapped(image_feats, total, 2 * step) for step in range(1, group // 2)]
    own_text, scalars = pl.pallas_call(
        own_kernel,
        in_specs=[SMEM] * 2 + [VMEM],
        out_specs=[VMEM] * 2,
        out_shape=[jax.ShapeDtypeStruct((rows, width), BF16), jax.ShapeDtypeStruct((8, LANES), F32)],
        compiler_params=limit(4),
        cost_estimate=hint(10**10),
        name="own_text",
    )(log_scale, logit_bias, text_embed)
    own_half = pl.pallas_call(
        stack_kernel,
        in_specs=[SMEM] + [VMEM] * (group // 2),
        out_specs=VMEM,
        out_shape=jax.ShapeDtypeStruct((images // 2, width), BF16),
        compiler_params=limit(4),
        name="stack",
    )(member, image_feats, *got_feats)
    got_half = swapped(own_half, total, 1)
    own_proj = pl.pallas_call(
        project_kernel,
        in_specs=[VMEM] * 2,
        out_specs=VMEM,
        out_shape=jax.ShapeDtypeStruct((images // 2, width), F32),
        compiler_params=limit(8),
        name="own_projection",
    )(own_half, proj_weight)
    own_proj, *texts = lax.optimization_barrier((own_proj, *texts[::-1]))
    text_emb = pl.pallas_call(
        text_kernel,
        in_specs=[VMEM] * spread,
        out_specs=VMEM,
        out_shape=jax.ShapeDtypeStruct((spread * rows, width), BF16),
        compiler_params=limit(4 if spread <= 4 else 16),
        cost_estimate=hint(10**10),
        name="text_unit",
    )(own_text, *texts)

    results = pl.pallas_call(
        functools.partial(pair_kernel, narrow, group),
        in_specs=[SMEM] + [VMEM] * 6,
        out_specs=[VMEM] * 6,
        out_shape=[
            jax.ShapeDtypeStruct((images, width), BF16),
            jax.ShapeDtypeStruct((1, images), F32),
            jax.ShapeDtypeStruct((width, images), BF16),
            jax.ShapeDtypeStruct((spread * rows, images), BF16),
            jax.ShapeDtypeStruct((group // 2, share + 8, images), F32),
            jax.ShapeDtypeStruct((group // 2, share + STAT_ROWS, images), BF16),
        ],
        scratch_shapes=[
            pltpu.VMEM((width, images), F32),
            pltpu.VMEM((width, images), F32),
            pltpu.VMEM((images, width), F32),
        ],
        compiler_params=limit(24 if spread <= 4 else 40),
        name="pairs",
    )(member, scalars, proj_weight, own_half, own_proj, got_half, text_emb)
    all_feats, inv_part, img_emb, grad_tile, own_part, sent_part = results
    got_part = swapped(sent_part, total, 1)
    own_text, *sent_text = pl.pallas_call(
        functools.partial(caption_kernel, rows),
        in_specs=[VMEM] * 2,
        out_specs=[VMEM] * spread,
        out_shape=[jax.ShapeDtypeStruct((rows, width), F32)]
        + [jax.ShapeDtypeStruct((rows, width), BF16)] * (spread - 1),
        compiler_params=limit(12 if spread <= 4 else 24),
        name="captions",
    )(grad_tile, img_emb)
    feats_t = pl.pallas_call(
        turn_kernel,
        in_specs=[VMEM],
        out_specs=VMEM,
        out_shape=jax.ShapeDtypeStruct((width, images), BF16),
        compiler_params=limit(8),
        name="turn",
    )(all_feats)
    own_part, got_part, feats_t, sent_text[:1], sent_text[2:] = lax.optimization_barrier(
        (own_part, got_part, feats_t, sent_text[:1], sent_text[2:])
    )
    got_text = [swapped(value, total, step * group) for step, value in enumerate(sent_text, 1)]
    own_part, *chip_parts = pl.pallas_call(
        chip_kernel,
        in_specs=[VMEM] * 2,
        out_specs=[VMEM] * (group // 2),
        out_shape=[jax.ShapeDtypeStruct((share + 8, images), F32)]
        + [jax.ShapeDtypeStruct((share + STAT_ROWS, images), BF16)] * (group // 2 - 1),
        compiler_params=limit(12),
        name="chip_sum",
    )(own_part, got_part)
    got = [swapped(value, total, 2 * index) for index, value in enumerate(chip_parts, 1)]
    own_text = add_text(own_text, got_text[1:2], hint(10**10))
    own_text, got = lax.optimization_barrier((own_text, got))

    out_rows = width // wide
    rest = share - LANES
    packed = out_rows + 2 * rest
    direct = LANES < out_rows <= 2 * LANES and out_rows % 16 == 0 and rest % 16 == 0
    if direct:
        loss_line, sent_weight = pl.pallas_call(
            functools.partial(weight_kernel, group, wide),
            in_specs=[VMEM] * (3 + group // 2),
            out_specs=[VMEM] * 2,
            out_shape=[
                jax.ShapeDtypeStruct((1, images), F32),
                jax.ShapeDtypeStruct((wide, packed, LANES), BF16),
            ],
            compiler_params=limit(12),
            name="weights",
        )(own_part, *got, inv_part, all_feats, feats_t)
        got_weight = lax.all_to_all(sent_weight, AXES[:2], 0, 0)
        d_proj = pl.pallas_call(
            functools.partial(total_kernel, rest),
            in_specs=[VMEM],
            out_specs=VMEM,
            out_shape=jax.ShapeDtypeStruct((out_rows, 2 * share), F32),
            compiler_params=limit(4),
            name="weight_total",
        )(got_weight)
    else:

        def gradient_kernel(*refs):
            own_ref, blocks = refs[0], refs[1 : group // 2]
            inv_ref, loss_out, d_out = refs[group // 2 :]
            d_out[...] = gathered_gradient(own_ref, blocks, inv_ref, loss_out)

        loss_line, d_zproj = pl.pallas_call(
            gradient_kernel,
            in_specs=[VMEM] * (1 + group // 2),
            out_specs=[VMEM] * 2,
            out_shape=[jax.ShapeDtypeStruct((1, images), F32), jax.ShapeDtypeStruct((share, images), F32)],
            compiler_params=limit(12),
            name="gradient",
        )(own_part, *got, inv_part)
        partial = sum(
            lax.dot_general(feats_t, part, NT, preferred_element_type=F32) for part in split_pair(d_zproj)
        )
        left = lax.axis_index("inner") == 0
        both = jnp.concatenate([jnp.where(left, partial, 0.0), jnp.where(left, 0.0, partial)], axis=1)
        d_proj = lax.psum_scatter(both, AXES[:2], scatter_dimension=0, tiled=True)

    d_text_unit = add_text(own_text, [*got_text[:1:-1], *got_text[:1]], hint(5 * 10**9))
    image_loss = lax.dynamic_slice_in_dim(loss_line[0], first_image(member[0], rows, group), rows, 0)
    return (image_loss, d_text_unit, d_proj)


def solution(mesh):
    wide, narrow = mesh.shape["wide"], mesh.shape["narrow"]
    cut = jax.sharding.Mesh(mesh.devices.reshape(wide // 2, 2, narrow), AXES)
    placed = (P(AXES, None), P(), P(AXES, None), P(), P())
    return jax.shard_map(
        functools.partial(local, wide, narrow),
        mesh=cut,
        in_specs=placed,
        out_specs=(P(AXES), P(AXES, None), P(AXES[:2], "narrow")),
        check_vma=False,
    )
```

```python
import functools

import jax
import jax.numpy as jnp
from jax import lax
from jax.experimental import pallas as pl
from jax.experimental.pallas import tpu as pltpu
from jax.sharding import PartitionSpec as P

AXES = ("outer", "inner", "narrow")
F32 = jnp.float32
BF16 = jnp.bfloat16
LANES = 128
STAT_ROWS = 16
VMEM = pl.BlockSpec(memory_space=pltpu.VMEM)
SMEM = pl.BlockSpec(memory_space=pltpu.SMEM)
NT = (((1,), (1,)), ((), ()))
TN = (((0,), (0,)), ((), ()))
MIB = 1024 * 1024


def limit(mebibytes):
    return pltpu.CompilerParams(vmem_limit_bytes=mebibytes * MIB)


def hint(flops):
    return pl.CostEstimate(flops=flops, bytes_accessed=0, transcendentals=0)


def swapped(value, total, mask):
    return lax.ppermute(value, AXES, [(source, source ^ mask) for source in range(total)])


def split_pair(values):
    high = values.astype(BF16)
    return high, (values - high.astype(F32)).astype(BF16)


def loss_rows(loss):
    row = lax.broadcasted_iota(jnp.int32, (STAT_ROWS, loss.shape[1]), 0)
    high, low = split_pair(loss)
    rows = jnp.where(row == 0, high.astype(F32), jnp.where(row == 1, low.astype(F32), 0.0))
    return rows.astype(BF16)


def loss_of(rows):
    rows = rows.astype(F32)
    return rows[0:1, :] + rows[1:2, :]


def column_block(member, narrow):
    return (member % narrow) * 2 + member // narrow


def unit_text(text):
    values = text.astype(F32)
    inverse = lax.rsqrt(jnp.sum(values * values, axis=1, keepdims=True) + 1e-06)
    return (values * inverse).astype(BF16)


def own_kernel(log_scale_ref, bias_ref, text_ref, text_out, scalars_out):
    text_out[...] = unit_text(text_ref[...])
    row = lax.broadcasted_iota(jnp.int32, scalars_out.shape, 0)
    scale = jnp.exp(jnp.full(scalars_out.shape, log_scale_ref[0], F32))
    scalars_out[...] = jnp.where(row == 0, scale, bias_ref[0])


def stack_kernel(member_ref, *refs):
    blocks, half_out = refs[:-1], refs[-1]
    rows = blocks[0].shape[0]
    chip = member_ref[0] // 2
    for step, block in enumerate(blocks):
        place = pl.multiple_of((chip ^ step) * rows, rows)
        half_out[pl.ds(place, rows), :] = block[...]


def text_kernel(*refs):
    texts, out = refs[:-1], refs[-1]
    rows = texts[0].shape[0]
    out[:rows, :] = texts[0][...]
    for place, text in enumerate(texts[1:], 1):
        step = len(texts) - place
        out[step * rows : (step + 1) * rows, :] = unit_text(text[...])


def project_kernel(feats_ref, weight_ref, out):
    out[...] = jnp.dot(feats_ref[...], weight_ref[...], preferred_element_type=F32)


def first_image(member, rows, group):
    return (member % 2) * (group // 2 * rows) + (member // 2) * rows


def pair_kernel(
    narrow,
    group,
    member_ref,
    scalars_ref,
    weight,
    own_half,
    own_proj,
    got_half,
    text_all,
    feats_ref,
    inv_out,
    emb_out,
    grad_out,
    own_out,
    send_out,
    unit_all,
    d_all,
    proj_all,
):
    images, width = feats_ref.shape
    rows = images // group
    spread = text_all.shape[0] // rows
    half = images // 2
    share = width // group
    member = member_ref[0]

    place = pl.multiple_of((member % 2) * half, half)
    feats_ref[pl.ds(place, half), :] = own_half[...]
    proj_all[pl.ds(place, half), :] = own_proj[...]
    place = pl.multiple_of((1 - member % 2) * half, half)
    feats_ref[pl.ds(place, half), :] = got_half[...]
    proj_all[pl.ds(place, half), :] = jnp.dot(got_half[...], weight[...], preferred_element_type=F32)
    for start in range(0, images, LANES):
        cols = slice(start, start + LANES)
        turned = proj_all[cols, :].T
        inverse = lax.rsqrt(jnp.sum(turned * turned, axis=0, keepdims=True) + 1e-06)
        unit = turned * inverse
        inv_out[:, cols] = inverse
        unit_all[:, cols] = unit
        emb_out[:, cols] = unit.astype(BF16)

    scale = scalars_ref[0:1, 0:1]
    shift = scalars_ref[1:2, 0:1]
    count = 4 * rows if spread % 4 == 0 else rows
    chunks = spread * rows // count

    def one_chunk(chunk, loss_sum, dot_sum, first):
        here = pl.ds(pl.multiple_of(chunk * count, count), count)
        text = text_all[here, :]
        products = jnp.dot(text, emb_out[...], preferred_element_type=F32)
        logits = scale * products + shift
        caption = lax.broadcasted_iota(jnp.int32, (count, images), 0) + chunk * count
        image = lax.broadcasted_iota(jnp.int32, (count, images), 1)
        own = jnp.logical_and(caption < rows, image == first_image(member, rows, group) + caption)
        sign = jnp.where(own, 1.0, -1.0).astype(F32)
        away = -sign * logits
        small = jnp.exp(-jnp.abs(away))
        loss = jnp.maximum(away, 0.0) + jnp.log1p(small)
        chance = jnp.where(away >= 0.0, 1.0, small) / (1.0 + small)
        grad = (-scale * sign * chance).astype(BF16)
        grad_out[here, :] = grad
        loss_sum = loss_sum + jnp.sum(loss, axis=0, keepdims=True)
        dot_sum = dot_sum + jnp.sum(grad.astype(F32) * products, axis=0, keepdims=True)
        d_img = lax.dot_general(text, grad, TN, preferred_element_type=F32)
        if first:
            d_all[...] = d_img
        else:
            d_all[...] += d_img
        return loss_sum, dot_sum

    zero = jnp.zeros((1, images), F32)
    sums = one_chunk(0, zero, zero, True)
    if chunks > 1:
        sums = lax.fori_loop(1, chunks, lambda c, s: one_chunk(c, *s, False), sums)
    loss_sum, dot_sum = sums

    def projected(index):
        part = pl.ds(pl.multiple_of(column_block(member ^ index, narrow) * share, share), share)
        return d_all[part, :] - unit_all[part, :] * dot_sum

    losses = loss_rows(loss_sum)
    for index in range(group // 2):
        own_out[index, :share, :] = projected(2 * index)
        send_out[index, :share, :] = projected(2 * index + 1).astype(BF16)
        send_out[index, share:, :] = losses
    own_out[0, share : share + 1, :] = loss_sum


def chip_kernel(own_ref, got_ref, own_out, *send_out):
    share = own_out.shape[0] - 8
    loss = own_ref[0, share : share + 1, :] + loss_of(got_ref[0, share:, :])
    own_out[:share, :] = own_ref[0, :share, :] + got_ref[0, :share, :].astype(F32)
    own_out[share : share + 1, :] = loss
    losses = loss_rows(loss)
    for index, target in enumerate(send_out, 1):
        target[:share, :] = (own_ref[index, :share, :] + got_ref[index, :share, :].astype(F32)).astype(BF16)
        target[share:, :] = losses


def caption_kernel(rows, grad_ref, emb_ref, feats_ref, feats_t, *outs):
    product = lax.dot_general(grad_ref[...], emb_ref[...], NT, preferred_element_type=F32)
    for step, target in enumerate(outs):
        target[...] = product[step * rows : (step + 1) * rows, :].astype(target.dtype)
    for start in range(0, feats_ref.shape[0], LANES):
        cols = slice(start, start + LANES)
        feats_t[:, cols] = feats_ref[cols, :].astype(F32).T.astype(BF16)


def gathered_gradient(own_ref, got, inv_ref, loss_out):
    share = own_ref.shape[0] - 8
    total = own_ref[:share, :]
    loss = own_ref[share : share + 1, :]
    for block in got:
        total = total + block[:share, :].astype(F32)
        loss = loss + loss_of(block[share:, :])
    loss_out[...] = loss
    return inv_ref[...] * total


def weight_kernel(group, wide, *refs):
    own_ref, got = refs[0], refs[1 : group // 2]
    inv_ref, feats_ref, feats_t_ref, loss_out, send_out = refs[group // 2 :]
    rows = feats_t_ref.shape[0] // wide
    high, low = split_pair(gathered_gradient(own_ref, got, inv_ref, loss_out))
    rest = high.shape[0] - LANES
    both = jnp.concatenate([high[LANES:, :], low[LANES:, :]], axis=0)
    tail = jnp.dot(both, feats_ref[...], preferred_element_type=F32)
    tail = (tail[:rest, :] + tail[rest:, :]).astype(BF16)
    both = jnp.concatenate([high[:LANES, :], low[:LANES, :]], axis=0)
    main = lax.dot_general(feats_t_ref[...], both, NT, preferred_element_type=F32)
    main = (main[:, :LANES] + main[:, LANES:]).astype(BF16)
    for place in range(wide):
        begin = place * rows
        send_out[place, :rows, :] = main[begin : begin + rows, :]
        send_out[place, rows : rows + rest, :] = tail[:, begin : begin + LANES]
        send_out[place, rows + rest :, :] = jnp.zeros((rest, LANES), BF16)
        send_out[place, rows + rest :, : rows - LANES] = tail[:, begin + LANES : begin + rows]


def total_kernel(rest, got_ref, out):
    rows = out.shape[0]
    for side in range(2):
        half = got_ref[side].astype(F32)
        for place in range(side + 2, got_ref.shape[0], 2):
            half = half + got_ref[place].astype(F32)
        left = side * (LANES + rest)
        out[:, left : left + LANES] = half[:rows, :]
        out[:LANES, left + LANES : left + LANES + rest] = half[rows : rows + rest, :].T
        out[LANES:, left + LANES : left + LANES + rest] = half[rows + rest :, :].T[: rows - LANES, :]


def sum_kernel(*refs):
    total = refs[0][...]
    for block in refs[1:-1]:
        total = total + block[...].astype(F32)
    refs[-1][...] = total


def local(wide, narrow, image_feats, proj_weight, text_embed, log_scale, logit_bias):
    rows, width = image_feats.shape
    total = wide * narrow
    group = 2 * narrow
    spread = wide // 2
    share = width // group
    images = group * rows
    member = lax.axis_index(AXES[1:]).astype(jnp.int32).reshape(1)

    texts = [swapped(text_embed, total, step * group) for step in range(1, spread)]
    got_feats = [swapped(image_feats, total, 2 * step) for step in range(1, group // 2)]
    own_text, scalars = pl.pallas_call(
        own_kernel,
        in_specs=[SMEM] * 2 + [VMEM],
        out_specs=[VMEM] * 2,
        out_shape=[jax.ShapeDtypeStruct((rows, width), BF16), jax.ShapeDtypeStruct((8, LANES), F32)],
        compiler_params=limit(4),
        cost_estimate=hint(10**10),
        name="own_text",
    )(log_scale, logit_bias, text_embed)
    own_half = pl.pallas_call(
        stack_kernel,
        in_specs=[SMEM] + [VMEM] * (group // 2),
        out_specs=VMEM,
        out_shape=jax.ShapeDtypeStruct((images // 2, width), BF16),
        compiler_params=limit(4),
        name="stack",
    )(member, image_feats, *got_feats)
    got_half = swapped(own_half, total, 1)
    own_proj = pl.pallas_call(
        project_kernel,
        in_specs=[VMEM] * 2,
        out_specs=VMEM,
        out_shape=jax.ShapeDtypeStruct((images // 2, width), F32),
        compiler_params=limit(8),
        name="own_projection",
    )(own_half, proj_weight)
    own_proj, *texts = lax.optimization_barrier((own_proj, *texts[::-1]))
    text_emb = pl.pallas_call(
        text_kernel,
        in_specs=[VMEM] * spread,
        out_specs=VMEM,
        out_shape=jax.ShapeDtypeStruct((spread * rows, width), BF16),
        compiler_params=limit(4 if spread <= 4 else 16),
        cost_estimate=hint(10**10),
        name="text_unit",
    )(own_text, *texts)

    results = pl.pallas_call(
        functools.partial(pair_kernel, narrow, group),
        in_specs=[SMEM] + [VMEM] * 6,
        out_specs=[VMEM] * 6,
        out_shape=[
            jax.ShapeDtypeStruct((images, width), BF16),
            jax.ShapeDtypeStruct((1, images), F32),
            jax.ShapeDtypeStruct((width, images), BF16),
            jax.ShapeDtypeStruct((spread * rows, images), BF16),
            jax.ShapeDtypeStruct((group // 2, share + 8, images), F32),
            jax.ShapeDtypeStruct((group // 2, share + STAT_ROWS, images), BF16),
        ],
        scratch_shapes=[
            pltpu.VMEM((width, images), F32),
            pltpu.VMEM((width, images), F32),
            pltpu.VMEM((images, width), F32),
        ],
        compiler_params=limit(24 if spread <= 4 else 40),
        name="pairs",
    )(member, scalars, proj_weight, own_half, own_proj, got_half, text_emb)
    all_feats, inv_part, img_emb, grad_tile, own_part, sent_part = results
    got_part = swapped(sent_part, total, 1)
    feats_t, own_text, *sent_text = pl.pallas_call(
        functools.partial(caption_kernel, rows),
        in_specs=[VMEM] * 3,
        out_specs=[VMEM] * (1 + spread),
        out_shape=[jax.ShapeDtypeStruct((width, images), BF16), jax.ShapeDtypeStruct((rows, width), F32)]
        + [jax.ShapeDtypeStruct((rows, width), BF16)] * (spread - 1),
        compiler_params=limit(12 if spread <= 4 else 32),
        name="captions",
    )(grad_tile, img_emb, all_feats)
    own_part, got_part, sent_text = lax.optimization_barrier((own_part, got_part, sent_text))
    got_text = [swapped(value, total, step * group) for step, value in enumerate(sent_text, 1)]
    own_part, *chip_parts = pl.pallas_call(
        chip_kernel,
        in_specs=[VMEM] * 2,
        out_specs=[VMEM] * (group // 2),
        out_shape=[jax.ShapeDtypeStruct((share + 8, images), F32)]
        + [jax.ShapeDtypeStruct((share + STAT_ROWS, images), BF16)] * (group // 2 - 1),
        compiler_params=limit(12),
        name="chip_sum",
    )(own_part, got_part)
    got = [swapped(value, total, 2 * index) for index, value in enumerate(chip_parts, 1)]

    out_rows = width // wide
    rest = share - LANES
    packed = out_rows + 2 * rest
    direct = LANES < out_rows <= 2 * LANES and out_rows % 16 == 0 and rest % 16 == 0
    if direct:
        loss_line, sent_weight = pl.pallas_call(
            functools.partial(weight_kernel, group, wide),
            in_specs=[VMEM] * (3 + group // 2),
            out_specs=[VMEM] * 2,
            out_shape=[
                jax.ShapeDtypeStruct((1, images), F32),
                jax.ShapeDtypeStruct((wide, packed, LANES), BF16),
            ],
            compiler_params=limit(12),
            name="weights",
        )(own_part, *got, inv_part, all_feats, feats_t)
        got_weight = lax.all_to_all(sent_weight, AXES[:2], 0, 0)
        d_proj = pl.pallas_call(
            functools.partial(total_kernel, rest),
            in_specs=[VMEM],
            out_specs=VMEM,
            out_shape=jax.ShapeDtypeStruct((out_rows, 2 * share), F32),
            compiler_params=limit(4),
            name="weight_total",
        )(got_weight)
    else:

        def gradient_kernel(*refs):
            own_ref, blocks = refs[0], refs[1 : group // 2]
            inv_ref, loss_out, d_out = refs[group // 2 :]
            d_out[...] = gathered_gradient(own_ref, blocks, inv_ref, loss_out)

        loss_line, d_zproj = pl.pallas_call(
            gradient_kernel,
            in_specs=[VMEM] * (1 + group // 2),
            out_specs=[VMEM] * 2,
            out_shape=[jax.ShapeDtypeStruct((1, images), F32), jax.ShapeDtypeStruct((share, images), F32)],
            compiler_params=limit(12),
            name="gradient",
        )(own_part, *got, inv_part)
        partial = sum(
            lax.dot_general(feats_t, part, NT, preferred_element_type=F32) for part in split_pair(d_zproj)
        )
        left = lax.axis_index("inner") == 0
        both = jnp.concatenate([jnp.where(left, partial, 0.0), jnp.where(left, 0.0, partial)], axis=1)
        d_proj = lax.psum_scatter(both, AXES[:2], scatter_dimension=0, tiled=True)

    d_text_unit = pl.pallas_call(
        sum_kernel,
        in_specs=[VMEM] * spread,
        out_specs=VMEM,
        out_shape=jax.ShapeDtypeStruct((rows, width), F32),
        compiler_params=limit(12),
        cost_estimate=hint(5 * 10**9),
        name="caption_total",
    )(own_text, *got_text[::-1])
    image_loss = lax.dynamic_slice_in_dim(loss_line[0], first_image(member[0], rows, group), rows, 0)
    return (image_loss, d_text_unit, d_proj)


def solution(mesh):
    wide, narrow = mesh.shape["wide"], mesh.shape["narrow"]
    cut = jax.sharding.Mesh(mesh.devices.reshape(wide // 2, 2, narrow), AXES)
    placed = (P(AXES, None), P(), P(AXES, None), P(), P())
    return jax.shard_map(
        functools.partial(local, wide, narrow),
        mesh=cut,
        in_specs=placed,
        out_specs=(P(AXES), P(AXES, None), P(AXES[:2], "narrow")),
        check_vma=False,
    )
```

```python
import functools

import jax
import jax.numpy as jnp
from jax import lax
from jax.experimental import pallas as pl
from jax.experimental.pallas import tpu as pltpu
from jax.sharding import PartitionSpec as P

AXES = ("outer", "inner", "narrow")
F32 = jnp.float32
BF16 = jnp.bfloat16
LANES = 128
STAT_ROWS = 16
VMEM = pl.BlockSpec(memory_space=pltpu.VMEM)
SMEM = pl.BlockSpec(memory_space=pltpu.SMEM)
NT = (((1,), (1,)), ((), ()))
TN = (((0,), (0,)), ((), ()))
MIB = 1024 * 1024


def limit(mebibytes):
    return pltpu.CompilerParams(vmem_limit_bytes=mebibytes * MIB)


def hint(flops):
    return pl.CostEstimate(flops=flops, bytes_accessed=0, transcendentals=0)


def swapped(value, total, mask):
    return lax.ppermute(value, AXES, [(source, source ^ mask) for source in range(total)])


def split_pair(values):
    high = values.astype(BF16)
    return high, (values - high.astype(F32)).astype(BF16)


def loss_rows(loss):
    row = lax.broadcasted_iota(jnp.int32, (STAT_ROWS, loss.shape[1]), 0)
    high, low = split_pair(loss)
    rows = jnp.where(row == 0, high.astype(F32), jnp.where(row == 1, low.astype(F32), 0.0))
    return rows.astype(BF16)


def loss_of(rows):
    rows = rows.astype(F32)
    return rows[0:1, :] + rows[1:2, :]


def column_block(member, narrow):
    return (member % narrow) * 2 + member // narrow


def unit_text(text):
    values = text.astype(F32)
    inverse = lax.rsqrt(jnp.sum(values * values, axis=1, keepdims=True) + 1e-06)
    return (values * inverse).astype(BF16)


def own_kernel(log_scale_ref, bias_ref, text_ref, text_out, scalars_out):
    text_out[...] = unit_text(text_ref[...])
    row = lax.broadcasted_iota(jnp.int32, scalars_out.shape, 0)
    scale = jnp.exp(jnp.full(scalars_out.shape, log_scale_ref[0], F32))
    scalars_out[...] = jnp.where(row == 0, scale, bias_ref[0])


def stack_kernel(member_ref, *refs):
    blocks, half_out = refs[:-1], refs[-1]
    rows = blocks[0].shape[0]
    chip = member_ref[0] // 2
    for step, block in enumerate(blocks):
        place = pl.multiple_of((chip ^ step) * rows, rows)
        half_out[pl.ds(place, rows), :] = block[...]


def text_kernel(*refs):
    texts, out = refs[:-1], refs[-1]
    rows = texts[0].shape[0]
    out[:rows, :] = texts[0][...]
    for place, text in enumerate(texts[1:], 1):
        step = len(texts) - place
        out[step * rows : (step + 1) * rows, :] = unit_text(text[...])


def project_kernel(feats_ref, weight_ref, out):
    out[...] = jnp.dot(feats_ref[...], weight_ref[...], preferred_element_type=F32)


def first_image(member, rows, group):
    return (member % 2) * (group // 2 * rows) + (member // 2) * rows


def pair_kernel(
    narrow,
    group,
    member_ref,
    scalars_ref,
    weight,
    own_half,
    own_proj,
    got_half,
    text_all,
    feats_ref,
    inv_out,
    emb_out,
    grad_out,
    own_out,
    near_out,
    far_out,
    unit_all,
    d_all,
    proj_all,
):
    images, width = feats_ref.shape
    rows = images // group
    spread = text_all.shape[0] // rows
    half = images // 2
    share = width // group
    member = member_ref[0]

    place = pl.multiple_of((member % 2) * half, half)
    feats_ref[pl.ds(place, half), :] = own_half[...]
    proj_all[pl.ds(place, half), :] = own_proj[...]
    place = pl.multiple_of((1 - member % 2) * half, half)
    feats_ref[pl.ds(place, half), :] = got_half[...]
    proj_all[pl.ds(place, half), :] = jnp.dot(got_half[...], weight[...], preferred_element_type=F32)
    for start in range(0, images, LANES):
        cols = slice(start, start + LANES)
        turned = proj_all[cols, :].T
        inverse = lax.rsqrt(jnp.sum(turned * turned, axis=0, keepdims=True) + 1e-06)
        unit = turned * inverse
        inv_out[:, cols] = inverse
        unit_all[:, cols] = unit
        emb_out[:, cols] = unit.astype(BF16)

    scale = scalars_ref[0:1, 0:1]
    shift = scalars_ref[1:2, 0:1]
    count = 4 * rows if spread % 4 == 0 else rows
    chunks = spread * rows // count

    def one_chunk(chunk, loss_sum, dot_sum, first):
        here = pl.ds(pl.multiple_of(chunk * count, count), count)
        text = text_all[here, :]
        products = jnp.dot(text, emb_out[...], preferred_element_type=F32)
        logits = scale * products + shift
        caption = lax.broadcasted_iota(jnp.int32, (count, images), 0) + chunk * count
        image = lax.broadcasted_iota(jnp.int32, (count, images), 1)
        own = jnp.logical_and(caption < rows, image == first_image(member, rows, group) + caption)
        sign = jnp.where(own, 1.0, -1.0).astype(F32)
        away = -sign * logits
        small = jnp.exp(-jnp.abs(away))
        loss = jnp.maximum(away, 0.0) + jnp.log1p(small)
        chance = jnp.where(away >= 0.0, 1.0, small) / (1.0 + small)
        grad = (-scale * sign * chance).astype(BF16)
        grad_out[here, :] = grad
        loss_sum = loss_sum + jnp.sum(loss, axis=0, keepdims=True)
        dot_sum = dot_sum + jnp.sum(grad.astype(F32) * products, axis=0, keepdims=True)
        d_img = lax.dot_general(text, grad, TN, preferred_element_type=F32)
        if first:
            d_all[...] = d_img
        else:
            d_all[...] += d_img
        return loss_sum, dot_sum

    zero = jnp.zeros((1, images), F32)
    sums = one_chunk(0, zero, zero, True)
    if chunks > 1:
        sums = lax.fori_loop(1, chunks, lambda c, s: one_chunk(c, *s, False), sums)
    loss_sum, dot_sum = sums

    def projected(index):
        part = pl.ds(pl.multiple_of(column_block(member ^ index, narrow) * share, share), share)
        return d_all[part, :] - unit_all[part, :] * dot_sum

    losses = loss_rows(loss_sum)
    for index in range(group // 2):
        own_out[index, :share, :] = projected(2 * index)
        target = (near_out, far_out)[index * 4 // group].at[index % (group // 4)]
        target[:share, :] = projected(2 * index + 1).astype(BF16)
        target[share:, :] = losses
    own_out[0, share : share + 1, :] = loss_sum


def chip_kernel(first, own_ref, got_ref, *outs):
    share = own_ref.shape[1] - 8
    loss = own_ref[0, share : share + 1, :] + loss_of(got_ref[0, share:, :])
    for index, target in enumerate(outs):
        total = own_ref[first + index, :share, :] + got_ref[index, :share, :].astype(F32)
        target[:share, :] = total.astype(target.dtype)
        if target.dtype == BF16:
            target[share:, :] = loss_rows(loss)
        else:
            target[share : share + 1, :] = loss


def caption_kernel(rows, grad_ref, emb_ref, feats_ref, feats_t, *outs):
    product = lax.dot_general(grad_ref[...], emb_ref[...], NT, preferred_element_type=F32)
    for step, target in enumerate(outs):
        target[...] = product[step * rows : (step + 1) * rows, :].astype(target.dtype)
    for start in range(0, feats_ref.shape[0], LANES):
        cols = slice(start, start + LANES)
        feats_t[:, cols] = feats_ref[cols, :].astype(F32).T.astype(BF16)


def far_sum_kernel(*refs):
    own_ref, got, out = refs[0], refs[1:-1], refs[-1]
    share = own_ref.shape[0] - 8
    total, loss = own_ref[:share, :], own_ref[share : share + 1, :]
    for block in got:
        total = total + block[:share, :].astype(F32)
        loss = loss + loss_of(block[share:, :])
    out[:share, :] = total
    out[share : share + 1, :] = loss


def gathered_gradient(own_ref, got, inv_ref, loss_out):
    share = own_ref.shape[0] - 8
    total = own_ref[:share, :]
    loss = own_ref[share : share + 1, :]
    for block in got:
        total = total + block[:share, :].astype(F32)
        loss = loss + loss_of(block[share:, :])
    loss_out[...] = loss
    return inv_ref[...] * total


def weight_kernel(group, wide, *refs):
    own_ref, got = refs[0], refs[1 : group // 4]
    inv_ref, feats_ref, feats_t_ref, loss_out, send_out = refs[group // 4 :]
    rows = feats_t_ref.shape[0] // wide
    high, low = split_pair(gathered_gradient(own_ref, got, inv_ref, loss_out))
    rest = high.shape[0] - LANES
    both = jnp.concatenate([high[LANES:, :], low[LANES:, :]], axis=0)
    tail = jnp.dot(both, feats_ref[...], preferred_element_type=F32)
    tail = (tail[:rest, :] + tail[rest:, :]).astype(BF16)
    both = jnp.concatenate([high[:LANES, :], low[:LANES, :]], axis=0)
    main = lax.dot_general(feats_t_ref[...], both, NT, preferred_element_type=F32)
    main = (main[:, :LANES] + main[:, LANES:]).astype(BF16)
    for place in range(wide):
        begin = place * rows
        send_out[place, :rows, :] = main[begin : begin + rows, :]
        send_out[place, rows : rows + rest, :] = tail[:, begin : begin + LANES]
        send_out[place, rows + rest :, :] = jnp.zeros((rest, LANES), BF16)
        send_out[place, rows + rest :, : rows - LANES] = tail[:, begin + LANES : begin + rows]


def total_kernel(rest, got_ref, out):
    rows = out.shape[0]
    for side in range(2):
        half = got_ref[side].astype(F32)
        for place in range(side + 2, got_ref.shape[0], 2):
            half = half + got_ref[place].astype(F32)
        left = side * (LANES + rest)
        out[:, left : left + LANES] = half[:rows, :]
        out[:LANES, left + LANES : left + LANES + rest] = half[rows : rows + rest, :].T
        out[LANES:, left + LANES : left + LANES + rest] = half[rows + rest :, :].T[: rows - LANES, :]


def sum_kernel(*refs):
    total = refs[0][...]
    for block in refs[1:-1]:
        total = total + block[...].astype(F32)
    refs[-1][...] = total


def local(wide, narrow, image_feats, proj_weight, text_embed, log_scale, logit_bias):
    rows, width = image_feats.shape
    total = wide * narrow
    group = 2 * narrow
    spread = wide // 2
    share = width // group
    images = group * rows
    member = lax.axis_index(AXES[1:]).astype(jnp.int32).reshape(1)

    texts = [swapped(text_embed, total, step * group) for step in range(1, spread)]
    got_feats = [swapped(image_feats, total, 2 * step) for step in range(1, group // 2)]
    own_text, scalars = pl.pallas_call(
        own_kernel,
        in_specs=[SMEM] * 2 + [VMEM],
        out_specs=[VMEM] * 2,
        out_shape=[jax.ShapeDtypeStruct((rows, width), BF16), jax.ShapeDtypeStruct((8, LANES), F32)],
        compiler_params=limit(4),
        cost_estimate=hint(10**10),
        name="own_text",
    )(log_scale, logit_bias, text_embed)
    own_half = pl.pallas_call(
        stack_kernel,
        in_specs=[SMEM] + [VMEM] * (group // 2),
        out_specs=VMEM,
        out_shape=jax.ShapeDtypeStruct((images // 2, width), BF16),
        compiler_params=limit(4),
        name="stack",
    )(member, image_feats, *got_feats)
    got_half = swapped(own_half, total, 1)
    own_proj = pl.pallas_call(
        project_kernel,
        in_specs=[VMEM] * 2,
        out_specs=VMEM,
        out_shape=jax.ShapeDtypeStruct((images // 2, width), F32),
        compiler_params=limit(8),
        name="own_projection",
    )(own_half, proj_weight)
    own_proj, *texts = lax.optimization_barrier((own_proj, *texts[::-1]))
    text_emb = pl.pallas_call(
        text_kernel,
        in_specs=[VMEM] * spread,
        out_specs=VMEM,
        out_shape=jax.ShapeDtypeStruct((spread * rows, width), BF16),
        compiler_params=limit(4 if spread <= 4 else 16),
        cost_estimate=hint(10**10),
        name="text_unit",
    )(own_text, *texts)

    results = pl.pallas_call(
        functools.partial(pair_kernel, narrow, group),
        in_specs=[SMEM] + [VMEM] * 6,
        out_specs=[VMEM] * 7,
        out_shape=[
            jax.ShapeDtypeStruct((images, width), BF16),
            jax.ShapeDtypeStruct((1, images), F32),
            jax.ShapeDtypeStruct((width, images), BF16),
            jax.ShapeDtypeStruct((spread * rows, images), BF16),
            jax.ShapeDtypeStruct((group // 2, share + 8, images), F32),
        ]
        + [jax.ShapeDtypeStruct((group // 4, share + STAT_ROWS, images), BF16)] * 2,
        scratch_shapes=[
            pltpu.VMEM((width, images), F32),
            pltpu.VMEM((width, images), F32),
            pltpu.VMEM((images, width), F32),
        ],
        compiler_params=limit(24 if spread <= 4 else 40),
        name="pairs",
    )(member, scalars, proj_weight, own_half, own_proj, got_half, text_emb)
    all_feats, inv_part, img_emb, grad_tile, own_part, near_part, far_part = results
    got_far = swapped(far_part, total, 1)
    got_near = swapped(near_part, total, 1)
    sent_block = jax.ShapeDtypeStruct((share + STAT_ROWS, images), BF16)
    kept_block = jax.ShapeDtypeStruct((share + 8, images), F32)
    half = group // 4
    far = pl.pallas_call(
        functools.partial(chip_kernel, half),
        in_specs=[VMEM] * 2,
        out_specs=[VMEM] * half,
        out_shape=[sent_block] * half,
        compiler_params=limit(8),
        name="chip_far",
    )(own_part, got_far)
    far = [swapped(value, total, 2 * (half + index)) for index, value in enumerate(far)]
    feats_t, own_text, *sent_text = pl.pallas_call(
        functools.partial(caption_kernel, rows),
        in_specs=[VMEM] * 3,
        out_specs=[VMEM] * (1 + spread),
        out_shape=[jax.ShapeDtypeStruct((width, images), BF16), jax.ShapeDtypeStruct((rows, width), F32)]
        + [jax.ShapeDtypeStruct((rows, width), BF16)] * (spread - 1),
        compiler_params=limit(12 if spread <= 4 else 32),
        name="captions",
    )(grad_tile, img_emb, all_feats)
    own_part, got_near, sent_text = lax.optimization_barrier((own_part, got_near, sent_text))
    got_text = [swapped(value, total, step * group) for step, value in enumerate(sent_text, 1)]
    own_part, *near = pl.pallas_call(
        functools.partial(chip_kernel, 0),
        in_specs=[VMEM] * 2,
        out_specs=[VMEM] * half,
        out_shape=[kept_block] + [sent_block] * (half - 1),
        compiler_params=limit(8),
        name="chip_near",
    )(own_part, got_near)
    near = [swapped(value, total, 2 * index) for index, value in enumerate(near, 1)]
    own_part = pl.pallas_call(
        far_sum_kernel,
        in_specs=[VMEM] * (1 + half),
        out_specs=VMEM,
        out_shape=kept_block,
        compiler_params=limit(8),
        cost_estimate=hint(5 * 10**8),
        name="far_sum",
    )(own_part, *far)

    out_rows = width // wide
    rest = share - LANES
    packed = out_rows + 2 * rest
    direct = LANES < out_rows <= 2 * LANES and out_rows % 16 == 0 and rest % 16 == 0
    if direct:
        loss_line, sent_weight = pl.pallas_call(
            functools.partial(weight_kernel, group, wide),
            in_specs=[VMEM] * (3 + group // 4),
            out_specs=[VMEM] * 2,
            out_shape=[
                jax.ShapeDtypeStruct((1, images), F32),
                jax.ShapeDtypeStruct((wide, packed, LANES), BF16),
            ],
            compiler_params=limit(12),
            name="weights",
        )(own_part, *near, inv_part, all_feats, feats_t)
        got_weight = lax.all_to_all(sent_weight, AXES[:2], 0, 0)
        d_proj = pl.pallas_call(
            functools.partial(total_kernel, rest),
            in_specs=[VMEM],
            out_specs=VMEM,
            out_shape=jax.ShapeDtypeStruct((out_rows, 2 * share), F32),
            compiler_params=limit(4),
            name="weight_total",
        )(got_weight)
    else:

        def gradient_kernel(*refs):
            own_ref, blocks = refs[0], refs[1 : group // 4]
            inv_ref, loss_out, d_out = refs[group // 4 :]
            d_out[...] = gathered_gradient(own_ref, blocks, inv_ref, loss_out)

        loss_line, d_zproj = pl.pallas_call(
            gradient_kernel,
            in_specs=[VMEM] * (1 + group // 4),
            out_specs=[VMEM] * 2,
            out_shape=[jax.ShapeDtypeStruct((1, images), F32), jax.ShapeDtypeStruct((share, images), F32)],
            compiler_params=limit(12),
            name="gradient",
        )(own_part, *near, inv_part)
        partial = sum(
            lax.dot_general(feats_t, part, NT, preferred_element_type=F32) for part in split_pair(d_zproj)
        )
        left = lax.axis_index("inner") == 0
        both = jnp.concatenate([jnp.where(left, partial, 0.0), jnp.where(left, 0.0, partial)], axis=1)
        d_proj = lax.psum_scatter(both, AXES[:2], scatter_dimension=0, tiled=True)

    d_text_unit = pl.pallas_call(
        sum_kernel,
        in_specs=[VMEM] * spread,
        out_specs=VMEM,
        out_shape=jax.ShapeDtypeStruct((rows, width), F32),
        compiler_params=limit(12),
        cost_estimate=hint(5 * 10**9),
        name="caption_total",
    )(own_text, *got_text[::-1])
    image_loss = lax.dynamic_slice_in_dim(loss_line[0], first_image(member[0], rows, group), rows, 0)
    return (image_loss, d_text_unit, d_proj)


def solution(mesh):
    wide, narrow = mesh.shape["wide"], mesh.shape["narrow"]
    cut = jax.sharding.Mesh(mesh.devices.reshape(wide // 2, 2, narrow), AXES)
    placed = (P(AXES, None), P(), P(AXES, None), P(), P())
    return jax.shard_map(
        functools.partial(local, wide, narrow),
        mesh=cut,
        in_specs=placed,
        out_specs=(P(AXES), P(AXES, None), P(AXES[:2], "narrow")),
        check_vma=False,
    )
```

```python
import functools

import jax
import jax.numpy as jnp
from jax import lax
from jax.experimental import pallas as pl
from jax.experimental.pallas import tpu as pltpu
from jax.sharding import PartitionSpec as P

AXES = ("outer", "inner", "narrow")
F32 = jnp.float32
BF16 = jnp.bfloat16
LANES = 128
STAT_ROWS = 16
VMEM = pl.BlockSpec(memory_space=pltpu.VMEM)
SMEM = pl.BlockSpec(memory_space=pltpu.SMEM)
NT = (((1,), (1,)), ((), ()))
TN = (((0,), (0,)), ((), ()))
MIB = 1024 * 1024


def limit(mebibytes):
    return pltpu.CompilerParams(vmem_limit_bytes=mebibytes * MIB)


def hint(flops):
    return pl.CostEstimate(flops=flops, bytes_accessed=0, transcendentals=0)


def swapped(value, total, mask):
    return lax.ppermute(value, AXES, [(source, source ^ mask) for source in range(total)])


def split_pair(values):
    high = values.astype(BF16)
    return high, (values - high.astype(F32)).astype(BF16)


def loss_rows(loss):
    row = lax.broadcasted_iota(jnp.int32, (STAT_ROWS, loss.shape[1]), 0)
    high, low = split_pair(loss)
    rows = jnp.where(row == 0, high.astype(F32), jnp.where(row == 1, low.astype(F32), 0.0))
    return rows.astype(BF16)


def loss_of(rows):
    rows = rows.astype(F32)
    return rows[0:1, :] + rows[1:2, :]


def column_block(member, narrow):
    return (member % narrow) * 2 + member // narrow


def unit_text(text):
    values = text.astype(F32)
    inverse = lax.rsqrt(jnp.sum(values * values, axis=1, keepdims=True) + 1e-06)
    return (values * inverse).astype(BF16)


def own_kernel(log_scale_ref, bias_ref, text_ref, text_out, scalars_out):
    text_out[...] = unit_text(text_ref[...])
    row = lax.broadcasted_iota(jnp.int32, scalars_out.shape, 0)
    scale = jnp.exp(jnp.full(scalars_out.shape, log_scale_ref[0], F32))
    scalars_out[...] = jnp.where(row == 0, scale, bias_ref[0])


def stack_kernel(member_ref, *refs):
    blocks, half_out = refs[:-1], refs[-1]
    rows = blocks[0].shape[0]
    chip = member_ref[0] // 2
    for step, block in enumerate(blocks):
        place = pl.multiple_of((chip ^ step) * rows, rows)
        half_out[pl.ds(place, rows), :] = block[...]


def text_kernel(*refs):
    texts, out = refs[:-1], refs[-1]
    rows = texts[0].shape[0]
    out[:rows, :] = texts[0][...]
    for place, text in enumerate(texts[1:], 1):
        step = len(texts) - place
        out[step * rows : (step + 1) * rows, :] = unit_text(text[...])


def project_kernel(feats_ref, weight_ref, out):
    out[...] = jnp.dot(feats_ref[...], weight_ref[...], preferred_element_type=F32)


def first_image(member, rows, group):
    return (member % 2) * (group // 2 * rows) + (member // 2) * rows


def pair_kernel(
    narrow,
    group,
    member_ref,
    scalars_ref,
    weight,
    own_half,
    own_proj,
    got_half,
    text_all,
    feats_ref,
    inv_out,
    emb_out,
    grad_out,
    own_out,
    near_out,
    far_out,
    unit_all,
    d_all,
    proj_all,
):
    images, width = feats_ref.shape
    rows = images // group
    spread = text_all.shape[0] // rows
    half = images // 2
    share = width // group
    member = member_ref[0]

    place = pl.multiple_of((member % 2) * half, half)
    feats_ref[pl.ds(place, half), :] = own_half[...]
    proj_all[pl.ds(place, half), :] = own_proj[...]
    place = pl.multiple_of((1 - member % 2) * half, half)
    feats_ref[pl.ds(place, half), :] = got_half[...]
    proj_all[pl.ds(place, half), :] = jnp.dot(got_half[...], weight[...], preferred_element_type=F32)
    for start in range(0, images, LANES):
        cols = slice(start, start + LANES)
        turned = proj_all[cols, :].T
        inverse = lax.rsqrt(jnp.sum(turned * turned, axis=0, keepdims=True) + 1e-06)
        unit = turned * inverse
        inv_out[:, cols] = inverse
        unit_all[:, cols] = unit
        emb_out[:, cols] = unit.astype(BF16)

    scale = scalars_ref[0:1, 0:1]
    shift = scalars_ref[1:2, 0:1]
    count = 4 * rows if spread % 4 == 0 else rows
    chunks = spread * rows // count

    def one_chunk(chunk, loss_sum, dot_sum, first):
        here = pl.ds(pl.multiple_of(chunk * count, count), count)
        text = text_all[here, :]
        products = jnp.dot(text, emb_out[...], preferred_element_type=F32)
        logits = scale * products + shift
        caption = lax.broadcasted_iota(jnp.int32, (count, images), 0) + chunk * count
        image = lax.broadcasted_iota(jnp.int32, (count, images), 1)
        own = jnp.logical_and(caption < rows, image == first_image(member, rows, group) + caption)
        sign = jnp.where(own, 1.0, -1.0).astype(F32)
        away = -sign * logits
        small = jnp.exp(-jnp.abs(away))
        loss = jnp.maximum(away, 0.0) + jnp.log1p(small)
        chance = jnp.where(away >= 0.0, 1.0, small) / (1.0 + small)
        grad = (-scale * sign * chance).astype(BF16)
        grad_out[here, :] = grad
        loss_sum = loss_sum + jnp.sum(loss, axis=0, keepdims=True)
        dot_sum = dot_sum + jnp.sum(grad.astype(F32) * products, axis=0, keepdims=True)
        d_img = lax.dot_general(text, grad, TN, preferred_element_type=F32)
        if first:
            d_all[...] = d_img
        else:
            d_all[...] += d_img
        return loss_sum, dot_sum

    zero = jnp.zeros((1, images), F32)
    sums = one_chunk(0, zero, zero, True)
    if chunks > 1:
        sums = lax.fori_loop(1, chunks, lambda c, s: one_chunk(c, *s, False), sums)
    loss_sum, dot_sum = sums

    def projected(index):
        part = pl.ds(pl.multiple_of(column_block(member ^ index, narrow) * share, share), share)
        return d_all[part, :] - unit_all[part, :] * dot_sum

    losses = loss_rows(loss_sum)
    for index in range(group // 2):
        own_out[index, :share, :] = projected(2 * index)
        target = (near_out, far_out)[index * 4 // group].at[index % (group // 4)]
        target[:share, :] = projected(2 * index + 1).astype(BF16)
        target[share:, :] = losses
    own_out[0, share : share + 1, :] = loss_sum


def chip_kernel(first, own_ref, got_ref, *outs):
    share = own_ref.shape[1] - 8
    loss = own_ref[0, share : share + 1, :] + loss_of(got_ref[0, share:, :])
    for index, target in enumerate(outs):
        total = own_ref[first + index, :share, :] + got_ref[index, :share, :].astype(F32)
        target[:share, :] = total.astype(target.dtype)
        if target.dtype == BF16:
            target[share:, :] = loss_rows(loss)
        else:
            target[share : share + 1, :] = loss


def caption_kernel(rows, grad_ref, emb_ref, feats_ref, feats_t, *outs):
    product = lax.dot_general(grad_ref[...], emb_ref[...], NT, preferred_element_type=F32)
    for step, target in enumerate(outs):
        target[...] = product[step * rows : (step + 1) * rows, :].astype(target.dtype)
    for start in range(0, feats_ref.shape[0], LANES):
        cols = slice(start, start + LANES)
        feats_t[:, cols] = feats_ref[cols, :].astype(F32).T.astype(BF16)


def far_sum_kernel(*refs):
    own_ref, got, out = refs[0], refs[1:-1], refs[-1]
    share = own_ref.shape[0] - 8
    total, loss = own_ref[:share, :], own_ref[share : share + 1, :]
    for block in got:
        total = total + block[:share, :].astype(F32)
        loss = loss + loss_of(block[share:, :])
    out[:share, :] = total
    out[share : share + 1, :] = loss


def gathered_gradient(own_ref, got, inv_ref, loss_out):
    share = own_ref.shape[0] - 8
    total = own_ref[:share, :]
    loss = own_ref[share : share + 1, :]
    for block in got:
        total = total + block[:share, :].astype(F32)
        loss = loss + loss_of(block[share:, :])
    loss_out[...] = loss
    return inv_ref[...] * total


def weight_kernel(group, wide, *refs):
    own_ref, got = refs[0], refs[1 : group // 4]
    inv_ref, feats_ref, feats_t_ref, loss_out, send_out = refs[group // 4 :]
    rows = feats_t_ref.shape[0] // wide
    high, low = split_pair(gathered_gradient(own_ref, got, inv_ref, loss_out))
    rest = high.shape[0] - LANES
    both = jnp.concatenate([high[LANES:, :], low[LANES:, :]], axis=0)
    tail = jnp.dot(both, feats_ref[...], preferred_element_type=F32)
    tail = (tail[:rest, :] + tail[rest:, :]).astype(BF16)
    both = jnp.concatenate([high[:LANES, :], low[:LANES, :]], axis=0)
    main = lax.dot_general(feats_t_ref[...], both, NT, preferred_element_type=F32)
    main = (main[:, :LANES] + main[:, LANES:]).astype(BF16)
    for place in range(wide):
        begin = place * rows
        send_out[place, :rows, :] = main[begin : begin + rows, :]
        send_out[place, rows : rows + rest, :] = tail[:, begin : begin + LANES]
        send_out[place, rows + rest :, :] = jnp.zeros((rest, LANES), BF16)
        send_out[place, rows + rest :, : rows - LANES] = tail[:, begin + LANES : begin + rows]


def total_kernel(rest, got_ref, out):
    rows = out.shape[0]
    for side in range(2):
        half = got_ref[side].astype(F32)
        for place in range(side + 2, got_ref.shape[0], 2):
            half = half + got_ref[place].astype(F32)
        left = side * (LANES + rest)
        out[:, left : left + LANES] = half[:rows, :]
        out[:LANES, left + LANES : left + LANES + rest] = half[rows : rows + rest, :].T
        out[LANES:, left + LANES : left + LANES + rest] = half[rows + rest :, :].T[: rows - LANES, :]


def sum_kernel(*refs):
    total = refs[0][...]
    for block in refs[1:-1]:
        total = total + block[...].astype(F32)
    refs[-1][...] = total


def local(wide, narrow, image_feats, proj_weight, text_embed, log_scale, logit_bias):
    rows, width = image_feats.shape
    total = wide * narrow
    group = 2 * narrow
    spread = wide // 2
    share = width // group
    images = group * rows
    member = lax.axis_index(AXES[1:]).astype(jnp.int32).reshape(1)

    texts = [swapped(text_embed, total, step * group) for step in range(1, spread)]
    got_feats = [swapped(image_feats, total, 2 * step) for step in range(1, group // 2)]
    own_text, scalars = pl.pallas_call(
        own_kernel,
        in_specs=[SMEM] * 2 + [VMEM],
        out_specs=[VMEM] * 2,
        out_shape=[jax.ShapeDtypeStruct((rows, width), BF16), jax.ShapeDtypeStruct((8, LANES), F32)],
        compiler_params=limit(4),
        cost_estimate=hint(10**10),
        name="own_text",
    )(log_scale, logit_bias, text_embed)
    own_half = pl.pallas_call(
        stack_kernel,
        in_specs=[SMEM] + [VMEM] * (group // 2),
        out_specs=VMEM,
        out_shape=jax.ShapeDtypeStruct((images // 2, width), BF16),
        compiler_params=limit(4),
        name="stack",
    )(member, image_feats, *got_feats)
    got_half = swapped(own_half, total, 1)
    own_proj = pl.pallas_call(
        project_kernel,
        in_specs=[VMEM] * 2,
        out_specs=VMEM,
        out_shape=jax.ShapeDtypeStruct((images // 2, width), F32),
        compiler_params=limit(8),
        name="own_projection",
    )(own_half, proj_weight)
    own_proj, *texts = lax.optimization_barrier((own_proj, *texts[::-1]))
    text_emb = pl.pallas_call(
        text_kernel,
        in_specs=[VMEM] * spread,
        out_specs=VMEM,
        out_shape=jax.ShapeDtypeStruct((spread * rows, width), BF16),
        compiler_params=limit(4 if spread <= 4 else 16),
        cost_estimate=hint(10**10),
        name="text_unit",
    )(own_text, *texts)

    results = pl.pallas_call(
        functools.partial(pair_kernel, narrow, group),
        in_specs=[SMEM] + [VMEM] * 6,
        out_specs=[VMEM] * 7,
        out_shape=[
            jax.ShapeDtypeStruct((images, width), BF16),
            jax.ShapeDtypeStruct((1, images), F32),
            jax.ShapeDtypeStruct((width, images), BF16),
            jax.ShapeDtypeStruct((spread * rows, images), BF16),
            jax.ShapeDtypeStruct((group // 2, share + 8, images), F32),
        ]
        + [jax.ShapeDtypeStruct((group // 4, share + STAT_ROWS, images), BF16)] * 2,
        scratch_shapes=[
            pltpu.VMEM((width, images), F32),
            pltpu.VMEM((width, images), F32),
            pltpu.VMEM((images, width), F32),
        ],
        compiler_params=limit(24 if spread <= 4 else 40),
        name="pairs",
    )(member, scalars, proj_weight, own_half, own_proj, got_half, text_emb)
    all_feats, inv_part, img_emb, grad_tile, own_part, near_part, far_part = results
    got_far = swapped(far_part, total, 1)
    got_near = swapped(near_part, total, 1)
    sent_block = jax.ShapeDtypeStruct((share + STAT_ROWS, images), BF16)
    kept_block = jax.ShapeDtypeStruct((share + 8, images), F32)
    half = group // 4
    far = pl.pallas_call(
        functools.partial(chip_kernel, half),
        in_specs=[VMEM] * 2,
        out_specs=[VMEM] * half,
        out_shape=[sent_block] * half,
        compiler_params=limit(8),
        name="chip_far",
    )(own_part, got_far)
    far = [swapped(value, total, 2 * (half + index)) for index, value in enumerate(far)]
    feats_t, own_text, *sent_text = pl.pallas_call(
        functools.partial(caption_kernel, rows),
        in_specs=[VMEM] * 3,
        out_specs=[VMEM] * (1 + spread),
        out_shape=[jax.ShapeDtypeStruct((width, images), BF16), jax.ShapeDtypeStruct((rows, width), F32)]
        + [jax.ShapeDtypeStruct((rows, width), BF16)] * (spread - 1),
        compiler_params=limit(12 if spread <= 4 else 32),
        name="captions",
    )(grad_tile, img_emb, all_feats)
    got_text = [swapped(value, total, step * group) for step, value in enumerate(sent_text, 1)]
    own_part, *near = pl.pallas_call(
        functools.partial(chip_kernel, 0),
        in_specs=[VMEM] * 2,
        out_specs=[VMEM] * half,
        out_shape=[kept_block] + [sent_block] * (half - 1),
        compiler_params=limit(8),
        name="chip_near",
    )(own_part, got_near)
    near = [swapped(value, total, 2 * index) for index, value in enumerate(near, 1)]
    own_part = pl.pallas_call(
        far_sum_kernel,
        in_specs=[VMEM] * (1 + half),
        out_specs=VMEM,
        out_shape=kept_block,
        compiler_params=limit(8),
        cost_estimate=hint(5 * 10**8),
        name="far_sum",
    )(own_part, *far)

    out_rows = width // wide
    rest = share - LANES
    packed = out_rows + 2 * rest
    direct = LANES < out_rows <= 2 * LANES and out_rows % 16 == 0 and rest % 16 == 0
    if direct:
        loss_line, sent_weight = pl.pallas_call(
            functools.partial(weight_kernel, group, wide),
            in_specs=[VMEM] * (3 + group // 4),
            out_specs=[VMEM] * 2,
            out_shape=[
                jax.ShapeDtypeStruct((1, images), F32),
                jax.ShapeDtypeStruct((wide, packed, LANES), BF16),
            ],
            compiler_params=limit(12),
            name="weights",
        )(own_part, *near, inv_part, all_feats, feats_t)
        got_weight = lax.all_to_all(sent_weight, AXES[:2], 0, 0)
        d_proj = pl.pallas_call(
            functools.partial(total_kernel, rest),
            in_specs=[VMEM],
            out_specs=VMEM,
            out_shape=jax.ShapeDtypeStruct((out_rows, 2 * share), F32),
            compiler_params=limit(4),
            name="weight_total",
        )(got_weight)
    else:

        def gradient_kernel(*refs):
            own_ref, blocks = refs[0], refs[1 : group // 4]
            inv_ref, loss_out, d_out = refs[group // 4 :]
            d_out[...] = gathered_gradient(own_ref, blocks, inv_ref, loss_out)

        loss_line, d_zproj = pl.pallas_call(
            gradient_kernel,
            in_specs=[VMEM] * (1 + group // 4),
            out_specs=[VMEM] * 2,
            out_shape=[jax.ShapeDtypeStruct((1, images), F32), jax.ShapeDtypeStruct((share, images), F32)],
            compiler_params=limit(12),
            name="gradient",
        )(own_part, *near, inv_part)
        partial = sum(
            lax.dot_general(feats_t, part, NT, preferred_element_type=F32) for part in split_pair(d_zproj)
        )
        left = lax.axis_index("inner") == 0
        both = jnp.concatenate([jnp.where(left, partial, 0.0), jnp.where(left, 0.0, partial)], axis=1)
        d_proj = lax.psum_scatter(both, AXES[:2], scatter_dimension=0, tiled=True)

    d_text_unit = pl.pallas_call(
        sum_kernel,
        in_specs=[VMEM] * spread,
        out_specs=VMEM,
        out_shape=jax.ShapeDtypeStruct((rows, width), F32),
        compiler_params=limit(12),
        cost_estimate=hint(5 * 10**9),
        name="caption_total",
    )(own_text, *got_text[::-1])
    image_loss = lax.dynamic_slice_in_dim(loss_line[0], first_image(member[0], rows, group), rows, 0)
    return (image_loss, d_text_unit, d_proj)


def solution(mesh):
    wide, narrow = mesh.shape["wide"], mesh.shape["narrow"]
    cut = jax.sharding.Mesh(mesh.devices.reshape(wide // 2, 2, narrow), AXES)
    placed = (P(AXES, None), P(), P(AXES, None), P(), P())
    return jax.shard_map(
        functools.partial(local, wide, narrow),
        mesh=cut,
        in_specs=placed,
        out_specs=(P(AXES), P(AXES, None), P(AXES[:2], "narrow")),
        check_vma=False,
    )
```

```python
import functools

import jax
import jax.numpy as jnp
from jax import lax
from jax.experimental import pallas as pl
from jax.experimental.pallas import tpu as pltpu
from jax.sharding import PartitionSpec as P

AXES = ("outer", "inner", "narrow")
F32 = jnp.float32
BF16 = jnp.bfloat16
LANES = 128
STAT_ROWS = 16
VMEM = pl.BlockSpec(memory_space=pltpu.VMEM)
SMEM = pl.BlockSpec(memory_space=pltpu.SMEM)
NT = (((1,), (1,)), ((), ()))
TN = (((0,), (0,)), ((), ()))
MIB = 1024 * 1024


def limit(mebibytes):
    return pltpu.CompilerParams(vmem_limit_bytes=mebibytes * MIB)


def hint(flops):
    return pl.CostEstimate(flops=flops, bytes_accessed=0, transcendentals=0)


def swapped(value, total, mask):
    return lax.ppermute(value, AXES, [(source, source ^ mask) for source in range(total)])


def split_pair(values):
    high = values.astype(BF16)
    return high, (values - high.astype(F32)).astype(BF16)


def loss_rows(loss):
    row = lax.broadcasted_iota(jnp.int32, (STAT_ROWS, loss.shape[1]), 0)
    high, low = split_pair(loss)
    rows = jnp.where(row == 0, high.astype(F32), jnp.where(row == 1, low.astype(F32), 0.0))
    return rows.astype(BF16)


def loss_of(rows):
    rows = rows.astype(F32)
    return rows[0:1, :] + rows[1:2, :]


def column_block(member, narrow):
    return (member % narrow) * 2 + member // narrow


def unit_text(text):
    values = text.astype(F32)
    inverse = lax.rsqrt(jnp.sum(values * values, axis=1, keepdims=True) + 1e-06)
    return (values * inverse).astype(BF16)


def own_kernel(log_scale_ref, bias_ref, text_ref, text_out, scalars_out):
    text_out[...] = unit_text(text_ref[...])
    row = lax.broadcasted_iota(jnp.int32, scalars_out.shape, 0)
    scale = jnp.exp(jnp.full(scalars_out.shape, log_scale_ref[0], F32))
    scalars_out[...] = jnp.where(row == 0, scale, bias_ref[0])


def stack_kernel(member_ref, *refs):
    blocks, half_out = refs[:-1], refs[-1]
    rows = blocks[0].shape[0]
    chip = member_ref[0] // 2
    for step, block in enumerate(blocks):
        place = pl.multiple_of((chip ^ step) * rows, rows)
        half_out[pl.ds(place, rows), :] = block[...]


def text_kernel(*refs):
    texts, out = refs[:-1], refs[-1]
    rows = texts[0].shape[0]
    out[:rows, :] = texts[0][...]
    for place, text in enumerate(texts[1:], 1):
        step = len(texts) - place
        out[step * rows : (step + 1) * rows, :] = unit_text(text[...])


def project_kernel(feats_ref, weight_ref, out):
    out[...] = jnp.dot(feats_ref[...], weight_ref[...], preferred_element_type=F32)


def first_image(member, rows, group):
    return (member % 2) * (group // 2 * rows) + (member // 2) * rows


def pair_kernel(
    narrow,
    group,
    member_ref,
    scalars_ref,
    weight,
    own_half,
    own_proj,
    got_half,
    text_all,
    feats_ref,
    inv_out,
    emb_out,
    grad_out,
    own_out,
    near_out,
    far_out,
    unit_all,
    d_all,
    proj_all,
):
    images, width = feats_ref.shape
    rows = images // group
    spread = text_all.shape[0] // rows
    half = images // 2
    share = width // group
    member = member_ref[0]

    place = pl.multiple_of((member % 2) * half, half)
    feats_ref[pl.ds(place, half), :] = own_half[...]
    proj_all[pl.ds(place, half), :] = own_proj[...]
    place = pl.multiple_of((1 - member % 2) * half, half)
    feats_ref[pl.ds(place, half), :] = got_half[...]
    proj_all[pl.ds(place, half), :] = jnp.dot(got_half[...], weight[...], preferred_element_type=F32)
    for start in range(0, images, LANES):
        cols = slice(start, start + LANES)
        turned = proj_all[cols, :].T
        inverse = lax.rsqrt(jnp.sum(turned * turned, axis=0, keepdims=True) + 1e-06)
        unit = turned * inverse
        inv_out[:, cols] = inverse
        unit_all[:, cols] = unit
        emb_out[:, cols] = unit.astype(BF16)

    scale = scalars_ref[0:1, 0:1]
    shift = scalars_ref[1:2, 0:1]
    count = 4 * rows if spread % 4 == 0 else rows
    chunks = spread * rows // count

    def one_chunk(chunk, loss_sum, dot_sum, first):
        here = pl.ds(pl.multiple_of(chunk * count, count), count)
        text = text_all[here, :]
        products = jnp.dot(text, emb_out[...], preferred_element_type=F32)
        logits = scale * products + shift
        caption = lax.broadcasted_iota(jnp.int32, (count, images), 0) + chunk * count
        image = lax.broadcasted_iota(jnp.int32, (count, images), 1)
        own = jnp.logical_and(caption < rows, image == first_image(member, rows, group) + caption)
        sign = jnp.where(own, 1.0, -1.0).astype(F32)
        away = -sign * logits
        small = jnp.exp(-jnp.abs(away))
        loss = jnp.maximum(away, 0.0) + jnp.log1p(small)
        chance = jnp.where(away >= 0.0, 1.0, small) / (1.0 + small)
        grad = (-scale * sign * chance).astype(BF16)
        grad_out[here, :] = grad
        loss_sum = loss_sum + jnp.sum(loss, axis=0, keepdims=True)
        dot_sum = dot_sum + jnp.sum(grad.astype(F32) * products, axis=0, keepdims=True)
        d_img = lax.dot_general(text, grad, TN, preferred_element_type=F32)
        if first:
            d_all[...] = d_img
        else:
            d_all[...] += d_img
        return loss_sum, dot_sum

    zero = jnp.zeros((1, images), F32)
    sums = one_chunk(0, zero, zero, True)
    if chunks > 1:
        sums = lax.fori_loop(1, chunks, lambda c, s: one_chunk(c, *s, False), sums)
    loss_sum, dot_sum = sums

    def projected(index):
        part = pl.ds(pl.multiple_of(column_block(member ^ index, narrow) * share, share), share)
        return d_all[part, :] - unit_all[part, :] * dot_sum

    losses = loss_rows(loss_sum)
    for index in range(group // 2):
        own_out[index, :share, :] = projected(2 * index)
        target = (near_out, far_out)[index * 4 // group].at[index % (group // 4)]
        target[:share, :] = projected(2 * index + 1).astype(BF16)
        target[share:, :] = losses
    own_out[0, share : share + 1, :] = loss_sum


def chip_kernel(first, own_ref, got_ref, *outs):
    share = own_ref.shape[1] - 8
    loss = own_ref[0, share : share + 1, :] + loss_of(got_ref[0, share:, :])
    for index, target in enumerate(outs):
        total = own_ref[first + index, :share, :] + got_ref[index, :share, :].astype(F32)
        target[:share, :] = total.astype(target.dtype)
        if target.dtype == BF16:
            target[share:, :] = loss_rows(loss)
        else:
            target[share : share + 1, :] = loss


def caption_kernel(rows, grad_ref, emb_ref, feats_ref, feats_t, *outs):
    product = lax.dot_general(grad_ref[...], emb_ref[...], NT, preferred_element_type=F32)
    for step, target in enumerate(outs):
        target[...] = product[step * rows : (step + 1) * rows, :].astype(target.dtype)
    for start in range(0, feats_ref.shape[0], LANES):
        cols = slice(start, start + LANES)
        feats_t[:, cols] = feats_ref[cols, :].astype(F32).T.astype(BF16)


def far_sum_kernel(*refs):
    own_ref, got, out = refs[0], refs[1:-1], refs[-1]
    share = own_ref.shape[0] - 8
    total, loss = own_ref[:share, :], own_ref[share : share + 1, :]
    for block in got:
        total = total + block[:share, :].astype(F32)
        loss = loss + loss_of(block[share:, :])
    out[:share, :] = total
    out[share : share + 1, :] = loss


def gathered_gradient(own_ref, got, inv_ref, loss_out):
    share = own_ref.shape[0] - 8
    total = own_ref[:share, :]
    loss = own_ref[share : share + 1, :]
    for block in got:
        total = total + block[:share, :].astype(F32)
        loss = loss + loss_of(block[share:, :])
    loss_out[...] = loss
    return inv_ref[...] * total


def weight_kernel(group, wide, *refs):
    own_ref, got = refs[0], refs[1 : group // 4]
    inv_ref, feats_ref, feats_t_ref, loss_out, send_out = refs[group // 4 :]
    rows = feats_t_ref.shape[0] // wide
    high, low = split_pair(gathered_gradient(own_ref, got, inv_ref, loss_out))
    rest = high.shape[0] - LANES
    both = jnp.concatenate([high[LANES:, :], low[LANES:, :]], axis=0)
    tail = jnp.dot(both, feats_ref[...], preferred_element_type=F32)
    tail = (tail[:rest, :] + tail[rest:, :]).astype(BF16)
    both = jnp.concatenate([high[:LANES, :], low[:LANES, :]], axis=0)
    main = lax.dot_general(feats_t_ref[...], both, NT, preferred_element_type=F32)
    main = (main[:, :LANES] + main[:, LANES:]).astype(BF16)
    for place in range(wide):
        begin = place * rows
        send_out[place, :rows, :] = main[begin : begin + rows, :]
        send_out[place, rows : rows + rest, :] = tail[:, begin : begin + LANES]
        send_out[place, rows + rest :, :] = jnp.zeros((rest, LANES), BF16)
        send_out[place, rows + rest :, : rows - LANES] = tail[:, begin + LANES : begin + rows]


def total_kernel(rest, got_ref, out):
    rows = out.shape[0]
    for side in range(2):
        half = got_ref[side].astype(F32)
        for place in range(side + 2, got_ref.shape[0], 2):
            half = half + got_ref[place].astype(F32)
        left = side * (LANES + rest)
        out[:, left : left + LANES] = half[:rows, :]
        out[:LANES, left + LANES : left + LANES + rest] = half[rows : rows + rest, :].T
        out[LANES:, left + LANES : left + LANES + rest] = half[rows + rest :, :].T[: rows - LANES, :]


def sum_kernel(*refs):
    total = refs[0][...]
    for block in refs[1:-1]:
        total = total + block[...].astype(F32)
    refs[-1][...] = total


def added(own, parts, cost):
    return pl.pallas_call(
        sum_kernel,
        in_specs=[VMEM] * (1 + len(parts)),
        out_specs=VMEM,
        out_shape=jax.ShapeDtypeStruct(own.shape, F32),
        compiler_params=limit(12),
        cost_estimate=cost,
        name="caption_sum",
    )(own, *parts)


def local(wide, narrow, image_feats, proj_weight, text_embed, log_scale, logit_bias):
    rows, width = image_feats.shape
    total = wide * narrow
    group = 2 * narrow
    spread = wide // 2
    share = width // group
    images = group * rows
    member = lax.axis_index(AXES[1:]).astype(jnp.int32).reshape(1)

    texts = [swapped(text_embed, total, step * group) for step in range(1, spread)]
    got_feats = [swapped(image_feats, total, 2 * step) for step in range(1, group // 2)]
    own_text, scalars = pl.pallas_call(
        own_kernel,
        in_specs=[SMEM] * 2 + [VMEM],
        out_specs=[VMEM] * 2,
        out_shape=[jax.ShapeDtypeStruct((rows, width), BF16), jax.ShapeDtypeStruct((8, LANES), F32)],
        compiler_params=limit(4),
        cost_estimate=hint(10**10),
        name="own_text",
    )(log_scale, logit_bias, text_embed)
    own_half = pl.pallas_call(
        stack_kernel,
        in_specs=[SMEM] + [VMEM] * (group // 2),
        out_specs=VMEM,
        out_shape=jax.ShapeDtypeStruct((images // 2, width), BF16),
        compiler_params=limit(4),
        name="stack",
    )(member, image_feats, *got_feats)
    got_half = swapped(own_half, total, 1)
    own_proj = pl.pallas_call(
        project_kernel,
        in_specs=[VMEM] * 2,
        out_specs=VMEM,
        out_shape=jax.ShapeDtypeStruct((images // 2, width), F32),
        compiler_params=limit(8),
        name="own_projection",
    )(own_half, proj_weight)
    own_proj, *texts = lax.optimization_barrier((own_proj, *texts[::-1]))
    text_emb = pl.pallas_call(
        text_kernel,
        in_specs=[VMEM] * spread,
        out_specs=VMEM,
        out_shape=jax.ShapeDtypeStruct((spread * rows, width), BF16),
        compiler_params=limit(4 if spread <= 4 else 16),
        cost_estimate=hint(10**10),
        name="text_unit",
    )(own_text, *texts)

    results = pl.pallas_call(
        functools.partial(pair_kernel, narrow, group),
        in_specs=[SMEM] + [VMEM] * 6,
        out_specs=[VMEM] * 7,
        out_shape=[
            jax.ShapeDtypeStruct((images, width), BF16),
            jax.ShapeDtypeStruct((1, images), F32),
            jax.ShapeDtypeStruct((width, images), BF16),
            jax.ShapeDtypeStruct((spread * rows, images), BF16),
            jax.ShapeDtypeStruct((group // 2, share + 8, images), F32),
        ]
        + [jax.ShapeDtypeStruct((group // 4, share + STAT_ROWS, images), BF16)] * 2,
        scratch_shapes=[
            pltpu.VMEM((width, images), F32),
            pltpu.VMEM((width, images), F32),
            pltpu.VMEM((images, width), F32),
        ],
        compiler_params=limit(24 if spread <= 4 else 40),
        name="pairs",
    )(member, scalars, proj_weight, own_half, own_proj, got_half, text_emb)
    all_feats, inv_part, img_emb, grad_tile, own_part, near_part, far_part = results
    got_far = swapped(far_part, total, 1)
    got_near = swapped(near_part, total, 1)
    sent_block = jax.ShapeDtypeStruct((share + STAT_ROWS, images), BF16)
    kept_block = jax.ShapeDtypeStruct((share + 8, images), F32)
    half = group // 4
    far = pl.pallas_call(
        functools.partial(chip_kernel, half),
        in_specs=[VMEM] * 2,
        out_specs=[VMEM] * half,
        out_shape=[sent_block] * half,
        compiler_params=limit(8),
        name="chip_far",
    )(own_part, got_far)
    far = [swapped(value, total, 2 * (half + index)) for index, value in enumerate(far)]
    feats_t, own_text, *sent_text = pl.pallas_call(
        functools.partial(caption_kernel, rows),
        in_specs=[VMEM] * 3,
        out_specs=[VMEM] * (1 + spread),
        out_shape=[jax.ShapeDtypeStruct((width, images), BF16), jax.ShapeDtypeStruct((rows, width), F32)]
        + [jax.ShapeDtypeStruct((rows, width), BF16)] * (spread - 1),
        compiler_params=limit(12 if spread <= 4 else 32),
        name="captions",
    )(grad_tile, img_emb, all_feats)
    got_text = [swapped(value, total, step * group) for step, value in enumerate(sent_text, 1)]
    own_part, *near = pl.pallas_call(
        functools.partial(chip_kernel, 0),
        in_specs=[VMEM] * 2,
        out_specs=[VMEM] * half,
        out_shape=[kept_block] + [sent_block] * (half - 1),
        compiler_params=limit(8),
        name="chip_near",
    )(own_part, got_near)
    near = [swapped(value, total, 2 * index) for index, value in enumerate(near, 1)]
    own_part = pl.pallas_call(
        far_sum_kernel,
        in_specs=[VMEM] * (1 + half),
        out_specs=VMEM,
        out_shape=kept_block,
        compiler_params=limit(8),
        cost_estimate=hint(5 * 10**8),
        name="far_sum",
    )(own_part, *far)

    out_rows = width // wide
    rest = share - LANES
    packed = out_rows + 2 * rest
    direct = LANES < out_rows <= 2 * LANES and out_rows % 16 == 0 and rest % 16 == 0
    if direct:
        loss_line, sent_weight = pl.pallas_call(
            functools.partial(weight_kernel, group, wide),
            in_specs=[VMEM] * (3 + group // 4),
            out_specs=[VMEM] * 2,
            out_shape=[
                jax.ShapeDtypeStruct((1, images), F32),
                jax.ShapeDtypeStruct((wide, packed, LANES), BF16),
            ],
            compiler_params=limit(12),
            name="weights",
        )(own_part, *near, inv_part, all_feats, feats_t)
        got_weight = lax.all_to_all(sent_weight, AXES[:2], 0, 0)
        d_proj = pl.pallas_call(
            functools.partial(total_kernel, rest),
            in_specs=[VMEM],
            out_specs=VMEM,
            out_shape=jax.ShapeDtypeStruct((out_rows, 2 * share), F32),
            compiler_params=limit(4),
            name="weight_total",
        )(got_weight)
    else:

        def gradient_kernel(*refs):
            own_ref, blocks = refs[0], refs[1 : group // 4]
            inv_ref, loss_out, d_out = refs[group // 4 :]
            d_out[...] = gathered_gradient(own_ref, blocks, inv_ref, loss_out)

        loss_line, d_zproj = pl.pallas_call(
            gradient_kernel,
            in_specs=[VMEM] * (1 + group // 4),
            out_specs=[VMEM] * 2,
            out_shape=[jax.ShapeDtypeStruct((1, images), F32), jax.ShapeDtypeStruct((share, images), F32)],
            compiler_params=limit(12),
            name="gradient",
        )(own_part, *near, inv_part)
        partial = sum(
            lax.dot_general(feats_t, part, NT, preferred_element_type=F32) for part in split_pair(d_zproj)
        )
        left = lax.axis_index("inner") == 0
        both = jnp.concatenate([jnp.where(left, partial, 0.0), jnp.where(left, 0.0, partial)], axis=1)
        d_proj = lax.psum_scatter(both, AXES[:2], scatter_dimension=0, tiled=True)

    if len(got_text) > 1:
        own_text = added(own_text, got_text[:0:-1], hint(5 * 10**9))
    d_text_unit = added(own_text, got_text[:1], None)
    image_loss = lax.dynamic_slice_in_dim(loss_line[0], first_image(member[0], rows, group), rows, 0)
    return (image_loss, d_text_unit, d_proj)


def solution(mesh):
    wide, narrow = mesh.shape["wide"], mesh.shape["narrow"]
    cut = jax.sharding.Mesh(mesh.devices.reshape(wide // 2, 2, narrow), AXES)
    placed = (P(AXES, None), P(), P(AXES, None), P(), P())
    return jax.shard_map(
        functools.partial(local, wide, narrow),
        mesh=cut,
        in_specs=placed,
        out_specs=(P(AXES), P(AXES, None), P(AXES[:2], "narrow")),
        check_vma=False,
    )
```

```python
import functools

import jax
import jax.numpy as jnp
from jax import lax
from jax.experimental import pallas as pl
from jax.experimental.pallas import tpu as pltpu
from jax.sharding import PartitionSpec as P

AXES = ("outer", "inner", "narrow")
F32 = jnp.float32
BF16 = jnp.bfloat16
LANES = 128
STAT_ROWS = 16
VMEM = pl.BlockSpec(memory_space=pltpu.VMEM)
SMEM = pl.BlockSpec(memory_space=pltpu.SMEM)
NT = (((1,), (1,)), ((), ()))
TN = (((0,), (0,)), ((), ()))
MIB = 1024 * 1024


def limit(mebibytes):
    return pltpu.CompilerParams(vmem_limit_bytes=mebibytes * MIB)


def hint(flops):
    return pl.CostEstimate(flops=flops, bytes_accessed=0, transcendentals=0)


def swapped(value, total, mask):
    return lax.ppermute(value, AXES, [(source, source ^ mask) for source in range(total)])


def split_pair(values):
    high = values.astype(BF16)
    return high, (values - high.astype(F32)).astype(BF16)


def loss_rows(loss):
    row = lax.broadcasted_iota(jnp.int32, (STAT_ROWS, loss.shape[1]), 0)
    high, low = split_pair(loss)
    rows = jnp.where(row == 0, high.astype(F32), jnp.where(row == 1, low.astype(F32), 0.0))
    return rows.astype(BF16)


def loss_of(rows):
    rows = rows.astype(F32)
    return rows[0:1, :] + rows[1:2, :]


def column_block(member, narrow):
    return (member % narrow) * 2 + member // narrow


def unit_text(text):
    values = text.astype(F32)
    inverse = lax.rsqrt(jnp.sum(values * values, axis=1, keepdims=True) + 1e-06)
    return (values * inverse).astype(BF16)


def own_kernel(log_scale_ref, bias_ref, text_ref, text_out, scalars_out):
    text_out[...] = unit_text(text_ref[...])
    row = lax.broadcasted_iota(jnp.int32, scalars_out.shape, 0)
    scale = jnp.exp(jnp.full(scalars_out.shape, log_scale_ref[0], F32))
    scalars_out[...] = jnp.where(row == 0, scale, bias_ref[0])


def stack_kernel(member_ref, *refs):
    blocks, half_out = refs[:-1], refs[-1]
    rows = blocks[0].shape[0]
    chip = member_ref[0] // 2
    for step, block in enumerate(blocks):
        place = pl.multiple_of((chip ^ step) * rows, rows)
        half_out[pl.ds(place, rows), :] = block[...]


def text_kernel(*refs):
    texts, out = refs[:-1], refs[-1]
    rows = texts[0].shape[0]
    out[:rows, :] = texts[0][...]
    for place, text in enumerate(texts[1:], 1):
        step = len(texts) - place
        out[step * rows : (step + 1) * rows, :] = unit_text(text[...])


def project_kernel(feats_ref, weight_ref, out):
    out[...] = jnp.dot(feats_ref[...], weight_ref[...], preferred_element_type=F32)


def first_image(member, rows, group):
    return (member % 2) * (group // 2 * rows) + (member // 2) * rows


def pair_kernel(
    narrow,
    group,
    member_ref,
    scalars_ref,
    weight,
    own_half,
    own_proj,
    got_half,
    text_all,
    feats_ref,
    inv_out,
    emb_out,
    grad_out,
    own_out,
    near_out,
    far_out,
    unit_all,
    d_all,
    proj_all,
):
    images, width = feats_ref.shape
    rows = images // group
    spread = text_all.shape[0] // rows
    half = images // 2
    share = width // group
    member = member_ref[0]

    place = pl.multiple_of((member % 2) * half, half)
    feats_ref[pl.ds(place, half), :] = own_half[...]
    proj_all[pl.ds(place, half), :] = own_proj[...]
    place = pl.multiple_of((1 - member % 2) * half, half)
    feats_ref[pl.ds(place, half), :] = got_half[...]
    proj_all[pl.ds(place, half), :] = jnp.dot(got_half[...], weight[...], preferred_element_type=F32)
    for start in range(0, images, LANES):
        cols = slice(start, start + LANES)
        turned = proj_all[cols, :].T
        inverse = lax.rsqrt(jnp.sum(turned * turned, axis=0, keepdims=True) + 1e-06)
        unit = turned * inverse
        inv_out[:, cols] = inverse
        unit_all[:, cols] = unit
        emb_out[:, cols] = unit.astype(BF16)

    scale = scalars_ref[0:1, 0:1]
    shift = scalars_ref[1:2, 0:1]
    count = 4 * rows if spread % 4 == 0 else rows
    chunks = spread * rows // count

    def one_chunk(chunk, loss_sum, dot_sum, first):
        here = pl.ds(pl.multiple_of(chunk * count, count), count)
        text = text_all[here, :]
        products = jnp.dot(text, emb_out[...], preferred_element_type=F32)
        logits = scale * products + shift
        caption = lax.broadcasted_iota(jnp.int32, (count, images), 0) + chunk * count
        image = lax.broadcasted_iota(jnp.int32, (count, images), 1)
        own = jnp.logical_and(caption < rows, image == first_image(member, rows, group) + caption)
        sign = jnp.where(own, 1.0, -1.0).astype(F32)
        away = -sign * logits
        small = jnp.exp(-jnp.abs(away))
        loss = jnp.maximum(away, 0.0) + jnp.log1p(small)
        chance = jnp.where(away >= 0.0, 1.0, small) / (1.0 + small)
        grad = (-scale * sign * chance).astype(BF16)
        grad_out[here, :] = grad
        loss_sum = loss_sum + jnp.sum(loss, axis=0, keepdims=True)
        dot_sum = dot_sum + jnp.sum(grad.astype(F32) * products, axis=0, keepdims=True)
        d_img = lax.dot_general(text, grad, TN, preferred_element_type=F32)
        if first:
            d_all[...] = d_img
        else:
            d_all[...] += d_img
        return loss_sum, dot_sum

    zero = jnp.zeros((1, images), F32)
    sums = one_chunk(0, zero, zero, True)
    if chunks > 1:
        sums = lax.fori_loop(1, chunks, lambda c, s: one_chunk(c, *s, False), sums)
    loss_sum, dot_sum = sums

    def projected(index):
        part = pl.ds(pl.multiple_of(column_block(member ^ index, narrow) * share, share), share)
        return d_all[part, :] - unit_all[part, :] * dot_sum

    losses = loss_rows(loss_sum)
    for index in range(group // 2):
        own_out[index, :share, :] = projected(2 * index)
        target = (near_out, far_out)[index * 4 // group].at[index % (group // 4)]
        target[:share, :] = projected(2 * index + 1).astype(BF16)
        target[share:, :] = losses
    own_out[0, share : share + 1, :] = loss_sum


def chip_kernel(first, own_ref, got_ref, *outs):
    share = own_ref.shape[1] - 8
    loss = own_ref[0, share : share + 1, :] + loss_of(got_ref[0, share:, :])
    for index, target in enumerate(outs):
        total = own_ref[first + index, :share, :] + got_ref[index, :share, :].astype(F32)
        target[:share, :] = total.astype(target.dtype)
        if target.dtype == BF16:
            target[share:, :] = loss_rows(loss)
        else:
            target[share : share + 1, :] = loss


def caption_kernel(rows, grad_ref, emb_ref, feats_ref, feats_t, *outs):
    product = lax.dot_general(grad_ref[...], emb_ref[...], NT, preferred_element_type=F32)
    for step, target in enumerate(outs):
        target[...] = product[step * rows : (step + 1) * rows, :].astype(target.dtype)
    for start in range(0, feats_ref.shape[0], LANES):
        cols = slice(start, start + LANES)
        feats_t[:, cols] = feats_ref[cols, :].astype(F32).T.astype(BF16)


def far_sum_kernel(*refs):
    own_ref, got, out = refs[0], refs[1:-1], refs[-1]
    share = own_ref.shape[0] - 8
    total, loss = own_ref[:share, :], own_ref[share : share + 1, :]
    for block in got:
        total = total + block[:share, :].astype(F32)
        loss = loss + loss_of(block[share:, :])
    out[:share, :] = total
    out[share : share + 1, :] = loss


def gathered_gradient(own_ref, got, inv_ref, loss_out):
    share = own_ref.shape[0] - 8
    total = own_ref[:share, :]
    loss = own_ref[share : share + 1, :]
    for block in got:
        total = total + block[:share, :].astype(F32)
        loss = loss + loss_of(block[share:, :])
    loss_out[...] = loss
    return inv_ref[...] * total


def weight_kernel(group, wide, *refs):
    own_ref, got = refs[0], refs[1 : group // 4]
    inv_ref, feats_ref, feats_t_ref, loss_out, send_out = refs[group // 4 :]
    rows = feats_t_ref.shape[0] // wide
    high, low = split_pair(gathered_gradient(own_ref, got, inv_ref, loss_out))
    rest = high.shape[0] - LANES
    both = jnp.concatenate([high[LANES:, :], low[LANES:, :]], axis=0)
    tail = jnp.dot(both, feats_ref[...], preferred_element_type=F32)
    tail = (tail[:rest, :] + tail[rest:, :]).astype(BF16)
    both = jnp.concatenate([high[:LANES, :], low[:LANES, :]], axis=0)
    main = lax.dot_general(feats_t_ref[...], both, NT, preferred_element_type=F32)
    main = (main[:, :LANES] + main[:, LANES:]).astype(BF16)
    for place in range(wide):
        begin = place * rows
        send_out[place, :rows, :] = main[begin : begin + rows, :]
        send_out[place, rows : rows + rest, :] = tail[:, begin : begin + LANES]
        send_out[place, rows + rest :, :] = jnp.zeros((rest, LANES), BF16)
        send_out[place, rows + rest :, : rows - LANES] = tail[:, begin + LANES : begin + rows]


def total_kernel(rest, got_ref, out):
    rows = out.shape[0]
    for side in range(2):
        half = got_ref[side].astype(F32)
        for place in range(side + 2, got_ref.shape[0], 2):
            half = half + got_ref[place].astype(F32)
        left = side * (LANES + rest)
        out[:, left : left + LANES] = half[:rows, :]
        out[:LANES, left + LANES : left + LANES + rest] = half[rows : rows + rest, :].T
        out[LANES:, left + LANES : left + LANES + rest] = half[rows + rest :, :].T[: rows - LANES, :]


def sum_kernel(*refs):
    total = refs[0][...]
    for block in refs[1:-1]:
        total = total + block[...].astype(F32)
    refs[-1][...] = total


def local(wide, narrow, image_feats, proj_weight, text_embed, log_scale, logit_bias):
    rows, width = image_feats.shape
    total = wide * narrow
    group = 2 * narrow
    spread = wide // 2
    share = width // group
    images = group * rows
    member = lax.axis_index(AXES[1:]).astype(jnp.int32).reshape(1)

    texts = [swapped(text_embed, total, step * group) for step in range(1, spread)]
    got_feats = [swapped(image_feats, total, 2 * step) for step in range(1, group // 2)]
    own_text, scalars = pl.pallas_call(
        own_kernel,
        in_specs=[SMEM] * 2 + [VMEM],
        out_specs=[VMEM] * 2,
        out_shape=[jax.ShapeDtypeStruct((rows, width), BF16), jax.ShapeDtypeStruct((8, LANES), F32)],
        compiler_params=limit(4),
        cost_estimate=hint(10**10),
        name="own_text",
    )(log_scale, logit_bias, text_embed)
    own_half = pl.pallas_call(
        stack_kernel,
        in_specs=[SMEM] + [VMEM] * (group // 2),
        out_specs=VMEM,
        out_shape=jax.ShapeDtypeStruct((images // 2, width), BF16),
        compiler_params=limit(4),
        name="stack",
    )(member, image_feats, *got_feats)
    got_half = swapped(own_half, total, 1)
    own_proj = pl.pallas_call(
        project_kernel,
        in_specs=[VMEM] * 2,
        out_specs=VMEM,
        out_shape=jax.ShapeDtypeStruct((images // 2, width), F32),
        compiler_params=limit(8),
        name="own_projection",
    )(own_half, proj_weight)
    own_proj, *texts = lax.optimization_barrier((own_proj, *texts[::-1]))
    text_emb = pl.pallas_call(
        text_kernel,
        in_specs=[VMEM] * spread,
        out_specs=VMEM,
        out_shape=jax.ShapeDtypeStruct((spread * rows, width), BF16),
        compiler_params=limit(4 if spread <= 4 else 16),
        cost_estimate=hint(10**10),
        name="text_unit",
    )(own_text, *texts)

    results = pl.pallas_call(
        functools.partial(pair_kernel, narrow, group),
        in_specs=[SMEM] + [VMEM] * 6,
        out_specs=[VMEM] * 7,
        out_shape=[
            jax.ShapeDtypeStruct((images, width), BF16),
            jax.ShapeDtypeStruct((1, images), F32),
            jax.ShapeDtypeStruct((width, images), BF16),
            jax.ShapeDtypeStruct((spread * rows, images), BF16),
            jax.ShapeDtypeStruct((group // 2, share + 8, images), F32),
        ]
        + [jax.ShapeDtypeStruct((group // 4, share + STAT_ROWS, images), BF16)] * 2,
        scratch_shapes=[
            pltpu.VMEM((width, images), F32),
            pltpu.VMEM((width, images), F32),
            pltpu.VMEM((images, width), F32),
        ],
        compiler_params=limit(24 if spread <= 4 else 40),
        name="pairs",
    )(member, scalars, proj_weight, own_half, own_proj, got_half, text_emb)
    all_feats, inv_part, img_emb, grad_tile, own_part, near_part, far_part = results
    got_far = swapped(far_part, total, 1)
    got_near = swapped(near_part, total, 1)
    feats_t, own_text, *sent_text = pl.pallas_call(
        functools.partial(caption_kernel, rows),
        in_specs=[VMEM] * 3,
        out_specs=[VMEM] * (1 + spread),
        out_shape=[jax.ShapeDtypeStruct((width, images), BF16), jax.ShapeDtypeStruct((rows, width), F32)]
        + [jax.ShapeDtypeStruct((rows, width), BF16)] * (spread - 1),
        compiler_params=limit(12 if spread <= 4 else 32),
        name="captions",
    )(grad_tile, img_emb, all_feats)
    own_part, got_far, sent_text = lax.optimization_barrier((own_part, got_far, sent_text))
    sent_block = jax.ShapeDtypeStruct((share + STAT_ROWS, images), BF16)
    kept_block = jax.ShapeDtypeStruct((share + 8, images), F32)
    half = group // 4
    far = pl.pallas_call(
        functools.partial(chip_kernel, half),
        in_specs=[VMEM] * 2,
        out_specs=[VMEM] * half,
        out_shape=[sent_block] * half,
        compiler_params=limit(8),
        name="chip_far",
    )(own_part, got_far)
    far = [swapped(value, total, 2 * (half + index)) for index, value in enumerate(far)]
    got_text = [swapped(value, total, step * group) for step, value in enumerate(sent_text, 1)]
    own_part, *near = pl.pallas_call(
        functools.partial(chip_kernel, 0),
        in_specs=[VMEM] * 2,
        out_specs=[VMEM] * half,
        out_shape=[kept_block] + [sent_block] * (half - 1),
        compiler_params=limit(8),
        name="chip_near",
    )(own_part, got_near)
    near = [swapped(value, total, 2 * index) for index, value in enumerate(near, 1)]
    own_part = pl.pallas_call(
        far_sum_kernel,
        in_specs=[VMEM] * (1 + half),
        out_specs=VMEM,
        out_shape=kept_block,
        compiler_params=limit(8),
        cost_estimate=hint(5 * 10**8),
        name="far_sum",
    )(own_part, *far)

    out_rows = width // wide
    rest = share - LANES
    packed = out_rows + 2 * rest
    direct = LANES < out_rows <= 2 * LANES and out_rows % 16 == 0 and rest % 16 == 0
    if direct:
        loss_line, sent_weight = pl.pallas_call(
            functools.partial(weight_kernel, group, wide),
            in_specs=[VMEM] * (3 + group // 4),
            out_specs=[VMEM] * 2,
            out_shape=[
                jax.ShapeDtypeStruct((1, images), F32),
                jax.ShapeDtypeStruct((wide, packed, LANES), BF16),
            ],
            compiler_params=limit(12),
            name="weights",
        )(own_part, *near, inv_part, all_feats, feats_t)
        got_weight = lax.all_to_all(sent_weight, AXES[:2], 0, 0)
        d_proj = pl.pallas_call(
            functools.partial(total_kernel, rest),
            in_specs=[VMEM],
            out_specs=VMEM,
            out_shape=jax.ShapeDtypeStruct((out_rows, 2 * share), F32),
            compiler_params=limit(4),
            name="weight_total",
        )(got_weight)
    else:

        def gradient_kernel(*refs):
            own_ref, blocks = refs[0], refs[1 : group // 4]
            inv_ref, loss_out, d_out = refs[group // 4 :]
            d_out[...] = gathered_gradient(own_ref, blocks, inv_ref, loss_out)

        loss_line, d_zproj = pl.pallas_call(
            gradient_kernel,
            in_specs=[VMEM] * (1 + group // 4),
            out_specs=[VMEM] * 2,
            out_shape=[jax.ShapeDtypeStruct((1, images), F32), jax.ShapeDtypeStruct((share, images), F32)],
            compiler_params=limit(12),
            name="gradient",
        )(own_part, *near, inv_part)
        partial = sum(
            lax.dot_general(feats_t, part, NT, preferred_element_type=F32) for part in split_pair(d_zproj)
        )
        left = lax.axis_index("inner") == 0
        both = jnp.concatenate([jnp.where(left, partial, 0.0), jnp.where(left, 0.0, partial)], axis=1)
        d_proj = lax.psum_scatter(both, AXES[:2], scatter_dimension=0, tiled=True)

    d_text_unit = pl.pallas_call(
        sum_kernel,
        in_specs=[VMEM] * spread,
        out_specs=VMEM,
        out_shape=jax.ShapeDtypeStruct((rows, width), F32),
        compiler_params=limit(12),
        cost_estimate=hint(5 * 10**9),
        name="caption_total",
    )(own_text, *got_text[::-1])
    image_loss = lax.dynamic_slice_in_dim(loss_line[0], first_image(member[0], rows, group), rows, 0)
    return (image_loss, d_text_unit, d_proj)


def solution(mesh):
    wide, narrow = mesh.shape["wide"], mesh.shape["narrow"]
    cut = jax.sharding.Mesh(mesh.devices.reshape(wide // 2, 2, narrow), AXES)
    placed = (P(AXES, None), P(), P(AXES, None), P(), P())
    return jax.shard_map(
        functools.partial(local, wide, narrow),
        mesh=cut,
        in_specs=placed,
        out_specs=(P(AXES), P(AXES, None), P(AXES[:2], "narrow")),
        check_vma=False,
    )
```

```python
import functools

import jax
import jax.numpy as jnp
from jax import lax
from jax.experimental import pallas as pl
from jax.experimental.pallas import tpu as pltpu
from jax.sharding import PartitionSpec as P

AXES = ("outer", "inner", "narrow")
F32 = jnp.float32
BF16 = jnp.bfloat16
LANES = 128
STAT_ROWS = 16
VMEM = pl.BlockSpec(memory_space=pltpu.VMEM)
SMEM = pl.BlockSpec(memory_space=pltpu.SMEM)
NT = (((1,), (1,)), ((), ()))
TN = (((0,), (0,)), ((), ()))
MIB = 1024 * 1024


def limit(mebibytes):
    return pltpu.CompilerParams(vmem_limit_bytes=mebibytes * MIB)


def hint(flops):
    return pl.CostEstimate(flops=flops, bytes_accessed=0, transcendentals=0)


def swapped(value, total, mask):
    return lax.ppermute(value, AXES, [(source, source ^ mask) for source in range(total)])


def split_pair(values):
    high = values.astype(BF16)
    return high, (values - high.astype(F32)).astype(BF16)


def loss_rows(loss):
    row = lax.broadcasted_iota(jnp.int32, (STAT_ROWS, loss.shape[1]), 0)
    high, low = split_pair(loss)
    rows = jnp.where(row == 0, high.astype(F32), jnp.where(row == 1, low.astype(F32), 0.0))
    return rows.astype(BF16)


def loss_of(rows):
    rows = rows.astype(F32)
    return rows[0:1, :] + rows[1:2, :]


def column_block(member, narrow):
    return (member % narrow) * 2 + member // narrow


def unit_text(text):
    values = text.astype(F32)
    inverse = lax.rsqrt(jnp.sum(values * values, axis=1, keepdims=True) + 1e-06)
    return (values * inverse).astype(BF16)


def own_kernel(log_scale_ref, bias_ref, text_ref, text_out, scalars_out):
    text_out[...] = unit_text(text_ref[...])
    row = lax.broadcasted_iota(jnp.int32, scalars_out.shape, 0)
    scale = jnp.exp(jnp.full(scalars_out.shape, log_scale_ref[0], F32))
    scalars_out[...] = jnp.where(row == 0, scale, bias_ref[0])


def stack_kernel(member_ref, *refs):
    blocks, half_out = refs[:-1], refs[-1]
    rows = blocks[0].shape[0]
    chip = member_ref[0] // 2
    for step, block in enumerate(blocks):
        place = pl.multiple_of((chip ^ step) * rows, rows)
        half_out[pl.ds(place, rows), :] = block[...]


def text_kernel(*refs):
    texts, out = refs[:-1], refs[-1]
    rows = texts[0].shape[0]
    out[:rows, :] = texts[0][...]
    for place, text in enumerate(texts[1:], 1):
        step = len(texts) - place
        out[step * rows : (step + 1) * rows, :] = unit_text(text[...])


def project_kernel(feats_ref, weight_ref, out):
    out[...] = jnp.dot(feats_ref[...], weight_ref[...], preferred_element_type=F32)


def first_image(member, rows, group):
    return (member % 2) * (group // 2 * rows) + (member // 2) * rows


def pair_kernel(
    narrow,
    group,
    member_ref,
    scalars_ref,
    weight,
    own_half,
    own_proj,
    got_half,
    text_all,
    feats_ref,
    inv_out,
    emb_out,
    grad_out,
    own_out,
    near_out,
    far_out,
    unit_all,
    d_all,
    proj_all,
):
    images, width = feats_ref.shape
    rows = images // group
    spread = text_all.shape[0] // rows
    half = images // 2
    share = width // group
    member = member_ref[0]

    place = pl.multiple_of((member % 2) * half, half)
    feats_ref[pl.ds(place, half), :] = own_half[...]
    proj_all[pl.ds(place, half), :] = own_proj[...]
    place = pl.multiple_of((1 - member % 2) * half, half)
    feats_ref[pl.ds(place, half), :] = got_half[...]
    proj_all[pl.ds(place, half), :] = jnp.dot(got_half[...], weight[...], preferred_element_type=F32)
    for start in range(0, images, LANES):
        cols = slice(start, start + LANES)
        turned = proj_all[cols, :].T
        inverse = lax.rsqrt(jnp.sum(turned * turned, axis=0, keepdims=True) + 1e-06)
        unit = turned * inverse
        inv_out[:, cols] = inverse
        unit_all[:, cols] = unit
        emb_out[:, cols] = unit.astype(BF16)

    scale = scalars_ref[0:1, 0:1]
    shift = scalars_ref[1:2, 0:1]
    count = 4 * rows if spread % 4 == 0 else rows
    chunks = spread * rows // count

    def one_chunk(chunk, loss_sum, dot_sum, first):
        here = pl.ds(pl.multiple_of(chunk * count, count), count)
        text = text_all[here, :]
        products = jnp.dot(text, emb_out[...], preferred_element_type=F32)
        logits = scale * products + shift
        caption = lax.broadcasted_iota(jnp.int32, (count, images), 0) + chunk * count
        image = lax.broadcasted_iota(jnp.int32, (count, images), 1)
        own = jnp.logical_and(caption < rows, image == first_image(member, rows, group) + caption)
        sign = jnp.where(own, 1.0, -1.0).astype(F32)
        away = -sign * logits
        small = jnp.exp(-jnp.abs(away))
        loss = jnp.maximum(away, 0.0) + jnp.log1p(small)
        chance = jnp.where(away >= 0.0, 1.0, small) / (1.0 + small)
        grad = (-scale * sign * chance).astype(BF16)
        grad_out[here, :] = grad
        loss_sum = loss_sum + jnp.sum(loss, axis=0, keepdims=True)
        dot_sum = dot_sum + jnp.sum(grad.astype(F32) * products, axis=0, keepdims=True)
        d_img = lax.dot_general(text, grad, TN, preferred_element_type=F32)
        if first:
            d_all[...] = d_img
        else:
            d_all[...] += d_img
        return loss_sum, dot_sum

    zero = jnp.zeros((1, images), F32)
    sums = one_chunk(0, zero, zero, True)
    if chunks > 1:
        sums = lax.fori_loop(1, chunks, lambda c, s: one_chunk(c, *s, False), sums)
    loss_sum, dot_sum = sums

    def projected(index):
        part = pl.ds(pl.multiple_of(column_block(member ^ index, narrow) * share, share), share)
        return d_all[part, :] - unit_all[part, :] * dot_sum

    losses = loss_rows(loss_sum)
    for index in range(group // 2):
        own_out[index, :share, :] = projected(2 * index)
        target = (near_out, far_out)[index * 4 // group].at[index % (group // 4)]
        target[:share, :] = projected(2 * index + 1).astype(BF16)
    near_out[0, share:, :] = losses
    own_out[0, share : share + 1, :] = loss_sum


def chip_kernel(first, own_ref, got_ref, *outs):
    share = own_ref.shape[1] - 8
    for index, target in enumerate(outs):
        total = own_ref[first + index, :share, :] + got_ref[index, :share, :].astype(F32)
        target[...] = total.astype(target.dtype)


def near_kernel(own_ref, got_ref, loss_out, *outs):
    chip_kernel(0, own_ref, got_ref, *outs)
    share = own_ref.shape[1] - 8
    loss = own_ref[0, share : share + 1, :] + loss_of(got_ref[0, share:, :])
    loss_out[...] = jnp.broadcast_to(loss, loss_out.shape)


def caption_kernel(rows, grad_ref, emb_ref, feats_ref, feats_t, *outs):
    product = lax.dot_general(grad_ref[...], emb_ref[...], NT, preferred_element_type=F32)
    for step, target in enumerate(outs):
        target[...] = product[step * rows : (step + 1) * rows, :].astype(target.dtype)
    for start in range(0, feats_ref.shape[0], LANES):
        cols = slice(start, start + LANES)
        feats_t[:, cols] = feats_ref[cols, :].astype(F32).T.astype(BF16)


def gathered_gradient(own_ref, got, inv_ref):
    total = own_ref[...]
    for block in got:
        total = total + block[...].astype(F32)
    return inv_ref[...] * total


def weight_kernel(group, wide, *refs):
    own_ref, got = refs[0], refs[1 : group // 4]
    inv_ref, feats_ref, feats_t_ref, send_out = refs[group // 4 :]
    rows = feats_t_ref.shape[0] // wide
    high, low = split_pair(gathered_gradient(own_ref, got, inv_ref))
    rest = high.shape[0] - LANES
    both = jnp.concatenate([high[LANES:, :], low[LANES:, :]], axis=0)
    tail = jnp.dot(both, feats_ref[...], preferred_element_type=F32)
    tail = (tail[:rest, :] + tail[rest:, :]).astype(BF16)
    both = jnp.concatenate([high[:LANES, :], low[:LANES, :]], axis=0)
    main = lax.dot_general(feats_t_ref[...], both, NT, preferred_element_type=F32)
    main = (main[:, :LANES] + main[:, LANES:]).astype(BF16)
    for place in range(wide):
        begin = place * rows
        send_out[place, :rows, :] = main[begin : begin + rows, :]
        send_out[place, rows : rows + rest, :] = tail[:, begin : begin + LANES]
        send_out[place, rows + rest :, :] = jnp.zeros((rest, LANES), BF16)
        send_out[place, rows + rest :, : rows - LANES] = tail[:, begin + LANES : begin + rows]


def total_kernel(rest, got_ref, out):
    rows = out.shape[0]
    for side in range(2):
        half = got_ref[side].astype(F32)
        for place in range(side + 2, got_ref.shape[0], 2):
            half = half + got_ref[place].astype(F32)
        left = side * (LANES + rest)
        out[:, left : left + LANES] = half[:rows, :]
        out[:LANES, left + LANES : left + LANES + rest] = half[rows : rows + rest, :].T
        out[LANES:, left + LANES : left + LANES + rest] = half[rows + rest :, :].T[: rows - LANES, :]


def sum_kernel(*refs):
    total = refs[0][...]
    for block in refs[1:-1]:
        total = total + block[...].astype(F32)
    refs[-1][...] = total


def local(wide, narrow, image_feats, proj_weight, text_embed, log_scale, logit_bias):
    rows, width = image_feats.shape
    total = wide * narrow
    group = 2 * narrow
    spread = wide // 2
    share = width // group
    images = group * rows
    member = lax.axis_index(AXES[1:]).astype(jnp.int32).reshape(1)

    texts = [swapped(text_embed, total, step * group) for step in range(1, spread)]
    got_feats = [swapped(image_feats, total, 2 * step) for step in range(1, group // 2)]
    own_text, scalars = pl.pallas_call(
        own_kernel,
        in_specs=[SMEM] * 2 + [VMEM],
        out_specs=[VMEM] * 2,
        out_shape=[jax.ShapeDtypeStruct((rows, width), BF16), jax.ShapeDtypeStruct((8, LANES), F32)],
        compiler_params=limit(4),
        cost_estimate=hint(10**10),
        name="own_text",
    )(log_scale, logit_bias, text_embed)
    own_half = pl.pallas_call(
        stack_kernel,
        in_specs=[SMEM] + [VMEM] * (group // 2),
        out_specs=VMEM,
        out_shape=jax.ShapeDtypeStruct((images // 2, width), BF16),
        compiler_params=limit(4),
        name="stack",
    )(member, image_feats, *got_feats)
    got_half = swapped(own_half, total, 1)
    own_proj = pl.pallas_call(
        project_kernel,
        in_specs=[VMEM] * 2,
        out_specs=VMEM,
        out_shape=jax.ShapeDtypeStruct((images // 2, width), F32),
        compiler_params=limit(8),
        name="own_projection",
    )(own_half, proj_weight)
    own_proj, *texts = lax.optimization_barrier((own_proj, *texts[::-1]))
    text_emb = pl.pallas_call(
        text_kernel,
        in_specs=[VMEM] * spread,
        out_specs=VMEM,
        out_shape=jax.ShapeDtypeStruct((spread * rows, width), BF16),
        compiler_params=limit(4 if spread <= 4 else 16),
        cost_estimate=hint(10**10),
        name="text_unit",
    )(own_text, *texts)

    results = pl.pallas_call(
        functools.partial(pair_kernel, narrow, group),
        in_specs=[SMEM] + [VMEM] * 6,
        out_specs=[VMEM] * 7,
        out_shape=[
            jax.ShapeDtypeStruct((images, width), BF16),
            jax.ShapeDtypeStruct((1, images), F32),
            jax.ShapeDtypeStruct((width, images), BF16),
            jax.ShapeDtypeStruct((spread * rows, images), BF16),
            jax.ShapeDtypeStruct((group // 2, share + 8, images), F32),
        ]
        + [jax.ShapeDtypeStruct((group // 4, share + extra, images), BF16) for extra in (STAT_ROWS, 0)],
        scratch_shapes=[
            pltpu.VMEM((width, images), F32),
            pltpu.VMEM((width, images), F32),
            pltpu.VMEM((images, width), F32),
        ],
        compiler_params=limit(24 if spread <= 4 else 40),
        name="pairs",
    )(member, scalars, proj_weight, own_half, own_proj, got_half, text_emb)
    all_feats, inv_part, img_emb, grad_tile, own_part, near_part, far_part = results
    got_far = swapped(far_part, total, 1)
    got_near = swapped(near_part, total, 1)
    feats_t, own_text, *sent_text = pl.pallas_call(
        functools.partial(caption_kernel, rows),
        in_specs=[VMEM] * 3,
        out_specs=[VMEM] * (1 + spread),
        out_shape=[jax.ShapeDtypeStruct((width, images), BF16), jax.ShapeDtypeStruct((rows, width), F32)]
        + [jax.ShapeDtypeStruct((rows, width), BF16)] * (spread - 1),
        compiler_params=limit(12 if spread <= 4 else 32),
        name="captions",
    )(grad_tile, img_emb, all_feats)
    own_part, got_far, sent_text = lax.optimization_barrier((own_part, got_far, sent_text))
    sent_block = jax.ShapeDtypeStruct((share, images), BF16)
    kept_block = jax.ShapeDtypeStruct((share, images), F32)
    loss_block = jax.ShapeDtypeStruct((8, images), F32)
    half = group // 4
    far = pl.pallas_call(
        functools.partial(chip_kernel, half),
        in_specs=[VMEM] * 2,
        out_specs=[VMEM] * half,
        out_shape=[sent_block] * half,
        compiler_params=limit(8),
        name="chip_far",
    )(own_part, got_far)
    far = [swapped(value, total, 2 * (half + index)) for index, value in enumerate(far)]
    got_text = [swapped(value, total, step * group) for step, value in enumerate(sent_text, 1)]
    loss, own_part, *near = pl.pallas_call(
        near_kernel,
        in_specs=[VMEM] * 2,
        out_specs=[VMEM] * (1 + half),
        out_shape=[loss_block, kept_block] + [sent_block] * (half - 1),
        compiler_params=limit(8),
        name="chip_near",
    )(own_part, got_near)
    near = [swapped(value, total, 2 * index) for index, value in enumerate(near, 1)]
    own_part = pl.pallas_call(
        sum_kernel,
        in_specs=[VMEM] * (1 + half),
        out_specs=VMEM,
        out_shape=kept_block,
        compiler_params=limit(8),
        cost_estimate=hint(5 * 10**8),
        name="far_sum",
    )(own_part, *far)

    out_rows = width // wide
    rest = share - LANES
    packed = out_rows + 2 * rest
    direct = LANES < out_rows <= 2 * LANES and out_rows % 16 == 0 and rest % 16 == 0
    if direct:
        sent_weight = pl.pallas_call(
            functools.partial(weight_kernel, group, wide),
            in_specs=[VMEM] * (3 + group // 4),
            out_specs=VMEM,
            out_shape=jax.ShapeDtypeStruct((wide, packed, LANES), BF16),
            compiler_params=limit(12),
            name="weights",
        )(own_part, *near, inv_part, all_feats, feats_t)
        got_weight = lax.all_to_all(sent_weight, AXES[:2], 0, 0)
        d_proj = pl.pallas_call(
            functools.partial(total_kernel, rest),
            in_specs=[VMEM],
            out_specs=VMEM,
            out_shape=jax.ShapeDtypeStruct((out_rows, 2 * share), F32),
            compiler_params=limit(4),
            name="weight_total",
        )(got_weight)
    else:

        def gradient_kernel(*refs):
            own_ref, blocks = refs[0], refs[1 : group // 4]
            inv_ref, d_out = refs[group // 4 :]
            d_out[...] = gathered_gradient(own_ref, blocks, inv_ref)

        d_zproj = pl.pallas_call(
            gradient_kernel,
            in_specs=[VMEM] * (1 + group // 4),
            out_specs=VMEM,
            out_shape=kept_block,
            compiler_params=limit(12),
            name="gradient",
        )(own_part, *near, inv_part)
        partial = sum(
            lax.dot_general(feats_t, part, NT, preferred_element_type=F32) for part in split_pair(d_zproj)
        )
        left = lax.axis_index("inner") == 0
        both = jnp.concatenate([jnp.where(left, partial, 0.0), jnp.where(left, 0.0, partial)], axis=1)
        d_proj = lax.psum_scatter(both, AXES[:2], scatter_dimension=0, tiled=True)

    d_text_unit = pl.pallas_call(
        sum_kernel,
        in_specs=[VMEM] * spread,
        out_specs=VMEM,
        out_shape=jax.ShapeDtypeStruct((rows, width), F32),
        compiler_params=limit(12),
        cost_estimate=hint(5 * 10**9),
        name="caption_total",
    )(own_text, *got_text)
    loss, d_text_unit = lax.optimization_barrier((loss, d_text_unit))
    losses = [swapped(loss, total, 2 * step) for step in range(1, group // 2)]
    loss = pl.pallas_call(
        sum_kernel,
        in_specs=[VMEM] * (group // 2),
        out_specs=VMEM,
        out_shape=loss_block,
        compiler_params=limit(4),
        name="loss_sum",
    )(loss, *losses)
    image_loss = lax.dynamic_slice_in_dim(loss[0], first_image(member[0], rows, group), rows, 0)
    return (image_loss, d_text_unit, d_proj)


def solution(mesh):
    wide, narrow = mesh.shape["wide"], mesh.shape["narrow"]
    cut = jax.sharding.Mesh(mesh.devices.reshape(wide // 2, 2, narrow), AXES)
    placed = (P(AXES, None), P(), P(AXES, None), P(), P())
    return jax.shard_map(
        functools.partial(local, wide, narrow),
        mesh=cut,
        in_specs=placed,
        out_specs=(P(AXES), P(AXES, None), P(AXES[:2], "narrow")),
        check_vma=False,
    )
```

```python
import functools

import jax
import jax.numpy as jnp
from jax import lax
from jax.experimental import pallas as pl
from jax.experimental.pallas import tpu as pltpu
from jax.sharding import PartitionSpec as P

AXES = ("outer", "inner", "narrow")
F32 = jnp.float32
BF16 = jnp.bfloat16
LANES = 128
STAT_ROWS = 16
VMEM = pl.BlockSpec(memory_space=pltpu.VMEM)
SMEM = pl.BlockSpec(memory_space=pltpu.SMEM)
NT = (((1,), (1,)), ((), ()))
TN = (((0,), (0,)), ((), ()))
MIB = 1024 * 1024


def limit(mebibytes):
    return pltpu.CompilerParams(vmem_limit_bytes=mebibytes * MIB)


def hint(flops):
    return pl.CostEstimate(flops=flops, bytes_accessed=0, transcendentals=0)


def swapped(value, total, mask):
    return lax.ppermute(value, AXES, [(source, source ^ mask) for source in range(total)])


def split_pair(values):
    high = values.astype(BF16)
    return high, (values - high.astype(F32)).astype(BF16)


def loss_rows(loss):
    row = lax.broadcasted_iota(jnp.int32, (STAT_ROWS, loss.shape[1]), 0)
    high, low = split_pair(loss)
    rows = jnp.where(row == 0, high.astype(F32), jnp.where(row == 1, low.astype(F32), 0.0))
    return rows.astype(BF16)


def loss_of(rows):
    rows = rows.astype(F32)
    return rows[0:1, :] + rows[1:2, :]


def column_block(member, narrow):
    return (member % narrow) * 2 + member // narrow


def unit_text(text):
    values = text.astype(F32)
    inverse = lax.rsqrt(jnp.sum(values * values, axis=1, keepdims=True) + 1e-06)
    return (values * inverse).astype(BF16)


def own_kernel(log_scale_ref, bias_ref, text_ref, text_out, scalars_out):
    text_out[...] = unit_text(text_ref[...])
    row = lax.broadcasted_iota(jnp.int32, scalars_out.shape, 0)
    scale = jnp.exp(jnp.full(scalars_out.shape, log_scale_ref[0], F32))
    scalars_out[...] = jnp.where(row == 0, scale, bias_ref[0])


def stack_kernel(member_ref, *refs):
    blocks, half_out = refs[:-1], refs[-1]
    rows = blocks[0].shape[0]
    chip = member_ref[0] // 2
    for step, block in enumerate(blocks):
        place = pl.multiple_of((chip ^ step) * rows, rows)
        half_out[pl.ds(place, rows), :] = block[...]


def text_kernel(*refs):
    texts, out = refs[:-1], refs[-1]
    rows = texts[0].shape[0]
    out[:rows, :] = texts[0][...]
    for place, text in enumerate(texts[1:], 1):
        step = len(texts) - place
        out[step * rows : (step + 1) * rows, :] = unit_text(text[...])


def project_kernel(feats_ref, weight_ref, out):
    out[...] = jnp.dot(feats_ref[...], weight_ref[...], preferred_element_type=F32)


def first_image(member, rows, group):
    return (member % 2) * (group // 2 * rows) + (member // 2) * rows


def pair_kernel(
    narrow,
    group,
    member_ref,
    scalars_ref,
    weight,
    own_half,
    own_proj,
    got_half,
    text_all,
    feats_ref,
    inv_out,
    emb_out,
    grad_out,
    own_out,
    near_out,
    far_out,
    unit_all,
    d_all,
    proj_all,
):
    images, width = feats_ref.shape
    rows = images // group
    spread = text_all.shape[0] // rows
    half = images // 2
    share = width // group
    member = member_ref[0]

    place = pl.multiple_of((member % 2) * half, half)
    feats_ref[pl.ds(place, half), :] = own_half[...]
    proj_all[pl.ds(place, half), :] = own_proj[...]
    place = pl.multiple_of((1 - member % 2) * half, half)
    feats_ref[pl.ds(place, half), :] = got_half[...]
    proj_all[pl.ds(place, half), :] = jnp.dot(got_half[...], weight[...], preferred_element_type=F32)
    for start in range(0, images, LANES):
        cols = slice(start, start + LANES)
        turned = proj_all[cols, :].T
        inverse = lax.rsqrt(jnp.sum(turned * turned, axis=0, keepdims=True) + 1e-06)
        unit = turned * inverse
        inv_out[:, cols] = inverse
        unit_all[:, cols] = unit
        emb_out[:, cols] = unit.astype(BF16)

    scale = scalars_ref[0:1, 0:1]
    shift = scalars_ref[1:2, 0:1]
    count = 4 * rows if spread % 4 == 0 else rows
    chunks = spread * rows // count

    def one_chunk(chunk, loss_sum, dot_sum, first):
        here = pl.ds(pl.multiple_of(chunk * count, count), count)
        text = text_all[here, :]
        products = jnp.dot(text, emb_out[...], preferred_element_type=F32)
        logits = scale * products + shift
        caption = lax.broadcasted_iota(jnp.int32, (count, images), 0) + chunk * count
        image = lax.broadcasted_iota(jnp.int32, (count, images), 1)
        own = jnp.logical_and(caption < rows, image == first_image(member, rows, group) + caption)
        sign = jnp.where(own, 1.0, -1.0).astype(F32)
        away = -sign * logits
        small = jnp.exp(-jnp.abs(away))
        loss = jnp.maximum(away, 0.0) + jnp.log1p(small)
        chance = jnp.where(away >= 0.0, 1.0, small) / (1.0 + small)
        grad = (-scale * sign * chance).astype(BF16)
        grad_out[here, :] = grad
        loss_sum = loss_sum + jnp.sum(loss, axis=0, keepdims=True)
        dot_sum = dot_sum + jnp.sum(grad.astype(F32) * products, axis=0, keepdims=True)
        d_img = lax.dot_general(text, grad, TN, preferred_element_type=F32)
        if first:
            d_all[...] = d_img
        else:
            d_all[...] += d_img
        return loss_sum, dot_sum

    zero = jnp.zeros((1, images), F32)
    sums = one_chunk(0, zero, zero, True)
    if chunks > 1:
        sums = lax.fori_loop(1, chunks, lambda c, s: one_chunk(c, *s, False), sums)
    loss_sum, dot_sum = sums

    def projected(index):
        part = pl.ds(pl.multiple_of(column_block(member ^ index, narrow) * share, share), share)
        return d_all[part, :] - unit_all[part, :] * dot_sum

    losses = loss_rows(loss_sum)
    for index in range(group // 2):
        own_out[index, :share, :] = projected(2 * index)
        target = (near_out, far_out)[index * 4 // group].at[index % (group // 4)]
        target[:share, :] = projected(2 * index + 1).astype(BF16)
        target[share:, :] = losses
    own_out[0, share : share + 1, :] = loss_sum


def chip_kernel(first, own_ref, got_ref, *outs):
    share = own_ref.shape[1] - 8
    loss = own_ref[0, share : share + 1, :] + loss_of(got_ref[0, share:, :])
    for index, target in enumerate(outs):
        total = own_ref[first + index, :share, :] + got_ref[index, :share, :].astype(F32)
        target[:share, :] = total.astype(target.dtype)
        if target.dtype == BF16:
            target[share:, :] = loss_rows(loss)
        else:
            target[share : share + 1, :] = loss


def caption_kernel(rows, grad_ref, emb_ref, feats_ref, feats_t, *outs):
    product = lax.dot_general(grad_ref[...], emb_ref[...], NT, preferred_element_type=F32)
    for step, target in enumerate(outs):
        target[...] = product[step * rows : (step + 1) * rows, :].astype(target.dtype)
    for start in range(0, feats_ref.shape[0], LANES):
        cols = slice(start, start + LANES)
        feats_t[:, cols] = feats_ref[cols, :].astype(F32).T.astype(BF16)


def far_sum_kernel(*refs):
    own_ref, got, out = refs[0], refs[1:-1], refs[-1]
    share = own_ref.shape[0] - 8
    total, loss = own_ref[:share, :], own_ref[share : share + 1, :]
    for block in got:
        total = total + block[:share, :].astype(F32)
        loss = loss + loss_of(block[share:, :])
    out[:share, :] = total
    out[share : share + 1, :] = loss


def gathered_gradient(own_ref, got, inv_ref, loss_out):
    share = own_ref.shape[0] - 8
    total = own_ref[:share, :]
    loss = own_ref[share : share + 1, :]
    for block in got:
        total = total + block[:share, :].astype(F32)
        loss = loss + loss_of(block[share:, :])
    loss_out[...] = loss
    return inv_ref[...] * total


def weight_kernel(group, spread, *refs):
    wide_ref, own_ref = refs[:2]
    got = refs[2 : 1 + group // 4]
    inv_ref, feats_ref, feats_t_ref, loss_out, own_out = refs[1 + group // 4 : 6 + group // 4]
    send_out = refs[6 + group // 4 : 5 + group // 4 + spread]
    main_all, rest_all = refs[5 + group // 4 + spread :]
    wide = 2 * spread
    rows = feats_t_ref.shape[0] // wide
    high, low = split_pair(gathered_gradient(own_ref, got, inv_ref, loss_out))
    rest = high.shape[0] - LANES
    both = jnp.concatenate([high[:LANES, :], low[:LANES, :]], axis=0)
    main = lax.dot_general(feats_t_ref[...], both, NT, preferred_element_type=F32)
    main_all[...] = main[:, :LANES] + main[:, LANES:]
    both = jnp.concatenate([high[LANES:, :], low[LANES:, :]], axis=0)
    tail = jnp.dot(both, feats_ref[...], preferred_element_type=F32)
    tail = tail[:rest, :] + tail[rest:, :]
    for place in range(wide):
        begin = place * rows
        rest_all[place, :rest, :] = tail[:, begin : begin + LANES]
        rest_all[place, rest:, :] = jnp.zeros((rest, LANES), F32)
        rest_all[place, rest:, : rows - LANES] = tail[:, begin + LANES : begin + rows]
    for step in range(spread):
        target = send_out[step - 1] if step else own_out
        for side in range(2):
            place = wide_ref[0] ^ (2 * step + side)
            begin = side * (rows + 2 * rest)
            part = main_all[pl.ds(pl.multiple_of(place * rows, rows), rows), :]
            target[begin : begin + rows, :] = part.astype(target.dtype)
            target[begin + rows : begin + rows + 2 * rest, :] = rest_all[place].astype(target.dtype)


def line_kernel(*refs):
    blocks, (own_out, send_out) = refs[:-2], refs[-2:]
    total = blocks[0][...]
    for block in blocks[1:]:
        total = total + block[...].astype(F32)
    packed = own_out.shape[0]
    own_out[...] = total[:packed, :]
    send_out[...] = total[packed:, :].astype(BF16)


def total_kernel(rest, wide_ref, same_ref, other_ref, out):
    rows = out.shape[0]
    same, other = same_ref[...], other_ref[...].astype(F32)
    left_is_same = wide_ref[0] % 2 == 0
    halves = (jnp.where(left_is_same, same, other), jnp.where(left_is_same, other, same))
    for side, half in enumerate(halves):
        left = side * (LANES + rest)
        out[:, left : left + LANES] = half[:rows, :]
        out[:LANES, left + LANES : left + LANES + rest] = half[rows : rows + rest, :].T
        out[LANES:, left + LANES : left + LANES + rest] = half[rows + rest :, :].T[: rows - LANES, :]


def sum_kernel(*refs):
    total = refs[0][...]
    for block in refs[1:-1]:
        total = total + block[...].astype(F32)
    refs[-1][...] = total


def local(wide, narrow, image_feats, proj_weight, text_embed, log_scale, logit_bias):
    rows, width = image_feats.shape
    total = wide * narrow
    group = 2 * narrow
    spread = wide // 2
    share = width // group
    images = group * rows
    member = lax.axis_index(AXES[1:]).astype(jnp.int32).reshape(1)

    texts = [swapped(text_embed, total, step * group) for step in range(1, spread)]
    got_feats = [swapped(image_feats, total, 2 * step) for step in range(1, group // 2)]
    own_text, scalars = pl.pallas_call(
        own_kernel,
        in_specs=[SMEM] * 2 + [VMEM],
        out_specs=[VMEM] * 2,
        out_shape=[jax.ShapeDtypeStruct((rows, width), BF16), jax.ShapeDtypeStruct((8, LANES), F32)],
        compiler_params=limit(4),
        cost_estimate=hint(10**10),
        name="own_text",
    )(log_scale, logit_bias, text_embed)
    own_half = pl.pallas_call(
        stack_kernel,
        in_specs=[SMEM] + [VMEM] * (group // 2),
        out_specs=VMEM,
        out_shape=jax.ShapeDtypeStruct((images // 2, width), BF16),
        compiler_params=limit(4),
        name="stack",
    )(member, image_feats, *got_feats)
    got_half = swapped(own_half, total, 1)
    own_proj = pl.pallas_call(
        project_kernel,
        in_specs=[VMEM] * 2,
        out_specs=VMEM,
        out_shape=jax.ShapeDtypeStruct((images // 2, width), F32),
        compiler_params=limit(8),
        name="own_projection",
    )(own_half, proj_weight)
    own_proj, *texts = lax.optimization_barrier((own_proj, *texts[::-1]))
    text_emb = pl.pallas_call(
        text_kernel,
        in_specs=[VMEM] * spread,
        out_specs=VMEM,
        out_shape=jax.ShapeDtypeStruct((spread * rows, width), BF16),
        compiler_params=limit(4 if spread <= 4 else 16),
        cost_estimate=hint(10**10),
        name="text_unit",
    )(own_text, *texts)

    results = pl.pallas_call(
        functools.partial(pair_kernel, narrow, group),
        in_specs=[SMEM] + [VMEM] * 6,
        out_specs=[VMEM] * 7,
        out_shape=[
            jax.ShapeDtypeStruct((images, width), BF16),
            jax.ShapeDtypeStruct((1, images), F32),
            jax.ShapeDtypeStruct((width, images), BF16),
            jax.ShapeDtypeStruct((spread * rows, images), BF16),
            jax.ShapeDtypeStruct((group // 2, share + 8, images), F32),
        ]
        + [jax.ShapeDtypeStruct((group // 4, share + STAT_ROWS, images), BF16)] * 2,
        scratch_shapes=[
            pltpu.VMEM((width, images), F32),
            pltpu.VMEM((width, images), F32),
            pltpu.VMEM((images, width), F32),
        ],
        compiler_params=limit(24 if spread <= 4 else 40),
        name="pairs",
    )(member, scalars, proj_weight, own_half, own_proj, got_half, text_emb)
    all_feats, inv_part, img_emb, grad_tile, own_part, near_part, far_part = results
    got_far = swapped(far_part, total, 1)
    got_near = swapped(near_part, total, 1)
    feats_t, own_text, *sent_text = pl.pallas_call(
        functools.partial(caption_kernel, rows),
        in_specs=[VMEM] * 3,
        out_specs=[VMEM] * (1 + spread),
        out_shape=[jax.ShapeDtypeStruct((width, images), BF16), jax.ShapeDtypeStruct((rows, width), F32)]
        + [jax.ShapeDtypeStruct((rows, width), BF16)] * (spread - 1),
        compiler_params=limit(12 if spread <= 4 else 32),
        name="captions",
    )(grad_tile, img_emb, all_feats)
    own_part, got_far, sent_text = lax.optimization_barrier((own_part, got_far, sent_text))
    sent_block = jax.ShapeDtypeStruct((share + STAT_ROWS, images), BF16)
    kept_block = jax.ShapeDtypeStruct((share + 8, images), F32)
    half = group // 4
    far = pl.pallas_call(
        functools.partial(chip_kernel, half),
        in_specs=[VMEM] * 2,
        out_specs=[VMEM] * half,
        out_shape=[sent_block] * half,
        compiler_params=limit(8),
        name="chip_far",
    )(own_part, got_far)
    far = [swapped(value, total, 2 * (half + index)) for index, value in enumerate(far)]
    got_text = [swapped(value, total, step * group) for step, value in enumerate(sent_text, 1)]
    own_part, *near = pl.pallas_call(
        functools.partial(chip_kernel, 0),
        in_specs=[VMEM] * 2,
        out_specs=[VMEM] * half,
        out_shape=[kept_block] + [sent_block] * (half - 1),
        compiler_params=limit(8),
        name="chip_near",
    )(own_part, got_near)
    near = [swapped(value, total, 2 * index) for index, value in enumerate(near, 1)]
    own_part = pl.pallas_call(
        far_sum_kernel,
        in_specs=[VMEM] * (1 + half),
        out_specs=VMEM,
        out_shape=kept_block,
        compiler_params=limit(8),
        cost_estimate=hint(5 * 10**8),
        name="far_sum",
    )(own_part, *far)

    out_rows = width // wide
    rest = share - LANES
    packed = out_rows + 2 * rest
    direct = LANES < out_rows <= 2 * LANES and out_rows % 16 == 0 and rest % 16 == 0
    if direct:
        wide_pos = lax.axis_index(AXES[:2]).astype(jnp.int32).reshape(1)
        loss_line, own_weight, *sent_weight = pl.pallas_call(
            functools.partial(weight_kernel, group, spread),
            in_specs=[SMEM] + [VMEM] * (3 + group // 4),
            out_specs=[VMEM] * (1 + spread),
            out_shape=[jax.ShapeDtypeStruct((1, images), F32), jax.ShapeDtypeStruct((2 * packed, LANES), F32)]
            + [jax.ShapeDtypeStruct((2 * packed, LANES), BF16)] * (spread - 1),
            scratch_shapes=[pltpu.VMEM((width, LANES), F32), pltpu.VMEM((wide, 2 * rest, LANES), F32)],
            compiler_params=limit(12),
            name="weights",
        )(wide_pos, own_part, *near, inv_part, all_feats, feats_t)
        got_weight = [swapped(value, total, step * group) for step, value in enumerate(sent_weight, 1)]
        own_weight, sent_weight = pl.pallas_call(
            line_kernel,
            in_specs=[VMEM] * spread,
            out_specs=[VMEM] * 2,
            out_shape=[jax.ShapeDtypeStruct((packed, LANES), kind) for kind in (F32, BF16)],
            compiler_params=limit(4),
            name="weight_line",
        )(own_weight, *got_weight[::-1])
        got_weight = swapped(sent_weight, total, narrow)
        d_proj = pl.pallas_call(
            functools.partial(total_kernel, rest),
            in_specs=[SMEM] + [VMEM] * 2,
            out_specs=VMEM,
            out_shape=jax.ShapeDtypeStruct((out_rows, 2 * share), F32),
            compiler_params=limit(4),
            name="weight_total",
        )(wide_pos, own_weight, got_weight)
    else:

        def gradient_kernel(*refs):
            own_ref, blocks = refs[0], refs[1 : group // 4]
            inv_ref, loss_out, d_out = refs[group // 4 :]
            d_out[...] = gathered_gradient(own_ref, blocks, inv_ref, loss_out)

        loss_line, d_zproj = pl.pallas_call(
            gradient_kernel,
            in_specs=[VMEM] * (1 + group // 4),
            out_specs=[VMEM] * 2,
            out_shape=[jax.ShapeDtypeStruct((1, images), F32), jax.ShapeDtypeStruct((share, images), F32)],
            compiler_params=limit(12),
            name="gradient",
        )(own_part, *near, inv_part)
        partial = sum(
            lax.dot_general(feats_t, part, NT, preferred_element_type=F32) for part in split_pair(d_zproj)
        )
        left = lax.axis_index("inner") == 0
        both = jnp.concatenate([jnp.where(left, partial, 0.0), jnp.where(left, 0.0, partial)], axis=1)
        d_proj = lax.psum_scatter(both, AXES[:2], scatter_dimension=0, tiled=True)

    d_text_unit = pl.pallas_call(
        sum_kernel,
        in_specs=[VMEM] * spread,
        out_specs=VMEM,
        out_shape=jax.ShapeDtypeStruct((rows, width), F32),
        compiler_params=limit(12),
        cost_estimate=hint(5 * 10**9),
        name="caption_total",
    )(own_text, *got_text[::-1])
    image_loss = lax.dynamic_slice_in_dim(loss_line[0], first_image(member[0], rows, group), rows, 0)
    return (image_loss, d_text_unit, d_proj)


def solution(mesh):
    wide, narrow = mesh.shape["wide"], mesh.shape["narrow"]
    cut = jax.sharding.Mesh(mesh.devices.reshape(wide // 2, 2, narrow), AXES)
    placed = (P(AXES, None), P(), P(AXES, None), P(), P())
    return jax.shard_map(
        functools.partial(local, wide, narrow),
        mesh=cut,
        in_specs=placed,
        out_specs=(P(AXES), P(AXES, None), P(AXES[:2], "narrow")),
        check_vma=False,
    )
```

```python
import functools

import jax
import jax.numpy as jnp
from jax import lax
from jax.experimental import pallas as pl
from jax.experimental.pallas import tpu as pltpu
from jax.sharding import PartitionSpec as P

AXES = ("outer", "inner", "narrow")
F32 = jnp.float32
BF16 = jnp.bfloat16
LANES = 128
STAT_ROWS = 16
VMEM = pl.BlockSpec(memory_space=pltpu.VMEM)
SMEM = pl.BlockSpec(memory_space=pltpu.SMEM)
NT = (((1,), (1,)), ((), ()))
TN = (((0,), (0,)), ((), ()))
MIB = 1024 * 1024


def limit(mebibytes):
    return pltpu.CompilerParams(vmem_limit_bytes=mebibytes * MIB)


def hint(flops):
    return pl.CostEstimate(flops=flops, bytes_accessed=0, transcendentals=0)


def swapped(value, total, mask):
    return lax.ppermute(value, AXES, [(source, source ^ mask) for source in range(total)])


def split_pair(values):
    high = values.astype(BF16)
    return high, (values - high.astype(F32)).astype(BF16)


def loss_rows(loss):
    row = lax.broadcasted_iota(jnp.int32, (STAT_ROWS, loss.shape[1]), 0)
    high, low = split_pair(loss)
    rows = jnp.where(row == 0, high.astype(F32), jnp.where(row == 1, low.astype(F32), 0.0))
    return rows.astype(BF16)


def loss_of(rows):
    rows = rows.astype(F32)
    return rows[0:1, :] + rows[1:2, :]


def column_block(member, narrow):
    return (member % narrow) * 2 + member // narrow


def unit_text(text):
    values = text.astype(F32)
    inverse = lax.rsqrt(jnp.sum(values * values, axis=1, keepdims=True) + 1e-06)
    return (values * inverse).astype(BF16)


def own_kernel(log_scale_ref, bias_ref, text_ref, text_out, scalars_out):
    text_out[...] = unit_text(text_ref[...])
    row = lax.broadcasted_iota(jnp.int32, scalars_out.shape, 0)
    scale = jnp.exp(jnp.full(scalars_out.shape, log_scale_ref[0], F32))
    scalars_out[...] = jnp.where(row == 0, scale, bias_ref[0])


def stack_kernel(member_ref, *refs):
    blocks, half_out = refs[:-1], refs[-1]
    rows = blocks[0].shape[0]
    chip = member_ref[0] // 2
    for step, block in enumerate(blocks):
        place = pl.multiple_of((chip ^ step) * rows, rows)
        half_out[pl.ds(place, rows), :] = block[...]


def text_kernel(*refs):
    texts, out = refs[:-1], refs[-1]
    rows = texts[0].shape[0]
    out[:rows, :] = texts[0][...]
    for place, text in enumerate(texts[1:], 1):
        step = len(texts) - place
        out[step * rows : (step + 1) * rows, :] = unit_text(text[...])


def project_kernel(feats_ref, weight_ref, out):
    out[...] = jnp.dot(feats_ref[...], weight_ref[...], preferred_element_type=F32)


def first_image(member, rows, group):
    return (member % 2) * (group // 2 * rows) + (member // 2) * rows


def pair_kernel(
    narrow,
    group,
    member_ref,
    scalars_ref,
    weight,
    own_half,
    own_proj,
    got_half,
    text_all,
    feats_ref,
    inv_out,
    emb_out,
    grad_out,
    own_out,
    near_out,
    far_out,
    unit_all,
    d_all,
    proj_all,
):
    images, width = feats_ref.shape
    rows = images // group
    spread = text_all.shape[0] // rows
    half = images // 2
    share = width // group
    member = member_ref[0]

    place = pl.multiple_of((member % 2) * half, half)
    feats_ref[pl.ds(place, half), :] = own_half[...]
    proj_all[pl.ds(place, half), :] = own_proj[...]
    place = pl.multiple_of((1 - member % 2) * half, half)
    feats_ref[pl.ds(place, half), :] = got_half[...]
    proj_all[pl.ds(place, half), :] = jnp.dot(got_half[...], weight[...], preferred_element_type=F32)
    for start in range(0, images, LANES):
        cols = slice(start, start + LANES)
        turned = proj_all[cols, :].T
        inverse = lax.rsqrt(jnp.sum(turned * turned, axis=0, keepdims=True) + 1e-06)
        unit = turned * inverse
        inv_out[:, cols] = inverse
        unit_all[:, cols] = unit
        emb_out[:, cols] = unit.astype(BF16)

    scale = scalars_ref[0:1, 0:1]
    shift = scalars_ref[1:2, 0:1]
    count = 4 * rows if spread % 4 == 0 else rows
    chunks = spread * rows // count

    def one_chunk(chunk, loss_sum, dot_sum, first):
        here = pl.ds(pl.multiple_of(chunk * count, count), count)
        text = text_all[here, :]
        products = jnp.dot(text, emb_out[...], preferred_element_type=F32)
        logits = scale * products + shift
        caption = lax.broadcasted_iota(jnp.int32, (count, images), 0) + chunk * count
        image = lax.broadcasted_iota(jnp.int32, (count, images), 1)
        own = jnp.logical_and(caption < rows, image == first_image(member, rows, group) + caption)
        sign = jnp.where(own, 1.0, -1.0).astype(F32)
        away = -sign * logits
        small = jnp.exp(-jnp.abs(away))
        loss = jnp.maximum(away, 0.0) + jnp.log1p(small)
        chance = jnp.where(away >= 0.0, 1.0, small) / (1.0 + small)
        grad = (-scale * sign * chance).astype(BF16)
        grad_out[here, :] = grad
        loss_sum = loss_sum + jnp.sum(loss, axis=0, keepdims=True)
        dot_sum = dot_sum + jnp.sum(grad.astype(F32) * products, axis=0, keepdims=True)
        d_img = lax.dot_general(text, grad, TN, preferred_element_type=F32)
        if first:
            d_all[...] = d_img
        else:
            d_all[...] += d_img
        return loss_sum, dot_sum

    zero = jnp.zeros((1, images), F32)
    sums = one_chunk(0, zero, zero, True)
    if chunks > 1:
        sums = lax.fori_loop(1, chunks, lambda c, s: one_chunk(c, *s, False), sums)
    loss_sum, dot_sum = sums

    def projected(index):
        part = pl.ds(pl.multiple_of(column_block(member ^ index, narrow) * share, share), share)
        return d_all[part, :] - unit_all[part, :] * dot_sum

    losses = loss_rows(loss_sum)
    for index in range(group // 2):
        own_out[index, :share, :] = projected(2 * index)
        target = far_out.at[0] if index == group // 2 - 1 else near_out.at[index]
        target[:share, :] = projected(2 * index + 1).astype(BF16)
        target[share:, :] = losses
    own_out[0, share : share + 1, :] = loss_sum


def chip_kernel(first, own_ref, got_ref, *outs):
    share = own_ref.shape[1] - 8
    loss = own_ref[0, share : share + 1, :] + loss_of(got_ref[0, share:, :])
    for index, target in enumerate(outs):
        total = own_ref[first + index, :share, :] + got_ref[index, :share, :].astype(F32)
        target[:share, :] = total.astype(target.dtype)
        if target.dtype == BF16:
            target[share:, :] = loss_rows(loss)
        else:
            target[share : share + 1, :] = loss


def caption_kernel(rows, grad_ref, emb_ref, feats_ref, feats_t, *outs):
    product = lax.dot_general(grad_ref[...], emb_ref[...], NT, preferred_element_type=F32)
    for step, target in enumerate(outs):
        target[...] = product[step * rows : (step + 1) * rows, :].astype(target.dtype)
    for start in range(0, feats_ref.shape[0], LANES):
        cols = slice(start, start + LANES)
        feats_t[:, cols] = feats_ref[cols, :].astype(F32).T.astype(BF16)


def far_sum_kernel(*refs):
    own_ref, got, out = refs[0], refs[1:-1], refs[-1]
    share = own_ref.shape[0] - 8
    total, loss = own_ref[:share, :], own_ref[share : share + 1, :]
    for block in got:
        total = total + block[:share, :].astype(F32)
        loss = loss + loss_of(block[share:, :])
    out[:share, :] = total
    out[share : share + 1, :] = loss


def gathered_gradient(own_ref, got, inv_ref, loss_out):
    share = own_ref.shape[0] - 8
    total = own_ref[:share, :]
    loss = own_ref[share : share + 1, :]
    for block in got:
        total = total + block[:share, :].astype(F32)
        loss = loss + loss_of(block[share:, :])
    loss_out[...] = loss
    return inv_ref[...] * total


def weight_kernel(group, wide, *refs):
    own_ref, got = refs[0], refs[1 : group // 2 - 1]
    inv_ref, feats_ref, feats_t_ref, loss_out, send_out = refs[group // 2 - 1 :]
    rows = feats_t_ref.shape[0] // wide
    high, low = split_pair(gathered_gradient(own_ref, got, inv_ref, loss_out))
    rest = high.shape[0] - LANES
    both = jnp.concatenate([high[LANES:, :], low[LANES:, :]], axis=0)
    tail = jnp.dot(both, feats_ref[...], preferred_element_type=F32)
    tail = (tail[:rest, :] + tail[rest:, :]).astype(BF16)
    both = jnp.concatenate([high[:LANES, :], low[:LANES, :]], axis=0)
    main = lax.dot_general(feats_t_ref[...], both, NT, preferred_element_type=F32)
    main = (main[:, :LANES] + main[:, LANES:]).astype(BF16)
    for place in range(wide):
        begin = place * rows
        send_out[place, :rows, :] = main[begin : begin + rows, :]
        send_out[place, rows : rows + rest, :] = tail[:, begin : begin + LANES]
        send_out[place, rows + rest :, :] = jnp.zeros((rest, LANES), BF16)
        send_out[place, rows + rest :, : rows - LANES] = tail[:, begin + LANES : begin + rows]


def total_kernel(rest, got_ref, out):
    rows = out.shape[0]
    for side in range(2):
        half = got_ref[side].astype(F32)
        for place in range(side + 2, got_ref.shape[0], 2):
            half = half + got_ref[place].astype(F32)
        left = side * (LANES + rest)
        out[:, left : left + LANES] = half[:rows, :]
        out[:LANES, left + LANES : left + LANES + rest] = half[rows : rows + rest, :].T
        out[LANES:, left + LANES : left + LANES + rest] = half[rows + rest :, :].T[: rows - LANES, :]


def sum_kernel(*refs):
    total = refs[0][...]
    for block in refs[1:-1]:
        total = total + block[...].astype(F32)
    refs[-1][...] = total


def local(wide, narrow, image_feats, proj_weight, text_embed, log_scale, logit_bias):
    rows, width = image_feats.shape
    total = wide * narrow
    group = 2 * narrow
    spread = wide // 2
    share = width // group
    images = group * rows
    member = lax.axis_index(AXES[1:]).astype(jnp.int32).reshape(1)

    texts = [swapped(text_embed, total, step * group) for step in range(1, spread)]
    got_feats = [swapped(image_feats, total, 2 * step) for step in range(1, group // 2)]
    own_text, scalars = pl.pallas_call(
        own_kernel,
        in_specs=[SMEM] * 2 + [VMEM],
        out_specs=[VMEM] * 2,
        out_shape=[jax.ShapeDtypeStruct((rows, width), BF16), jax.ShapeDtypeStruct((8, LANES), F32)],
        compiler_params=limit(4),
        cost_estimate=hint(10**10),
        name="own_text",
    )(log_scale, logit_bias, text_embed)
    own_half = pl.pallas_call(
        stack_kernel,
        in_specs=[SMEM] + [VMEM] * (group // 2),
        out_specs=VMEM,
        out_shape=jax.ShapeDtypeStruct((images // 2, width), BF16),
        compiler_params=limit(4),
        name="stack",
    )(member, image_feats, *got_feats)
    got_half = swapped(own_half, total, 1)
    own_proj = pl.pallas_call(
        project_kernel,
        in_specs=[VMEM] * 2,
        out_specs=VMEM,
        out_shape=jax.ShapeDtypeStruct((images // 2, width), F32),
        compiler_params=limit(8),
        name="own_projection",
    )(own_half, proj_weight)
    own_proj, *texts = lax.optimization_barrier((own_proj, *texts[::-1]))
    text_emb = pl.pallas_call(
        text_kernel,
        in_specs=[VMEM] * spread,
        out_specs=VMEM,
        out_shape=jax.ShapeDtypeStruct((spread * rows, width), BF16),
        compiler_params=limit(4 if spread <= 4 else 16),
        cost_estimate=hint(10**10),
        name="text_unit",
    )(own_text, *texts)

    results = pl.pallas_call(
        functools.partial(pair_kernel, narrow, group),
        in_specs=[SMEM] + [VMEM] * 6,
        out_specs=[VMEM] * 7,
        out_shape=[
            jax.ShapeDtypeStruct((images, width), BF16),
            jax.ShapeDtypeStruct((1, images), F32),
            jax.ShapeDtypeStruct((width, images), BF16),
            jax.ShapeDtypeStruct((spread * rows, images), BF16),
            jax.ShapeDtypeStruct((group // 2, share + 8, images), F32),
        ]
        + [jax.ShapeDtypeStruct((count, share + STAT_ROWS, images), BF16) for count in (group // 2 - 1, 1)],
        scratch_shapes=[
            pltpu.VMEM((width, images), F32),
            pltpu.VMEM((width, images), F32),
            pltpu.VMEM((images, width), F32),
        ],
        compiler_params=limit(24 if spread <= 4 else 40),
        name="pairs",
    )(member, scalars, proj_weight, own_half, own_proj, got_half, text_emb)
    all_feats, inv_part, img_emb, grad_tile, own_part, near_part, far_part = results
    got_far = swapped(far_part, total, 1)
    feats_t, own_text, *sent_text = pl.pallas_call(
        functools.partial(caption_kernel, rows),
        in_specs=[VMEM] * 3,
        out_specs=[VMEM] * (1 + spread),
        out_shape=[jax.ShapeDtypeStruct((width, images), BF16), jax.ShapeDtypeStruct((rows, width), F32)]
        + [jax.ShapeDtypeStruct((rows, width), BF16)] * (spread - 1),
        compiler_params=limit(12 if spread <= 4 else 32),
        name="captions",
    )(grad_tile, img_emb, all_feats)
    own_part, got_far, sent_text = lax.optimization_barrier((own_part, got_far, sent_text))
    sent_block = jax.ShapeDtypeStruct((share + STAT_ROWS, images), BF16)
    kept_block = jax.ShapeDtypeStruct((share + 8, images), F32)
    last = group // 2 - 1
    far = pl.pallas_call(
        functools.partial(chip_kernel, last),
        in_specs=[VMEM] * 2,
        out_specs=VMEM,
        out_shape=sent_block,
        compiler_params=limit(8),
        name="chip_far",
    )(own_part, got_far)
    far, near_part = lax.optimization_barrier((far, near_part))
    far = swapped(far, total, 2 * last)
    got_near = swapped(near_part, total, 1)
    got_text = [swapped(value, total, step * group) for step, value in enumerate(sent_text, 1)]
    own_part, *near = pl.pallas_call(
        functools.partial(chip_kernel, 0),
        in_specs=[VMEM] * 2,
        out_specs=[VMEM] * last,
        out_shape=[kept_block] + [sent_block] * (last - 1),
        compiler_params=limit(8),
        name="chip_near",
    )(own_part, got_near)
    near = [swapped(value, total, 2 * index) for index, value in enumerate(near, 1)]
    own_part = pl.pallas_call(
        far_sum_kernel,
        in_specs=[VMEM] * 2,
        out_specs=VMEM,
        out_shape=kept_block,
        compiler_params=limit(8),
        cost_estimate=hint(5 * 10**8),
        name="far_sum",
    )(own_part, far)

    out_rows = width // wide
    rest = share - LANES
    packed = out_rows + 2 * rest
    direct = LANES < out_rows <= 2 * LANES and out_rows % 16 == 0 and rest % 16 == 0
    if direct:
        loss_line, sent_weight = pl.pallas_call(
            functools.partial(weight_kernel, group, wide),
            in_specs=[VMEM] * (2 + group // 2),
            out_specs=[VMEM] * 2,
            out_shape=[
                jax.ShapeDtypeStruct((1, images), F32),
                jax.ShapeDtypeStruct((wide, packed, LANES), BF16),
            ],
            compiler_params=limit(12),
            name="weights",
        )(own_part, *near, inv_part, all_feats, feats_t)
        got_weight = lax.all_to_all(sent_weight, AXES[:2], 0, 0)
        d_proj = pl.pallas_call(
            functools.partial(total_kernel, rest),
            in_specs=[VMEM],
            out_specs=VMEM,
            out_shape=jax.ShapeDtypeStruct((out_rows, 2 * share), F32),
            compiler_params=limit(4),
            name="weight_total",
        )(got_weight)
    else:

        def gradient_kernel(*refs):
            own_ref, blocks = refs[0], refs[1 : group // 2 - 1]
            inv_ref, loss_out, d_out = refs[group // 2 - 1 :]
            d_out[...] = gathered_gradient(own_ref, blocks, inv_ref, loss_out)

        loss_line, d_zproj = pl.pallas_call(
            gradient_kernel,
            in_specs=[VMEM] * (group // 2),
            out_specs=[VMEM] * 2,
            out_shape=[jax.ShapeDtypeStruct((1, images), F32), jax.ShapeDtypeStruct((share, images), F32)],
            compiler_params=limit(12),
            name="gradient",
        )(own_part, *near, inv_part)
        partial = sum(
            lax.dot_general(feats_t, part, NT, preferred_element_type=F32) for part in split_pair(d_zproj)
        )
        left = lax.axis_index("inner") == 0
        both = jnp.concatenate([jnp.where(left, partial, 0.0), jnp.where(left, 0.0, partial)], axis=1)
        d_proj = lax.psum_scatter(both, AXES[:2], scatter_dimension=0, tiled=True)

    d_text_unit = pl.pallas_call(
        sum_kernel,
        in_specs=[VMEM] * spread,
        out_specs=VMEM,
        out_shape=jax.ShapeDtypeStruct((rows, width), F32),
        compiler_params=limit(12),
        cost_estimate=hint(5 * 10**9),
        name="caption_total",
    )(own_text, *got_text[::-1])
    image_loss = lax.dynamic_slice_in_dim(loss_line[0], first_image(member[0], rows, group), rows, 0)
    return (image_loss, d_text_unit, d_proj)


def solution(mesh):
    wide, narrow = mesh.shape["wide"], mesh.shape["narrow"]
    cut = jax.sharding.Mesh(mesh.devices.reshape(wide // 2, 2, narrow), AXES)
    placed = (P(AXES, None), P(), P(AXES, None), P(), P())
    return jax.shard_map(
        functools.partial(local, wide, narrow),
        mesh=cut,
        in_specs=placed,
        out_specs=(P(AXES), P(AXES, None), P(AXES[:2], "narrow")),
        check_vma=False,
    )
```

```python
import functools

import jax
import jax.numpy as jnp
from jax import lax
from jax.experimental import pallas as pl
from jax.experimental.pallas import tpu as pltpu
from jax.sharding import PartitionSpec as P

AXES = ("outer", "inner", "narrow")
F32 = jnp.float32
BF16 = jnp.bfloat16
LANES = 128
STAT_ROWS = 16
VMEM = pl.BlockSpec(memory_space=pltpu.VMEM)
SMEM = pl.BlockSpec(memory_space=pltpu.SMEM)
NT = (((1,), (1,)), ((), ()))
TN = (((0,), (0,)), ((), ()))
MIB = 1024 * 1024


def limit(mebibytes):
    return pltpu.CompilerParams(vmem_limit_bytes=mebibytes * MIB)


def hint(flops):
    return pl.CostEstimate(flops=flops, bytes_accessed=0, transcendentals=0)


def swapped(value, total, mask):
    return lax.ppermute(value, AXES, [(source, source ^ mask) for source in range(total)])


def split_pair(values):
    high = values.astype(BF16)
    return high, (values - high.astype(F32)).astype(BF16)


def loss_rows(loss):
    row = lax.broadcasted_iota(jnp.int32, (STAT_ROWS, loss.shape[1]), 0)
    high, low = split_pair(loss)
    rows = jnp.where(row == 0, high.astype(F32), jnp.where(row == 1, low.astype(F32), 0.0))
    return rows.astype(BF16)


def loss_of(rows):
    rows = rows.astype(F32)
    return rows[0:1, :] + rows[1:2, :]


def column_block(member, narrow):
    return (member % narrow) * 2 + member // narrow


def unit_text(text):
    values = text.astype(F32)
    inverse = lax.rsqrt(jnp.sum(values * values, axis=1, keepdims=True) + 1e-06)
    return (values * inverse).astype(BF16)


def own_kernel(log_scale_ref, bias_ref, text_ref, text_out, scalars_out):
    text_out[...] = unit_text(text_ref[...])
    row = lax.broadcasted_iota(jnp.int32, scalars_out.shape, 0)
    scale = jnp.exp(jnp.full(scalars_out.shape, log_scale_ref[0], F32))
    scalars_out[...] = jnp.where(row == 0, scale, bias_ref[0])


def stack_kernel(member_ref, *refs):
    blocks, half_out = refs[:-1], refs[-1]
    rows = blocks[0].shape[0]
    chip = member_ref[0] // 2
    for step, block in enumerate(blocks):
        place = pl.multiple_of((chip ^ step) * rows, rows)
        half_out[pl.ds(place, rows), :] = block[...]


def text_kernel(*refs):
    texts, out = refs[:-1], refs[-1]
    rows = texts[0].shape[0]
    out[:rows, :] = texts[0][...]
    for place, text in enumerate(texts[1:], 1):
        step = len(texts) - place
        out[step * rows : (step + 1) * rows, :] = unit_text(text[...])


def project_kernel(feats_ref, weight_ref, out):
    out[...] = jnp.dot(feats_ref[...], weight_ref[...], preferred_element_type=F32)


def first_image(member, rows, group):
    return (member % 2) * (group // 2 * rows) + (member // 2) * rows


def pair_kernel(
    narrow,
    group,
    member_ref,
    scalars_ref,
    weight,
    own_half,
    own_proj,
    got_half,
    text_all,
    feats_ref,
    inv_out,
    emb_out,
    grad_out,
    own_out,
    near_out,
    far_out,
    unit_all,
    d_all,
    proj_all,
):
    images, width = feats_ref.shape
    rows = images // group
    spread = text_all.shape[0] // rows
    half = images // 2
    share = width // group
    member = member_ref[0]

    place = pl.multiple_of((member % 2) * half, half)
    feats_ref[pl.ds(place, half), :] = own_half[...]
    proj_all[pl.ds(place, half), :] = own_proj[...]
    place = pl.multiple_of((1 - member % 2) * half, half)
    feats_ref[pl.ds(place, half), :] = got_half[...]
    proj_all[pl.ds(place, half), :] = jnp.dot(got_half[...], weight[...], preferred_element_type=F32)
    for start in range(0, images, LANES):
        cols = slice(start, start + LANES)
        turned = proj_all[cols, :].T
        inverse = lax.rsqrt(jnp.sum(turned * turned, axis=0, keepdims=True) + 1e-06)
        unit = turned * inverse
        inv_out[:, cols] = inverse
        unit_all[:, cols] = unit
        emb_out[:, cols] = unit.astype(BF16)

    scale = scalars_ref[0:1, 0:1]
    shift = scalars_ref[1:2, 0:1]
    count = 4 * rows if spread % 4 == 0 else rows
    chunks = spread * rows // count

    def one_chunk(chunk, loss_sum, dot_sum, first):
        here = pl.ds(pl.multiple_of(chunk * count, count), count)
        text = text_all[here, :]
        products = jnp.dot(text, emb_out[...], preferred_element_type=F32)
        logits = scale * products + shift
        caption = lax.broadcasted_iota(jnp.int32, (count, images), 0) + chunk * count
        image = lax.broadcasted_iota(jnp.int32, (count, images), 1)
        own = jnp.logical_and(caption < rows, image == first_image(member, rows, group) + caption)
        sign = jnp.where(own, 1.0, -1.0).astype(F32)
        away = -sign * logits
        small = jnp.exp(-jnp.abs(away))
        loss = jnp.maximum(away, 0.0) + jnp.log1p(small)
        chance = jnp.where(away >= 0.0, 1.0, small) / (1.0 + small)
        grad = (-scale * sign * chance).astype(BF16)
        grad_out[here, :] = grad
        loss_sum = loss_sum + jnp.sum(loss, axis=0, keepdims=True)
        dot_sum = dot_sum + jnp.sum(grad.astype(F32) * products, axis=0, keepdims=True)
        d_img = lax.dot_general(text, grad, TN, preferred_element_type=F32)
        if first:
            d_all[...] = d_img
        else:
            d_all[...] += d_img
        return loss_sum, dot_sum

    zero = jnp.zeros((1, images), F32)
    sums = one_chunk(0, zero, zero, True)
    if chunks > 1:
        sums = lax.fori_loop(1, chunks, lambda c, s: one_chunk(c, *s, False), sums)
    loss_sum, dot_sum = sums

    def projected(index):
        part = pl.ds(pl.multiple_of(column_block(member ^ index, narrow) * share, share), share)
        return d_all[part, :] - unit_all[part, :] * dot_sum

    losses = loss_rows(loss_sum)
    for index in range(group // 2):
        own_out[index, :share, :] = projected(2 * index)
        target = (near_out, far_out)[index * 4 // group].at[index % (group // 4)]
        target[:share, :] = projected(2 * index + 1).astype(BF16)
        target[share:, :] = losses
    own_out[0, share : share + 1, :] = loss_sum


def chip_kernel(first, own_ref, got_ref, *outs):
    share = own_ref.shape[1] - 8
    loss = own_ref[0, share : share + 1, :] + loss_of(got_ref[0, share:, :])
    for index, target in enumerate(outs):
        total = own_ref[first + index, :share, :] + got_ref[index, :share, :].astype(F32)
        target[:share, :] = total.astype(target.dtype)
        if target.dtype == BF16:
            target[share:, :] = loss_rows(loss)
        else:
            target[share : share + 1, :] = loss


def caption_kernel(rows, grad_ref, emb_ref, feats_ref, feats_t, *outs):
    product = lax.dot_general(grad_ref[...], emb_ref[...], NT, preferred_element_type=F32)
    for step, target in enumerate(outs):
        target[...] = product[step * rows : (step + 1) * rows, :].astype(target.dtype)
    for start in range(0, feats_ref.shape[0], LANES):
        cols = slice(start, start + LANES)
        feats_t[:, cols] = feats_ref[cols, :].astype(F32).T.astype(BF16)


def far_sum_kernel(*refs):
    own_ref, got, out = refs[0], refs[1:-1], refs[-1]
    share = own_ref.shape[0] - 8
    total, loss = own_ref[:share, :], own_ref[share : share + 1, :]
    for block in got:
        total = total + block[:share, :].astype(F32)
        loss = loss + loss_of(block[share:, :])
    out[:share, :] = total
    out[share : share + 1, :] = loss


def gathered_gradient(own_ref, got, inv_ref, loss_out):
    share = own_ref.shape[0] - 8
    total = own_ref[:share, :]
    loss = own_ref[share : share + 1, :]
    for block in got:
        total = total + block[:share, :].astype(F32)
        loss = loss + loss_of(block[share:, :])
    loss_out[...] = loss
    return inv_ref[...] * total


def weight_kernel(group, wide, *refs):
    own_ref, got = refs[0], refs[1 : group // 4]
    inv_ref, feats_ref, feats_t_ref, loss_out, send_out, blocks, sems = refs[group // 4 :]
    rows = feats_t_ref.shape[0] // wide
    high, low = split_pair(gathered_gradient(own_ref, got, inv_ref, loss_out))
    rest = high.shape[0] - LANES
    both = jnp.concatenate([high[LANES:, :], low[LANES:, :]], axis=0)
    tail = jnp.dot(both, feats_ref[...], preferred_element_type=F32)
    tail = (tail[:rest, :] + tail[rest:, :]).astype(BF16)
    both = jnp.concatenate([high[:LANES, :], low[:LANES, :]], axis=0)
    half = wide // 2
    copies = []
    for part in range(2):
        lines = slice(part * half * rows, (part + 1) * half * rows)
        main = lax.dot_general(feats_t_ref[lines, :], both, NT, preferred_element_type=F32)
        main = (main[:, :LANES] + main[:, LANES:]).astype(BF16)
        for index in range(half):
            place, begin = part * half + index, (part * half + index) * rows
            blocks[place, :rows, :] = main[index * rows : (index + 1) * rows, :]
            blocks[place, rows : rows + rest, :] = tail[:, begin : begin + LANES]
            blocks[place, rows + rest :, :] = jnp.zeros((rest, LANES), BF16)
            blocks[place, rows + rest :, : rows - LANES] = tail[:, begin + LANES : begin + rows]
        places = pl.ds(part * half, half)
        copies.append(pltpu.make_async_copy(blocks.at[places], send_out.at[places], sems.at[part]))
        copies[-1].start()
    for copy in copies:
        copy.wait()


def total_kernel(rest, got_ref, out):
    rows = out.shape[0]
    for side in range(2):
        half = got_ref[side].astype(F32)
        for place in range(side + 2, got_ref.shape[0], 2):
            half = half + got_ref[place].astype(F32)
        left = side * (LANES + rest)
        out[:, left : left + LANES] = half[:rows, :]
        out[:LANES, left + LANES : left + LANES + rest] = half[rows : rows + rest, :].T
        out[LANES:, left + LANES : left + LANES + rest] = half[rows + rest :, :].T[: rows - LANES, :]


def sum_kernel(*refs):
    total = refs[0][...]
    for block in refs[1:-1]:
        total = total + block[...].astype(F32)
    refs[-1][...] = total


def local(wide, narrow, image_feats, proj_weight, text_embed, log_scale, logit_bias):
    rows, width = image_feats.shape
    total = wide * narrow
    group = 2 * narrow
    spread = wide // 2
    share = width // group
    images = group * rows
    member = lax.axis_index(AXES[1:]).astype(jnp.int32).reshape(1)

    texts = [swapped(text_embed, total, step * group) for step in range(1, spread)]
    got_feats = [swapped(image_feats, total, 2 * step) for step in range(1, group // 2)]
    own_text, scalars = pl.pallas_call(
        own_kernel,
        in_specs=[SMEM] * 2 + [VMEM],
        out_specs=[VMEM] * 2,
        out_shape=[jax.ShapeDtypeStruct((rows, width), BF16), jax.ShapeDtypeStruct((8, LANES), F32)],
        compiler_params=limit(4),
        cost_estimate=hint(10**10),
        name="own_text",
    )(log_scale, logit_bias, text_embed)
    own_half = pl.pallas_call(
        stack_kernel,
        in_specs=[SMEM] + [VMEM] * (group // 2),
        out_specs=VMEM,
        out_shape=jax.ShapeDtypeStruct((images // 2, width), BF16),
        compiler_params=limit(4),
        name="stack",
    )(member, image_feats, *got_feats)
    got_half = swapped(own_half, total, 1)
    own_proj = pl.pallas_call(
        project_kernel,
        in_specs=[VMEM] * 2,
        out_specs=VMEM,
        out_shape=jax.ShapeDtypeStruct((images // 2, width), F32),
        compiler_params=limit(8),
        name="own_projection",
    )(own_half, proj_weight)
    own_proj, *texts = lax.optimization_barrier((own_proj, *texts[::-1]))
    text_emb = pl.pallas_call(
        text_kernel,
        in_specs=[VMEM] * spread,
        out_specs=VMEM,
        out_shape=jax.ShapeDtypeStruct((spread * rows, width), BF16),
        compiler_params=limit(4 if spread <= 4 else 16),
        cost_estimate=hint(10**10),
        name="text_unit",
    )(own_text, *texts)

    results = pl.pallas_call(
        functools.partial(pair_kernel, narrow, group),
        in_specs=[SMEM] + [VMEM] * 6,
        out_specs=[VMEM] * 7,
        out_shape=[
            jax.ShapeDtypeStruct((images, width), BF16),
            jax.ShapeDtypeStruct((1, images), F32),
            jax.ShapeDtypeStruct((width, images), BF16),
            jax.ShapeDtypeStruct((spread * rows, images), BF16),
            jax.ShapeDtypeStruct((group // 2, share + 8, images), F32),
        ]
        + [jax.ShapeDtypeStruct((group // 4, share + STAT_ROWS, images), BF16)] * 2,
        scratch_shapes=[
            pltpu.VMEM((width, images), F32),
            pltpu.VMEM((width, images), F32),
            pltpu.VMEM((images, width), F32),
        ],
        compiler_params=limit(24 if spread <= 4 else 40),
        name="pairs",
    )(member, scalars, proj_weight, own_half, own_proj, got_half, text_emb)
    all_feats, inv_part, img_emb, grad_tile, own_part, near_part, far_part = results
    got_far = swapped(far_part, total, 1)
    got_near = swapped(near_part, total, 1)
    feats_t, own_text, *sent_text = pl.pallas_call(
        functools.partial(caption_kernel, rows),
        in_specs=[VMEM] * 3,
        out_specs=[VMEM] * (1 + spread),
        out_shape=[jax.ShapeDtypeStruct((width, images), BF16), jax.ShapeDtypeStruct((rows, width), F32)]
        + [jax.ShapeDtypeStruct((rows, width), BF16)] * (spread - 1),
        compiler_params=limit(12 if spread <= 4 else 32),
        name="captions",
    )(grad_tile, img_emb, all_feats)
    own_part, got_far, sent_text = lax.optimization_barrier((own_part, got_far, sent_text))
    sent_block = jax.ShapeDtypeStruct((share + STAT_ROWS, images), BF16)
    kept_block = jax.ShapeDtypeStruct((share + 8, images), F32)
    half = group // 4
    far = pl.pallas_call(
        functools.partial(chip_kernel, half),
        in_specs=[VMEM] * 2,
        out_specs=[VMEM] * half,
        out_shape=[sent_block] * half,
        compiler_params=limit(8),
        name="chip_far",
    )(own_part, got_far)
    far = [swapped(value, total, 2 * (half + index)) for index, value in enumerate(far)]
    got_text = [swapped(value, total, step * group) for step, value in enumerate(sent_text, 1)]
    own_part, *near = pl.pallas_call(
        functools.partial(chip_kernel, 0),
        in_specs=[VMEM] * 2,
        out_specs=[VMEM] * half,
        out_shape=[kept_block] + [sent_block] * (half - 1),
        compiler_params=limit(8),
        name="chip_near",
    )(own_part, got_near)
    near = [swapped(value, total, 2 * index) for index, value in enumerate(near, 1)]
    own_part = pl.pallas_call(
        far_sum_kernel,
        in_specs=[VMEM] * (1 + half),
        out_specs=VMEM,
        out_shape=kept_block,
        compiler_params=limit(8),
        cost_estimate=hint(5 * 10**8),
        name="far_sum",
    )(own_part, *far)

    out_rows = width // wide
    rest = share - LANES
    packed = out_rows + 2 * rest
    direct = LANES < out_rows <= 2 * LANES and out_rows % 16 == 0 and rest % 16 == 0
    if direct:
        loss_line, sent_weight = pl.pallas_call(
            functools.partial(weight_kernel, group, wide),
            in_specs=[VMEM] * (3 + group // 4),
            out_specs=[VMEM, pl.BlockSpec(memory_space=pl.ANY)],
            out_shape=[
                jax.ShapeDtypeStruct((1, images), F32),
                jax.ShapeDtypeStruct((wide, packed, LANES), BF16),
            ],
            scratch_shapes=[pltpu.VMEM((wide, packed, LANES), BF16), pltpu.SemaphoreType.DMA((2,))],
            compiler_params=limit(12),
            name="weights",
        )(own_part, *near, inv_part, all_feats, feats_t)
        got_weight = lax.all_to_all(sent_weight, AXES[:2], 0, 0)
        d_proj = pl.pallas_call(
            functools.partial(total_kernel, rest),
            in_specs=[VMEM],
            out_specs=VMEM,
            out_shape=jax.ShapeDtypeStruct((out_rows, 2 * share), F32),
            compiler_params=limit(4),
            name="weight_total",
        )(got_weight)
    else:

        def gradient_kernel(*refs):
            own_ref, blocks = refs[0], refs[1 : group // 4]
            inv_ref, loss_out, d_out = refs[group // 4 :]
            d_out[...] = gathered_gradient(own_ref, blocks, inv_ref, loss_out)

        loss_line, d_zproj = pl.pallas_call(
            gradient_kernel,
            in_specs=[VMEM] * (1 + group // 4),
            out_specs=[VMEM] * 2,
            out_shape=[jax.ShapeDtypeStruct((1, images), F32), jax.ShapeDtypeStruct((share, images), F32)],
            compiler_params=limit(12),
            name="gradient",
        )(own_part, *near, inv_part)
        partial = sum(
            lax.dot_general(feats_t, part, NT, preferred_element_type=F32) for part in split_pair(d_zproj)
        )
        left = lax.axis_index("inner") == 0
        both = jnp.concatenate([jnp.where(left, partial, 0.0), jnp.where(left, 0.0, partial)], axis=1)
        d_proj = lax.psum_scatter(both, AXES[:2], scatter_dimension=0, tiled=True)

    d_text_unit = pl.pallas_call(
        sum_kernel,
        in_specs=[VMEM] * spread,
        out_specs=VMEM,
        out_shape=jax.ShapeDtypeStruct((rows, width), F32),
        compiler_params=limit(12),
        cost_estimate=hint(5 * 10**9),
        name="caption_total",
    )(own_text, *got_text[::-1])
    image_loss = lax.dynamic_slice_in_dim(loss_line[0], first_image(member[0], rows, group), rows, 0)
    return (image_loss, d_text_unit, d_proj)


def solution(mesh):
    wide, narrow = mesh.shape["wide"], mesh.shape["narrow"]
    cut = jax.sharding.Mesh(mesh.devices.reshape(wide // 2, 2, narrow), AXES)
    placed = (P(AXES, None), P(), P(AXES, None), P(), P())
    return jax.shard_map(
        functools.partial(local, wide, narrow),
        mesh=cut,
        in_specs=placed,
        out_specs=(P(AXES), P(AXES, None), P(AXES[:2], "narrow")),
        check_vma=False,
    )
```

```python
import functools

import jax
import jax.numpy as jnp
from jax import lax
from jax.experimental import pallas as pl
from jax.experimental.pallas import tpu as pltpu
from jax.sharding import PartitionSpec as P

AXES = ("outer", "inner", "narrow")
F32 = jnp.float32
BF16 = jnp.bfloat16
LANES = 128
STAT_ROWS = 16
VMEM = pl.BlockSpec(memory_space=pltpu.VMEM)
SMEM = pl.BlockSpec(memory_space=pltpu.SMEM)
NT = (((1,), (1,)), ((), ()))
TN = (((0,), (0,)), ((), ()))
MIB = 1024 * 1024


def limit(mebibytes):
    return pltpu.CompilerParams(vmem_limit_bytes=mebibytes * MIB)


def hint(flops):
    return pl.CostEstimate(flops=flops, bytes_accessed=0, transcendentals=0)


def swapped(value, total, mask):
    return lax.ppermute(value, AXES, [(source, source ^ mask) for source in range(total)])


def split_pair(values):
    high = values.astype(BF16)
    return high, (values - high.astype(F32)).astype(BF16)


def loss_rows(loss):
    row = lax.broadcasted_iota(jnp.int32, (STAT_ROWS, loss.shape[1]), 0)
    high, low = split_pair(loss)
    rows = jnp.where(row == 0, high.astype(F32), jnp.where(row == 1, low.astype(F32), 0.0))
    return rows.astype(BF16)


def loss_of(rows):
    rows = rows.astype(F32)
    return rows[0:1, :] + rows[1:2, :]


def column_block(member, narrow):
    return (member % narrow) * 2 + member // narrow


def unit_text(text):
    values = text.astype(F32)
    inverse = lax.rsqrt(jnp.sum(values * values, axis=1, keepdims=True) + 1e-06)
    return (values * inverse).astype(BF16)


def own_kernel(log_scale_ref, bias_ref, text_ref, text_out, scalars_out):
    text_out[...] = unit_text(text_ref[...])
    row = lax.broadcasted_iota(jnp.int32, scalars_out.shape, 0)
    scale = jnp.exp(jnp.full(scalars_out.shape, log_scale_ref[0], F32))
    scalars_out[...] = jnp.where(row == 0, scale, bias_ref[0])


def stack_kernel(member_ref, *refs):
    blocks, half_out = refs[:-1], refs[-1]
    rows = blocks[0].shape[0]
    chip = member_ref[0] // 2
    for step, block in enumerate(blocks):
        place = pl.multiple_of((chip ^ step) * rows, rows)
        half_out[pl.ds(place, rows), :] = block[...]


def text_kernel(*refs):
    texts, out = refs[:-1], refs[-1]
    rows = texts[0].shape[0]
    out[:rows, :] = texts[0][...]
    for place, text in enumerate(texts[1:], 1):
        step = len(texts) - place
        out[step * rows : (step + 1) * rows, :] = unit_text(text[...])


def project_kernel(feats_ref, weight_ref, out):
    out[...] = jnp.dot(feats_ref[...], weight_ref[...], preferred_element_type=F32)


def first_image(member, rows, group):
    return (member % 2) * (group // 2 * rows) + (member // 2) * rows


def pair_kernel(
    narrow,
    group,
    member_ref,
    scalars_ref,
    weight,
    own_half,
    own_proj,
    got_half,
    text_all,
    feats_ref,
    inv_out,
    emb_out,
    grad_out,
    own_out,
    near_out,
    far_out,
    unit_all,
    d_all,
    proj_all,
):
    images, width = feats_ref.shape
    rows = images // group
    spread = text_all.shape[0] // rows
    half = images // 2
    share = width // group
    member = member_ref[0]

    place = pl.multiple_of((member % 2) * half, half)
    feats_ref[pl.ds(place, half), :] = own_half[...]
    proj_all[pl.ds(place, half), :] = own_proj[...]
    place = pl.multiple_of((1 - member % 2) * half, half)
    feats_ref[pl.ds(place, half), :] = got_half[...]
    proj_all[pl.ds(place, half), :] = jnp.dot(got_half[...], weight[...], preferred_element_type=F32)
    for start in range(0, images, LANES):
        cols = slice(start, start + LANES)
        turned = proj_all[cols, :].T
        inverse = lax.rsqrt(jnp.sum(turned * turned, axis=0, keepdims=True) + 1e-06)
        unit = turned * inverse
        inv_out[:, cols] = inverse
        unit_all[:, cols] = unit
        emb_out[:, cols] = unit.astype(BF16)

    scale = scalars_ref[0:1, 0:1]
    shift = scalars_ref[1:2, 0:1]
    count = 4 * rows if spread % 4 == 0 else rows
    chunks = spread * rows // count

    def one_chunk(chunk, loss_sum, dot_sum, first):
        here = pl.ds(pl.multiple_of(chunk * count, count), count)
        text = text_all[here, :]
        products = jnp.dot(text, emb_out[...], preferred_element_type=F32)
        logits = scale * products + shift
        caption = lax.broadcasted_iota(jnp.int32, (count, images), 0) + chunk * count
        image = lax.broadcasted_iota(jnp.int32, (count, images), 1)
        own = jnp.logical_and(caption < rows, image == first_image(member, rows, group) + caption)
        sign = jnp.where(own, 1.0, -1.0).astype(F32)
        away = -sign * logits
        small = jnp.exp(-jnp.abs(away))
        loss = jnp.maximum(away, 0.0) + jnp.log1p(small)
        chance = jnp.where(away >= 0.0, 1.0, small) / (1.0 + small)
        grad = (-scale * sign * chance).astype(BF16)
        grad_out[here, :] = grad
        loss_sum = loss_sum + jnp.sum(loss, axis=0, keepdims=True)
        dot_sum = dot_sum + jnp.sum(grad.astype(F32) * products, axis=0, keepdims=True)
        d_img = lax.dot_general(text, grad, TN, preferred_element_type=F32)
        if first:
            d_all[...] = d_img
        else:
            d_all[...] += d_img
        return loss_sum, dot_sum

    zero = jnp.zeros((1, images), F32)
    sums = one_chunk(0, zero, zero, True)
    if chunks > 1:
        sums = lax.fori_loop(1, chunks, lambda c, s: one_chunk(c, *s, False), sums)
    loss_sum, dot_sum = sums

    def projected(index):
        part = pl.ds(pl.multiple_of(column_block(member ^ index, narrow) * share, share), share)
        return d_all[part, :] - unit_all[part, :] * dot_sum

    losses = loss_rows(loss_sum)
    for index in range(group // 2):
        own_out[index, :share, :] = projected(2 * index)
        target = (near_out, far_out)[index * 4 // group].at[index % (group // 4)]
        target[:share, :] = projected(2 * index + 1).astype(BF16)
        target[share:, :] = losses
    own_out[0, share : share + 1, :] = loss_sum


def chip_kernel(first, own_ref, got_ref, *outs):
    share = own_ref.shape[1] - 8
    loss = own_ref[0, share : share + 1, :] + loss_of(got_ref[0, share:, :])
    for index, target in enumerate(outs):
        total = own_ref[first + index, :share, :] + got_ref[index, :share, :].astype(F32)
        target[:share, :] = total.astype(target.dtype)
        if target.dtype == BF16:
            target[share:, :] = loss_rows(loss)
        else:
            target[share : share + 1, :] = loss


def caption_kernel(rows, grad_ref, emb_ref, feats_ref, feats_t, *outs):
    product = lax.dot_general(grad_ref[...], emb_ref[...], NT, preferred_element_type=F32)
    for step, target in enumerate(outs):
        target[...] = product[step * rows : (step + 1) * rows, :].astype(target.dtype)
    for start in range(0, feats_ref.shape[0], LANES):
        cols = slice(start, start + LANES)
        feats_t[:, cols] = feats_ref[cols, :].astype(F32).T.astype(BF16)


def far_sum_kernel(*refs):
    own_ref, got, out = refs[0], refs[1:-1], refs[-1]
    share = own_ref.shape[0] - 8
    total, loss = own_ref[:share, :], own_ref[share : share + 1, :]
    for block in got:
        total = total + block[:share, :].astype(F32)
        loss = loss + loss_of(block[share:, :])
    out[:share, :] = total
    out[share : share + 1, :] = loss


def gathered_gradient(own_ref, got, inv_ref, loss_out):
    share = own_ref.shape[0] - 8
    total = own_ref[:share, :]
    loss = own_ref[share : share + 1, :]
    for block in got:
        total = total + block[:share, :].astype(F32)
        loss = loss + loss_of(block[share:, :])
    loss_out[...] = loss
    return inv_ref[...] * total


def weight_kernel(group, wide, *refs):
    own_ref, got = refs[0], refs[1 : group // 4]
    inv_ref, feats_ref, feats_t_ref, loss_out, send_out = refs[group // 4 :]
    rows = feats_t_ref.shape[0] // wide
    high, low = split_pair(gathered_gradient(own_ref, got, inv_ref, loss_out))
    rest = high.shape[0] - LANES
    both = jnp.concatenate([high[LANES:, :], low[LANES:, :]], axis=0)
    tail = jnp.dot(both, feats_ref[...], preferred_element_type=F32)
    tail = (tail[:rest, :] + tail[rest:, :]).astype(BF16)
    both = jnp.concatenate([high[:LANES, :], low[:LANES, :]], axis=0)
    main = lax.dot_general(feats_t_ref[...], both, NT, preferred_element_type=F32)
    main = (main[:, :LANES] + main[:, LANES:]).astype(BF16)
    for place in range(wide):
        begin = place * rows
        send_out[place, :rows, :] = main[begin : begin + rows, :]
        send_out[place, rows : rows + rest, :] = tail[:, begin : begin + LANES]
        send_out[place, rows + rest :, :] = jnp.zeros((rest, LANES), BF16)
        send_out[place, rows + rest :, : rows - LANES] = tail[:, begin + LANES : begin + rows]


def total_kernel(rest, got_ref, out):
    rows = out.shape[0]
    for side in range(2):
        half = got_ref[side].astype(F32)
        for place in range(side + 2, got_ref.shape[0], 2):
            half = half + got_ref[place].astype(F32)
        left = side * (LANES + rest)
        out[:, left : left + LANES] = half[:rows, :]
        out[:LANES, left + LANES : left + LANES + rest] = half[rows : rows + rest, :].T
        out[LANES:, left + LANES : left + LANES + rest] = half[rows + rest :, :].T[: rows - LANES, :]


def sum_kernel(*refs):
    total = refs[0][...]
    for block in refs[1:-1]:
        total = total + block[...].astype(F32)
    refs[-1][...] = total


def local(wide, narrow, image_feats, proj_weight, text_embed, log_scale, logit_bias):
    rows, width = image_feats.shape
    total = wide * narrow
    group = 2 * narrow
    spread = wide // 2
    share = width // group
    images = group * rows
    member = lax.axis_index(AXES[1:]).astype(jnp.int32).reshape(1)

    texts = [swapped(text_embed, total, step * group) for step in range(1, spread)]
    got_feats = [swapped(image_feats, total, 2 * step) for step in range(1, group // 2)]
    own_text, scalars = pl.pallas_call(
        own_kernel,
        in_specs=[SMEM] * 2 + [VMEM],
        out_specs=[VMEM] * 2,
        out_shape=[jax.ShapeDtypeStruct((rows, width), BF16), jax.ShapeDtypeStruct((8, LANES), F32)],
        compiler_params=limit(4),
        cost_estimate=hint(10**10),
        name="own_text",
    )(log_scale, logit_bias, text_embed)
    own_half = pl.pallas_call(
        stack_kernel,
        in_specs=[SMEM] + [VMEM] * (group // 2),
        out_specs=VMEM,
        out_shape=jax.ShapeDtypeStruct((images // 2, width), BF16),
        compiler_params=limit(4),
        name="stack",
    )(member, image_feats, *got_feats)
    got_half = swapped(own_half, total, 1)
    own_proj = pl.pallas_call(
        project_kernel,
        in_specs=[VMEM] * 2,
        out_specs=VMEM,
        out_shape=jax.ShapeDtypeStruct((images // 2, width), F32),
        compiler_params=limit(8),
        name="own_projection",
    )(own_half, proj_weight)
    own_proj, *texts = lax.optimization_barrier((own_proj, *texts[::-1]))
    text_emb = pl.pallas_call(
        text_kernel,
        in_specs=[VMEM] * spread,
        out_specs=VMEM,
        out_shape=jax.ShapeDtypeStruct((spread * rows, width), BF16),
        compiler_params=limit(4 if spread <= 4 else 16),
        cost_estimate=hint(10**10),
        name="text_unit",
    )(own_text, *texts)

    results = pl.pallas_call(
        functools.partial(pair_kernel, narrow, group),
        in_specs=[SMEM] + [VMEM] * 6,
        out_specs=[VMEM] * 7,
        out_shape=[
            jax.ShapeDtypeStruct((images, width), BF16),
            jax.ShapeDtypeStruct((1, images), F32),
            jax.ShapeDtypeStruct((width, images), BF16),
            jax.ShapeDtypeStruct((spread * rows, images), BF16),
            jax.ShapeDtypeStruct((group // 2, share + 8, images), F32),
        ]
        + [jax.ShapeDtypeStruct((group // 4, share + STAT_ROWS, images), BF16)] * 2,
        scratch_shapes=[
            pltpu.VMEM((width, images), F32),
            pltpu.VMEM((width, images), F32),
            pltpu.VMEM((images, width), F32),
        ],
        compiler_params=limit(24 if spread <= 4 else 40),
        name="pairs",
    )(member, scalars, proj_weight, own_half, own_proj, got_half, text_emb)
    all_feats, inv_part, img_emb, grad_tile, own_part, near_part, far_part = results
    got_far = swapped(far_part, total, 1)
    got_near = swapped(near_part, total, 1)
    feats_t, own_text, *sent_text = pl.pallas_call(
        functools.partial(caption_kernel, rows),
        in_specs=[VMEM] * 3,
        out_specs=[VMEM] * (1 + spread),
        out_shape=[jax.ShapeDtypeStruct((width, images), BF16), jax.ShapeDtypeStruct((rows, width), F32)]
        + [jax.ShapeDtypeStruct((rows, width), BF16)] * (spread - 1),
        compiler_params=limit(12 if spread <= 4 else 32),
        name="captions",
    )(grad_tile, img_emb, all_feats)
    own_part, got_far, sent_text = lax.optimization_barrier((own_part, got_far, sent_text))
    sent_block = jax.ShapeDtypeStruct((share + STAT_ROWS, images), BF16)
    kept_block = jax.ShapeDtypeStruct((share + 8, images), F32)
    half = group // 4
    far = pl.pallas_call(
        functools.partial(chip_kernel, half),
        in_specs=[VMEM] * 2,
        out_specs=[VMEM] * half,
        out_shape=[sent_block] * half,
        compiler_params=limit(8),
        name="chip_far",
    )(own_part, got_far)
    far = [swapped(value, total, 2 * (half + index)) for index, value in enumerate(far)]
    got_text = [swapped(value, total, step * group) for step, value in enumerate(sent_text, 1)]
    own_part, *near = pl.pallas_call(
        functools.partial(chip_kernel, 0),
        in_specs=[VMEM] * 2,
        out_specs=[VMEM] * half,
        out_shape=[kept_block] + [sent_block] * (half - 1),
        compiler_params=limit(8),
        name="chip_near",
    )(own_part, got_near)
    near = [swapped(value, total, 2 * index) for index, value in enumerate(near, 1)]
    own_part = pl.pallas_call(
        far_sum_kernel,
        in_specs=[VMEM] * (1 + half),
        out_specs=VMEM,
        out_shape=kept_block,
        compiler_params=limit(8),
        cost_estimate=hint(5 * 10**8),
        name="far_sum",
    )(own_part, *far)

    out_rows = width // wide
    rest = share - LANES
    packed = out_rows + 2 * rest
    direct = LANES < out_rows <= 2 * LANES and out_rows % 16 == 0 and rest % 16 == 0
    if direct:
        loss_line, sent_weight = pl.pallas_call(
            functools.partial(weight_kernel, group, wide),
            in_specs=[VMEM] * (3 + group // 4),
            out_specs=[VMEM] * 2,
            out_shape=[
                jax.ShapeDtypeStruct((1, images), F32),
                jax.ShapeDtypeStruct((wide, packed, LANES), BF16),
            ],
            compiler_params=limit(12),
            name="weights",
        )(own_part, *near, inv_part, all_feats, feats_t)
        got_weight = lax.all_to_all(sent_weight, AXES[:2], 0, 0)
        d_proj = pl.pallas_call(
            functools.partial(total_kernel, rest),
            in_specs=[VMEM],
            out_specs=VMEM,
            out_shape=jax.ShapeDtypeStruct((out_rows, 2 * share), F32),
            compiler_params=limit(4),
            name="weight_total",
        )(got_weight)
    else:

        def gradient_kernel(*refs):
            own_ref, blocks = refs[0], refs[1 : group // 4]
            inv_ref, loss_out, d_out = refs[group // 4 :]
            d_out[...] = gathered_gradient(own_ref, blocks, inv_ref, loss_out)

        loss_line, d_zproj = pl.pallas_call(
            gradient_kernel,
            in_specs=[VMEM] * (1 + group // 4),
            out_specs=[VMEM] * 2,
            out_shape=[jax.ShapeDtypeStruct((1, images), F32), jax.ShapeDtypeStruct((share, images), F32)],
            compiler_params=limit(12),
            name="gradient",
        )(own_part, *near, inv_part)
        partial = sum(
            lax.dot_general(feats_t, part, NT, preferred_element_type=F32) for part in split_pair(d_zproj)
        )
        left = lax.axis_index("inner") == 0
        both = jnp.concatenate([jnp.where(left, partial, 0.0), jnp.where(left, 0.0, partial)], axis=1)
        d_proj = lax.psum_scatter(both, AXES[:2], scatter_dimension=0, tiled=True)

    d_text_unit = pl.pallas_call(
        sum_kernel,
        in_specs=[VMEM] * spread,
        out_specs=VMEM,
        out_shape=jax.ShapeDtypeStruct((rows, width), F32),
        compiler_params=limit(12),
        cost_estimate=hint(5 * 10**9),
        name="caption_total",
    )(own_text, *got_text[1:], got_text[0])
    image_loss = lax.dynamic_slice_in_dim(loss_line[0], first_image(member[0], rows, group), rows, 0)
    return (image_loss, d_text_unit, d_proj)


def solution(mesh):
    wide, narrow = mesh.shape["wide"], mesh.shape["narrow"]
    cut = jax.sharding.Mesh(mesh.devices.reshape(wide // 2, 2, narrow), AXES)
    placed = (P(AXES, None), P(), P(AXES, None), P(), P())
    return jax.shard_map(
        functools.partial(local, wide, narrow),
        mesh=cut,
        in_specs=placed,
        out_specs=(P(AXES), P(AXES, None), P(AXES[:2], "narrow")),
        check_vma=False,
    )
```

```python
import functools

import jax
import jax.numpy as jnp
from jax import lax
from jax.experimental import pallas as pl
from jax.experimental.pallas import tpu as pltpu
from jax.sharding import PartitionSpec as P

AXES = ("outer", "inner", "narrow")
F32 = jnp.float32
BF16 = jnp.bfloat16
LANES = 128
STAT_ROWS = 16
VMEM = pl.BlockSpec(memory_space=pltpu.VMEM)
SMEM = pl.BlockSpec(memory_space=pltpu.SMEM)
NT = (((1,), (1,)), ((), ()))
TN = (((0,), (0,)), ((), ()))
MIB = 1024 * 1024


def limit(mebibytes):
    return pltpu.CompilerParams(vmem_limit_bytes=mebibytes * MIB)


def hint(flops):
    return pl.CostEstimate(flops=flops, bytes_accessed=0, transcendentals=0)


def swapped(value, total, mask):
    return lax.ppermute(value, AXES, [(source, source ^ mask) for source in range(total)])


def split_pair(values):
    high = values.astype(BF16)
    return high, (values - high.astype(F32)).astype(BF16)


def loss_rows(loss):
    row = lax.broadcasted_iota(jnp.int32, (STAT_ROWS, loss.shape[1]), 0)
    high, low = split_pair(loss)
    rows = jnp.where(row == 0, high.astype(F32), jnp.where(row == 1, low.astype(F32), 0.0))
    return rows.astype(BF16)


def loss_of(rows):
    rows = rows.astype(F32)
    return rows[0:1, :] + rows[1:2, :]


def column_block(member, narrow):
    return (member % narrow) * 2 + member // narrow


def unit_text(text):
    values = text.astype(F32)
    inverse = lax.rsqrt(jnp.sum(values * values, axis=1, keepdims=True) + 1e-06)
    return (values * inverse).astype(BF16)


def own_kernel(log_scale_ref, bias_ref, text_ref, text_out, scalars_out):
    text_out[...] = unit_text(text_ref[...])
    row = lax.broadcasted_iota(jnp.int32, scalars_out.shape, 0)
    scale = jnp.exp(jnp.full(scalars_out.shape, log_scale_ref[0], F32))
    scalars_out[...] = jnp.where(row == 0, scale, bias_ref[0])


def stack_kernel(member_ref, *refs):
    blocks, half_out = refs[:-1], refs[-1]
    rows = blocks[0].shape[0]
    chip = member_ref[0] // 2
    for step, block in enumerate(blocks):
        place = pl.multiple_of((chip ^ step) * rows, rows)
        half_out[pl.ds(place, rows), :] = block[...]


def text_kernel(*refs):
    texts, out = refs[:-1], refs[-1]
    rows = texts[0].shape[0]
    out[:rows, :] = texts[0][...]
    for place, text in enumerate(texts[1:], 1):
        step = len(texts) - place
        out[step * rows : (step + 1) * rows, :] = unit_text(text[...])


def project_kernel(feats_ref, weight_ref, out):
    out[...] = jnp.dot(feats_ref[...], weight_ref[...], preferred_element_type=F32)


def first_image(member, rows, group):
    return (member % 2) * (group // 2 * rows) + (member // 2) * rows


def pair_kernel(
    narrow,
    group,
    member_ref,
    scalars_ref,
    weight,
    own_half,
    own_proj,
    got_half,
    text_all,
    feats_ref,
    inv_out,
    emb_out,
    grad_out,
    own_out,
    near_out,
    far_out,
    unit_all,
    d_all,
    proj_all,
):
    images, width = feats_ref.shape
    rows = images // group
    spread = text_all.shape[0] // rows
    half = images // 2
    share = width // group
    member = member_ref[0]

    place = pl.multiple_of((member % 2) * half, half)
    feats_ref[pl.ds(place, half), :] = own_half[...]
    proj_all[pl.ds(place, half), :] = own_proj[...]
    place = pl.multiple_of((1 - member % 2) * half, half)
    feats_ref[pl.ds(place, half), :] = got_half[...]
    proj_all[pl.ds(place, half), :] = jnp.dot(got_half[...], weight[...], preferred_element_type=F32)
    for start in range(0, images, LANES):
        cols = slice(start, start + LANES)
        turned = proj_all[cols, :].T
        inverse = lax.rsqrt(jnp.sum(turned * turned, axis=0, keepdims=True) + 1e-06)
        unit = turned * inverse
        inv_out[:, cols] = inverse
        unit_all[:, cols] = unit
        emb_out[:, cols] = unit.astype(BF16)

    scale = scalars_ref[0:1, 0:1]
    shift = scalars_ref[1:2, 0:1]
    count = 4 * rows if spread % 4 == 0 else rows
    chunks = spread * rows // count

    def one_chunk(chunk, loss_sum, dot_sum, first):
        here = pl.ds(pl.multiple_of(chunk * count, count), count)
        text = text_all[here, :]
        products = jnp.dot(text, emb_out[...], preferred_element_type=F32)
        logits = scale * products + shift
        caption = lax.broadcasted_iota(jnp.int32, (count, images), 0) + chunk * count
        image = lax.broadcasted_iota(jnp.int32, (count, images), 1)
        own = jnp.logical_and(caption < rows, image == first_image(member, rows, group) + caption)
        sign = jnp.where(own, 1.0, -1.0).astype(F32)
        away = -sign * logits
        small = jnp.exp(-jnp.abs(away))
        loss = jnp.maximum(away, 0.0) + jnp.log1p(small)
        chance = jnp.where(away >= 0.0, 1.0, small) / (1.0 + small)
        grad = (-scale * sign * chance).astype(BF16)
        grad_out[here, :] = grad
        loss_sum = loss_sum + jnp.sum(loss, axis=0, keepdims=True)
        dot_sum = dot_sum + jnp.sum(grad.astype(F32) * products, axis=0, keepdims=True)
        d_img = lax.dot_general(text, grad, TN, preferred_element_type=F32)
        if first:
            d_all[...] = d_img
        else:
            d_all[...] += d_img
        return loss_sum, dot_sum

    zero = jnp.zeros((1, images), F32)
    sums = one_chunk(0, zero, zero, True)
    if chunks > 1:
        sums = lax.fori_loop(1, chunks, lambda c, s: one_chunk(c, *s, False), sums)
    loss_sum, dot_sum = sums

    def projected(index):
        part = pl.ds(pl.multiple_of(column_block(member ^ index, narrow) * share, share), share)
        return d_all[part, :] - unit_all[part, :] * dot_sum

    losses = loss_rows(loss_sum)
    for index in range(group // 2):
        own_out[index, :share, :] = projected(2 * index)
        target = (near_out, far_out)[index * 4 // group].at[index % (group // 4)]
        target[:share, :] = projected(2 * index + 1).astype(BF16)
        target[share:, :] = losses
    own_out[0, share : share + 1, :] = loss_sum


def chip_kernel(first, own_ref, got_ref, *outs):
    share = own_ref.shape[1] - 8
    loss = own_ref[0, share : share + 1, :] + loss_of(got_ref[0, share:, :])
    for index, target in enumerate(outs):
        total = own_ref[first + index, :share, :] + got_ref[index, :share, :].astype(F32)
        target[:share, :] = total.astype(target.dtype)
        if target.dtype == BF16:
            target[share:, :] = loss_rows(loss)
        else:
            target[share : share + 1, :] = loss


def caption_kernel(rows, grad_ref, emb_ref, feats_ref, feats_t, *outs):
    product = lax.dot_general(grad_ref[...], emb_ref[...], NT, preferred_element_type=F32)
    for step, target in enumerate(outs):
        target[...] = product[step * rows : (step + 1) * rows, :].astype(target.dtype)
    for start in range(0, feats_ref.shape[0], LANES):
        cols = slice(start, start + LANES)
        feats_t[:, cols] = feats_ref[cols, :].astype(F32).T.astype(BF16)


def far_sum_kernel(*refs):
    own_ref, got, out = refs[0], refs[1:-1], refs[-1]
    share = own_ref.shape[0] - 8
    total, loss = own_ref[:share, :], own_ref[share : share + 1, :]
    for block in got:
        total = total + block[:share, :].astype(F32)
        loss = loss + loss_of(block[share:, :])
    out[:share, :] = total
    out[share : share + 1, :] = loss


def gathered_gradient(own_ref, got, inv_ref, loss_out):
    share = own_ref.shape[0] - 8
    total = own_ref[:share, :]
    loss = own_ref[share : share + 1, :]
    for block in got:
        total = total + block[:share, :].astype(F32)
        loss = loss + loss_of(block[share:, :])
    loss_out[...] = loss
    return inv_ref[...] * total


def weight_kernel(group, wide, *refs):
    own_ref, got = refs[0], refs[1 : group // 4]
    inv_ref, feats_ref, feats_t_ref, loss_out, send_out = refs[group // 4 :]
    rows = feats_t_ref.shape[0] // wide
    high, low = split_pair(gathered_gradient(own_ref, got, inv_ref, loss_out))
    rest = high.shape[0] - LANES
    both = jnp.concatenate([high[LANES:, :], low[LANES:, :]], axis=0)
    tail = jnp.dot(both, feats_ref[...], preferred_element_type=F32)
    tail = (tail[:rest, :] + tail[rest:, :]).astype(BF16)
    both = jnp.concatenate([high[:LANES, :], low[:LANES, :]], axis=0)
    main = lax.dot_general(feats_t_ref[...], both, NT, preferred_element_type=F32)
    main = (main[:, :LANES] + main[:, LANES:]).astype(BF16)
    for place in range(wide):
        begin = place * rows
        send_out[place, :rows, :] = main[begin : begin + rows, :]
        send_out[place, rows : rows + rest, :] = tail[:, begin : begin + LANES]
        send_out[place, rows + rest :, :] = jnp.zeros((rest, LANES), BF16)
        send_out[place, rows + rest :, : rows - LANES] = tail[:, begin + LANES : begin + rows]


def total_kernel(rest, got_ref, out):
    rows = out.shape[0]
    for side in range(2):
        half = got_ref[side].astype(F32)
        for place in range(side + 2, got_ref.shape[0], 2):
            half = half + got_ref[place].astype(F32)
        left = side * (LANES + rest)
        out[:, left : left + LANES] = half[:rows, :]
        out[:LANES, left + LANES : left + LANES + rest] = half[rows : rows + rest, :].T
        out[LANES:, left + LANES : left + LANES + rest] = half[rows + rest :, :].T[: rows - LANES, :]


def sum_kernel(*refs):
    total = refs[0][...]
    for block in refs[1:-1]:
        total = total + block[...].astype(F32)
    refs[-1][...] = total


def local(wide, narrow, image_feats, proj_weight, text_embed, log_scale, logit_bias):
    rows, width = image_feats.shape
    total = wide * narrow
    group = 2 * narrow
    spread = wide // 2
    share = width // group
    images = group * rows
    member = lax.axis_index(AXES[1:]).astype(jnp.int32).reshape(1)

    texts = [swapped(text_embed, total, step * group) for step in range(1, spread)]
    got_feats = [swapped(image_feats, total, 2 * step) for step in range(1, group // 2)]
    own_text, scalars = pl.pallas_call(
        own_kernel,
        in_specs=[SMEM] * 2 + [VMEM],
        out_specs=[VMEM] * 2,
        out_shape=[jax.ShapeDtypeStruct((rows, width), BF16), jax.ShapeDtypeStruct((8, LANES), F32)],
        compiler_params=limit(4),
        cost_estimate=hint(10**10),
        name="own_text",
    )(log_scale, logit_bias, text_embed)
    own_half = pl.pallas_call(
        stack_kernel,
        in_specs=[SMEM] + [VMEM] * (group // 2),
        out_specs=VMEM,
        out_shape=jax.ShapeDtypeStruct((images // 2, width), BF16),
        compiler_params=limit(4),
        name="stack",
    )(member, image_feats, *got_feats)
    got_half = swapped(own_half, total, 1)
    own_proj = pl.pallas_call(
        project_kernel,
        in_specs=[VMEM] * 2,
        out_specs=VMEM,
        out_shape=jax.ShapeDtypeStruct((images // 2, width), F32),
        compiler_params=limit(8),
        name="own_projection",
    )(own_half, proj_weight)
    own_proj, *texts = lax.optimization_barrier((own_proj, *texts[1:], texts[0]))
    texts = [*texts[-2::-1], texts[-1]]
    text_emb = pl.pallas_call(
        text_kernel,
        in_specs=[VMEM] * spread,
        out_specs=VMEM,
        out_shape=jax.ShapeDtypeStruct((spread * rows, width), BF16),
        compiler_params=limit(4 if spread <= 4 else 16),
        cost_estimate=hint(10**10),
        name="text_unit",
    )(own_text, *texts)

    results = pl.pallas_call(
        functools.partial(pair_kernel, narrow, group),
        in_specs=[SMEM] + [VMEM] * 6,
        out_specs=[VMEM] * 7,
        out_shape=[
            jax.ShapeDtypeStruct((images, width), BF16),
            jax.ShapeDtypeStruct((1, images), F32),
            jax.ShapeDtypeStruct((width, images), BF16),
            jax.ShapeDtypeStruct((spread * rows, images), BF16),
            jax.ShapeDtypeStruct((group // 2, share + 8, images), F32),
        ]
        + [jax.ShapeDtypeStruct((group // 4, share + STAT_ROWS, images), BF16)] * 2,
        scratch_shapes=[
            pltpu.VMEM((width, images), F32),
            pltpu.VMEM((width, images), F32),
            pltpu.VMEM((images, width), F32),
        ],
        compiler_params=limit(24 if spread <= 4 else 40),
        name="pairs",
    )(member, scalars, proj_weight, own_half, own_proj, got_half, text_emb)
    all_feats, inv_part, img_emb, grad_tile, own_part, near_part, far_part = results
    got_far = swapped(far_part, total, 1)
    got_near = swapped(near_part, total, 1)
    feats_t, own_text, *sent_text = pl.pallas_call(
        functools.partial(caption_kernel, rows),
        in_specs=[VMEM] * 3,
        out_specs=[VMEM] * (1 + spread),
        out_shape=[jax.ShapeDtypeStruct((width, images), BF16), jax.ShapeDtypeStruct((rows, width), F32)]
        + [jax.ShapeDtypeStruct((rows, width), BF16)] * (spread - 1),
        compiler_params=limit(12 if spread <= 4 else 32),
        name="captions",
    )(grad_tile, img_emb, all_feats)
    own_part, got_far, sent_text = lax.optimization_barrier((own_part, got_far, sent_text))
    sent_block = jax.ShapeDtypeStruct((share + STAT_ROWS, images), BF16)
    kept_block = jax.ShapeDtypeStruct((share + 8, images), F32)
    half = group // 4
    far = pl.pallas_call(
        functools.partial(chip_kernel, half),
        in_specs=[VMEM] * 2,
        out_specs=[VMEM] * half,
        out_shape=[sent_block] * half,
        compiler_params=limit(8),
        name="chip_far",
    )(own_part, got_far)
    far = [swapped(value, total, 2 * (half + index)) for index, value in enumerate(far)]
    got_text = [swapped(value, total, step * group) for step, value in enumerate(sent_text, 1)]
    own_part, *near = pl.pallas_call(
        functools.partial(chip_kernel, 0),
        in_specs=[VMEM] * 2,
        out_specs=[VMEM] * half,
        out_shape=[kept_block] + [sent_block] * (half - 1),
        compiler_params=limit(8),
        name="chip_near",
    )(own_part, got_near)
    near = [swapped(value, total, 2 * index) for index, value in enumerate(near, 1)]
    own_part = pl.pallas_call(
        far_sum_kernel,
        in_specs=[VMEM] * (1 + half),
        out_specs=VMEM,
        out_shape=kept_block,
        compiler_params=limit(8),
        cost_estimate=hint(5 * 10**8),
        name="far_sum",
    )(own_part, *far)

    out_rows = width // wide
    rest = share - LANES
    packed = out_rows + 2 * rest
    direct = LANES < out_rows <= 2 * LANES and out_rows % 16 == 0 and rest % 16 == 0
    if direct:
        loss_line, sent_weight = pl.pallas_call(
            functools.partial(weight_kernel, group, wide),
            in_specs=[VMEM] * (3 + group // 4),
            out_specs=[VMEM] * 2,
            out_shape=[
                jax.ShapeDtypeStruct((1, images), F32),
                jax.ShapeDtypeStruct((wide, packed, LANES), BF16),
            ],
            compiler_params=limit(12),
            name="weights",
        )(own_part, *near, inv_part, all_feats, feats_t)
        got_weight = lax.all_to_all(sent_weight, AXES[:2], 0, 0)
        d_proj = pl.pallas_call(
            functools.partial(total_kernel, rest),
            in_specs=[VMEM],
            out_specs=VMEM,
            out_shape=jax.ShapeDtypeStruct((out_rows, 2 * share), F32),
            compiler_params=limit(4),
            name="weight_total",
        )(got_weight)
    else:

        def gradient_kernel(*refs):
            own_ref, blocks = refs[0], refs[1 : group // 4]
            inv_ref, loss_out, d_out = refs[group // 4 :]
            d_out[...] = gathered_gradient(own_ref, blocks, inv_ref, loss_out)

        loss_line, d_zproj = pl.pallas_call(
            gradient_kernel,
            in_specs=[VMEM] * (1 + group // 4),
            out_specs=[VMEM] * 2,
            out_shape=[jax.ShapeDtypeStruct((1, images), F32), jax.ShapeDtypeStruct((share, images), F32)],
            compiler_params=limit(12),
            name="gradient",
        )(own_part, *near, inv_part)
        partial = sum(
            lax.dot_general(feats_t, part, NT, preferred_element_type=F32) for part in split_pair(d_zproj)
        )
        left = lax.axis_index("inner") == 0
        both = jnp.concatenate([jnp.where(left, partial, 0.0), jnp.where(left, 0.0, partial)], axis=1)
        d_proj = lax.psum_scatter(both, AXES[:2], scatter_dimension=0, tiled=True)

    d_text_unit = pl.pallas_call(
        sum_kernel,
        in_specs=[VMEM] * spread,
        out_specs=VMEM,
        out_shape=jax.ShapeDtypeStruct((rows, width), F32),
        compiler_params=limit(12),
        cost_estimate=hint(5 * 10**9),
        name="caption_total",
    )(own_text, *got_text[1:], got_text[0])
    image_loss = lax.dynamic_slice_in_dim(loss_line[0], first_image(member[0], rows, group), rows, 0)
    return (image_loss, d_text_unit, d_proj)


def solution(mesh):
    wide, narrow = mesh.shape["wide"], mesh.shape["narrow"]
    cut = jax.sharding.Mesh(mesh.devices.reshape(wide // 2, 2, narrow), AXES)
    placed = (P(AXES, None), P(), P(AXES, None), P(), P())
    return jax.shard_map(
        functools.partial(local, wide, narrow),
        mesh=cut,
        in_specs=placed,
        out_specs=(P(AXES), P(AXES, None), P(AXES[:2], "narrow")),
        check_vma=False,
    )
```
